32 devices in a mesh: dp: 16 (over z, y, x), tensor: 2 (over core).
Axes of the slice: x: 2, y: 2, z: 4, core: 2. Of those that a mesh axis runs over, the one named last changes fastest.
Arguments:
- tokens: bfloat16 [4096, 1024], P(('dp', 'tensor')), may hold values from -6 to 6
- lengths: int32 [16, 4], P('dp'), may hold values from 0 to 160, as said below
- attn_gain: float32 [1024], replicated, may hold values from 0.1 to 1.9
- query_gain: float32 [64], replicated, may hold values from 0.1 to 1.9
- key_gain: float32 [64], replicated, may hold values from 0.1 to 1.9
- ffn_gain: float32 [1024], replicated, may hold values from 0.1 to 1.9
- w_query: bfloat16 [1024, 1024], P('dp', 'tensor'), may hold values from -0.1875 to 0.1875
- w_key: bfloat16 [1024, 512], P('dp', 'tensor'), may hold values from -0.1875 to 0.1875
- w_value: bfloat16 [1024, 512], P('dp', 'tensor'), may hold values from -0.1875 to 0.1875
- w_out: bfloat16 [1024, 1024], P('dp', 'tensor'), may hold values from -0.75 to 0.75
- w_gate: bfloat16 [1024, 4608], P('dp', 'tensor'), may hold values from -0.1875 to 0.1875
- w_up: bfloat16 [1024, 4608], P('dp', 'tensor'), may hold values from -0.1875 to 0.1875
- w_down: bfloat16 [1024, 4608], P('dp', 'tensor'), may hold values from -0.09375 to 0.09375
- cotangent: bfloat16 [4096, 1024], P(('dp', 'tensor')), may hold values from -8 to 8
Outputs:
- block_out: bfloat16 [4096, 1024], P(('dp', 'tensor'))
- grad_tokens: float32 [4096, 1024], P(('dp', 'tensor'))
- grad_attn_gain: float32 [1024], replicated
- grad_query_gain: float32 [64], replicated
- grad_key_gain: float32 [64], replicated
- grad_ffn_gain: float32 [1024], replicated
- grad_w_query: float32 [1024, 1024], P('dp', 'tensor')
- grad_w_key: float32 [1024, 512], P('dp', 'tensor')
- grad_w_value: float32 [1024, 512], P('dp', 'tensor')
- grad_w_out: float32 [1024, 1024], P('dp', 'tensor')
- grad_w_gate: float32 [1024, 4608], P('dp', 'tensor')
- grad_w_up: float32 [1024, 4608], P('dp', 'tensor')
- grad_w_down: float32 [1024, 4608], P('dp', 'tensor')
The draws below stay inside these ranges and needn't reach their ends.
Inputs may be any that keep to these rules, and one draw needn't show every extreme that they name: `lengths`: row g belongs to dp index g. Its entries sum to between 192 and 256, both reached in every draw; exactly one entry of each row is longer than 128, and 160 is reached in every draw.
All inputs are finite; a program needn't handle non-finite values.
Results may differ from the reference program's by a relative error of at most 0.015.
Values may be sent and summed in bfloat16 or wider, within the bound.
No kernel may reach another device: no remote copies, remote signals or barrier semaphores. Data moves between devices by JAX's collectives and lax.ppermute only.
A program may use at most 128 MiB of HBM per device.

```python
import math
import jax
import jax.numpy as jnp
from jax import lax

D = 1024
HEADS = 16
KV_HEADS = 8
HEAD_DIM = 64
FF = 4608
TOK_DEV = 128
SLOTS = 4
GROUP = 256
TOKENS = 4096
N_DP = 16


def draw_lengths(key, part):
    key = jax.random.fold_in(key, 11)
    keys = jax.random.split(key, 6)
    groups = jnp.arange(N_DP, dtype=jnp.int32)
    full = jax.random.randint(keys[0], (), 0, N_DP)
    emptiest = (full + 1) % N_DP
    padding = jax.random.randint(keys[1], (N_DP,), 0, TOK_DEV // 2 + 1)
    padding = jnp.where(groups == full, 0, padding)
    padding = jnp.where(groups == emptiest, TOK_DEV // 2, padding)
    extra = jax.random.randint(keys[2], (N_DP,), 1, TOK_DEV // 4 + 1)
    extra = jnp.where(groups == full, TOK_DEV // 4, extra)
    longest = TOK_DEV + extra
    rest = 2 * TOK_DEV - padding - longest
    cut_one = jax.random.randint(keys[3], (N_DP,), 0, rest + 1)
    cut_two = jax.random.randint(keys[4], (N_DP,), 0, rest + 1)
    lower = jnp.minimum(cut_one, cut_two)
    upper = jnp.maximum(cut_one, cut_two)
    shorter = jnp.stack([lower, upper - lower, rest - upper], axis=1)
    slot = jax.random.randint(keys[5], (N_DP,), 0, 4)
    slot_ids = jnp.arange(4, dtype=jnp.int32)[None, :]
    zero_col = jnp.zeros((N_DP, 1), jnp.int32)
    same_place = jnp.concatenate([shorter, zero_col], axis=1)
    moved = jnp.concatenate([zero_col, shorter], axis=1)
    result = jnp.where(slot_ids == slot[:, None], longest[:, None], jnp.where(slot_ids < slot[:, None], same_place, moved))
    return result.astype(jnp.int32)


def draw_cotangent(key, part):
    key = jax.random.fold_in(key, 23)
    place = jnp.arange(TOKENS, dtype=jnp.float32)[:, None] / TOKENS
    base = jnp.clip(jax.random.normal(key, (TOKENS, D), jnp.float32), -5.0, 5.0)
    factor = 0.5 + place
    return (base * factor).astype(jnp.bfloat16)


def with_spikes(array, rng, source, target, shards_of, factor):
    def block_of(dim):
        return (jnp.arange(array.shape[dim]) // (array.shape[dim] // shards_of)).reshape((-1,) + (1,) * (array.ndim - 1 - dim))

    near = jax.random.permutation(rng, shards_of)[block_of(target)]
    far = (block_of(target) + shards_of // 2) % shards_of
    return jnp.where((block_of(source) == near) | (block_of(source) == far), factor * array, array)


def shard_levels(key, shape, pieces, smallest, largest):
    level = 1.0
    for axis_at, shards_of in pieces:
        heights = jax.random.uniform(jax.random.fold_in(jax.random.fold_in(key, 6), axis_at), (shards_of,), jnp.float32, smallest / len(pieces), largest / len(pieces))
        level = level * jnp.repeat(jnp.exp(heights), shape[axis_at] // shards_of).reshape((-1,) + (1,) * (len(shape) - 1 - axis_at))
    return level


def gaussian(stream_key, dims, spread, most, cuts=(), kind=jnp.bfloat16):
    values = jax.random.normal(stream_key, dims, jnp.float32) * spread
    if len(cuts) > 0:
        values = shard_levels(stream_key, dims, cuts, -0.22, 0.18) * values
    return jnp.clip(values, min=-most, max=most).astype(kind)


def gaussian_with(rng, dims, scale, limit, shards, heavy, kind=jnp.bfloat16):
    values = scale * jax.random.normal(rng, dims, jnp.float32)
    if shards:
        values = values * shard_levels(rng, dims, shards, -0.22, 0.18)
    return jnp.clip(with_spikes(values, jax.random.fold_in(rng, 3), *heavy), -limit, limit).astype(kind)


def setup_inputs(seed: int = 0) -> dict:
    seeds = jax.random.split(jax.random.key(seed), 15)
    tokens = gaussian_with(seeds[0], (TOKENS, D), 1.0, 6.0, ((0, 32),), (0, 1, 32, 2.75))
    lengths = draw_lengths(jax.random.fold_in(seeds[14], 71), 0)
    attn_gain = jnp.clip(1.0 + 0.18 * jax.random.normal(seeds[2], (D,), jnp.float32), 0.1, 1.9)
    query_gain = jnp.clip(1.0 + 0.18 * jax.random.normal(seeds[3], (HEAD_DIM,), jnp.float32), 0.1, 1.9)
    key_gain = jnp.clip(1.0 + 0.18 * jax.random.normal(seeds[4], (HEAD_DIM,), jnp.float32), 0.1, 1.9)
    ffn_gain = jnp.clip(1.0 + 0.18 * jax.random.normal(seeds[5], (D,), jnp.float32), 0.1, 1.9)
    w_query = gaussian(seeds[6], (D, HEADS * HEAD_DIM), D ** -0.5, 0.1875, ((0, 16), (1, 2)))
    w_key = gaussian(seeds[7], (D, KV_HEADS * HEAD_DIM), D ** -0.5, 0.1875, ((0, 16), (1, 2)))
    w_value = gaussian(seeds[8], (D, KV_HEADS * HEAD_DIM), D ** -0.5, 0.1875, ((0, 16), (1, 2)))
    w_out = gaussian(seeds[9], (D, HEADS * HEAD_DIM), HEAD_DIM ** -0.5, 0.75, ((0, 16), (1, 2)))
    w_gate = gaussian(seeds[10], (D, FF), D ** -0.5, 0.1875, ((0, 16), (1, 2)))
    w_up = gaussian(seeds[11], (D, FF), D ** -0.5, 0.1875, ((0, 16), (1, 2)))
    w_down = gaussian(seeds[12], (D, FF), FF ** -0.5, 0.09375, ((0, 16), (1, 2)))
    cotangent = draw_cotangent(jax.random.fold_in(seeds[14], 71), 0)
    return {"tokens": tokens, "lengths": lengths, "attn_gain": attn_gain, "query_gain": query_gain, "key_gain": key_gain, "ffn_gain": ffn_gain, "w_query": w_query, "w_key": w_key, "w_value": w_value, "w_out": w_out, "w_gate": w_gate, "w_up": w_up, "w_down": w_down, "cotangent": cotangent}


@jax.custom_vjp
def low(v):
    return lax.optimization_barrier(v.astype(jnp.bfloat16)).astype(jnp.float32)

@jax.custom_vjp
def low_back(v):
    return v

def low_keep(v):
    return (low(v), None)

def low_pass(kept, grad):
    return (grad,)

def back_keep(v):
    return (v, None)

def back_low(kept, grad):
    return (low(grad),)
low.defvjp(low_keep, low_pass)
low_back.defvjp(back_keep, back_low)
epsilon = 1e-05
rope_base = 1000000.0
masked_score = -1e+30
highest = lax.Precision.HIGHEST

def rms_norm(values):
    return values * lax.rsqrt(lax.optimization_barrier(jnp.mean(values * values, axis=-1, keepdims=True)) + epsilon)

def matmul(first_op, second_op):
    return jnp.dot(first_op, second_op, precision=highest, preferred_element_type=jnp.float32)

def seq_layout(seq_lengths, total_rows):
    ends = jnp.cumsum(seq_lengths, dtype=jnp.int32)
    starts = ends - seq_lengths
    row_ids = jnp.arange(total_rows, dtype=jnp.int32)
    segment = lax.optimization_barrier(jnp.sum((row_ids[:, None] >= ends[None, :]).astype(jnp.int32), axis=1, dtype=jnp.int32))
    slot_ids = jnp.arange(seq_lengths.shape[0], dtype=jnp.int32)
    picked = (segment[:, None] == slot_ids[None, :]).astype(jnp.int32)
    begin = lax.optimization_barrier(jnp.sum(picked * starts[None, :], axis=1, dtype=jnp.int32)) + (segment == seq_lengths.shape[0]).astype(jnp.int32) * ends[-1]
    allowed = (segment[:, None] == segment[None, :]) & (row_ids[:, None] >= row_ids[None, :])
    return (row_ids - begin, row_ids < ends[-1], allowed)

def rotate(values, position):
    half_dim = values.shape[-1] // 2
    freqs = rope_base ** (-jnp.arange(half_dim, dtype=jnp.float32) * 2.0 / values.shape[-1])
    angles = position.astype(jnp.float32)[:, None] * freqs[None, :]
    cosine = jnp.cos(angles)[:, None, :]
    sine = jnp.sin(angles)[:, None, :]
    first_half = values[..., :half_dim]
    second_half = values[..., half_dim:]
    return jnp.concatenate([first_half * cosine - second_half * sine, second_half * cosine + first_half * sine], axis=-1)

def group_forward(params, inputs, seq_lengths):
    g_attn, g_query, g_key, g_ffn, w_query, w_key, w_value, w_out, w_gate, w_up, w_down = params
    total_rows = inputs.shape[0]
    position, live, allowed = seq_layout(seq_lengths, total_rows)
    share = HEADS // KV_HEADS
    normed = low(rms_norm(inputs) * g_attn)
    query = low_back(matmul(normed, w_query)).reshape(total_rows, HEADS, HEAD_DIM)
    key_pre = low_back(matmul(normed, w_key)).reshape(total_rows, KV_HEADS, HEAD_DIM)
    value = low(low_back(matmul(normed, w_value))).reshape(total_rows, KV_HEADS, HEAD_DIM)
    query = low(rotate(rms_norm(query) * g_query, position))
    keys = low(rotate(rms_norm(key_pre) * g_key, position))
    grouped = query.reshape(total_rows, KV_HEADS, share, HEAD_DIM)
    scores = jnp.einsum('qgjd,kgd->gjqk', grouped, keys, precision=highest, preferred_element_type=jnp.float32)
    scores = low_back(scores * HEAD_DIM ** (-0.5))
    scores = jnp.where(allowed, scores, masked_score)
    top = lax.optimization_barrier(jnp.max(scores, axis=-1, keepdims=True))
    expd = jnp.exp(scores - top)
    probs = low(expd / lax.optimization_barrier(jnp.sum(expd, axis=-1, keepdims=True)))
    mixed = jnp.einsum('gjqk,kgd->qgjd', probs, value, precision=highest, preferred_element_type=jnp.float32)
    mixed = low(low_back(mixed.reshape(total_rows, HEADS * HEAD_DIM)))
    hidden = inputs + low_back(matmul(mixed, w_out.T))
    normed2 = low(rms_norm(hidden) * g_ffn)
    gate = low_back(matmul(normed2, w_gate))
    up_proj = low_back(matmul(normed2, w_up))
    act = low(gate * jax.nn.sigmoid(gate) * up_proj)
    return hidden + low_back(matmul(act, w_down.T))

def reference(tokens, lengths, attn_gain, query_gain, key_gain, ffn_gain, w_query, w_key, w_value, w_out, w_gate, w_up, w_down, cotangent):
    params = (attn_gain.astype(jnp.float32), query_gain.astype(jnp.float32), key_gain.astype(jnp.float32), ffn_gain.astype(jnp.float32), w_query.astype(jnp.float32), w_key.astype(jnp.float32), w_value.astype(jnp.float32), w_out.astype(jnp.float32), w_gate.astype(jnp.float32), w_up.astype(jnp.float32), w_down.astype(jnp.float32))
    batch = math.gcd(N_DP, max(1, 4096 // GROUP))
    steps_count = N_DP // batch
    inputs = tokens.astype(jnp.float32).reshape(steps_count, batch, GROUP, D)
    cotans = cotangent.astype(jnp.float32).reshape(steps_count, batch, GROUP, D)
    seq_all = lengths.reshape(steps_count, batch, SLOTS)

    def step(totals, item):
        block_in, block_cot, block_len = item

        def forward(weights, rows_in):
            return jax.vmap(group_forward, in_axes=(None, 0, 0))(weights, rows_in, block_len)
        outputs, pull = jax.vjp(forward, params, block_in)
        live = jax.vmap(lambda seq_lengths: seq_layout(seq_lengths, GROUP)[1])(block_len)
        grads, grad_in = pull(block_cot * live[..., None].astype(jnp.float32))
        totals = jax.tree.map(jnp.add, totals, grads)
        return (totals, (outputs.astype(jnp.bfloat16), grad_in))
    zeros = jax.tree.map(jnp.zeros_like, params)
    totals, (outs_all, grads_in) = lax.scan(step, zeros, (inputs, cotans, seq_all))
    return (outs_all.reshape(TOKENS, D), grads_in.reshape(TOKENS, D), totals[0], totals[1], totals[2], totals[3], totals[4], totals[5], totals[6], totals[7], totals[8], totals[9], totals[10])
```

```python
import jax
import jax.numpy as jnp
from jax import lax
from jax.sharding import PartitionSpec as P

HEAD_DIM = 64


epsilon = 1e-05
rope_base = 1000000.0
masked_score = -1e30


def inverse_rms(values):
    return lax.rsqrt(jnp.mean(values * values, axis=-1, keepdims=True) + epsilon)


def norm_back(grad_unit, unit, factor):
    return factor * (grad_unit - unit * jnp.mean(grad_unit * unit, axis=-1, keepdims=True))


def matmul(first_op, second_op):
    return jnp.dot(first_op, second_op, preferred_element_type=jnp.float32)


def matmul_nt(first_op, second_op):
    return lax.dot_general(
        first_op, second_op, (((1,), (1,)), ((), ())), preferred_element_type=jnp.float32
    )


def matmul_tn(first_op, second_op):
    return lax.dot_general(
        first_op, second_op, (((0,), (0,)), ((), ())), preferred_element_type=jnp.float32
    )


def seq_layout(seq_lengths, total_rows):
    ends = jnp.cumsum(seq_lengths, dtype=jnp.int32)
    starts = ends - seq_lengths
    row_ids = jnp.arange(total_rows, dtype=jnp.int32)
    segment = jnp.sum(
        (row_ids[:, None] >= ends[None, :]).astype(jnp.int32), axis=1, dtype=jnp.int32
    )
    slot_ids = jnp.arange(seq_lengths.shape[0], dtype=jnp.int32)
    picked = (segment[:, None] == slot_ids[None, :]).astype(jnp.int32)
    begin = (
        jnp.sum(picked * starts[None, :], axis=1, dtype=jnp.int32)
        + (segment == seq_lengths.shape[0]).astype(jnp.int32) * ends[-1]
    )
    allowed = (segment[:, None] == segment[None, :]) & (row_ids[:, None] >= row_ids[None, :])
    return (row_ids - begin, row_ids < ends[-1], allowed)


def rope_tables(position, head_size):
    half_dim = head_size // 2
    freqs = rope_base ** (-jnp.arange(half_dim, dtype=jnp.float32) * 2.0 / head_size)
    angles = position.astype(jnp.float32)[:, None] * freqs[None, :]
    return (jnp.cos(angles)[:, None, :], jnp.sin(angles)[:, None, :])


def rotate(values, cosine, sine):
    half_dim = values.shape[-1] // 2
    first_half = values[..., :half_dim]
    second_half = values[..., half_dim:]
    return jnp.concatenate(
        [first_half * cosine - second_half * sine, second_half * cosine + first_half * sine],
        axis=-1,
    )


def rotate_back(grads, cosine, sine):
    half_dim = grads.shape[-1] // 2
    first_half = grads[..., :half_dim]
    second_half = grads[..., half_dim:]
    return jnp.concatenate(
        [first_half * cosine + second_half * sine, second_half * cosine - first_half * sine],
        axis=-1,
    )


PLANE = 4


def send_plane(values, mask):
    count = lax.axis_size("dp")
    return lax.ppermute(values, "dp", [(i, i ^ mask) for i in range(count)])


def send_deep(values, step):
    count = lax.axis_size("dp")
    return lax.ppermute(values, "dp", [(i, (i + PLANE * step) % count) for i in range(count)])


def swap_cores(values):
    return lax.ppermute(values, "tensor", [(0, 1), (1, 0)])


def gather_weight(pieces):
    dp = lax.axis_index("dp")
    place, depth = dp % PLANE, dp // PLANE
    layers = lax.axis_size("dp") // PLANE
    _, rows, columns = pieces.shape
    plane = jnp.zeros((PLANE, rows, columns), pieces.dtype)
    for mask in range(PLANE):
        part = lax.dynamic_index_in_dim(pieces, place ^ mask, 0, keepdims=True)
        if mask:
            part = send_plane(part, mask)
        plane = lax.dynamic_update_slice(plane, part, (place ^ mask, 0, 0))
    plane = plane.reshape(1, PLANE * rows, columns)
    whole = jnp.zeros((layers, PLANE * rows, columns), pieces.dtype)
    for step in range(layers):
        part = send_deep(plane, step) if step else plane
        whole = lax.dynamic_update_slice(whole, part, ((depth - step) % layers, 0, 0))
    return whole.reshape(layers * PLANE * rows, columns)


def scatter_weight(partial):
    dp = lax.axis_index("dp")
    place, depth = dp % PLANE, dp // PLANE
    layers = lax.axis_size("dp") // PLANE
    all_rows, columns = partial.shape
    rows = all_rows // layers // PLANE
    partial = partial.reshape(layers, PLANE * rows, columns)
    low = partial.astype(jnp.bfloat16)
    total = lax.dynamic_index_in_dim(partial, depth, 0, keepdims=False)
    for step in range(1, layers):
        part = lax.dynamic_index_in_dim(low, (depth + step) % layers, 0, keepdims=False)
        total = total + send_deep(part, step).astype(jnp.float32)
    total = total.reshape(PLANE, rows, columns)
    low = total.astype(jnp.bfloat16)
    result = jnp.zeros((PLANE, rows, columns), jnp.float32)
    for mask in range(PLANE):
        if mask:
            part = lax.dynamic_index_in_dim(low, place ^ mask, 0, keepdims=True)
            part = send_plane(part, mask).astype(jnp.float32)
        else:
            part = lax.dynamic_index_in_dim(total, place, 0, keepdims=True)
        result = lax.dynamic_update_slice(result, part, (place ^ mask, 0, 0))
    return result.transpose(1, 0, 2)


def gather_rows(local):
    parts = [local] + [send_plane(local, mask) for mask in range(1, PLANE)]
    half = jnp.stack(parts)
    return lax.all_gather(half, "tensor", axis=0, tiled=False)


def scatter_rows(partial, rows):
    core = lax.axis_index("tensor")
    partial = partial.reshape(2, PLANE, rows, partial.shape[-1])
    other = lax.dynamic_index_in_dim(partial, 1 - core, 0, keepdims=False).astype(jnp.bfloat16)
    mine = lax.dynamic_index_in_dim(partial, core, 0, keepdims=False)
    chip = mine + swap_cores(other).astype(jnp.float32)
    low = chip.astype(jnp.bfloat16)
    total = chip[0]
    for mask in range(1, PLANE):
        total = total + send_plane(low[mask], mask).astype(jnp.float32)
    return total


def sum_all(values):
    dp = lax.axis_index("dp")
    layers = lax.axis_size("dp") // PLANE
    depth = dp // PLANE
    values = values + swap_cores(values)
    first = values + send_plane(values, 1)
    both = first + send_plane(first, 2)
    every = jnp.zeros((layers,) + both.shape, both.dtype)
    for step in range(layers):
        part = send_deep(both, step) if step else both
        every = lax.dynamic_update_slice(every, part[None], ((depth - step) % layers,) + (0,) * both.ndim)
    return jnp.sum(every, axis=0)


def by_group(values):
    values = values.reshape(2, PLANE, -1, values.shape[-1])
    return values.transpose(1, 0, 2, 3).reshape(PLANE, -1, values.shape[-1])


def by_row(values):
    values = values.reshape(PLANE, 2, -1, values.shape[-1])
    return values.transpose(1, 0, 2, 3).reshape(-1, values.shape[-1])


def split_places(weight):
    rows, columns = weight.shape
    return weight.reshape(rows, PLANE, columns // PLANE).transpose(1, 0, 2)


def body(
    tokens,
    lengths,
    attn_gain,
    query_gain,
    key_gain,
    ffn_gain,
    w_query,
    w_key,
    w_value,
    w_out,
    w_gate,
    w_up,
    w_down,
    cotangent,
):
    tensor_index = lax.axis_index("tensor")
    local_rows = tokens.shape[0]
    total_rows = local_rows * lax.axis_size("tensor")
    q_cols = w_query.shape[1] // PLANE
    kv_cols = w_key.shape[1] // PLANE
    ff_cols = w_gate.shape[1] // PLANE
    local_kv = kv_cols // HEAD_DIM
    share = q_cols // kv_cols
    score_scale = HEAD_DIM ** (-0.5)

    inputs = tokens.astype(jnp.float32)
    factor_a = inverse_rms(inputs)
    unit_a = inputs * factor_a
    normed = gather_rows((unit_a * attn_gain).astype(jnp.bfloat16)).reshape(-1, tokens.shape[1])
    attn_weight = gather_weight(
        jnp.concatenate([split_places(w) for w in (w_query, w_key, w_value, w_out)], axis=2)
    )
    full_qkv = attn_weight[:, : q_cols + 2 * kv_cols]
    full_out = attn_weight[:, q_cols + 2 * kv_cols :]

    all_lengths = jnp.concatenate([lengths] + [send_plane(lengths, m) for m in range(1, PLANE)])
    position, live, allowed = jax.vmap(lambda one: seq_layout(one, total_rows))(all_lengths)
    live_local = lax.dynamic_slice_in_dim(live[0], tensor_index * local_rows, local_rows)
    cosine, sine = jax.vmap(lambda one: rope_tables(one, HEAD_DIM))(position)
    grad_out = jnp.where(live_local[:, None], cotangent, jnp.zeros_like(cotangent))
    grad_rows = gather_rows(grad_out).reshape(-1, tokens.shape[1])
    gate_up = gather_weight(
        jnp.concatenate([split_places(w) for w in (w_gate, w_up)], axis=2)
    )
    full_down = gather_weight(split_places(w_down))

    pre = by_group(matmul(normed, full_qkv))
    query_pre = pre[..., :q_cols].reshape(PLANE, total_rows, local_kv * share, HEAD_DIM)
    key_pre = pre[..., q_cols : q_cols + kv_cols].reshape(PLANE, total_rows, local_kv, HEAD_DIM)
    value_low = (
        pre[..., q_cols + kv_cols :]
        .astype(jnp.bfloat16)
        .reshape(PLANE, total_rows, local_kv, HEAD_DIM)
    )
    factor_q = inverse_rms(query_pre)
    unit_q = query_pre * factor_q
    factor_k = inverse_rms(key_pre)
    unit_k = key_pre * factor_k
    query_low = rotate(unit_q * query_gain, cosine, sine).astype(jnp.bfloat16)
    key_low = rotate(unit_k * key_gain, cosine, sine).astype(jnp.bfloat16)
    grouped = query_low.reshape(PLANE, total_rows, local_kv, share, HEAD_DIM)
    scores = (
        jnp.einsum("bqgjd,bkgd->bgjqk", grouped, key_low, preferred_element_type=jnp.float32)
        * score_scale
    )
    scores = jnp.where(allowed[:, None, None], scores, masked_score)
    top = jnp.max(scores, axis=-1, keepdims=True)
    expd = jnp.exp(scores - top)
    totals = jnp.sum(expd, axis=-1, keepdims=True)
    probs = expd / totals
    probs_low = probs.astype(jnp.bfloat16)
    mixed = jnp.einsum(
        "bgjqk,bkgd->bqgjd", probs_low, value_low, preferred_element_type=jnp.float32
    )
    mixed_low = by_row(mixed.astype(jnp.bfloat16).reshape(PLANE, total_rows, q_cols))
    hidden = inputs + scatter_rows(matmul_nt(mixed_low, full_out), local_rows)
    factor_b = inverse_rms(hidden)
    unit_b = hidden * factor_b
    normed2 = gather_rows((unit_b * ffn_gain).astype(jnp.bfloat16)).reshape(-1, tokens.shape[1])

    both = matmul(normed2, gate_up)
    gate, up_proj = both[:, :ff_cols], both[:, ff_cols:]
    sigma = jax.nn.sigmoid(gate)
    silu_gate = gate * sigma
    act_low = (silu_gate * up_proj).astype(jnp.bfloat16)
    ffn_branch = scatter_rows(matmul_nt(act_low, full_down), local_rows)
    block_out = (hidden + ffn_branch).astype(jnp.bfloat16)

    d_act = matmul(grad_rows, full_down)
    own_down = scatter_weight(matmul_tn(grad_rows, act_low))
    d_gate = (d_act * up_proj * sigma * (1.0 + gate * (1.0 - sigma))).astype(jnp.bfloat16)
    d_up = (d_act * silu_gate).astype(jnp.bfloat16)
    d_both = jnp.concatenate([d_gate, d_up], axis=1)
    d_normed2 = scatter_rows(matmul_nt(d_both, gate_up), local_rows)
    own_both = scatter_weight(matmul_tn(normed2, d_both))
    gain_ffn = jnp.sum(d_normed2 * unit_b, axis=0)
    d_hidden = grad_out.astype(jnp.float32) + norm_back(d_normed2 * ffn_gain, unit_b, factor_b)
    hidden_rows = gather_rows(d_hidden.astype(jnp.bfloat16)).reshape(-1, tokens.shape[1])
    grad_out_proj = matmul_tn(hidden_rows, mixed_low)
    d_mixed = by_group(matmul(hidden_rows, full_out).astype(jnp.bfloat16)).reshape(
        PLANE, total_rows, local_kv, share, HEAD_DIM
    )
    d_value = jnp.einsum(
        "bgjqk,bqgjd->bkgd", probs_low, d_mixed, preferred_element_type=jnp.float32
    )
    d_value_low = d_value.astype(jnp.bfloat16).reshape(PLANE, total_rows, kv_cols)
    d_probs = jnp.einsum("bqgjd,bkgd->bgjqk", d_mixed, value_low, preferred_element_type=jnp.float32)
    centre = jnp.sum(probs * d_probs, axis=-1, keepdims=True)
    d_scores = (probs * (d_probs - centre)).astype(jnp.bfloat16)
    d_query_rot = jnp.einsum(
        "bgjqk,bkgd->bqgjd", d_scores, key_low, preferred_element_type=jnp.float32
    )
    d_query_rot = (
        d_query_rot.reshape(PLANE, total_rows, local_kv * share, HEAD_DIM) * score_scale
    )
    d_key_rot = (
        jnp.einsum("bgjqk,bqgjd->bkgd", d_scores, grouped, preferred_element_type=jnp.float32)
        * score_scale
    )
    turned_q = rotate_back(d_query_rot, cosine, sine)
    turned_k = rotate_back(d_key_rot, cosine, sine)
    gain_query = jnp.sum(turned_q * unit_q, axis=(0, 1, 2))
    gain_key = jnp.sum(turned_k * unit_k, axis=(0, 1, 2))
    d_query = (
        norm_back(turned_q * query_gain, unit_q, factor_q)
        .astype(jnp.bfloat16)
        .reshape(PLANE, total_rows, q_cols)
    )
    d_key = (
        norm_back(turned_k * key_gain, unit_k, factor_k)
        .astype(jnp.bfloat16)
        .reshape(PLANE, total_rows, kv_cols)
    )
    d_qkv = by_row(jnp.concatenate([d_query, d_key, d_value_low], axis=2))
    d_normed = scatter_rows(matmul_nt(d_qkv, full_qkv), local_rows)
    own_attn = scatter_weight(
        jnp.concatenate([matmul_tn(normed, d_qkv), grad_out_proj], axis=1)
    )
    gain_attn = jnp.sum(d_normed * unit_a, axis=0)
    grad_tokens = d_hidden + norm_back(d_normed * attn_gain, unit_a, factor_a)
    gains = sum_all(jnp.concatenate([gain_attn, gain_ffn, gain_query, gain_key]))
    width = tokens.shape[1]

    def joined(part):
        return part.reshape(part.shape[0], -1)

    marks = (q_cols, q_cols + kv_cols, q_cols + 2 * kv_cols)
    return (
        block_out,
        grad_tokens,
        gains[:width],
        gains[2 * width : 2 * width + HEAD_DIM],
        gains[2 * width + HEAD_DIM :],
        gains[width : 2 * width],
        joined(own_attn[..., : marks[0]]),
        joined(own_attn[..., marks[0] : marks[1]]),
        joined(own_attn[..., marks[1] : marks[2]]),
        joined(own_attn[..., marks[2] :]),
        joined(own_both[..., :ff_cols]),
        joined(own_both[..., ff_cols:]),
        joined(own_down),
    )


def solution(mesh):
    placed = (
        P(("dp", "tensor"), None),
        P("dp", None),
        P(),
        P(),
        P(),
        P(),
        P("dp", "tensor"),
        P("dp", "tensor"),
        P("dp", "tensor"),
        P("dp", "tensor"),
        P("dp", "tensor"),
        P("dp", "tensor"),
        P("dp", "tensor"),
        P(("dp", "tensor"), None),
    )
    return jax.shard_map(
        body,
        mesh=mesh,
        in_specs=placed,
        out_specs=(
            P(("dp", "tensor"), None),
            P(("dp", "tensor"), None),
            P(),
            P(),
            P(),
            P(),
            P("dp", "tensor"),
            P("dp", "tensor"),
            P("dp", "tensor"),
            P("dp", "tensor"),
            P("dp", "tensor"),
            P("dp", "tensor"),
            P("dp", "tensor"),
        ),
        check_vma=False,
    )
```

```python
import jax
import jax.numpy as jnp
from jax import lax
from jax.experimental import pallas as pl
from jax.experimental.pallas import tpu as pltpu
from jax.sharding import PartitionSpec as P

HEAD_DIM = 64


epsilon = 1e-05
rope_base = 1000000.0
masked_score = -1e30


def inverse_rms(values):
    return lax.rsqrt(jnp.mean(values * values, axis=-1, keepdims=True) + epsilon)


def norm_back(grad_unit, unit, factor):
    return factor * (grad_unit - unit * jnp.mean(grad_unit * unit, axis=-1, keepdims=True))


def matmul(first_op, second_op):
    return jnp.dot(first_op, second_op, preferred_element_type=jnp.float32)


def matmul_nt(first_op, second_op):
    return lax.dot_general(
        first_op, second_op, (((1,), (1,)), ((), ())), preferred_element_type=jnp.float32
    )


def matmul_tn(first_op, second_op):
    return lax.dot_general(
        first_op, second_op, (((0,), (0,)), ((), ())), preferred_element_type=jnp.float32
    )


def seq_layout(seq_lengths, total_rows):
    ends = jnp.cumsum(seq_lengths, dtype=jnp.int32)
    starts = ends - seq_lengths
    row_ids = jnp.arange(total_rows, dtype=jnp.int32)
    segment = jnp.sum(
        (row_ids[:, None] >= ends[None, :]).astype(jnp.int32), axis=1, dtype=jnp.int32
    )
    slot_ids = jnp.arange(seq_lengths.shape[0], dtype=jnp.int32)
    picked = (segment[:, None] == slot_ids[None, :]).astype(jnp.int32)
    begin = (
        jnp.sum(picked * starts[None, :], axis=1, dtype=jnp.int32)
        + (segment == seq_lengths.shape[0]).astype(jnp.int32) * ends[-1]
    )
    allowed = (segment[:, None] == segment[None, :]) & (row_ids[:, None] >= row_ids[None, :])
    return (row_ids - begin, row_ids < ends[-1], allowed)


def rope_tables(position, head_size):
    half_dim = head_size // 2
    freqs = rope_base ** (-jnp.arange(half_dim, dtype=jnp.float32) * 2.0 / head_size)
    angles = position.astype(jnp.float32)[:, None] * freqs[None, :]
    return (jnp.cos(angles)[:, None, :], jnp.sin(angles)[:, None, :])


def rotate(values, cosine, sine):
    half_dim = values.shape[-1] // 2
    first_half = values[..., :half_dim]
    second_half = values[..., half_dim:]
    return jnp.concatenate(
        [first_half * cosine - second_half * sine, second_half * cosine + first_half * sine],
        axis=-1,
    )


def rotate_back(grads, cosine, sine):
    half_dim = grads.shape[-1] // 2
    first_half = grads[..., :half_dim]
    second_half = grads[..., half_dim:]
    return jnp.concatenate(
        [first_half * cosine + second_half * sine, second_half * cosine - first_half * sine],
        axis=-1,
    )

PLANE = 4
LANES = 128
HALF = 64
VMEM_BYTES = 60 * 1024 * 1024
float32 = jnp.float32
bfloat16 = jnp.bfloat16


def send_plane(values, mask):
    count = lax.axis_size("dp")
    return lax.ppermute(values, "dp", [(i, i ^ mask) for i in range(count)])


def send_deep(values, step):
    count = lax.axis_size("dp")
    return lax.ppermute(values, "dp", [(i, (i + PLANE * step) % count) for i in range(count)])


def swap_cores(values):
    return lax.ppermute(values, "tensor", [(0, 1), (1, 0)])


def call(kernel, outs, *operands, scalars=0, scratch=(), flops=0, **more):
    specs = [pl.BlockSpec(memory_space=pltpu.SMEM)] * scalars
    specs += [pl.BlockSpec(memory_space=pltpu.VMEM)] * (len(operands) - scalars)
    shapes = [jax.ShapeDtypeStruct(shape, kind) for shape, kind in outs]
    moved = sum(x.size * x.dtype.itemsize for x in operands) + sum(
        s.size * s.dtype.itemsize for s in shapes
    )
    return pl.pallas_call(
        kernel,
        out_shape=shapes,
        in_specs=specs,
        out_specs=[pl.BlockSpec(memory_space=pltpu.VMEM)] * len(shapes),
        scratch_shapes=list(scratch),
        compiler_params=pltpu.CompilerParams(vmem_limit_bytes=VMEM_BYTES),
        cost_estimate=pl.CostEstimate(flops=flops, bytes_accessed=moved, transcendentals=0),
        **more,
    )(*operands)


def lane_ids(shape):
    return lax.broadcasted_iota(jnp.int32, shape, len(shape) - 1)


def half_tile(ref, first_tile, place, upper):
    start = pl.multiple_of((first_tile + place // 2) * LANES, LANES)
    tile = ref[:, pl.ds(start, LANES)].astype(float32)
    turned = pltpu.roll(tile, HALF, 1)
    odd = place % 2 == 1
    if upper:
        return jnp.where(odd, tile, turned)
    return jnp.where(odd, turned, tile)


def padded(values, rows):
    if values.shape[0] == rows:
        return values
    blank = jnp.zeros((rows - values.shape[0], values.shape[1]), values.dtype)
    return jnp.concatenate([values, blank], axis=0)


def attn_rows(rows):
    return (2, rows // 2) if rows % 32 == 0 else (1, max(rows, 16))


def pack_kernel(where_ref, lengths_ref, tok, cot, w_q, w_k, w_v, w_o, w_g, w_u, w_d, *outs):
    rows = w_q.shape[0]
    local = tok.shape[0]
    parts, high = attn_rows(rows)
    tall = max(rows, 16)
    big = w_g.shape[1] // LANES // PLANE * LANES
    last = w_g.shape[1] // LANES // PLANE * PLANE
    place = where_ref[0]
    lane = lane_ids((rows, LANES))
    for mask in range(PLANE):
        other = place ^ mask
        first, second = outs[mask], outs[PLANE + mask]
        at = pl.multiple_of(other * LANES, LANES)
        tile = jnp.where(
            lane < HALF, half_tile(w_k, 0, other, False), half_tile(w_v, 0, other, True)
        )
        piece = jnp.concatenate(
            [w_q[:, pl.ds(at, LANES)].astype(float32), tile, w_o[:, pl.ds(at, LANES)].astype(float32)],
            axis=1,
        )
        first[:local, :] = tok[...]
        pieces = [piece[: rows // 2], piece[rows // 2 :]] if parts == 2 else [padded(piece, high)]
        width = piece.shape[1]
        for part, values in enumerate(pieces):
            first[local:, part * width : (part + 1) * width] = values.astype(bfloat16)
        free = first.shape[1] - parts * width
        ids = lane_ids((high, free))
        marks = jnp.zeros((high, free), float32)
        for slot in range(lengths_ref.shape[1]):
            marks = jnp.where(ids == free - LANES + slot, lengths_ref[0, slot].astype(float32), marks)
        first[local:, parts * width :] = marks.astype(bfloat16)

        at = pl.multiple_of(other * big, LANES)
        second[:local, :] = cot[...]
        small = jnp.where(
            lane < HALF, half_tile(w_g, last, other, False), half_tile(w_u, last, other, True)
        )
        small_down = jnp.where(lane < HALF, half_tile(w_d, last, other, False), 0.0)
        upper = jnp.concatenate(
            [w_g[:, pl.ds(at, big)].astype(float32), w_u[:, pl.ds(at, big)].astype(float32)], axis=1
        )
        lower = jnp.concatenate(
            [w_d[:, pl.ds(at, big)].astype(float32), small, small_down], axis=1
        )
        second[local : local + tall, :] = padded(upper, tall).astype(bfloat16)
        second[local + tall :, : lower.shape[1]] = padded(lower, tall).astype(bfloat16)
        second[local + tall :, lower.shape[1] :] = jnp.zeros(
            (tall, second.shape[1] - lower.shape[1]), bfloat16
        )


def unpack_first_kernel(where_ref, own, one, two, three, tok_out, weight_out, lens_out, held):
    local = tok_out.shape[0] // PLANE
    rows = weight_out.shape[0] // PLANE
    width = weight_out.shape[1]
    parts, high = attn_rows(rows)
    place = where_ref[0]
    for mask, message in enumerate((own, one, two, three)):
        tok_out[mask * local : (mask + 1) * local, :] = message[:local, :]
        at = pl.multiple_of((place ^ mask) * rows, rows)
        values = [
            message[local:, part * width : (part + 1) * width].astype(float32)
            for part in range(parts)
        ]
        piece = jnp.concatenate(values, axis=0) if parts == 2 else values[0][:rows]
        held[pl.ds(at, rows), :] = piece
        ends = message[local : local + 16, message.shape[1] - LANES :].astype(float32)
        lens_out[mask * 8 : (mask + 1) * 8, :] = ends[:8]
    weight_out[...] = held[...].astype(bfloat16)


def unpack_second_kernel(where_ref, own, one, two, three, cot_out, weight_out, held):
    local = cot_out.shape[0] // PLANE
    rows = weight_out.shape[0] // PLANE
    tall = max(rows, 16)
    place = where_ref[0]
    for mask, message in enumerate((own, one, two, three)):
        cot_out[mask * local : (mask + 1) * local, :] = message[:local, :]
        at = pl.multiple_of((place ^ mask) * rows, rows)
        width = message.shape[1]
        held[pl.ds(at, rows), :width] = message[local : local + tall, :].astype(float32)[:rows]
        rest = held.shape[1] - width
        held[pl.ds(at, rows), width:] = message[local + tall :, :rest].astype(float32)[:rows]
    weight_out[...] = held[...].astype(bfloat16)


def stack_kernel(where_ref, *refs):
    *pieces, out = refs
    rows = pieces[0].shape[0]
    depth = where_ref[1]
    for step, piece in enumerate(pieces):
        at = lax.rem(depth - step + len(pieces), len(pieces)) * rows
        out[pl.ds(pl.multiple_of(at, rows), rows), :] = piece[...]


def ffn_kernel(layers, where_ref, ends_ref, x_o, x_m, g_o, g_m, *refs):
    pieces, refs = refs[:layers], refs[layers:]
    out_send, out_keep, dn_send, dn_keep, own_grad = refs[:5]
    grad_pieces = refs[5 : 4 + layers]
    weight, total = refs[4 + layers :]
    step = pl.program_id(0)
    depth, core = where_ref[1], where_ref[2]
    rows = pieces[0].shape[0]
    width = x_o.shape[1]
    both = width
    big = both // 2
    local = x_o.shape[0] // 2

    def row_of(index):
        at = lax.rem(depth + index + layers, layers) * rows
        return pl.ds(pl.multiple_of(at, rows), rows)

    @pl.when(step == 0)
    def _():
        for index, piece in enumerate(pieces):
            weight[row_of(-index), :] = piece[...]
        total[...] = jnp.zeros_like(total)

    def live_rows(values, group, at_core):
        ids = lax.broadcasted_iota(jnp.int32, values.shape, 0) + at_core * local
        return jnp.where(ids < ends_ref[group, ends_ref.shape[1] - 1], values, jnp.zeros_like(values))

    x = jnp.concatenate([x_o[...], x_m[...]], axis=0)
    grads = jnp.concatenate(
        [live_rows(g_o[k * local : (k + 1) * local, :], 2 * step + k, 1 - core) for k in range(2)]
        + [live_rows(g_m[k * local : (k + 1) * local, :], 2 * step + k, core) for k in range(2)],
        axis=0,
    )
    half = 2 * local
    w_both = weight[:, :both]
    w_down = weight[:, both : both + big]
    w_small = weight[:, both + big : both + big + LANES]
    w_small_down = weight[:, both + big + LANES :]
    lane = lane_ids((x.shape[0], LANES))

    def parts_of(gate, up, d_act):
        sigma = 1.0 / (1.0 + jnp.exp(-gate))
        silu = gate * sigma
        act = silu * up
        d_gate = d_act * up * sigma * (1.0 + gate * (1.0 - sigma))
        return act, d_gate, d_act * silu

    pre = matmul(x, w_both)
    act, d_gate, d_up = parts_of(pre[:, :big], pre[:, big:], matmul(grads, w_down))
    pre = matmul(x, w_small)
    act_s, d_gate_s, d_up_s = parts_of(
        pre, pltpu.roll(pre, HALF, 1), matmul(grads, w_small_down)
    )
    act_s = jnp.where(lane < HALF, act_s, 0.0).astype(bfloat16)
    d_small = jnp.where(lane < HALF, d_gate_s, pltpu.roll(d_up_s, HALF, 1)).astype(bfloat16)
    act = act.astype(bfloat16)
    d_both = jnp.concatenate([d_gate, d_up], axis=1).astype(bfloat16)

    partial = matmul_nt(act, w_down) + matmul_nt(act_s, w_small_down)
    out_send[...] = partial[:half].astype(bfloat16)
    out_keep[...] = partial[half:]
    partial = matmul_nt(d_both, w_both) + matmul_nt(d_small, w_small)
    dn_send[...] = partial[:half].astype(bfloat16)
    dn_keep[...] = partial[half:]
    total[:, :both] += matmul_tn(x, d_both)
    total[:, both : both + big] += matmul_tn(grads, act)
    total[:, both + big : both + big + LANES] += matmul_tn(x, d_small)
    total[:, both + big + LANES :] += matmul_tn(grads, act_s)

    @pl.when(step == pl.num_programs(0) - 1)
    def _():
        own_grad[...] = total[row_of(0), :]
        for index, piece in enumerate(grad_pieces):
            piece[...] = total[row_of(index + 1), :].astype(bfloat16)


def ffn(where, ends, x_mine, x_other, g_mine, g_other, pieces):
    layers = len(pieces)
    rows, width = x_mine.shape
    high, columns = pieces[0].shape
    block = rows // 2
    row_spec = pl.BlockSpec((block, width), lambda i: (i, 0))

    def whole(shape):
        return pl.BlockSpec(shape, lambda i: (0, 0), pipeline_mode=pl.Buffered(1))

    scalar = pl.BlockSpec(memory_space=pltpu.SMEM)
    flops = 2 * 2 * rows * width * columns // 3 * 9 // 2
    return pl.pallas_call(
        lambda *refs: ffn_kernel(layers, *refs),
        grid=(2,),
        in_specs=[scalar, scalar] + [row_spec] * 4 + [whole((high, columns))] * layers,
        out_specs=[row_spec] * 4 + [whole((high, columns))] * layers,
        out_shape=[
            jax.ShapeDtypeStruct((rows, width), bfloat16),
            jax.ShapeDtypeStruct((rows, width), float32),
            jax.ShapeDtypeStruct((rows, width), bfloat16),
            jax.ShapeDtypeStruct((rows, width), float32),
            jax.ShapeDtypeStruct((high, columns), float32),
        ]
        + [jax.ShapeDtypeStruct((high, columns), bfloat16)] * (layers - 1),
        scratch_shapes=[
            pltpu.VMEM((layers * high, columns), bfloat16),
            pltpu.VMEM((layers * high, columns), float32),
        ],
        compiler_params=pltpu.CompilerParams(vmem_limit_bytes=VMEM_BYTES),
        cost_estimate=pl.CostEstimate(
            flops=flops, bytes_accessed=40 * 1024 * 1024, transcendentals=0
        ),
    )(where, ends, x_other, x_mine, g_other, g_mine, *pieces)


def chip_sum_kernel(keep, received, *outs):
    rows = outs[0].shape[0]
    for mask, out in enumerate(outs):
        span = slice(mask * rows, (mask + 1) * rows)
        out[...] = (keep[span, :] + received[span, :].astype(float32)).astype(out.dtype)


def chip_sum(keep, received):
    shape = (keep.shape[0] // PLANE, keep.shape[1])
    own, *rest = call(
        chip_sum_kernel, [(shape, float32)] + [(shape, bfloat16)] * (PLANE - 1), keep, received
    )
    return [own] + [send_plane(part, mask + 1) for mask, part in enumerate(rest)]


def add_up(parts):
    return sum(part.astype(float32) for part in parts)


def plane_sum_kernel(where_ref, own, *refs):
    received, outs, held = refs[: -PLANE - 1], refs[-PLANE - 1 : -1], refs[-1]
    value = own[...]
    for part in received:
        value = value + part[...].astype(float32)
    held[...] = value
    place = where_ref[0]
    rows = outs[0].shape[0]
    for mask, out in enumerate(outs):
        at = pl.multiple_of((place ^ mask) * rows, rows)
        out[...] = held[pl.ds(at, rows), :].astype(out.dtype)


def plane_sum(where, own, grad_pieces):
    received = [send_deep(piece, step + 1) for step, piece in enumerate(grad_pieces)]
    shape = (own.shape[0] // PLANE, own.shape[1])
    mine, *rest = call(
        plane_sum_kernel,
        [(shape, float32)] + [(shape, bfloat16)] * (PLANE - 1),
        where,
        own,
        *received,
        scalars=1,
        scratch=[pltpu.VMEM(own.shape, float32)],
    )
    return [mine] + [send_plane(part, mask + 1) for mask, part in enumerate(rest)]


def pick_place(refs, place, target, columns):
    value = jnp.zeros((refs[0].shape[0], columns.stop - columns.start), float32)
    for mask, ref in enumerate(refs):
        value = jnp.where(place ^ mask == target, ref[:, columns].astype(float32), value)
    return value


def place_ffn_kernel(where_ref, own, one, two, three, out_g, out_u, out_d):
    place = where_ref[0]
    refs = (own, one, two, three)
    big = out_g.shape[1] // LANES // PLANE * LANES
    last = PLANE * big
    for mask, ref in enumerate(refs):
        at = pl.ds(pl.multiple_of((place ^ mask) * big, LANES), big)
        for number, out in enumerate((out_g, out_u, out_d)):
            out[:, at] = ref[:, number * big : (number + 1) * big].astype(float32)
    for pair in range(PLANE // 2):
        low = pick_place(refs, place, 2 * pair, slice(3 * big, 3 * big + 2 * LANES))
        high = pick_place(refs, place, 2 * pair + 1, slice(3 * big, 3 * big + 2 * LANES))
        lane = lane_ids((low.shape[0], LANES))
        span = slice(last + pair * LANES, last + (pair + 1) * LANES)
        gu_low, gu_high = low[:, :LANES], high[:, :LANES]
        out_g[:, span] = jnp.where(lane < HALF, gu_low, pltpu.roll(gu_high, HALF, 1))
        out_u[:, span] = jnp.where(lane < HALF, pltpu.roll(gu_low, HALF, 1), gu_high)
        out_d[:, span] = jnp.where(lane < HALF, low[:, LANES:], pltpu.roll(high[:, LANES:], HALF, 1))


def place_attn_kernel(where_ref, own, one, two, three, out_q, out_k, out_v, out_o):
    place = where_ref[0]
    refs = (own, one, two, three)
    for mask, ref in enumerate(refs):
        at = pl.ds(pl.multiple_of((place ^ mask) * LANES, LANES), LANES)
        out_q[:, at] = ref[:, :LANES].astype(float32)
        out_o[:, at] = ref[:, 2 * LANES :].astype(float32)
    for pair in range(PLANE // 2):
        low = pick_place(refs, place, 2 * pair, slice(LANES, 2 * LANES))
        high = pick_place(refs, place, 2 * pair + 1, slice(LANES, 2 * LANES))
        lane = lane_ids(low.shape)
        span = slice(pair * LANES, (pair + 1) * LANES)
        out_k[:, span] = jnp.where(lane < HALF, low, pltpu.roll(high, HALF, 1))
        out_v[:, span] = jnp.where(lane < HALF, pltpu.roll(low, HALF, 1), high)


def split_grad_kernel(where_ref, grad, own, *pieces):
    layers = len(pieces) + 1
    rows = own.shape[0]
    depth = where_ref[1]
    for step, out in enumerate((own,) + pieces):
        at = lax.rem(depth + step, layers) * rows
        out[...] = grad[pl.ds(pl.multiple_of(at, rows), rows), :].astype(out.dtype)


def gather_rows(local):
    mine = jnp.concatenate([local] + [send_plane(local, mask) for mask in range(1, PLANE)])
    return mine, swap_cores(mine)


def sum_all(values):
    dp = lax.axis_index("dp")
    layers = lax.axis_size("dp") // PLANE
    depth = dp // PLANE
    values = values + swap_cores(values)
    first = values + send_plane(values, 1)
    both = first + send_plane(first, 2)
    every = jnp.zeros((layers,) + both.shape, both.dtype)
    for step in range(layers):
        part = send_deep(both, step) if step else both
        every = lax.dynamic_update_slice(
            every, part[None], ((depth - step) % layers,) + (0,) * both.ndim
        )
    return jnp.sum(every, axis=0)


def body(
    tokens,
    lengths,
    attn_gain,
    query_gain,
    key_gain,
    ffn_gain,
    w_query,
    w_key,
    w_value,
    w_out,
    w_gate,
    w_up,
    w_down,
    cotangent,
):
    dp = lax.axis_index("dp")
    core = lax.axis_index("tensor")
    layers = lax.axis_size("dp") // PLANE
    where = jnp.stack([dp % PLANE, dp // PLANE, core]).astype(jnp.int32)
    local_rows, model = tokens.shape
    total_rows = local_rows * lax.axis_size("tensor")
    rows = w_query.shape[0]
    q_cols = w_query.shape[1] // PLANE
    kv_cols = w_key.shape[1] // PLANE
    local_kv = kv_cols // HEAD_DIM
    share = q_cols // kv_cols
    score_scale = HEAD_DIM ** (-0.5)
    attn_cols = 2 * q_cols + 2 * kv_cols
    ff_cols = 3 * (w_gate.shape[1] // LANES // PLANE * LANES) + 2 * LANES

    parts, high = attn_rows(rows)
    tall = max(rows, 16)
    messages = call(
        pack_kernel,
        [((local_rows + high, model), bfloat16)] * PLANE
        + [((local_rows + 2 * tall, model), bfloat16)] * PLANE,
        where,
        lengths,
        tokens,
        cotangent,
        w_query,
        w_key,
        w_value,
        w_out,
        w_gate,
        w_up,
        w_down,
        scalars=2,
    )
    first = [messages[0]] + [send_plane(messages[m], m) for m in range(1, PLANE)]
    second = [messages[PLANE]] + [send_plane(messages[PLANE + m], m) for m in range(1, PLANE)]
    tok_mine, attn_piece, lens = call(
        unpack_first_kernel,
        [
            ((PLANE * local_rows, model), bfloat16),
            ((PLANE * rows, attn_cols), bfloat16),
            ((PLANE * 8, LANES), float32),
        ],
        where,
        *first,
        scalars=1,
        scratch=[pltpu.VMEM((PLANE * rows, attn_cols), float32)],
    )
    attn_pieces = [attn_piece] + [send_deep(attn_piece, step) for step in range(1, layers)]
    tok_other = swap_cores(tok_mine)
    cot_mine, ff_piece = call(
        unpack_second_kernel,
        [((PLANE * local_rows, model), bfloat16), ((PLANE * rows, ff_cols), bfloat16)],
        where,
        *second,
        scalars=1,
        scratch=[pltpu.VMEM((PLANE * rows, ff_cols), float32)],
    )
    ff_pieces = [ff_piece] + [send_deep(ff_piece, step) for step in range(1, layers)]
    cot_other = swap_cores(cot_mine)
    (attn_weight,) = call(
        stack_kernel, [((model, attn_cols), bfloat16)], where, *attn_pieces, scalars=1
    )
    full_qkv = attn_weight[:, : q_cols + 2 * kv_cols]
    full_out = attn_weight[:, q_cols + 2 * kv_cols :]

    slots = lengths.shape[1]
    all_lengths = lens.reshape(PLANE, 8, LANES)[:, 0, :slots].astype(jnp.int32)
    ends = jnp.cumsum(all_lengths, axis=1, dtype=jnp.int32)
    row_ids = jnp.arange(total_rows, dtype=jnp.int32)
    begin = jnp.max(
        jnp.where(row_ids[None, :, None] >= ends[:, None, :], ends[:, None, :], 0), axis=2
    )
    position = row_ids[None, :] - begin
    allowed = (row_ids[None, None, :] >= begin[:, :, None]) & (
        row_ids[None, None, :] <= row_ids[None, :, None]
    )
    cosine, sine = jax.vmap(lambda one: rope_tables(one, HEAD_DIM))(position)

    def by_group(mine, other):
        mine = mine.reshape(PLANE, local_rows, -1)
        other = other.reshape(PLANE, local_rows, -1)
        low = jnp.where(core == 0, mine, other)
        upper = jnp.where(core == 0, other, mine)
        return jnp.concatenate([low, upper], axis=1)

    def by_core(values):
        low, upper = values[:, :local_rows], values[:, local_rows:]
        mine = jnp.where(core == 0, low, upper).reshape(PLANE * local_rows, -1)
        other = jnp.where(core == 0, upper, low).reshape(PLANE * local_rows, -1)
        return mine, other

    inputs = tokens.astype(jnp.float32)
    factor_a = inverse_rms(inputs)
    unit_a = inputs * factor_a
    group_tokens = by_group(tok_mine, tok_other).astype(jnp.float32)
    normed = (group_tokens * inverse_rms(group_tokens) * attn_gain).astype(jnp.bfloat16)
    normed = normed.reshape(-1, model)
    pre = matmul(normed, full_qkv).reshape(PLANE, total_rows, -1)
    query_pre = pre[..., :q_cols].reshape(PLANE, total_rows, local_kv * share, HEAD_DIM)
    key_pre = pre[..., q_cols : q_cols + kv_cols].reshape(PLANE, total_rows, local_kv, HEAD_DIM)
    value_low = (
        pre[..., q_cols + kv_cols :]
        .astype(jnp.bfloat16)
        .reshape(PLANE, total_rows, local_kv, HEAD_DIM)
    )
    factor_q = inverse_rms(query_pre)
    unit_q = query_pre * factor_q
    factor_k = inverse_rms(key_pre)
    unit_k = key_pre * factor_k
    query_low = rotate(unit_q * query_gain, cosine, sine).astype(jnp.bfloat16)
    key_low = rotate(unit_k * key_gain, cosine, sine).astype(jnp.bfloat16)
    grouped = query_low.reshape(PLANE, total_rows, local_kv, share, HEAD_DIM)
    scores = (
        jnp.einsum("bqgjd,bkgd->bgjqk", grouped, key_low, preferred_element_type=jnp.float32)
        * score_scale
    )
    scores = jnp.where(allowed[:, None, None], scores, masked_score)
    top = jnp.max(scores, axis=-1, keepdims=True)
    expd = jnp.exp(scores - top)
    totals = jnp.sum(expd, axis=-1, keepdims=True)
    probs = expd / totals
    probs_low = probs.astype(jnp.bfloat16)
    mixed = jnp.einsum(
        "bgjqk,bkgd->bqgjd", probs_low, value_low, preferred_element_type=jnp.float32
    )
    mixed_low = mixed.astype(jnp.bfloat16).reshape(PLANE, total_rows, q_cols)
    mixed_mine, mixed_other = by_core(mixed_low)
    received = swap_cores(matmul_nt(mixed_other, full_out).astype(jnp.bfloat16))
    hidden = inputs + add_up(chip_sum(matmul_nt(mixed_mine, full_out), received))
    factor_b = inverse_rms(hidden)
    unit_b = hidden * factor_b
    x_mine, x_other = gather_rows((unit_b * ffn_gain).astype(jnp.bfloat16))

    out_send, out_keep, dn_send, dn_keep, own_ff, *ff_grads = ffn(
        where, ends, x_mine, x_other, cot_mine, cot_other, ff_pieces
    )
    d_normed2 = add_up(chip_sum(dn_keep, swap_cores(dn_send)))
    grad_out = jnp.where(
        (jnp.arange(local_rows) + core * local_rows < ends[0, slots - 1])[:, None],
        cotangent,
        jnp.zeros_like(cotangent),
    )
    gain_ffn = jnp.sum(d_normed2 * unit_b, axis=0)
    d_hidden = grad_out.astype(jnp.float32) + norm_back(d_normed2 * ffn_gain, unit_b, factor_b)
    h_mine, h_other = gather_rows(d_hidden.astype(jnp.bfloat16))
    ff_parts = plane_sum(where, own_ff, ff_grads)
    block_out = (hidden + add_up(chip_sum(out_keep, swap_cores(out_send)))).astype(jnp.bfloat16)

    hidden_rows = by_group(h_mine, h_other).reshape(-1, model)
    grad_out_proj = matmul_tn(hidden_rows, mixed_low.reshape(-1, q_cols))
    d_mixed = matmul(hidden_rows, full_out).astype(jnp.bfloat16).reshape(
        PLANE, total_rows, local_kv, share, HEAD_DIM
    )
    d_value = jnp.einsum(
        "bgjqk,bqgjd->bkgd", probs_low, d_mixed, preferred_element_type=jnp.float32
    )
    d_value_low = d_value.astype(jnp.bfloat16).reshape(PLANE, total_rows, kv_cols)
    d_probs = jnp.einsum(
        "bqgjd,bkgd->bgjqk", d_mixed, value_low, preferred_element_type=jnp.float32
    )
    centre = jnp.sum(probs * d_probs, axis=-1, keepdims=True)
    d_scores = (probs * (d_probs - centre)).astype(jnp.bfloat16)
    d_query_rot = jnp.einsum(
        "bgjqk,bkgd->bqgjd", d_scores, key_low, preferred_element_type=jnp.float32
    )
    d_query_rot = (
        d_query_rot.reshape(PLANE, total_rows, local_kv * share, HEAD_DIM) * score_scale
    )
    d_key_rot = (
        jnp.einsum("bgjqk,bqgjd->bkgd", d_scores, grouped, preferred_element_type=jnp.float32)
        * score_scale
    )
    turned_q = rotate_back(d_query_rot, cosine, sine)
    turned_k = rotate_back(d_key_rot, cosine, sine)
    gain_query = jnp.sum(turned_q * unit_q, axis=(0, 1, 2))
    gain_key = jnp.sum(turned_k * unit_k, axis=(0, 1, 2))
    d_query = (
        norm_back(turned_q * query_gain, unit_q, factor_q)
        .astype(jnp.bfloat16)
        .reshape(PLANE, total_rows, q_cols)
    )
    d_key = (
        norm_back(turned_k * key_gain, unit_k, factor_k)
        .astype(jnp.bfloat16)
        .reshape(PLANE, total_rows, kv_cols)
    )
    d_qkv = jnp.concatenate([d_query, d_key, d_value_low], axis=2)
    attn_grad = jnp.concatenate(
        [matmul_tn(normed, d_qkv.reshape(-1, d_qkv.shape[-1])), grad_out_proj], axis=1
    )
    d_mine, d_other = by_core(d_qkv)
    received = swap_cores(matmul_nt(d_other, full_qkv).astype(jnp.bfloat16))
    d_normed = add_up(chip_sum(matmul_nt(d_mine, full_qkv), received))
    own_attn, *attn_grads = call(
        split_grad_kernel,
        [((PLANE * rows, attn_cols), float32)]
        + [((PLANE * rows, attn_cols), bfloat16)] * (layers - 1),
        where,
        attn_grad,
        scalars=1,
    )
    attn_parts = plane_sum(where, own_attn, attn_grads)
    gain_attn = jnp.sum(d_normed * unit_a, axis=0)
    grad_tokens = d_hidden + norm_back(d_normed * attn_gain, unit_a, factor_a)
    gains = sum_all(jnp.concatenate([gain_attn, gain_ffn, gain_query, gain_key]))
    grad_gate, grad_up, grad_down = call(
        place_ffn_kernel, [(w_gate.shape, float32)] * 3, where, *ff_parts, scalars=1
    )
    grad_query, grad_key, grad_value, grad_out_w = call(
        place_attn_kernel,
        [(w.shape, float32) for w in (w_query, w_key, w_value, w_out)],
        where,
        *attn_parts,
        scalars=1,
    )
    return (
        block_out,
        grad_tokens,
        gains[:model],
        gains[2 * model : 2 * model + HEAD_DIM],
        gains[2 * model + HEAD_DIM :],
        gains[model : 2 * model],
        grad_query,
        grad_key,
        grad_value,
        grad_out_w,
        grad_gate,
        grad_up,
        grad_down,
    )


def solution(mesh):
    placed = (
        P(("dp", "tensor"), None),
        P("dp", None),
        P(),
        P(),
        P(),
        P(),
        P("dp", "tensor"),
        P("dp", "tensor"),
        P("dp", "tensor"),
        P("dp", "tensor"),
        P("dp", "tensor"),
        P("dp", "tensor"),
        P("dp", "tensor"),
        P(("dp", "tensor"), None),
    )
    return jax.shard_map(
        body,
        mesh=mesh,
        in_specs=placed,
        out_specs=(
            P(("dp", "tensor"), None),
            P(("dp", "tensor"), None),
            P(),
            P(),
            P(),
            P(),
            P("dp", "tensor"),
            P("dp", "tensor"),
            P("dp", "tensor"),
            P("dp", "tensor"),
            P("dp", "tensor"),
            P("dp", "tensor"),
            P("dp", "tensor"),
        ),
        check_vma=False,
    )
```

```python
import jax
import jax.numpy as jnp
from jax import lax
from jax.experimental import pallas as pl
from jax.experimental.pallas import tpu as pltpu
from jax.sharding import PartitionSpec as P

HEAD_DIM = 64


epsilon = 1e-05
rope_base = 1000000.0
masked_score = -1e30


def inverse_rms(values):
    return lax.rsqrt(jnp.mean(values * values, axis=-1, keepdims=True) + epsilon)


def norm_back(grad_unit, unit, factor):
    return factor * (grad_unit - unit * jnp.mean(grad_unit * unit, axis=-1, keepdims=True))


def matmul(first_op, second_op):
    return jnp.dot(first_op, second_op, preferred_element_type=jnp.float32)


def matmul_nt(first_op, second_op):
    return lax.dot_general(
        first_op, second_op, (((1,), (1,)), ((), ())), preferred_element_type=jnp.float32
    )


def matmul_tn(first_op, second_op):
    return lax.dot_general(
        first_op, second_op, (((0,), (0,)), ((), ())), preferred_element_type=jnp.float32
    )


def seq_layout(seq_lengths, total_rows):
    ends = jnp.cumsum(seq_lengths, dtype=jnp.int32)
    starts = ends - seq_lengths
    row_ids = jnp.arange(total_rows, dtype=jnp.int32)
    segment = jnp.sum(
        (row_ids[:, None] >= ends[None, :]).astype(jnp.int32), axis=1, dtype=jnp.int32
    )
    slot_ids = jnp.arange(seq_lengths.shape[0], dtype=jnp.int32)
    picked = (segment[:, None] == slot_ids[None, :]).astype(jnp.int32)
    begin = (
        jnp.sum(picked * starts[None, :], axis=1, dtype=jnp.int32)
        + (segment == seq_lengths.shape[0]).astype(jnp.int32) * ends[-1]
    )
    allowed = (segment[:, None] == segment[None, :]) & (row_ids[:, None] >= row_ids[None, :])
    return (row_ids - begin, row_ids < ends[-1], allowed)


def rope_tables(position, head_size):
    half_dim = head_size // 2
    freqs = rope_base ** (-jnp.arange(half_dim, dtype=jnp.float32) * 2.0 / head_size)
    angles = position.astype(jnp.float32)[:, None] * freqs[None, :]
    return (jnp.cos(angles)[:, None, :], jnp.sin(angles)[:, None, :])


def rotate(values, cosine, sine):
    half_dim = values.shape[-1] // 2
    first_half = values[..., :half_dim]
    second_half = values[..., half_dim:]
    return jnp.concatenate(
        [first_half * cosine - second_half * sine, second_half * cosine + first_half * sine],
        axis=-1,
    )


def rotate_back(grads, cosine, sine):
    half_dim = grads.shape[-1] // 2
    first_half = grads[..., :half_dim]
    second_half = grads[..., half_dim:]
    return jnp.concatenate(
        [first_half * cosine + second_half * sine, second_half * cosine - first_half * sine],
        axis=-1,
    )

PLANE = 4
LANES = 128
HALF = 64
VMEM_BYTES = 60 * 1024 * 1024
COST = pl.CostEstimate(flops=1024, bytes_accessed=1024, transcendentals=0)
GAIN_ROWS = 8
float32 = jnp.float32
bfloat16 = jnp.bfloat16


def send_plane(values, mask):
    count = lax.axis_size("dp")
    return lax.ppermute(values, "dp", [(i, i ^ mask) for i in range(count)])


def send_deep(values, step):
    count = lax.axis_size("dp")
    return lax.ppermute(values, "dp", [(i, (i + PLANE * step) % count) for i in range(count)])


def swap_cores(values):
    return lax.ppermute(values, "tensor", [(0, 1), (1, 0)])


def call(kernel, outs, *operands, scalars=0, scratch=()):
    specs = [pl.BlockSpec(memory_space=pltpu.SMEM)] * scalars
    specs += [pl.BlockSpec(memory_space=pltpu.VMEM)] * (len(operands) - scalars)
    return pl.pallas_call(
        kernel,
        out_shape=[jax.ShapeDtypeStruct(shape, kind) for shape, kind in outs],
        in_specs=specs,
        out_specs=[pl.BlockSpec(memory_space=pltpu.VMEM)] * len(outs),
        scratch_shapes=list(scratch),
        compiler_params=pltpu.CompilerParams(vmem_limit_bytes=VMEM_BYTES),
        cost_estimate=COST,
    )(*operands)


def lane_ids(shape):
    return lax.broadcasted_iota(jnp.int32, shape, len(shape) - 1)


def half_tile(ref, first_tile, place, upper):
    start = pl.multiple_of((first_tile + place // 2) * LANES, LANES)
    tile = ref[:, pl.ds(start, LANES)].astype(float32)
    turned = pltpu.roll(tile, HALF, 1)
    odd = place % 2 == 1
    if upper:
        return jnp.where(odd, tile, turned)
    return jnp.where(odd, turned, tile)


def padded(values, rows):
    if values.shape[0] == rows:
        return values
    blank = jnp.zeros((rows - values.shape[0], values.shape[1]), values.dtype)
    return jnp.concatenate([values, blank], axis=0)


def attn_rows(rows):
    return (2, rows // 2) if rows % 32 == 0 else (1, max(rows, 16))


def pack_kernel(where_ref, lengths_ref, w_q, w_k, w_v, w_o, w_g, w_u, w_d, *outs):
    rows = w_q.shape[0]
    parts, high = attn_rows(rows)
    tall = max(rows, 16)
    big = w_g.shape[1] // LANES // PLANE * LANES
    last = w_g.shape[1] // LANES // PLANE * PLANE
    place = where_ref[0]
    lane = lane_ids((rows, LANES))
    for mask, out in enumerate(outs):
        other = place ^ mask
        at = pl.multiple_of(other * LANES, LANES)
        tile = jnp.where(
            lane < HALF, half_tile(w_k, 0, other, False), half_tile(w_v, 0, other, True)
        )
        piece = jnp.concatenate(
            [w_q[:, pl.ds(at, LANES)].astype(float32), tile, w_o[:, pl.ds(at, LANES)].astype(float32)],
            axis=1,
        )
        pieces = [piece[: rows // 2], piece[rows // 2 :]] if parts == 2 else [padded(piece, high)]
        width = piece.shape[1]
        for part, values in enumerate(pieces):
            out[:high, part * width : (part + 1) * width] = values.astype(bfloat16)
        free = out.shape[1] - parts * width
        ids = lane_ids((high, free))
        marks = jnp.zeros((high, free), float32)
        for slot in range(lengths_ref.shape[1]):
            marks = jnp.where(ids == free - LANES + slot, lengths_ref[0, slot].astype(float32), marks)
        out[:high, parts * width :] = marks.astype(bfloat16)

        at = pl.multiple_of(other * big, LANES)
        small = jnp.where(
            lane < HALF, half_tile(w_g, last, other, False), half_tile(w_u, last, other, True)
        )
        small_down = jnp.where(lane < HALF, half_tile(w_d, last, other, False), 0.0)
        upper = jnp.concatenate(
            [w_g[:, pl.ds(at, big)].astype(float32), w_u[:, pl.ds(at, big)].astype(float32)], axis=1
        )
        lower = jnp.concatenate(
            [w_d[:, pl.ds(at, big)].astype(float32), small, small_down], axis=1
        )
        out[high : high + tall, :] = padded(upper, tall).astype(bfloat16)
        out[high + tall :, : lower.shape[1]] = padded(lower, tall).astype(bfloat16)
        out[high + tall :, lower.shape[1] :] = jnp.zeros(
            (tall, out.shape[1] - lower.shape[1]), bfloat16
        )


def unpack_kernel(where_ref, own, one, two, three, attn_out, ffn_out, lens_out, held_attn, held_ffn):
    rows = attn_out.shape[0] // PLANE
    width = attn_out.shape[1]
    parts, high = attn_rows(rows)
    tall = max(rows, 16)
    place = where_ref[0]
    for mask, message in enumerate((own, one, two, three)):
        at = pl.ds(pl.multiple_of((place ^ mask) * rows, rows), rows)
        values = [
            message[:high, part * width : (part + 1) * width].astype(float32)
            for part in range(parts)
        ]
        held_attn[at, :] = jnp.concatenate(values, axis=0) if parts == 2 else values[0][:rows]
        lens = message[:16, message.shape[1] - LANES :].astype(float32)
        lens_out[mask * 8 : (mask + 1) * 8, :] = lens[:8]
        full = message.shape[1]
        held_ffn[at, :full] = message[high : high + tall, :].astype(float32)[:rows]
        rest = held_ffn.shape[1] - full
        held_ffn[at, full:] = message[high + tall :, :rest].astype(float32)[:rows]
    attn_out[...] = held_attn[...].astype(bfloat16)
    ffn_out[...] = held_ffn[...].astype(bfloat16)


def split_rows_kernel(own, one, two, three, tok_out, cot_out):
    local = own.shape[0] // 2
    for mask, message in enumerate((own, one, two, three)):
        span = slice(mask * local, (mask + 1) * local)
        tok_out[span, :] = message[:local, :]
        cot_out[span, :] = message[local:, :]


def head_mean(values):
    low = lane_ids(values.shape) < HALF
    first = jnp.sum(jnp.where(low, values, 0.0), axis=1, keepdims=True)
    second = jnp.sum(jnp.where(low, 0.0, values), axis=1, keepdims=True)
    return jnp.where(low, first, second) * (1.0 / HALF)


def turn_halves(values):
    first = lane_ids(values.shape) % HALF < HALF // 2
    return jnp.where(
        first, pltpu.roll(values, LANES - HALF // 2, 1), pltpu.roll(values, HALF // 2, 1)
    )


def at_head(values, head):
    low = lane_ids(values.shape) < HALF
    if head == 0:
        return jnp.where(low, values, 0.0).astype(bfloat16)
    return jnp.where(low, 0.0, pltpu.roll(values, HALF, 1)).astype(bfloat16)


def group_probs(query, key, begin, row_ids, col_ids):
    scores = matmul_nt(query, key) * HEAD_DIM ** (-0.5)
    scores = jnp.where((col_ids >= begin) & (col_ids <= row_ids), scores, masked_score)
    expd = jnp.exp(scores - jnp.max(scores, axis=1, keepdims=True))
    return expd / jnp.sum(expd, axis=1, keepdims=True)


def group_mask(ends_ref, group, rows):
    row_ids = lax.broadcasted_iota(jnp.int32, (rows, rows), 0)
    col_ids = lax.broadcasted_iota(jnp.int32, (rows, rows), 1)
    begin = jnp.zeros((rows, rows), jnp.int32)
    for slot in range(ends_ref.shape[1]):
        end = ends_ref[group, slot]
        begin = jnp.maximum(begin, jnp.where(row_ids >= end, end, 0))
    return begin, row_ids, col_ids


def group_rows(core, mine, other):
    first = jnp.where(core == 0, mine, other)
    second = jnp.where(core == 0, other, mine)
    return jnp.concatenate([first, second], axis=0)


def deep_rows(depth, step, layers, rows):
    at = lax.rem(depth + step + layers, layers) * rows
    return pl.ds(pl.multiple_of(at, rows), rows)


def attn_kernel(layers, where_ref, ends_ref, tok_m, tok_o, a_gain, q_gain, k_gain, cos, sin, *refs):
    pieces, refs = refs[:layers], refs[layers:]
    send, keep, pre_out, low_out, mixed_out, weight, held = refs
    group = pl.program_id(0)
    depth, core = where_ref[1], where_ref[2]
    local = tok_m.shape[0]

    @pl.when(group == 0)
    def _():
        for step, piece in enumerate(pieces):
            weight[deep_rows(depth, -step, layers, piece.shape[0]), :] = piece[...]

    x = group_rows(core, tok_m[...].astype(float32), tok_o[...].astype(float32))
    normed = (x * inverse_rms(x) * a_gain[...]).astype(bfloat16)
    pre = matmul(normed, weight[:, : 2 * LANES])
    pre_out[...] = pre
    cosine, sine = cos[...], sin[...]
    tiles = []
    for number, gain in enumerate((q_gain[...], k_gain[...])):
        tile = pre[:, number * LANES : (number + 1) * LANES]
        scaled = tile * lax.rsqrt(head_mean(tile * tile) + epsilon) * gain
        tiles.append(scaled * cosine + turn_halves(scaled) * sine)
    lane = lane_ids(tiles[0].shape)
    query = tiles[0].astype(bfloat16)
    key_value = jnp.where(lane < HALF, tiles[1], pre[:, LANES:])
    low_out[:, :LANES] = query
    low_out[:, LANES:] = key_value.astype(bfloat16)
    begin, row_ids, col_ids = group_mask(ends_ref, group, x.shape[0])
    turned = pltpu.roll(key_value, HALF, 1)
    mixed = jnp.zeros(tiles[0].shape, float32)
    for head in range(2):
        probs = group_probs(query, at_head(key_value, head), begin, row_ids, col_ids)
        mixed += matmul(probs.astype(bfloat16), at_head(turned, head))
    mixed = mixed.astype(bfloat16)
    mixed_out[...] = mixed
    held[...] = matmul_nt(mixed, weight[:, 2 * LANES :])
    mine = pl.multiple_of(core * local, local)
    other = pl.multiple_of((1 - core) * local, local)
    send[...] = held[pl.ds(other, local), :].astype(bfloat16)
    keep[...] = held[pl.ds(mine, local), :]


def attn_back_kernel(
    layers, where_ref, ends_ref, tok_m, tok_o, a_gain, q_gain, k_gain, cos, sin, dh_m, dh_o,
    pre_ref, low_ref, mixed_ref, weight, gain_ffn, *refs,
):
    send, keep, own, gains_out = refs[:4]
    pieces = refs[4 : 3 + layers]
    held, total, sum_a, sum_qk = refs[3 + layers :]
    group = pl.program_id(0)
    depth, core = where_ref[1], where_ref[2]
    local = tok_m.shape[0]

    @pl.when(group == 0)
    def _():
        total[...] = jnp.zeros_like(total)
        sum_a[...] = jnp.zeros_like(sum_a)
        sum_qk[...] = jnp.zeros_like(sum_qk)

    x = group_rows(core, tok_m[...].astype(float32), tok_o[...].astype(float32))
    unit_a = x * inverse_rms(x)
    normed = (unit_a * a_gain[...]).astype(bfloat16)
    d_hidden = group_rows(core, dh_m[...], dh_o[...])
    mixed = mixed_ref[...]
    total[:, 2 * LANES :] += matmul_tn(d_hidden, mixed)
    d_mixed = matmul(d_hidden, weight[:, 2 * LANES :]).astype(bfloat16)
    query = low_ref[:, :LANES]
    key_value = low_ref[:, LANES:].astype(float32)
    turned = pltpu.roll(key_value, HALF, 1)
    begin, row_ids, col_ids = group_mask(ends_ref, group, x.shape[0])
    scale = HEAD_DIM ** (-0.5)
    shape = mixed.shape
    d_query = jnp.zeros(shape, float32)
    d_keys, d_values = [], []
    for head in range(2):
        key = at_head(key_value, head)
        probs = group_probs(query, key, begin, row_ids, col_ids)
        d_values.append(matmul_tn(probs.astype(bfloat16), d_mixed))
        d_probs = matmul_nt(d_mixed, at_head(turned, head))
        centre = jnp.sum(probs * d_probs, axis=1, keepdims=True)
        d_scores = (probs * (d_probs - centre)).astype(bfloat16)
        d_query += matmul(d_scores, key)
        d_keys.append(matmul_tn(d_scores, query))
    d_key = d_keys[0] + pltpu.roll(d_keys[1], HALF, 1)
    d_value = pltpu.roll(d_values[0], HALF, 1) + d_values[1]
    lane = lane_ids(shape)
    cosine, sine = cos[...], sin[...]
    tiles = []
    for number, (grad, gain) in enumerate(((d_query, q_gain[...]), (d_key, k_gain[...]))):
        grad = grad * scale
        back = grad * cosine - turn_halves(grad) * sine
        tile = pre_ref[:, number * LANES : (number + 1) * LANES]
        factor = lax.rsqrt(head_mean(tile * tile) + epsilon)
        unit = tile * factor
        sum_qk[number : number + 1, :] += jnp.sum(back * unit, axis=0, keepdims=True)
        back = back * gain
        tiles.append(factor * (back - unit * head_mean(back * unit)))
    tiles[1] = jnp.where(lane < HALF, tiles[1], d_value)
    d_qkv = jnp.concatenate(tiles, axis=1).astype(bfloat16)
    total[:, : 2 * LANES] += matmul_tn(normed, d_qkv)
    held[...] = matmul_nt(d_qkv, weight[:, : 2 * LANES])
    sum_a[...] += jnp.sum(held[...] * unit_a, axis=0, keepdims=True)
    mine = pl.multiple_of(core * local, local)
    other = pl.multiple_of((1 - core) * local, local)
    send[...] = held[pl.ds(other, local), :].astype(bfloat16)
    keep[...] = held[pl.ds(mine, local), :]

    @pl.when(group == pl.num_programs(0) - 1)
    def _():
        for row in range(GAIN_ROWS):
            gains_out[row : row + 1, :LANES] = sum_a[:, row * LANES : (row + 1) * LANES]
            gains_out[row : row + 1, LANES : 2 * LANES] = gain_ffn[:, row * LANES : (row + 1) * LANES]
        q_sum = sum_qk[0:1, :] + pltpu.roll(sum_qk[0:1, :], HALF, 1)
        k_sum = pltpu.roll(sum_qk[1:2, :], HALF, 1)
        qk_sum = jnp.where(lane_ids(q_sum.shape) < HALF, q_sum, k_sum)
        ids = lax.broadcasted_iota(jnp.int32, (GAIN_ROWS, LANES), 0)
        gains_out[:, 2 * LANES :] = jnp.where(ids == 0, qk_sum, 0.0)
        gains = gains_out[...]
        top = gains.astype(bfloat16)
        rest = (gains - top.astype(float32)).astype(bfloat16)
        tail = jnp.concatenate([top.astype(float32), rest.astype(float32)], axis=0).astype(bfloat16)
        rows = own.shape[0]
        own[...] = total[deep_rows(depth, 0, layers, rows), :]
        for index, piece in enumerate(pieces):
            piece[:rows, :] = total[deep_rows(depth, index + 1, layers, rows), :].astype(bfloat16)
            piece[rows:, :] = tail


def attn_specs(rows, width, group_height):
    scalar = pl.BlockSpec(memory_space=pltpu.SMEM)
    block = pl.BlockSpec((rows, width), lambda i: (i, 0))
    gain = pl.BlockSpec((1, width), lambda i: (0, 0))
    small = pl.BlockSpec((1, LANES), lambda i: (0, 0))
    table = pl.BlockSpec((group_height, LANES), lambda i: (i, 0))
    wide = pl.BlockSpec((group_height, 2 * LANES), lambda i: (i, 0))
    return scalar, block, gain, small, table, wide


def whole_spec(shape):
    return pl.BlockSpec(shape, lambda i: (0, 0), pipeline_mode=pl.Buffered(1))


def attn(where, ends, tok_mine, tok_other, gains, tables, pieces):
    layers = len(pieces)
    rows, width = tok_mine.shape
    local = rows // PLANE
    scalar, block, gain, small, table, wide = attn_specs(local, width, 2 * local)
    high, columns = pieces[0].shape
    weight = (layers * high, columns)
    return pl.pallas_call(
        lambda *refs: attn_kernel(layers, *refs),
        grid=(PLANE,),
        in_specs=[scalar, scalar, block, block, gain, small, small, table, table]
        + [whole_spec((high, columns))] * layers,
        out_specs=[block, block, wide, wide, table, whole_spec(weight)],
        out_shape=[
            jax.ShapeDtypeStruct((rows, width), bfloat16),
            jax.ShapeDtypeStruct((rows, width), float32),
            jax.ShapeDtypeStruct((2 * rows, 2 * LANES), float32),
            jax.ShapeDtypeStruct((2 * rows, 2 * LANES), bfloat16),
            jax.ShapeDtypeStruct((2 * rows, LANES), bfloat16),
            jax.ShapeDtypeStruct(weight, bfloat16),
        ],
        scratch_shapes=[pltpu.VMEM((2 * local, width), float32)],
        compiler_params=pltpu.CompilerParams(vmem_limit_bytes=VMEM_BYTES),
        cost_estimate=COST,
    )(where, ends, tok_mine, tok_other, *gains, *tables, *pieces)


def attn_back(where, ends, layers, tok_mine, tok_other, gains, tables, dh, saved, weight, gain_ffn):
    rows, width = tok_mine.shape
    local = rows // PLANE
    scalar, block, gain, small, table, wide = attn_specs(local, width, 2 * local)
    high, columns = weight.shape[0] // layers, weight.shape[1]
    tail = 2 * GAIN_ROWS
    return pl.pallas_call(
        lambda *refs: attn_back_kernel(layers, *refs),
        grid=(PLANE,),
        in_specs=[scalar, scalar, block, block, gain, small, small, table, table, block, block]
        + [wide, wide, table, whole_spec(weight.shape), gain],
        out_specs=[block, block, whole_spec((high, columns)), whole_spec((GAIN_ROWS, columns))]
        + [whole_spec((high + tail, columns))] * (layers - 1),
        out_shape=[
            jax.ShapeDtypeStruct((rows, width), bfloat16),
            jax.ShapeDtypeStruct((rows, width), float32),
            jax.ShapeDtypeStruct((high, columns), float32),
            jax.ShapeDtypeStruct((GAIN_ROWS, columns), float32),
        ]
        + [jax.ShapeDtypeStruct((high + tail, columns), bfloat16)] * (layers - 1),
        scratch_shapes=[
            pltpu.VMEM((2 * local, width), float32),
            pltpu.VMEM(weight.shape, float32),
            pltpu.VMEM((1, width), float32),
            pltpu.VMEM((8, LANES), float32),
        ],
        compiler_params=pltpu.CompilerParams(vmem_limit_bytes=VMEM_BYTES),
        cost_estimate=COST,
    )(where, ends, tok_mine, tok_other, *gains, *tables, *dh, *saved, weight, gain_ffn)


def ffn_kernel(layers, where_ref, ends_ref, x_o, x_m, g_o, g_m, *refs):
    pieces, refs = refs[:layers], refs[layers:]
    out_send, out_keep, dn_send, dn_keep, own_grad = refs[:5]
    grad_pieces = refs[5 : 4 + layers]
    weight, total = refs[4 + layers :]
    step = pl.program_id(0)
    depth, core = where_ref[1], where_ref[2]
    rows = pieces[0].shape[0]
    width = x_o.shape[1]
    both = width
    big = both // 2
    local = x_o.shape[0] // 2

    def row_of(index):
        at = lax.rem(depth + index + layers, layers) * rows
        return pl.ds(pl.multiple_of(at, rows), rows)

    @pl.when(step == 0)
    def _():
        for index, piece in enumerate(pieces):
            weight[row_of(-index), :] = piece[...]
        total[...] = jnp.zeros_like(total)

    def live_rows(values, group, at_core):
        ids = lax.broadcasted_iota(jnp.int32, values.shape, 0) + at_core * local
        return jnp.where(ids < ends_ref[group, ends_ref.shape[1] - 1], values, jnp.zeros_like(values))

    x = jnp.concatenate([x_o[...], x_m[...]], axis=0)
    grads = jnp.concatenate(
        [live_rows(g_o[k * local : (k + 1) * local, :], 2 * step + k, 1 - core) for k in range(2)]
        + [live_rows(g_m[k * local : (k + 1) * local, :], 2 * step + k, core) for k in range(2)],
        axis=0,
    )
    half = 2 * local
    w_both = weight[:, :both]
    w_down = weight[:, both : both + big]
    w_small = weight[:, both + big : both + big + LANES]
    w_small_down = weight[:, both + big + LANES :]
    lane = lane_ids((x.shape[0], LANES))

    def parts_of(gate, up, d_act):
        sigma = 1.0 / (1.0 + jnp.exp(-gate))
        silu = gate * sigma
        act = silu * up
        d_gate = d_act * up * sigma * (1.0 + gate * (1.0 - sigma))
        return act, d_gate, d_act * silu

    pre = matmul(x, w_both)
    act, d_gate, d_up = parts_of(pre[:, :big], pre[:, big:], matmul(grads, w_down))
    pre = matmul(x, w_small)
    act_s, d_gate_s, d_up_s = parts_of(
        pre, pltpu.roll(pre, HALF, 1), matmul(grads, w_small_down)
    )
    act_s = jnp.where(lane < HALF, act_s, 0.0).astype(bfloat16)
    d_small = jnp.where(lane < HALF, d_gate_s, pltpu.roll(d_up_s, HALF, 1)).astype(bfloat16)
    act = act.astype(bfloat16)
    d_both = jnp.concatenate([d_gate, d_up], axis=1).astype(bfloat16)

    partial = matmul_nt(act, w_down) + matmul_nt(act_s, w_small_down)
    out_send[...] = partial[:half].astype(bfloat16)
    out_keep[...] = partial[half:]
    partial = matmul_nt(d_both, w_both) + matmul_nt(d_small, w_small)
    dn_send[...] = partial[:half].astype(bfloat16)
    dn_keep[...] = partial[half:]
    total[:, :both] += matmul_tn(x, d_both)
    total[:, both : both + big] += matmul_tn(grads, act)
    total[:, both + big : both + big + LANES] += matmul_tn(x, d_small)
    total[:, both + big + LANES :] += matmul_tn(grads, act_s)

    @pl.when(step == pl.num_programs(0) - 1)
    def _():
        own_grad[...] = total[row_of(0), :]
        for index, piece in enumerate(grad_pieces):
            piece[...] = total[row_of(index + 1), :].astype(bfloat16)


def ffn(where, ends, x_mine, x_other, g_mine, g_other, pieces):
    layers = len(pieces)
    rows, width = x_mine.shape
    high, columns = pieces[0].shape
    block = rows // 2
    row_spec = pl.BlockSpec((block, width), lambda i: (i, 0))

    scalar = pl.BlockSpec(memory_space=pltpu.SMEM)
    return pl.pallas_call(
        lambda *refs: ffn_kernel(layers, *refs),
        grid=(2,),
        in_specs=[scalar, scalar] + [row_spec] * 4 + [whole_spec((high, columns))] * layers,
        out_specs=[row_spec] * 4 + [whole_spec((high, columns))] * layers,
        out_shape=[
            jax.ShapeDtypeStruct((rows, width), bfloat16),
            jax.ShapeDtypeStruct((rows, width), float32),
            jax.ShapeDtypeStruct((rows, width), bfloat16),
            jax.ShapeDtypeStruct((rows, width), float32),
            jax.ShapeDtypeStruct((high, columns), float32),
        ]
        + [jax.ShapeDtypeStruct((high, columns), bfloat16)] * (layers - 1),
        scratch_shapes=[
            pltpu.VMEM((layers * high, columns), bfloat16),
            pltpu.VMEM((layers * high, columns), float32),
        ],
        compiler_params=pltpu.CompilerParams(vmem_limit_bytes=VMEM_BYTES),
        cost_estimate=COST,
    )(where, ends, x_other, x_mine, g_other, g_mine, *pieces)


def chip_sum_kernel(keep, received, *outs):
    rows = outs[0].shape[0]
    for mask, out in enumerate(outs):
        span = slice(mask * rows, (mask + 1) * rows)
        out[...] = (keep[span, :] + received[span, :].astype(float32)).astype(out.dtype)


def chip_sum(keep, received):
    shape = (keep.shape[0] // PLANE, keep.shape[1])
    own, *rest = call(
        chip_sum_kernel, [(shape, float32)] + [(shape, bfloat16)] * (PLANE - 1), keep, received
    )
    return [own] + [send_plane(part, mask + 1) for mask, part in enumerate(rest)]


def add_up(parts):
    return sum(part.astype(float32) for part in parts)


def plane_sum_kernel(where_ref, own, *refs):
    received, outs, held = refs[: -PLANE - 1], refs[-PLANE - 1 : -1], refs[-1]
    value = own[...]
    high = own.shape[0]
    for part in received:
        value = value + part[:high, :].astype(float32)
    held[...] = value
    place = where_ref[0]
    rows = high // PLANE
    for mask, out in enumerate(outs):
        at = pl.multiple_of((place ^ mask) * rows, rows)
        out[...] = held[pl.ds(at, rows), :].astype(out.dtype)


def joined_gains(tail):
    return tail[:GAIN_ROWS] + tail[GAIN_ROWS:]


def split_gains(gains):
    top = gains.astype(bfloat16).astype(float32)
    rest = (gains - top).astype(bfloat16).astype(float32)
    return jnp.concatenate([top, rest], axis=0)


def plane_sum_attn_kernel(where_ref, own, gains, *refs):
    received, outs = refs[: -PLANE - 2], refs[-PLANE - 2 : -2]
    held, held_gains = refs[-2:]
    layers = len(received) + 1
    value = own[...]
    high = own.shape[0]
    depth = where_ref[1]
    held_gains[deep_rows(depth, 0, layers, GAIN_ROWS), :] = joined_gains(split_gains(gains[...]))
    for step, part in enumerate(received):
        value = value + part[:high, :].astype(float32)
        held_gains[deep_rows(depth, -1 - step, layers, GAIN_ROWS), :] = joined_gains(
            part[high:, :].astype(float32)
        )
    held[...] = value
    sums = held_gains[:GAIN_ROWS, :]
    for layer in range(1, layers):
        sums = sums + held_gains[layer * GAIN_ROWS : (layer + 1) * GAIN_ROWS, :]
    tail = split_gains(sums)
    place = where_ref[0]
    rows = high // PLANE
    for mask, out in enumerate(outs):
        at = pl.multiple_of((place ^ mask) * rows, rows)
        part = held[pl.ds(at, rows), :]
        if mask:
            tall = out.shape[0] - tail.shape[0]
            out[:tall, :] = padded(part, tall).astype(bfloat16)
            out[tall:, :] = tail.astype(bfloat16)
        else:
            out[:rows, :] = part
            out[rows:, :] = tail


def plane_sum(where, own, grad_pieces, gains=None):
    received = [send_deep(piece, step + 1) for step, piece in enumerate(grad_pieces)]
    rows, columns = own.shape[0] // PLANE, own.shape[1]
    scratch = [pltpu.VMEM(own.shape, float32)]
    if gains is None:
        shapes = [((rows, columns), float32)] + [((rows, columns), bfloat16)] * (PLANE - 1)
        outs = call(plane_sum_kernel, shapes, where, own, *received, scalars=1, scratch=scratch)
    else:
        tail = 2 * GAIN_ROWS
        shapes = [((rows + tail, columns), float32)]
        shapes += [((max(rows, 16) + tail, columns), bfloat16)] * (PLANE - 1)
        scratch.append(pltpu.VMEM(((len(received) + 1) * GAIN_ROWS, columns), float32))
        outs = call(
            plane_sum_attn_kernel, shapes, where, own, gains, *received, scalars=1, scratch=scratch
        )
    return [outs[0]] + [send_plane(part, mask + 1) for mask, part in enumerate(outs[1:])]


def pick_place(refs, place, target, columns, rows):
    value = jnp.zeros((rows, columns.stop - columns.start), float32)
    for mask, ref in enumerate(refs):
        value = jnp.where(place ^ mask == target, ref[:, columns].astype(float32)[:rows], value)
    return value


def place_ffn_kernel(where_ref, own, one, two, three, out_g, out_u, out_d):
    place = where_ref[0]
    refs = (own, one, two, three)
    big = out_g.shape[1] // LANES // PLANE * LANES
    last = PLANE * big
    for mask, ref in enumerate(refs):
        at = pl.ds(pl.multiple_of((place ^ mask) * big, LANES), big)
        for number, out in enumerate((out_g, out_u, out_d)):
            out[:, at] = ref[:, number * big : (number + 1) * big].astype(float32)
    for pair in range(PLANE // 2):
        low = pick_place(refs, place, 2 * pair, slice(3 * big, 3 * big + 2 * LANES), out_g.shape[0])
        high = pick_place(refs, place, 2 * pair + 1, slice(3 * big, 3 * big + 2 * LANES), out_g.shape[0])
        lane = lane_ids((low.shape[0], LANES))
        span = slice(last + pair * LANES, last + (pair + 1) * LANES)
        gu_low, gu_high = low[:, :LANES], high[:, :LANES]
        out_g[:, span] = jnp.where(lane < HALF, gu_low, pltpu.roll(gu_high, HALF, 1))
        out_u[:, span] = jnp.where(lane < HALF, pltpu.roll(gu_low, HALF, 1), gu_high)
        out_d[:, span] = jnp.where(lane < HALF, low[:, LANES:], pltpu.roll(high[:, LANES:], HALF, 1))


def place_attn_kernel(where_ref, own, one, two, three, out_q, out_k, out_v, out_o, out_gains):
    place = where_ref[0]
    refs = (own, one, two, three)
    rows = out_q.shape[0]
    for mask, ref in enumerate(refs):
        at = pl.ds(pl.multiple_of((place ^ mask) * LANES, LANES), LANES)
        out_q[:, at] = ref[:, :LANES].astype(float32)[:rows]
        out_o[:, at] = ref[:, 2 * LANES :].astype(float32)[:rows]
    for pair in range(PLANE // 2):
        low = pick_place(refs, place, 2 * pair, slice(LANES, 2 * LANES), rows)
        high = pick_place(refs, place, 2 * pair + 1, slice(LANES, 2 * LANES), rows)
        lane = lane_ids(low.shape)
        span = slice(pair * LANES, (pair + 1) * LANES)
        out_k[:, span] = jnp.where(lane < HALF, low, pltpu.roll(high, HALF, 1))
        out_v[:, span] = jnp.where(lane < HALF, pltpu.roll(low, HALF, 1), high)
    tails = [joined_gains(ref[ref.shape[0] - 2 * GAIN_ROWS :, :].astype(float32)) for ref in refs]
    out_gains[...] = (tails[0] + tails[1]) + (tails[2] + tails[3])


def gather_rows(local):
    mine = jnp.concatenate([local] + [send_plane(local, mask) for mask in range(1, PLANE)])
    return mine, swap_cores(mine)


def body(
    tokens,
    lengths,
    attn_gain,
    query_gain,
    key_gain,
    ffn_gain,
    w_query,
    w_key,
    w_value,
    w_out,
    w_gate,
    w_up,
    w_down,
    cotangent,
):
    dp = lax.axis_index("dp")
    core = lax.axis_index("tensor")
    layers = lax.axis_size("dp") // PLANE
    where = jnp.stack([dp % PLANE, dp // PLANE, core]).astype(jnp.int32)
    local_rows, model = tokens.shape
    total_rows = local_rows * lax.axis_size("tensor")
    rows = w_query.shape[0]
    q_cols = w_query.shape[1] // PLANE
    kv_cols = w_key.shape[1] // PLANE
    local_kv = kv_cols // HEAD_DIM
    share = q_cols // kv_cols
    attn_cols = 2 * q_cols + 2 * kv_cols
    ff_cols = 3 * (w_gate.shape[1] // LANES // PLANE * LANES) + 2 * LANES

    parts, high = attn_rows(rows)
    tall = max(rows, 16)
    messages = call(
        pack_kernel,
        [((high + 2 * tall, model), bfloat16)] * PLANE,
        where,
        lengths,
        w_query,
        w_key,
        w_value,
        w_out,
        w_gate,
        w_up,
        w_down,
        scalars=2,
    )
    messages = [messages[0]] + [send_plane(messages[m], m) for m in range(1, PLANE)]
    attn_piece, ff_piece, lens = call(
        unpack_kernel,
        [
            ((PLANE * rows, attn_cols), bfloat16),
            ((PLANE * rows, ff_cols), bfloat16),
            ((PLANE * 8, LANES), float32),
        ],
        where,
        *messages,
        scalars=1,
        scratch=[
            pltpu.VMEM((PLANE * rows, attn_cols), float32),
            pltpu.VMEM((PLANE * rows, ff_cols), float32),
        ],
    )
    attn_pieces = [attn_piece] + [send_deep(attn_piece, step) for step in range(1, layers)]
    ff_pieces = [ff_piece] + [send_deep(ff_piece, step) for step in range(1, layers)]
    local = jnp.concatenate([tokens, cotangent])
    tok_mine, cot_mine = call(
        split_rows_kernel,
        [((PLANE * local_rows, model), bfloat16)] * 2,
        local,
        *[send_plane(local, m) for m in range(1, PLANE)],
    )
    tok_other = swap_cores(tok_mine)
    cot_other = swap_cores(cot_mine)

    slots = lengths.shape[1]
    all_lengths = lens.reshape(PLANE, 8, LANES)[:, 0, :slots].astype(jnp.int32)
    ends = jnp.cumsum(all_lengths, axis=1, dtype=jnp.int32)
    row_ids = jnp.arange(total_rows, dtype=jnp.int32)
    begin = jnp.max(
        jnp.where(row_ids[None, :, None] >= ends[:, None, :], ends[:, None, :], 0), axis=2
    )
    position = (row_ids[None, :] - begin).reshape(-1).astype(jnp.float32)
    spread = jnp.arange(LANES, dtype=jnp.int32) % (HEAD_DIM // 2)
    freqs = rope_base ** (-spread.astype(jnp.float32) * 2.0 / HEAD_DIM)
    angles = position[:, None] * freqs[None, :]
    sign = jnp.where(jnp.arange(LANES) % HEAD_DIM < HEAD_DIM // 2, -1.0, 1.0).astype(jnp.float32)
    tables = (jnp.cos(angles), jnp.sin(angles) * sign)
    gains = (
        attn_gain[None, :],
        jnp.concatenate([query_gain, query_gain])[None, :],
        jnp.concatenate([key_gain, key_gain])[None, :],
    )

    inputs = tokens.astype(jnp.float32)
    factor_a = inverse_rms(inputs)
    unit_a = inputs * factor_a
    send, keep, *saved, attn_weight = attn(
        where, ends, tok_mine, tok_other, gains, tables, attn_pieces
    )
    hidden = inputs + add_up(chip_sum(keep, swap_cores(send)))
    factor_b = inverse_rms(hidden)
    unit_b = hidden * factor_b
    x_mine, x_other = gather_rows((unit_b * ffn_gain).astype(jnp.bfloat16))

    out_send, out_keep, dn_send, dn_keep, own_ff, *ff_grads = ffn(
        where, ends, x_mine, x_other, cot_mine, cot_other, ff_pieces
    )
    d_normed2 = add_up(chip_sum(dn_keep, swap_cores(dn_send)))
    grad_out = jnp.where(
        (jnp.arange(local_rows) + core * local_rows < ends[0, slots - 1])[:, None],
        cotangent,
        jnp.zeros_like(cotangent),
    )
    gain_ffn = jnp.sum(d_normed2 * unit_b, axis=0)
    d_hidden = grad_out.astype(jnp.float32) + norm_back(d_normed2 * ffn_gain, unit_b, factor_b)
    h_mine, h_other = gather_rows(d_hidden.astype(jnp.bfloat16))
    ff_parts = plane_sum(where, own_ff, ff_grads)
    block_out = (hidden + add_up(chip_sum(out_keep, swap_cores(out_send)))).astype(jnp.bfloat16)

    send, keep, own_attn, part_gains, *attn_grads = attn_back(
        where, ends, layers, tok_mine, tok_other, gains, tables, (h_mine, h_other), saved,
        attn_weight, gain_ffn[None, :],
    )
    attn_parts = plane_sum(where, own_attn, attn_grads, part_gains)
    d_normed = add_up(chip_sum(keep, swap_cores(send)))
    grad_tokens = d_hidden + norm_back(d_normed * attn_gain, unit_a, factor_a)
    grad_gate, grad_up, grad_down = call(
        place_ffn_kernel, [(w_gate.shape, float32)] * 3, where, *ff_parts, scalars=1
    )
    grad_query, grad_key, grad_value, grad_out_w, sums = call(
        place_attn_kernel,
        [(w.shape, float32) for w in (w_query, w_key, w_value, w_out)]
        + [((GAIN_ROWS, attn_cols), float32)],
        where,
        *attn_parts,
        scalars=1,
    )
    sums = sums + swap_cores(sums)
    return (
        block_out,
        grad_tokens,
        sums[:, :LANES].reshape(-1),
        sums[0, 2 * LANES : 2 * LANES + HEAD_DIM],
        sums[0, 2 * LANES + HEAD_DIM :],
        sums[:, LANES : 2 * LANES].reshape(-1),
        grad_query,
        grad_key,
        grad_value,
        grad_out_w,
        grad_gate,
        grad_up,
        grad_down,
    )


def solution(mesh):
    placed = (
        P(("dp", "tensor"), None),
        P("dp", None),
        P(),
        P(),
        P(),
        P(),
        P("dp", "tensor"),
        P("dp", "tensor"),
        P("dp", "tensor"),
        P("dp", "tensor"),
        P("dp", "tensor"),
        P("dp", "tensor"),
        P("dp", "tensor"),
        P(("dp", "tensor"), None),
    )
    return jax.shard_map(
        body,
        mesh=mesh,
        in_specs=placed,
        out_specs=(
            P(("dp", "tensor"), None),
            P(("dp", "tensor"), None),
            P(),
            P(),
            P(),
            P(),
            P("dp", "tensor"),
            P("dp", "tensor"),
            P("dp", "tensor"),
            P("dp", "tensor"),
            P("dp", "tensor"),
            P("dp", "tensor"),
            P("dp", "tensor"),
        ),
        check_vma=False,
    )
```

```python
import jax
import jax.numpy as jnp
from jax import lax
from jax.experimental import pallas as pl
from jax.experimental.pallas import tpu as pltpu
from jax.sharding import PartitionSpec as P

HEAD_DIM = 64


epsilon = 1e-05
rope_base = 1000000.0
masked_score = -1e30


def inverse_rms(values):
    return lax.rsqrt(jnp.mean(values * values, axis=-1, keepdims=True) + epsilon)


def norm_back(grad_unit, unit, factor):
    return factor * (grad_unit - unit * jnp.mean(grad_unit * unit, axis=-1, keepdims=True))


def matmul(first_op, second_op):
    return jnp.dot(first_op, second_op, preferred_element_type=jnp.float32)


def matmul_nt(first_op, second_op):
    return lax.dot_general(
        first_op, second_op, (((1,), (1,)), ((), ())), preferred_element_type=jnp.float32
    )


def matmul_tn(first_op, second_op):
    return lax.dot_general(
        first_op, second_op, (((0,), (0,)), ((), ())), preferred_element_type=jnp.float32
    )


def seq_layout(seq_lengths, total_rows):
    ends = jnp.cumsum(seq_lengths, dtype=jnp.int32)
    starts = ends - seq_lengths
    row_ids = jnp.arange(total_rows, dtype=jnp.int32)
    segment = jnp.sum(
        (row_ids[:, None] >= ends[None, :]).astype(jnp.int32), axis=1, dtype=jnp.int32
    )
    slot_ids = jnp.arange(seq_lengths.shape[0], dtype=jnp.int32)
    picked = (segment[:, None] == slot_ids[None, :]).astype(jnp.int32)
    begin = (
        jnp.sum(picked * starts[None, :], axis=1, dtype=jnp.int32)
        + (segment == seq_lengths.shape[0]).astype(jnp.int32) * ends[-1]
    )
    allowed = (segment[:, None] == segment[None, :]) & (row_ids[:, None] >= row_ids[None, :])
    return (row_ids - begin, row_ids < ends[-1], allowed)


def rope_tables(position, head_size):
    half_dim = head_size // 2
    freqs = rope_base ** (-jnp.arange(half_dim, dtype=jnp.float32) * 2.0 / head_size)
    angles = position.astype(jnp.float32)[:, None] * freqs[None, :]
    return (jnp.cos(angles)[:, None, :], jnp.sin(angles)[:, None, :])


def rotate(values, cosine, sine):
    half_dim = values.shape[-1] // 2
    first_half = values[..., :half_dim]
    second_half = values[..., half_dim:]
    return jnp.concatenate(
        [first_half * cosine - second_half * sine, second_half * cosine + first_half * sine],
        axis=-1,
    )


def rotate_back(grads, cosine, sine):
    half_dim = grads.shape[-1] // 2
    first_half = grads[..., :half_dim]
    second_half = grads[..., half_dim:]
    return jnp.concatenate(
        [first_half * cosine + second_half * sine, second_half * cosine - first_half * sine],
        axis=-1,
    )

PLANE = 4
LANES = 128
HALF = 64
VMEM_BYTES = 60 * 1024 * 1024
COST = pl.CostEstimate(flops=1024, bytes_accessed=1024, transcendentals=0)
GAIN_ROWS = 8
float32 = jnp.float32
bfloat16 = jnp.bfloat16


def send_plane(values, mask):
    count = lax.axis_size("dp")
    return lax.ppermute(values, "dp", [(i, i ^ mask) for i in range(count)])


def send_deep(values, step):
    count = lax.axis_size("dp")
    return lax.ppermute(values, "dp", [(i, (i + PLANE * step) % count) for i in range(count)])


def swap_cores(values):
    return lax.ppermute(values, "tensor", [(0, 1), (1, 0)])


def call(kernel, outs, *operands, scalars=0, scratch=()):
    specs = [pl.BlockSpec(memory_space=pltpu.SMEM)] * scalars
    specs += [pl.BlockSpec(memory_space=pltpu.VMEM)] * (len(operands) - scalars)
    return pl.pallas_call(
        kernel,
        out_shape=[jax.ShapeDtypeStruct(shape, kind) for shape, kind in outs],
        in_specs=specs,
        out_specs=[pl.BlockSpec(memory_space=pltpu.VMEM)] * len(outs),
        scratch_shapes=list(scratch),
        compiler_params=pltpu.CompilerParams(vmem_limit_bytes=VMEM_BYTES),
        cost_estimate=COST,
    )(*operands)


def lane_ids(shape):
    return lax.broadcasted_iota(jnp.int32, shape, len(shape) - 1)


def half_tile(ref, first_tile, place, upper):
    start = pl.multiple_of((first_tile + place // 2) * LANES, LANES)
    tile = ref[:, pl.ds(start, LANES)].astype(float32)
    turned = pltpu.roll(tile, HALF, 1)
    odd = place % 2 == 1
    if upper:
        return jnp.where(odd, tile, turned)
    return jnp.where(odd, turned, tile)


def padded(values, rows):
    if values.shape[0] == rows:
        return values
    blank = jnp.zeros((rows - values.shape[0], values.shape[1]), values.dtype)
    return jnp.concatenate([values, blank], axis=0)


def attn_rows(rows):
    return (2, rows // 2) if rows % 32 == 0 else (1, max(rows, 16))


def pack_kernel(where_ref, lengths_ref, w_q, w_k, w_v, w_o, w_g, w_u, w_d, *outs):
    rows = w_q.shape[0]
    parts, high = attn_rows(rows)
    tall = max(rows, 16)
    big = w_g.shape[1] // LANES // PLANE * LANES
    last = w_g.shape[1] // LANES // PLANE * PLANE
    place = where_ref[0]
    lane = lane_ids((rows, LANES))
    for mask, out in enumerate(outs):
        other = place ^ mask
        at = pl.multiple_of(other * LANES, LANES)
        tile = jnp.where(
            lane < HALF, half_tile(w_k, 0, other, False), half_tile(w_v, 0, other, True)
        )
        piece = jnp.concatenate(
            [w_q[:, pl.ds(at, LANES)].astype(float32), tile, w_o[:, pl.ds(at, LANES)].astype(float32)],
            axis=1,
        )
        pieces = [piece[: rows // 2], piece[rows // 2 :]] if parts == 2 else [padded(piece, high)]
        width = piece.shape[1]
        for part, values in enumerate(pieces):
            out[:high, part * width : (part + 1) * width] = values.astype(bfloat16)
        free = out.shape[1] - parts * width
        ids = lane_ids((high, free))
        marks = jnp.zeros((high, free), float32)
        for slot in range(lengths_ref.shape[1]):
            marks = jnp.where(ids == free - LANES + slot, lengths_ref[0, slot].astype(float32), marks)
        out[:high, parts * width :] = marks.astype(bfloat16)

        at = pl.multiple_of(other * big, LANES)
        small = jnp.where(
            lane < HALF, half_tile(w_g, last, other, False), half_tile(w_u, last, other, True)
        )
        small_down = jnp.where(lane < HALF, half_tile(w_d, last, other, False), 0.0)
        upper = jnp.concatenate(
            [w_g[:, pl.ds(at, big)].astype(float32), w_u[:, pl.ds(at, big)].astype(float32)], axis=1
        )
        lower = jnp.concatenate(
            [w_d[:, pl.ds(at, big)].astype(float32), small, small_down], axis=1
        )
        out[high : high + tall, :] = padded(upper, tall).astype(bfloat16)
        out[high + tall :, : lower.shape[1]] = padded(lower, tall).astype(bfloat16)
        out[high + tall :, lower.shape[1] :] = jnp.zeros(
            (tall, out.shape[1] - lower.shape[1]), bfloat16
        )


def unpack_kernel(where_ref, own, one, two, three, attn_out, ffn_out, lens_out, held_attn, held_ffn):
    rows = attn_out.shape[0] // PLANE
    width = attn_out.shape[1]
    parts, high = attn_rows(rows)
    tall = max(rows, 16)
    place = where_ref[0]
    for mask, message in enumerate((own, one, two, three)):
        at = pl.ds(pl.multiple_of((place ^ mask) * rows, rows), rows)
        values = [
            message[:high, part * width : (part + 1) * width].astype(float32)
            for part in range(parts)
        ]
        held_attn[at, :] = jnp.concatenate(values, axis=0) if parts == 2 else values[0][:rows]
        lens = message[:16, message.shape[1] - LANES :].astype(float32)
        lens_out[mask * 8 : (mask + 1) * 8, :] = lens[:8]
        full = message.shape[1]
        held_ffn[at, :full] = message[high : high + tall, :].astype(float32)[:rows]
        rest = held_ffn.shape[1] - full
        held_ffn[at, full:] = message[high + tall :, :rest].astype(float32)[:rows]
    attn_out[...] = held_attn[...].astype(bfloat16)
    ffn_out[...] = held_ffn[...].astype(bfloat16)


def split_rows_kernel(own, one, two, three, tok_out, cot_out):
    local = own.shape[0] // 2
    for mask, message in enumerate((own, one, two, three)):
        span = slice(mask * local, (mask + 1) * local)
        tok_out[span, :] = message[:local, :]
        cot_out[span, :] = message[local:, :]


def head_mean(values):
    low = lane_ids(values.shape) < HALF
    first = jnp.sum(jnp.where(low, values, 0.0), axis=1, keepdims=True)
    second = jnp.sum(jnp.where(low, 0.0, values), axis=1, keepdims=True)
    return jnp.where(low, first, second) * (1.0 / HALF)


def turn_halves(values):
    first = lane_ids(values.shape) % HALF < HALF // 2
    return jnp.where(
        first, pltpu.roll(values, LANES - HALF // 2, 1), pltpu.roll(values, HALF // 2, 1)
    )


def at_head(values, head):
    low = lane_ids(values.shape) < HALF
    if head == 0:
        return jnp.where(low, values, 0.0).astype(bfloat16)
    return jnp.where(low, 0.0, pltpu.roll(values, HALF, 1)).astype(bfloat16)


def group_probs(query, key, begin, row_ids, col_ids):
    scores = matmul_nt(query, key) * HEAD_DIM ** (-0.5)
    scores = jnp.where((col_ids >= begin) & (col_ids <= row_ids), scores, masked_score)
    expd = jnp.exp(scores - jnp.max(scores, axis=1, keepdims=True))
    return expd / jnp.sum(expd, axis=1, keepdims=True)


def group_mask(ends_ref, group, rows):
    row_ids = lax.broadcasted_iota(jnp.int32, (rows, rows), 0)
    col_ids = lax.broadcasted_iota(jnp.int32, (rows, rows), 1)
    begin = jnp.zeros((rows, rows), jnp.int32)
    for slot in range(ends_ref.shape[1]):
        end = ends_ref[group, slot]
        begin = jnp.maximum(begin, jnp.where(row_ids >= end, end, 0))
    return begin, row_ids, col_ids


def group_rows(core, mine, other):
    first = jnp.where(core == 0, mine, other)
    second = jnp.where(core == 0, other, mine)
    return jnp.concatenate([first, second], axis=0)


def deep_rows(depth, step, layers, rows):
    at = lax.rem(depth + step + layers, layers) * rows
    return pl.ds(pl.multiple_of(at, rows), rows)


def attn_kernel(layers, where_ref, ends_ref, tok_m, tok_o, a_gain, q_gain, k_gain, cos, sin, *refs):
    pieces, refs = refs[:layers], refs[layers:]
    send, keep, pre_out, low_out, mixed_out, weight, held = refs
    group = pl.program_id(0)
    depth, core = where_ref[1], where_ref[2]
    local = tok_m.shape[0]

    @pl.when(group == 0)
    def _():
        for step, piece in enumerate(pieces):
            weight[deep_rows(depth, -step, layers, piece.shape[0]), :] = piece[...]

    x = group_rows(core, tok_m[...].astype(float32), tok_o[...].astype(float32))
    normed = (x * inverse_rms(x) * a_gain[...]).astype(bfloat16)
    pre = matmul(normed, weight[:, : 2 * LANES])
    pre_out[...] = pre
    cosine, sine = cos[...], sin[...]
    tiles = []
    for number, gain in enumerate((q_gain[...], k_gain[...])):
        tile = pre[:, number * LANES : (number + 1) * LANES]
        scaled = tile * lax.rsqrt(head_mean(tile * tile) + epsilon) * gain
        tiles.append(scaled * cosine + turn_halves(scaled) * sine)
    lane = lane_ids(tiles[0].shape)
    query = tiles[0].astype(bfloat16)
    key_value = jnp.where(lane < HALF, tiles[1], pre[:, LANES:])
    low_out[:, :LANES] = query
    low_out[:, LANES:] = key_value.astype(bfloat16)
    begin, row_ids, col_ids = group_mask(ends_ref, group, x.shape[0])
    turned = pltpu.roll(key_value, HALF, 1)
    mixed = jnp.zeros(tiles[0].shape, float32)
    for head in range(2):
        probs = group_probs(query, at_head(key_value, head), begin, row_ids, col_ids)
        mixed += matmul(probs.astype(bfloat16), at_head(turned, head))
    mixed = mixed.astype(bfloat16)
    mixed_out[...] = mixed
    held[...] = matmul_nt(mixed, weight[:, 2 * LANES :])
    mine = pl.multiple_of(core * local, local)
    other = pl.multiple_of((1 - core) * local, local)
    send[...] = held[pl.ds(other, local), :].astype(bfloat16)
    keep[...] = held[pl.ds(mine, local), :]


def attn_back_kernel(
    layers, where_ref, ends_ref, tok_m, tok_o, a_gain, q_gain, k_gain, cos, sin, dh_m, dh_o,
    pre_ref, low_ref, mixed_ref, weight, gain_ffn, *refs,
):
    send, keep, own, gains_out = refs[:4]
    pieces = refs[4 : 3 + layers]
    held, total, sum_a, sum_qk = refs[3 + layers :]
    group = pl.program_id(0)
    depth, core = where_ref[1], where_ref[2]
    local = tok_m.shape[0]

    @pl.when(group == 0)
    def _():
        total[...] = jnp.zeros_like(total)
        sum_a[...] = jnp.zeros_like(sum_a)
        sum_qk[...] = jnp.zeros_like(sum_qk)

    x = group_rows(core, tok_m[...].astype(float32), tok_o[...].astype(float32))
    unit_a = x * inverse_rms(x)
    normed = (unit_a * a_gain[...]).astype(bfloat16)
    d_hidden = group_rows(core, dh_m[...], dh_o[...])
    mixed = mixed_ref[...]
    total[:, 2 * LANES :] += matmul_tn(d_hidden, mixed)
    d_mixed = matmul(d_hidden, weight[:, 2 * LANES :]).astype(bfloat16)
    query = low_ref[:, :LANES]
    key_value = low_ref[:, LANES:].astype(float32)
    turned = pltpu.roll(key_value, HALF, 1)
    begin, row_ids, col_ids = group_mask(ends_ref, group, x.shape[0])
    scale = HEAD_DIM ** (-0.5)
    shape = mixed.shape
    d_query = jnp.zeros(shape, float32)
    d_keys, d_values = [], []
    for head in range(2):
        key = at_head(key_value, head)
        probs = group_probs(query, key, begin, row_ids, col_ids)
        d_values.append(matmul_tn(probs.astype(bfloat16), d_mixed))
        d_probs = matmul_nt(d_mixed, at_head(turned, head))
        centre = jnp.sum(probs * d_probs, axis=1, keepdims=True)
        d_scores = (probs * (d_probs - centre)).astype(bfloat16)
        d_query += matmul(d_scores, key)
        d_keys.append(matmul_tn(d_scores, query))
    d_key = d_keys[0] + pltpu.roll(d_keys[1], HALF, 1)
    d_value = pltpu.roll(d_values[0], HALF, 1) + d_values[1]
    lane = lane_ids(shape)
    cosine, sine = cos[...], sin[...]
    tiles = []
    for number, (grad, gain) in enumerate(((d_query, q_gain[...]), (d_key, k_gain[...]))):
        grad = grad * scale
        back = grad * cosine - turn_halves(grad) * sine
        tile = pre_ref[:, number * LANES : (number + 1) * LANES]
        factor = lax.rsqrt(head_mean(tile * tile) + epsilon)
        unit = tile * factor
        sum_qk[number : number + 1, :] += jnp.sum(back * unit, axis=0, keepdims=True)
        back = back * gain
        tiles.append(factor * (back - unit * head_mean(back * unit)))
    tiles[1] = jnp.where(lane < HALF, tiles[1], d_value)
    d_qkv = jnp.concatenate(tiles, axis=1).astype(bfloat16)
    total[:, : 2 * LANES] += matmul_tn(normed, d_qkv)
    held[...] = matmul_nt(d_qkv, weight[:, : 2 * LANES])
    sum_a[...] += jnp.sum(held[...] * unit_a, axis=0, keepdims=True)
    mine = pl.multiple_of(core * local, local)
    other = pl.multiple_of((1 - core) * local, local)
    send[...] = held[pl.ds(other, local), :].astype(bfloat16)
    keep[...] = held[pl.ds(mine, local), :]

    @pl.when(group == pl.num_programs(0) - 1)
    def _():
        for row in range(GAIN_ROWS):
            gains_out[row : row + 1, :LANES] = sum_a[:, row * LANES : (row + 1) * LANES]
            gains_out[row : row + 1, LANES : 2 * LANES] = gain_ffn[:, row * LANES : (row + 1) * LANES]
        q_sum = sum_qk[0:1, :] + pltpu.roll(sum_qk[0:1, :], HALF, 1)
        k_sum = pltpu.roll(sum_qk[1:2, :], HALF, 1)
        qk_sum = jnp.where(lane_ids(q_sum.shape) < HALF, q_sum, k_sum)
        ids = lax.broadcasted_iota(jnp.int32, (GAIN_ROWS, LANES), 0)
        gains_out[:, 2 * LANES :] = jnp.where(ids == 0, qk_sum, 0.0)
        gains = gains_out[...]
        top = gains.astype(bfloat16)
        rest = (gains - top.astype(float32)).astype(bfloat16)
        tail = jnp.concatenate([top.astype(float32), rest.astype(float32)], axis=0).astype(bfloat16)
        rows = own.shape[0]
        own[...] = total[deep_rows(depth, 0, layers, rows), :]
        for index, piece in enumerate(pieces):
            piece[:rows, :] = total[deep_rows(depth, index + 1, layers, rows), :].astype(bfloat16)
            piece[rows:, :] = tail


def attn_specs(rows, width, group_height):
    scalar = pl.BlockSpec(memory_space=pltpu.SMEM)
    block = pl.BlockSpec((rows, width), lambda i: (i, 0))
    gain = pl.BlockSpec((1, width), lambda i: (0, 0))
    small = pl.BlockSpec((1, LANES), lambda i: (0, 0))
    table = pl.BlockSpec((group_height, LANES), lambda i: (i, 0))
    wide = pl.BlockSpec((group_height, 2 * LANES), lambda i: (i, 0))
    return scalar, block, gain, small, table, wide


def whole_spec(shape):
    return pl.BlockSpec(shape, lambda i: (0, 0), pipeline_mode=pl.Buffered(1))


def attn(where, ends, tok_mine, tok_other, gains, tables, pieces):
    layers = len(pieces)
    rows, width = tok_mine.shape
    local = rows // PLANE
    scalar, block, gain, small, table, wide = attn_specs(local, width, 2 * local)
    high, columns = pieces[0].shape
    weight = (layers * high, columns)
    return pl.pallas_call(
        lambda *refs: attn_kernel(layers, *refs),
        grid=(PLANE,),
        in_specs=[scalar, scalar, block, block, gain, small, small, table, table]
        + [whole_spec((high, columns))] * layers,
        out_specs=[block, block, wide, wide, table, whole_spec(weight)],
        out_shape=[
            jax.ShapeDtypeStruct((rows, width), bfloat16),
            jax.ShapeDtypeStruct((rows, width), float32),
            jax.ShapeDtypeStruct((2 * rows, 2 * LANES), float32),
            jax.ShapeDtypeStruct((2 * rows, 2 * LANES), bfloat16),
            jax.ShapeDtypeStruct((2 * rows, LANES), bfloat16),
            jax.ShapeDtypeStruct(weight, bfloat16),
        ],
        scratch_shapes=[pltpu.VMEM((2 * local, width), float32)],
        compiler_params=pltpu.CompilerParams(vmem_limit_bytes=VMEM_BYTES),
        cost_estimate=COST,
    )(where, ends, tok_mine, tok_other, *gains, *tables, *pieces)


def attn_back(where, ends, layers, tok_mine, tok_other, gains, tables, dh, saved, weight, gain_ffn):
    rows, width = tok_mine.shape
    local = rows // PLANE
    scalar, block, gain, small, table, wide = attn_specs(local, width, 2 * local)
    high, columns = weight.shape[0] // layers, weight.shape[1]
    tail = 2 * GAIN_ROWS
    return pl.pallas_call(
        lambda *refs: attn_back_kernel(layers, *refs),
        grid=(PLANE,),
        in_specs=[scalar, scalar, block, block, gain, small, small, table, table, block, block]
        + [wide, wide, table, whole_spec(weight.shape), gain],
        out_specs=[block, block, whole_spec((high, columns)), whole_spec((GAIN_ROWS, columns))]
        + [whole_spec((high + tail, columns))] * (layers - 1),
        out_shape=[
            jax.ShapeDtypeStruct((rows, width), bfloat16),
            jax.ShapeDtypeStruct((rows, width), float32),
            jax.ShapeDtypeStruct((high, columns), float32),
            jax.ShapeDtypeStruct((GAIN_ROWS, columns), float32),
        ]
        + [jax.ShapeDtypeStruct((high + tail, columns), bfloat16)] * (layers - 1),
        scratch_shapes=[
            pltpu.VMEM((2 * local, width), float32),
            pltpu.VMEM(weight.shape, float32),
            pltpu.VMEM((1, width), float32),
            pltpu.VMEM((8, LANES), float32),
        ],
        compiler_params=pltpu.CompilerParams(vmem_limit_bytes=VMEM_BYTES),
        cost_estimate=COST,
    )(where, ends, tok_mine, tok_other, *gains, *tables, *dh, *saved, weight, gain_ffn)


def ffn_kernel(where_ref, ends_ref, x_o, x_m, g_o, g_m, weight, *refs):
    out_send, out_keep, dn_send, dn_keep, grad_out, total = refs
    step = pl.program_id(0)
    core = where_ref[2]
    both = x_o.shape[1]
    big = both // 2
    local = x_o.shape[0] // 2

    @pl.when(step == 0)
    def _():
        total[...] = jnp.zeros_like(total)

    def live_rows(values, group, at_core):
        ids = lax.broadcasted_iota(jnp.int32, values.shape, 0) + at_core * local
        return jnp.where(ids < ends_ref[group, ends_ref.shape[1] - 1], values, jnp.zeros_like(values))

    x = jnp.concatenate([x_o[...], x_m[...]], axis=0)
    grads = jnp.concatenate(
        [live_rows(g_o[k * local : (k + 1) * local, :], 2 * step + k, 1 - core) for k in range(2)]
        + [live_rows(g_m[k * local : (k + 1) * local, :], 2 * step + k, core) for k in range(2)],
        axis=0,
    )
    half = 2 * local
    w_both = weight[:, :both]
    w_down = weight[:, both : both + big]
    w_small = weight[:, both + big : both + big + LANES]
    w_small_down = weight[:, both + big + LANES :]
    lane = lane_ids((x.shape[0], LANES))

    def parts_of(gate, up, d_act):
        sigma = 1.0 / (1.0 + jnp.exp(-gate))
        silu = gate * sigma
        act = silu * up
        d_gate = d_act * up * sigma * (1.0 + gate * (1.0 - sigma))
        return act, d_gate, d_act * silu

    pre = matmul(x, w_both)
    act, d_gate, d_up = parts_of(pre[:, :big], pre[:, big:], matmul(grads, w_down))
    pre = matmul(x, w_small)
    act_s, d_gate_s, d_up_s = parts_of(
        pre, pltpu.roll(pre, HALF, 1), matmul(grads, w_small_down)
    )
    act_s = jnp.where(lane < HALF, act_s, 0.0).astype(bfloat16)
    d_small = jnp.where(lane < HALF, d_gate_s, pltpu.roll(d_up_s, HALF, 1)).astype(bfloat16)
    act = act.astype(bfloat16)
    d_both = jnp.concatenate([d_gate, d_up], axis=1).astype(bfloat16)

    partial = matmul_nt(act, w_down) + matmul_nt(act_s, w_small_down)
    out_send[...] = partial[:half].astype(bfloat16)
    out_keep[...] = partial[half:]
    partial = matmul_nt(d_both, w_both) + matmul_nt(d_small, w_small)
    dn_send[...] = partial[:half].astype(bfloat16)
    dn_keep[...] = partial[half:]
    total[:, :both] += matmul_tn(x, d_both)
    total[:, both : both + big] += matmul_tn(grads, act)
    total[:, both + big : both + big + LANES] += matmul_tn(x, d_small)
    total[:, both + big + LANES :] += matmul_tn(grads, act_s)

    @pl.when(step == pl.num_programs(0) - 1)
    def _():
        grad_out[...] = total[...].astype(bfloat16)


def ffn(where, ends, x_mine, x_other, g_mine, g_other, weight):
    rows, width = x_mine.shape
    row_spec = pl.BlockSpec((rows // 2, width), lambda i: (i, 0))
    scalar = pl.BlockSpec(memory_space=pltpu.SMEM)
    return pl.pallas_call(
        ffn_kernel,
        grid=(2,),
        in_specs=[scalar, scalar] + [row_spec] * 4 + [whole_spec(weight.shape)],
        out_specs=[row_spec] * 4 + [whole_spec(weight.shape)],
        out_shape=[
            jax.ShapeDtypeStruct((rows, width), bfloat16),
            jax.ShapeDtypeStruct((rows, width), float32),
            jax.ShapeDtypeStruct((rows, width), bfloat16),
            jax.ShapeDtypeStruct((rows, width), float32),
            jax.ShapeDtypeStruct(weight.shape, bfloat16),
        ],
        scratch_shapes=[pltpu.VMEM(weight.shape, float32)],
        compiler_params=pltpu.CompilerParams(vmem_limit_bytes=VMEM_BYTES),
        cost_estimate=COST,
    )(where, ends, x_other, x_mine, g_other, g_mine, weight)


def chip_sum_kernel(keep, received, *outs):
    rows = outs[0].shape[0]
    for mask, out in enumerate(outs):
        span = slice(mask * rows, (mask + 1) * rows)
        out[...] = (keep[span, :] + received[span, :].astype(float32)).astype(out.dtype)


def chip_sum(keep, received):
    shape = (keep.shape[0] // PLANE, keep.shape[1])
    own, *rest = call(
        chip_sum_kernel, [(shape, float32)] + [(shape, bfloat16)] * (PLANE - 1), keep, received
    )
    return [own] + [send_plane(part, mask + 1) for mask, part in enumerate(rest)]


def add_up(parts):
    return sum(part.astype(float32) for part in parts)


def plane_sum_kernel(where_ref, own, *refs):
    received, outs, held = refs[: -PLANE - 1], refs[-PLANE - 1 : -1], refs[-1]
    value = own[...].astype(float32)
    high = own.shape[0]
    for part in received:
        value = value + part[:high, :].astype(float32)
    held[...] = value
    place = where_ref[0]
    rows = high // PLANE
    for mask, out in enumerate(outs):
        at = pl.multiple_of((place ^ mask) * rows, rows)
        out[...] = held[pl.ds(at, rows), :].astype(out.dtype)


def joined_gains(tail):
    return tail[:GAIN_ROWS] + tail[GAIN_ROWS:]


def split_gains(gains):
    top = gains.astype(bfloat16).astype(float32)
    rest = (gains - top).astype(bfloat16).astype(float32)
    return jnp.concatenate([top, rest], axis=0)


def plane_sum_attn_kernel(where_ref, own, gains, *refs):
    received, outs = refs[: -PLANE - 2], refs[-PLANE - 2 : -2]
    held, held_gains = refs[-2:]
    layers = len(received) + 1
    value = own[...]
    high = own.shape[0]
    depth = where_ref[1]
    held_gains[deep_rows(depth, 0, layers, GAIN_ROWS), :] = joined_gains(split_gains(gains[...]))
    for step, part in enumerate(received):
        value = value + part[:high, :].astype(float32)
        held_gains[deep_rows(depth, -1 - step, layers, GAIN_ROWS), :] = joined_gains(
            part[high:, :].astype(float32)
        )
    held[...] = value
    sums = held_gains[:GAIN_ROWS, :]
    for layer in range(1, layers):
        sums = sums + held_gains[layer * GAIN_ROWS : (layer + 1) * GAIN_ROWS, :]
    tail = split_gains(sums)
    place = where_ref[0]
    rows = high // PLANE
    for mask, out in enumerate(outs):
        at = pl.multiple_of((place ^ mask) * rows, rows)
        part = held[pl.ds(at, rows), :]
        if mask:
            tall = out.shape[0] - tail.shape[0]
            out[:tall, :] = padded(part, tall).astype(bfloat16)
            out[tall:, :] = tail.astype(bfloat16)
        else:
            out[:rows, :] = part
            out[rows:, :] = tail


def plane_sum(where, own, grad_pieces, gains=None):
    received = [send_deep(piece, step + 1) for step, piece in enumerate(grad_pieces)]
    rows, columns = own.shape[0] // PLANE, own.shape[1]
    scratch = [pltpu.VMEM(own.shape, float32)]
    if gains is None:
        shapes = [((rows, columns), float32)] + [((rows, columns), bfloat16)] * (PLANE - 1)
        outs = call(plane_sum_kernel, shapes, where, own, *received, scalars=1, scratch=scratch)
    else:
        tail = 2 * GAIN_ROWS
        shapes = [((rows + tail, columns), float32)]
        shapes += [((max(rows, 16) + tail, columns), bfloat16)] * (PLANE - 1)
        scratch.append(pltpu.VMEM(((len(received) + 1) * GAIN_ROWS, columns), float32))
        outs = call(
            plane_sum_attn_kernel, shapes, where, own, gains, *received, scalars=1, scratch=scratch
        )
    return [outs[0]] + [send_plane(part, mask + 1) for mask, part in enumerate(outs[1:])]


def pick_place(refs, place, target, columns, rows):
    value = jnp.zeros((rows, columns.stop - columns.start), float32)
    for mask, ref in enumerate(refs):
        value = jnp.where(place ^ mask == target, ref[:, columns].astype(float32)[:rows], value)
    return value


def place_ffn_kernel(where_ref, own, one, two, three, out_g, out_u, out_d):
    place = where_ref[0]
    refs = (own, one, two, three)
    big = out_g.shape[1] // LANES // PLANE * LANES
    last = PLANE * big
    for mask, ref in enumerate(refs):
        at = pl.ds(pl.multiple_of((place ^ mask) * big, LANES), big)
        for number, out in enumerate((out_g, out_u, out_d)):
            out[:, at] = ref[:, number * big : (number + 1) * big].astype(float32)
    for pair in range(PLANE // 2):
        low = pick_place(refs, place, 2 * pair, slice(3 * big, 3 * big + 2 * LANES), out_g.shape[0])
        high = pick_place(refs, place, 2 * pair + 1, slice(3 * big, 3 * big + 2 * LANES), out_g.shape[0])
        lane = lane_ids((low.shape[0], LANES))
        span = slice(last + pair * LANES, last + (pair + 1) * LANES)
        gu_low, gu_high = low[:, :LANES], high[:, :LANES]
        out_g[:, span] = jnp.where(lane < HALF, gu_low, pltpu.roll(gu_high, HALF, 1))
        out_u[:, span] = jnp.where(lane < HALF, pltpu.roll(gu_low, HALF, 1), gu_high)
        out_d[:, span] = jnp.where(lane < HALF, low[:, LANES:], pltpu.roll(high[:, LANES:], HALF, 1))


def place_attn_kernel(where_ref, own, one, two, three, out_q, out_k, out_v, out_o, out_gains):
    place = where_ref[0]
    refs = (own, one, two, three)
    rows = out_q.shape[0]
    for mask, ref in enumerate(refs):
        at = pl.ds(pl.multiple_of((place ^ mask) * LANES, LANES), LANES)
        out_q[:, at] = ref[:, :LANES].astype(float32)[:rows]
        out_o[:, at] = ref[:, 2 * LANES :].astype(float32)[:rows]
    for pair in range(PLANE // 2):
        low = pick_place(refs, place, 2 * pair, slice(LANES, 2 * LANES), rows)
        high = pick_place(refs, place, 2 * pair + 1, slice(LANES, 2 * LANES), rows)
        lane = lane_ids(low.shape)
        span = slice(pair * LANES, (pair + 1) * LANES)
        out_k[:, span] = jnp.where(lane < HALF, low, pltpu.roll(high, HALF, 1))
        out_v[:, span] = jnp.where(lane < HALF, pltpu.roll(low, HALF, 1), high)
    tails = [joined_gains(ref[ref.shape[0] - 2 * GAIN_ROWS :, :].astype(float32)) for ref in refs]
    out_gains[...] = (tails[0] + tails[1]) + (tails[2] + tails[3])


def gather_rows(local):
    mine = jnp.concatenate([local] + [send_plane(local, mask) for mask in range(1, PLANE)])
    return mine, swap_cores(mine)


def body(
    tokens,
    lengths,
    attn_gain,
    query_gain,
    key_gain,
    ffn_gain,
    w_query,
    w_key,
    w_value,
    w_out,
    w_gate,
    w_up,
    w_down,
    cotangent,
):
    dp = lax.axis_index("dp")
    core = lax.axis_index("tensor")
    layers = lax.axis_size("dp") // PLANE
    where = jnp.stack([dp % PLANE, dp // PLANE, core]).astype(jnp.int32)
    local_rows, model = tokens.shape
    total_rows = local_rows * lax.axis_size("tensor")
    rows = w_query.shape[0]
    q_cols = w_query.shape[1] // PLANE
    kv_cols = w_key.shape[1] // PLANE
    local_kv = kv_cols // HEAD_DIM
    share = q_cols // kv_cols
    attn_cols = 2 * q_cols + 2 * kv_cols
    ff_cols = 3 * (w_gate.shape[1] // LANES // PLANE * LANES) + 2 * LANES

    parts, high = attn_rows(rows)
    tall = max(rows, 16)
    messages = call(
        pack_kernel,
        [((high + 2 * tall, model), bfloat16)] * PLANE,
        where,
        lengths,
        w_query,
        w_key,
        w_value,
        w_out,
        w_gate,
        w_up,
        w_down,
        scalars=2,
    )
    messages = [messages[0]] + [send_plane(messages[m], m) for m in range(1, PLANE)]
    attn_piece, ff_piece, lens = call(
        unpack_kernel,
        [
            ((PLANE * rows, attn_cols), bfloat16),
            ((PLANE * rows, ff_cols), bfloat16),
            ((PLANE * 8, LANES), float32),
        ],
        where,
        *messages,
        scalars=1,
        scratch=[
            pltpu.VMEM((PLANE * rows, attn_cols), float32),
            pltpu.VMEM((PLANE * rows, ff_cols), float32),
        ],
    )
    attn_pieces = [attn_piece] + [send_deep(attn_piece, step) for step in range(1, layers)]
    columns = [list(range(k, layers * PLANE, PLANE)) for k in range(PLANE)]
    ff_weight = lax.all_gather(
        ff_piece, "dp", axis=0, tiled=True, axis_index_groups=columns
    )
    local = jnp.concatenate([tokens, cotangent])
    tok_mine, cot_mine = call(
        split_rows_kernel,
        [((PLANE * local_rows, model), bfloat16)] * 2,
        local,
        *[send_plane(local, m) for m in range(1, PLANE)],
    )
    tok_other = swap_cores(tok_mine)
    cot_other = swap_cores(cot_mine)

    slots = lengths.shape[1]
    all_lengths = lens.reshape(PLANE, 8, LANES)[:, 0, :slots].astype(jnp.int32)
    ends = jnp.cumsum(all_lengths, axis=1, dtype=jnp.int32)
    row_ids = jnp.arange(total_rows, dtype=jnp.int32)
    begin = jnp.max(
        jnp.where(row_ids[None, :, None] >= ends[:, None, :], ends[:, None, :], 0), axis=2
    )
    position = (row_ids[None, :] - begin).reshape(-1).astype(jnp.float32)
    spread = jnp.arange(LANES, dtype=jnp.int32) % (HEAD_DIM // 2)
    freqs = rope_base ** (-spread.astype(jnp.float32) * 2.0 / HEAD_DIM)
    angles = position[:, None] * freqs[None, :]
    sign = jnp.where(jnp.arange(LANES) % HEAD_DIM < HEAD_DIM // 2, -1.0, 1.0).astype(jnp.float32)
    tables = (jnp.cos(angles), jnp.sin(angles) * sign)
    gains = (
        attn_gain[None, :],
        jnp.concatenate([query_gain, query_gain])[None, :],
        jnp.concatenate([key_gain, key_gain])[None, :],
    )

    inputs = tokens.astype(jnp.float32)
    factor_a = inverse_rms(inputs)
    unit_a = inputs * factor_a
    send, keep, *saved, attn_weight = attn(
        where, ends, tok_mine, tok_other, gains, tables, attn_pieces
    )
    hidden = inputs + add_up(chip_sum(keep, swap_cores(send)))
    factor_b = inverse_rms(hidden)
    unit_b = hidden * factor_b
    x_mine, x_other = gather_rows((unit_b * ffn_gain).astype(jnp.bfloat16))

    out_send, out_keep, dn_send, dn_keep, ff_grad = ffn(
        where, ends, x_mine, x_other, cot_mine, cot_other, ff_weight
    )
    d_normed2 = add_up(chip_sum(dn_keep, swap_cores(dn_send)))
    grad_out = jnp.where(
        (jnp.arange(local_rows) + core * local_rows < ends[0, slots - 1])[:, None],
        cotangent,
        jnp.zeros_like(cotangent),
    )
    gain_ffn = jnp.sum(d_normed2 * unit_b, axis=0)
    d_hidden = grad_out.astype(jnp.float32) + norm_back(d_normed2 * ffn_gain, unit_b, factor_b)
    h_mine, h_other = gather_rows(d_hidden.astype(jnp.bfloat16))
    own_ff = lax.psum_scatter(
        ff_grad, "dp", scatter_dimension=0, tiled=True, axis_index_groups=columns
    )
    ff_parts = plane_sum(where, own_ff, [])
    block_out = (hidden + add_up(chip_sum(out_keep, swap_cores(out_send)))).astype(jnp.bfloat16)

    send, keep, own_attn, part_gains, *attn_grads = attn_back(
        where, ends, layers, tok_mine, tok_other, gains, tables, (h_mine, h_other), saved,
        attn_weight, gain_ffn[None, :],
    )
    attn_parts = plane_sum(where, own_attn, attn_grads, part_gains)
    d_normed = add_up(chip_sum(keep, swap_cores(send)))
    grad_tokens = d_hidden + norm_back(d_normed * attn_gain, unit_a, factor_a)
    grad_gate, grad_up, grad_down = call(
        place_ffn_kernel, [(w_gate.shape, float32)] * 3, where, *ff_parts, scalars=1
    )
    grad_query, grad_key, grad_value, grad_out_w, sums = call(
        place_attn_kernel,
        [(w.shape, float32) for w in (w_query, w_key, w_value, w_out)]
        + [((GAIN_ROWS, attn_cols), float32)],
        where,
        *attn_parts,
        scalars=1,
    )
    sums = sums + swap_cores(sums)
    return (
        block_out,
        grad_tokens,
        sums[:, :LANES].reshape(-1),
        sums[0, 2 * LANES : 2 * LANES + HEAD_DIM],
        sums[0, 2 * LANES + HEAD_DIM :],
        sums[:, LANES : 2 * LANES].reshape(-1),
        grad_query,
        grad_key,
        grad_value,
        grad_out_w,
        grad_gate,
        grad_up,
        grad_down,
    )


def solution(mesh):
    placed = (
        P(("dp", "tensor"), None),
        P("dp", None),
        P(),
        P(),
        P(),
        P(),
        P("dp", "tensor"),
        P("dp", "tensor"),
        P("dp", "tensor"),
        P("dp", "tensor"),
        P("dp", "tensor"),
        P("dp", "tensor"),
        P("dp", "tensor"),
        P(("dp", "tensor"), None),
    )
    return jax.shard_map(
        body,
        mesh=mesh,
        in_specs=placed,
        out_specs=(
            P(("dp", "tensor"), None),
            P(("dp", "tensor"), None),
            P(),
            P(),
            P(),
            P(),
            P("dp", "tensor"),
            P("dp", "tensor"),
            P("dp", "tensor"),
            P("dp", "tensor"),
            P("dp", "tensor"),
            P("dp", "tensor"),
            P("dp", "tensor"),
        ),
        check_vma=False,
    )
```

```python
import jax
import jax.numpy as jnp
from jax import lax
from jax.experimental import pallas as pl
from jax.experimental.pallas import tpu as pltpu
from jax.sharding import PartitionSpec as P

HEAD_DIM = 64


epsilon = 1e-05
rope_base = 1000000.0
masked_score = -1e30


def inverse_rms(values):
    return lax.rsqrt(jnp.mean(values * values, axis=-1, keepdims=True) + epsilon)


def norm_back(grad_unit, unit, factor):
    return factor * (grad_unit - unit * jnp.mean(grad_unit * unit, axis=-1, keepdims=True))


def matmul(first_op, second_op):
    return jnp.dot(first_op, second_op, preferred_element_type=jnp.float32)


def matmul_nt(first_op, second_op):
    return lax.dot_general(
        first_op, second_op, (((1,), (1,)), ((), ())), preferred_element_type=jnp.float32
    )


def matmul_tn(first_op, second_op):
    return lax.dot_general(
        first_op, second_op, (((0,), (0,)), ((), ())), preferred_element_type=jnp.float32
    )


def seq_layout(seq_lengths, total_rows):
    ends = jnp.cumsum(seq_lengths, dtype=jnp.int32)
    starts = ends - seq_lengths
    row_ids = jnp.arange(total_rows, dtype=jnp.int32)
    segment = jnp.sum(
        (row_ids[:, None] >= ends[None, :]).astype(jnp.int32), axis=1, dtype=jnp.int32
    )
    slot_ids = jnp.arange(seq_lengths.shape[0], dtype=jnp.int32)
    picked = (segment[:, None] == slot_ids[None, :]).astype(jnp.int32)
    begin = (
        jnp.sum(picked * starts[None, :], axis=1, dtype=jnp.int32)
        + (segment == seq_lengths.shape[0]).astype(jnp.int32) * ends[-1]
    )
    allowed = (segment[:, None] == segment[None, :]) & (row_ids[:, None] >= row_ids[None, :])
    return (row_ids - begin, row_ids < ends[-1], allowed)


def rope_tables(position, head_size):
    half_dim = head_size // 2
    freqs = rope_base ** (-jnp.arange(half_dim, dtype=jnp.float32) * 2.0 / head_size)
    angles = position.astype(jnp.float32)[:, None] * freqs[None, :]
    return (jnp.cos(angles)[:, None, :], jnp.sin(angles)[:, None, :])


def rotate(values, cosine, sine):
    half_dim = values.shape[-1] // 2
    first_half = values[..., :half_dim]
    second_half = values[..., half_dim:]
    return jnp.concatenate(
        [first_half * cosine - second_half * sine, second_half * cosine + first_half * sine],
        axis=-1,
    )


def rotate_back(grads, cosine, sine):
    half_dim = grads.shape[-1] // 2
    first_half = grads[..., :half_dim]
    second_half = grads[..., half_dim:]
    return jnp.concatenate(
        [first_half * cosine + second_half * sine, second_half * cosine - first_half * sine],
        axis=-1,
    )

PLANE = 4
LANES = 128
HALF = 64
VMEM_BYTES = 60 * 1024 * 1024
COST = pl.CostEstimate(flops=1024, bytes_accessed=1024, transcendentals=0)
GAIN_ROWS = 8
float32 = jnp.float32
bfloat16 = jnp.bfloat16


def send_plane(values, mask):
    count = lax.axis_size("dp")
    return lax.ppermute(values, "dp", [(i, i ^ mask) for i in range(count)])


def send_deep(values, step):
    count = lax.axis_size("dp")
    return lax.ppermute(values, "dp", [(i, (i + PLANE * step) % count) for i in range(count)])


def swap_cores(values):
    return lax.ppermute(values, "tensor", [(0, 1), (1, 0)])


def call(kernel, outs, *operands, scalars=0, scratch=()):
    specs = [pl.BlockSpec(memory_space=pltpu.SMEM)] * scalars
    specs += [pl.BlockSpec(memory_space=pltpu.VMEM)] * (len(operands) - scalars)
    return pl.pallas_call(
        kernel,
        out_shape=[jax.ShapeDtypeStruct(shape, kind) for shape, kind in outs],
        in_specs=specs,
        out_specs=[pl.BlockSpec(memory_space=pltpu.VMEM)] * len(outs),
        scratch_shapes=list(scratch),
        compiler_params=pltpu.CompilerParams(vmem_limit_bytes=VMEM_BYTES),
        cost_estimate=COST,
    )(*operands)


def ordered(first, second):
    return lax.optimization_barrier((first, second))


def lane_ids(shape):
    return lax.broadcasted_iota(jnp.int32, shape, len(shape) - 1)


def half_tile(ref, first_tile, place, upper):
    start = pl.multiple_of((first_tile + place // 2) * LANES, LANES)
    tile = ref[:, pl.ds(start, LANES)].astype(float32)
    turned = pltpu.roll(tile, HALF, 1)
    odd = place % 2 == 1
    if upper:
        return jnp.where(odd, tile, turned)
    return jnp.where(odd, turned, tile)


def padded(values, rows):
    if values.shape[0] == rows:
        return values
    blank = jnp.zeros((rows - values.shape[0], values.shape[1]), values.dtype)
    return jnp.concatenate([values, blank], axis=0)


def attn_rows(rows):
    return (2, rows // 2) if rows % 32 == 0 else (1, max(rows, 16))


def pack_kernel(where_ref, lengths_ref, w_q, w_k, w_v, w_o, w_g, w_u, w_d, *outs):
    rows = w_q.shape[0]
    parts, high = attn_rows(rows)
    tall = max(rows, 16)
    big = w_g.shape[1] // LANES // PLANE * LANES
    last = w_g.shape[1] // LANES // PLANE * PLANE
    place = where_ref[0]
    lane = lane_ids((rows, LANES))
    for mask, out in enumerate(outs):
        other = place ^ mask
        at = pl.multiple_of(other * LANES, LANES)
        tile = jnp.where(
            lane < HALF, half_tile(w_k, 0, other, False), half_tile(w_v, 0, other, True)
        )
        piece = jnp.concatenate(
            [w_q[:, pl.ds(at, LANES)].astype(float32), tile, w_o[:, pl.ds(at, LANES)].astype(float32)],
            axis=1,
        )
        pieces = [piece[: rows // 2], piece[rows // 2 :]] if parts == 2 else [padded(piece, high)]
        width = piece.shape[1]
        for part, values in enumerate(pieces):
            out[:high, part * width : (part + 1) * width] = values.astype(bfloat16)
        free = out.shape[1] - parts * width
        ids = lane_ids((high, free))
        marks = jnp.zeros((high, free), float32)
        for slot in range(lengths_ref.shape[1]):
            marks = jnp.where(ids == free - LANES + slot, lengths_ref[0, slot].astype(float32), marks)
        out[:high, parts * width :] = marks.astype(bfloat16)

        at = pl.multiple_of(other * big, LANES)
        small = jnp.where(
            lane < HALF, half_tile(w_g, last, other, False), half_tile(w_u, last, other, True)
        )
        small_down = jnp.where(lane < HALF, half_tile(w_d, last, other, False), 0.0)
        upper = jnp.concatenate(
            [w_g[:, pl.ds(at, big)].astype(float32), w_u[:, pl.ds(at, big)].astype(float32)], axis=1
        )
        lower = jnp.concatenate(
            [w_d[:, pl.ds(at, big)].astype(float32), small, small_down], axis=1
        )
        out[high : high + tall, :] = padded(upper, tall).astype(bfloat16)
        out[high + tall :, : lower.shape[1]] = padded(lower, tall).astype(bfloat16)
        out[high + tall :, lower.shape[1] :] = jnp.zeros(
            (tall, out.shape[1] - lower.shape[1]), bfloat16
        )


def unpack_kernel(where_ref, own, one, two, three, attn_out, ffn_out, lens_out, held_attn, held_ffn):
    rows = attn_out.shape[0] // PLANE
    width = attn_out.shape[1]
    parts, high = attn_rows(rows)
    tall = max(rows, 16)
    place = where_ref[0]
    for mask, message in enumerate((own, one, two, three)):
        at = pl.ds(pl.multiple_of((place ^ mask) * rows, rows), rows)
        values = [
            message[:high, part * width : (part + 1) * width].astype(float32)
            for part in range(parts)
        ]
        held_attn[at, :] = jnp.concatenate(values, axis=0) if parts == 2 else values[0][:rows]
        lens = message[:16, message.shape[1] - LANES :].astype(float32)
        lens_out[mask * 8 : (mask + 1) * 8, :] = lens[:8]
        full = message.shape[1]
        held_ffn[at, :full] = message[high : high + tall, :].astype(float32)[:rows]
        rest = held_ffn.shape[1] - full
        held_ffn[at, full:] = message[high + tall :, :rest].astype(float32)[:rows]
    attn_out[...] = held_attn[...].astype(bfloat16)
    ffn_out[...] = held_ffn[...].astype(bfloat16)


def split_rows_kernel(own, one, two, three, tok_out, cot_out):
    local = own.shape[0] // 2
    for mask, message in enumerate((own, one, two, three)):
        span = slice(mask * local, (mask + 1) * local)
        tok_out[span, :] = message[:local, :]
        cot_out[span, :] = message[local:, :]


def head_mean(values):
    low = lane_ids(values.shape) < HALF
    first = jnp.sum(jnp.where(low, values, 0.0), axis=1, keepdims=True)
    second = jnp.sum(jnp.where(low, 0.0, values), axis=1, keepdims=True)
    return jnp.where(low, first, second) * (1.0 / HALF)


def turn_halves(values):
    first = lane_ids(values.shape) % HALF < HALF // 2
    return jnp.where(
        first, pltpu.roll(values, LANES - HALF // 2, 1), pltpu.roll(values, HALF // 2, 1)
    )


def at_head(values, head):
    low = lane_ids(values.shape) < HALF
    if head == 0:
        return jnp.where(low, values, 0.0).astype(bfloat16)
    return jnp.where(low, 0.0, pltpu.roll(values, HALF, 1)).astype(bfloat16)


def group_probs(query, key, begin, row_ids, col_ids):
    scores = matmul_nt(query, key) * HEAD_DIM ** (-0.5)
    scores = jnp.where((col_ids >= begin) & (col_ids <= row_ids), scores, masked_score)
    expd = jnp.exp(scores - jnp.max(scores, axis=1, keepdims=True))
    return expd / jnp.sum(expd, axis=1, keepdims=True)


def group_mask(ends_ref, group, rows):
    row_ids = lax.broadcasted_iota(jnp.int32, (rows, rows), 0)
    col_ids = lax.broadcasted_iota(jnp.int32, (rows, rows), 1)
    begin = jnp.zeros((rows, rows), jnp.int32)
    for slot in range(ends_ref.shape[1]):
        end = ends_ref[group, slot]
        begin = jnp.maximum(begin, jnp.where(row_ids >= end, end, 0))
    return begin, row_ids, col_ids


def group_rows(core, mine, other):
    first = jnp.where(core == 0, mine, other)
    second = jnp.where(core == 0, other, mine)
    return jnp.concatenate([first, second], axis=0)


def deep_rows(depth, step, layers, rows):
    at = lax.rem(depth + step + layers, layers) * rows
    return pl.ds(pl.multiple_of(at, rows), rows)


def attn_kernel(layers, where_ref, ends_ref, tok_m, tok_o, a_gain, q_gain, k_gain, cos, sin, *refs):
    pieces, refs = refs[:layers], refs[layers:]
    send, keep, pre_out, low_out, mixed_out, weight, held = refs
    group = pl.program_id(0)
    depth, core = where_ref[1], where_ref[2]
    local = tok_m.shape[0]

    @pl.when(group == 0)
    def _():
        for step, piece in enumerate(pieces):
            weight[deep_rows(depth, -step, layers, piece.shape[0]), :] = piece[...]

    x = group_rows(core, tok_m[...].astype(float32), tok_o[...].astype(float32))
    normed = (x * inverse_rms(x) * a_gain[...]).astype(bfloat16)
    pre = matmul(normed, weight[:, : 2 * LANES])
    pre_out[...] = pre
    cosine, sine = cos[...], sin[...]
    tiles = []
    for number, gain in enumerate((q_gain[...], k_gain[...])):
        tile = pre[:, number * LANES : (number + 1) * LANES]
        scaled = tile * lax.rsqrt(head_mean(tile * tile) + epsilon) * gain
        tiles.append(scaled * cosine + turn_halves(scaled) * sine)
    lane = lane_ids(tiles[0].shape)
    query = tiles[0].astype(bfloat16)
    key_value = jnp.where(lane < HALF, tiles[1], pre[:, LANES:])
    low_out[:, :LANES] = query
    low_out[:, LANES:] = key_value.astype(bfloat16)
    begin, row_ids, col_ids = group_mask(ends_ref, group, x.shape[0])
    turned = pltpu.roll(key_value, HALF, 1)
    mixed = jnp.zeros(tiles[0].shape, float32)
    for head in range(2):
        probs = group_probs(query, at_head(key_value, head), begin, row_ids, col_ids)
        mixed += matmul(probs.astype(bfloat16), at_head(turned, head))
    mixed = mixed.astype(bfloat16)
    mixed_out[...] = mixed
    held[...] = matmul_nt(mixed, weight[:, 2 * LANES :])
    mine = pl.multiple_of(core * local, local)
    other = pl.multiple_of((1 - core) * local, local)
    send[...] = held[pl.ds(other, local), :].astype(bfloat16)
    keep[...] = held[pl.ds(mine, local), :]


def attn_back_kernel(
    layers, where_ref, ends_ref, tok_m, tok_o, a_gain, q_gain, k_gain, cos, sin, dh_m, dh_o,
    pre_ref, low_ref, mixed_ref, weight, gain_ffn, *refs,
):
    send, keep, own, gains_out = refs[:4]
    pieces = refs[4 : 3 + layers]
    held, total, sum_a, sum_qk = refs[3 + layers :]
    group = pl.program_id(0)
    depth, core = where_ref[1], where_ref[2]
    local = tok_m.shape[0]

    @pl.when(group == 0)
    def _():
        total[...] = jnp.zeros_like(total)
        sum_a[...] = jnp.zeros_like(sum_a)
        sum_qk[...] = jnp.zeros_like(sum_qk)

    x = group_rows(core, tok_m[...].astype(float32), tok_o[...].astype(float32))
    unit_a = x * inverse_rms(x)
    normed = (unit_a * a_gain[...]).astype(bfloat16)
    d_hidden = group_rows(core, dh_m[...], dh_o[...])
    mixed = mixed_ref[...]
    total[:, 2 * LANES :] += matmul_tn(d_hidden, mixed)
    d_mixed = matmul(d_hidden, weight[:, 2 * LANES :]).astype(bfloat16)
    query = low_ref[:, :LANES]
    key_value = low_ref[:, LANES:].astype(float32)
    turned = pltpu.roll(key_value, HALF, 1)
    begin, row_ids, col_ids = group_mask(ends_ref, group, x.shape[0])
    scale = HEAD_DIM ** (-0.5)
    shape = mixed.shape
    d_query = jnp.zeros(shape, float32)
    d_keys, d_values = [], []
    for head in range(2):
        key = at_head(key_value, head)
        probs = group_probs(query, key, begin, row_ids, col_ids)
        d_values.append(matmul_tn(probs.astype(bfloat16), d_mixed))
        d_probs = matmul_nt(d_mixed, at_head(turned, head))
        centre = jnp.sum(probs * d_probs, axis=1, keepdims=True)
        d_scores = (probs * (d_probs - centre)).astype(bfloat16)
        d_query += matmul(d_scores, key)
        d_keys.append(matmul_tn(d_scores, query))
    d_key = d_keys[0] + pltpu.roll(d_keys[1], HALF, 1)
    d_value = pltpu.roll(d_values[0], HALF, 1) + d_values[1]
    lane = lane_ids(shape)
    cosine, sine = cos[...], sin[...]
    tiles = []
    for number, (grad, gain) in enumerate(((d_query, q_gain[...]), (d_key, k_gain[...]))):
        grad = grad * scale
        back = grad * cosine - turn_halves(grad) * sine
        tile = pre_ref[:, number * LANES : (number + 1) * LANES]
        factor = lax.rsqrt(head_mean(tile * tile) + epsilon)
        unit = tile * factor
        sum_qk[number : number + 1, :] += jnp.sum(back * unit, axis=0, keepdims=True)
        back = back * gain
        tiles.append(factor * (back - unit * head_mean(back * unit)))
    tiles[1] = jnp.where(lane < HALF, tiles[1], d_value)
    d_qkv = jnp.concatenate(tiles, axis=1).astype(bfloat16)
    total[:, : 2 * LANES] += matmul_tn(normed, d_qkv)
    held[...] = matmul_nt(d_qkv, weight[:, : 2 * LANES])
    sum_a[...] += jnp.sum(held[...] * unit_a, axis=0, keepdims=True)
    mine = pl.multiple_of(core * local, local)
    other = pl.multiple_of((1 - core) * local, local)
    send[...] = held[pl.ds(other, local), :].astype(bfloat16)
    keep[...] = held[pl.ds(mine, local), :]

    @pl.when(group == pl.num_programs(0) - 1)
    def _():
        for row in range(GAIN_ROWS):
            gains_out[row : row + 1, :LANES] = sum_a[:, row * LANES : (row + 1) * LANES]
            gains_out[row : row + 1, LANES : 2 * LANES] = gain_ffn[:, row * LANES : (row + 1) * LANES]
        q_sum = sum_qk[0:1, :] + pltpu.roll(sum_qk[0:1, :], HALF, 1)
        k_sum = pltpu.roll(sum_qk[1:2, :], HALF, 1)
        qk_sum = jnp.where(lane_ids(q_sum.shape) < HALF, q_sum, k_sum)
        ids = lax.broadcasted_iota(jnp.int32, (GAIN_ROWS, LANES), 0)
        gains_out[:, 2 * LANES :] = jnp.where(ids == 0, qk_sum, 0.0)
        gains = gains_out[...]
        top = gains.astype(bfloat16)
        rest = (gains - top.astype(float32)).astype(bfloat16)
        tail = jnp.concatenate([top.astype(float32), rest.astype(float32)], axis=0).astype(bfloat16)
        rows = own.shape[0]
        own[...] = total[deep_rows(depth, 0, layers, rows), :]
        for index, piece in enumerate(pieces):
            piece[:rows, :] = total[deep_rows(depth, index + 1, layers, rows), :].astype(bfloat16)
            piece[rows:, :] = tail


def attn_specs(rows, width, group_height):
    scalar = pl.BlockSpec(memory_space=pltpu.SMEM)
    block = pl.BlockSpec((rows, width), lambda i: (i, 0))
    gain = pl.BlockSpec((1, width), lambda i: (0, 0))
    small = pl.BlockSpec((1, LANES), lambda i: (0, 0))
    table = pl.BlockSpec((group_height, LANES), lambda i: (i, 0))
    wide = pl.BlockSpec((group_height, 2 * LANES), lambda i: (i, 0))
    return scalar, block, gain, small, table, wide


def whole_spec(shape):
    return pl.BlockSpec(shape, lambda i: (0, 0), pipeline_mode=pl.Buffered(1))


def attn(where, ends, tok_mine, tok_other, gains, tables, pieces):
    layers = len(pieces)
    rows, width = tok_mine.shape
    local = rows // PLANE
    scalar, block, gain, small, table, wide = attn_specs(local, width, 2 * local)
    high, columns = pieces[0].shape
    weight = (layers * high, columns)
    return pl.pallas_call(
        lambda *refs: attn_kernel(layers, *refs),
        grid=(PLANE,),
        in_specs=[scalar, scalar, block, block, gain, small, small, table, table]
        + [whole_spec((high, columns))] * layers,
        out_specs=[block, block, wide, wide, table, whole_spec(weight)],
        out_shape=[
            jax.ShapeDtypeStruct((rows, width), bfloat16),
            jax.ShapeDtypeStruct((rows, width), float32),
            jax.ShapeDtypeStruct((2 * rows, 2 * LANES), float32),
            jax.ShapeDtypeStruct((2 * rows, 2 * LANES), bfloat16),
            jax.ShapeDtypeStruct((2 * rows, LANES), bfloat16),
            jax.ShapeDtypeStruct(weight, bfloat16),
        ],
        scratch_shapes=[pltpu.VMEM((2 * local, width), float32)],
        compiler_params=pltpu.CompilerParams(vmem_limit_bytes=VMEM_BYTES),
        cost_estimate=COST,
    )(where, ends, tok_mine, tok_other, *gains, *tables, *pieces)


def attn_back(where, ends, layers, tok_mine, tok_other, gains, tables, dh, saved, weight, gain_ffn):
    rows, width = tok_mine.shape
    local = rows // PLANE
    scalar, block, gain, small, table, wide = attn_specs(local, width, 2 * local)
    high, columns = weight.shape[0] // layers, weight.shape[1]
    tail = 2 * GAIN_ROWS
    return pl.pallas_call(
        lambda *refs: attn_back_kernel(layers, *refs),
        grid=(PLANE,),
        in_specs=[scalar, scalar, block, block, gain, small, small, table, table, block, block]
        + [wide, wide, table, whole_spec(weight.shape), gain],
        out_specs=[block, block, whole_spec((high, columns)), whole_spec((GAIN_ROWS, columns))]
        + [whole_spec((high + tail, columns))] * (layers - 1),
        out_shape=[
            jax.ShapeDtypeStruct((rows, width), bfloat16),
            jax.ShapeDtypeStruct((rows, width), float32),
            jax.ShapeDtypeStruct((high, columns), float32),
            jax.ShapeDtypeStruct((GAIN_ROWS, columns), float32),
        ]
        + [jax.ShapeDtypeStruct((high + tail, columns), bfloat16)] * (layers - 1),
        scratch_shapes=[
            pltpu.VMEM((2 * local, width), float32),
            pltpu.VMEM(weight.shape, float32),
            pltpu.VMEM((1, width), float32),
            pltpu.VMEM((8, LANES), float32),
        ],
        compiler_params=pltpu.CompilerParams(vmem_limit_bytes=VMEM_BYTES),
        cost_estimate=COST,
    )(where, ends, tok_mine, tok_other, *gains, *tables, *dh, *saved, weight, gain_ffn)


def ffn_kernel(where_ref, ends_ref, x_o, x_m, g_o, g_m, weight, *refs):
    out_send, out_keep, dn_send, dn_keep, grad_out, total = refs
    step = pl.program_id(0)
    core = where_ref[2]
    both = x_o.shape[1]
    big = both // 2
    local = x_o.shape[0] // 2

    @pl.when(step == 0)
    def _():
        total[...] = jnp.zeros_like(total)

    def live_rows(values, group, at_core):
        ids = lax.broadcasted_iota(jnp.int32, values.shape, 0) + at_core * local
        return jnp.where(ids < ends_ref[group, ends_ref.shape[1] - 1], values, jnp.zeros_like(values))

    x = jnp.concatenate([x_o[...], x_m[...]], axis=0)
    grads = jnp.concatenate(
        [live_rows(g_o[k * local : (k + 1) * local, :], 2 * step + k, 1 - core) for k in range(2)]
        + [live_rows(g_m[k * local : (k + 1) * local, :], 2 * step + k, core) for k in range(2)],
        axis=0,
    )
    half = 2 * local
    w_both = weight[:, :both]
    w_down = weight[:, both : both + big]
    w_small = weight[:, both + big : both + big + LANES]
    w_small_down = weight[:, both + big + LANES :]
    lane = lane_ids((x.shape[0], LANES))

    def parts_of(gate, up, d_act):
        sigma = 1.0 / (1.0 + jnp.exp(-gate))
        silu = gate * sigma
        act = silu * up
        d_gate = d_act * up * sigma * (1.0 + gate * (1.0 - sigma))
        return act, d_gate, d_act * silu

    pre = matmul(x, w_both)
    act, d_gate, d_up = parts_of(pre[:, :big], pre[:, big:], matmul(grads, w_down))
    pre = matmul(x, w_small)
    act_s, d_gate_s, d_up_s = parts_of(
        pre, pltpu.roll(pre, HALF, 1), matmul(grads, w_small_down)
    )
    act_s = jnp.where(lane < HALF, act_s, 0.0).astype(bfloat16)
    d_small = jnp.where(lane < HALF, d_gate_s, pltpu.roll(d_up_s, HALF, 1)).astype(bfloat16)
    act = act.astype(bfloat16)
    d_both = jnp.concatenate([d_gate, d_up], axis=1).astype(bfloat16)

    partial = matmul_nt(act, w_down) + matmul_nt(act_s, w_small_down)
    out_send[...] = partial[:half].astype(bfloat16)
    out_keep[...] = partial[half:]
    partial = matmul_nt(d_both, w_both) + matmul_nt(d_small, w_small)
    dn_send[...] = partial[:half].astype(bfloat16)
    dn_keep[...] = partial[half:]
    total[:, :both] += matmul_tn(x, d_both)
    total[:, both : both + big] += matmul_tn(grads, act)
    total[:, both + big : both + big + LANES] += matmul_tn(x, d_small)
    total[:, both + big + LANES :] += matmul_tn(grads, act_s)

    @pl.when(step == pl.num_programs(0) - 1)
    def _():
        grad_out[...] = total[...].astype(bfloat16)


def ffn(where, ends, x_mine, x_other, g_mine, g_other, weight):
    rows, width = x_mine.shape
    row_spec = pl.BlockSpec((rows // 2, width), lambda i: (i, 0))
    scalar = pl.BlockSpec(memory_space=pltpu.SMEM)
    return pl.pallas_call(
        ffn_kernel,
        grid=(2,),
        in_specs=[scalar, scalar] + [row_spec] * 4 + [whole_spec(weight.shape)],
        out_specs=[row_spec] * 4 + [whole_spec(weight.shape)],
        out_shape=[
            jax.ShapeDtypeStruct((rows, width), bfloat16),
            jax.ShapeDtypeStruct((rows, width), float32),
            jax.ShapeDtypeStruct((rows, width), bfloat16),
            jax.ShapeDtypeStruct((rows, width), float32),
            jax.ShapeDtypeStruct(weight.shape, bfloat16),
        ],
        scratch_shapes=[pltpu.VMEM(weight.shape, float32)],
        compiler_params=pltpu.CompilerParams(vmem_limit_bytes=VMEM_BYTES),
        cost_estimate=COST,
    )(where, ends, x_other, x_mine, g_other, g_mine, weight)


def chip_sum_kernel(keep, received, *outs):
    rows = outs[0].shape[0]
    for mask, out in enumerate(outs):
        span = slice(mask * rows, (mask + 1) * rows)
        out[...] = (keep[span, :] + received[span, :].astype(float32)).astype(out.dtype)


def chip_sum(keep, received):
    rows, width = keep.shape
    shape = (rows // PLANE, width)
    block = 2 * LANES

    def columns(height):
        return pl.BlockSpec((height, block), lambda i: (0, i))

    return pl.pallas_call(
        chip_sum_kernel,
        grid=(width // block,),
        in_specs=[columns(rows)] * 2,
        out_specs=[columns(shape[0])] * PLANE,
        out_shape=[jax.ShapeDtypeStruct(shape, float32)]
        + [jax.ShapeDtypeStruct(shape, bfloat16)] * (PLANE - 1),
        compiler_params=pltpu.CompilerParams(vmem_limit_bytes=VMEM_BYTES),
        cost_estimate=COST,
    )(keep, received)


def plane_total(parts):
    return add_up([parts[0]] + [send_plane(part, mask + 1) for mask, part in enumerate(parts[1:])])


def add_up(parts):
    return sum(part.astype(float32) for part in parts)


def plane_split_kernel(where_ref, own, *refs):
    outs, held = refs[:-1], refs[-1]
    held[...] = own[...].astype(float32)
    place = where_ref[0]
    rows = own.shape[0] // PLANE
    for mask, out in enumerate(outs):
        at = pl.multiple_of((place ^ mask) * rows, rows)
        out[...] = held[pl.ds(at, rows), :].astype(out.dtype)


def plane_split(where, own):
    shape = (own.shape[0] // PLANE, own.shape[1])
    return call(
        plane_split_kernel,
        [(shape, bfloat16)] * PLANE,
        where,
        own,
        scalars=1,
        scratch=[pltpu.VMEM(own.shape, float32)],
    )


def joined_gains(tail):
    return tail[:GAIN_ROWS] + tail[GAIN_ROWS:]


def split_gains(gains):
    top = gains.astype(bfloat16).astype(float32)
    rest = (gains - top).astype(bfloat16).astype(float32)
    return jnp.concatenate([top, rest], axis=0)


def plane_sum_attn_kernel(where_ref, own, gains, *refs):
    received, outs = refs[: -PLANE - 2], refs[-PLANE - 2 : -2]
    held, held_gains = refs[-2:]
    layers = len(received) + 1
    value = own[...]
    high = own.shape[0]
    depth = where_ref[1]
    held_gains[deep_rows(depth, 0, layers, GAIN_ROWS), :] = joined_gains(split_gains(gains[...]))
    for step, part in enumerate(received):
        value = value + part[:high, :].astype(float32)
        held_gains[deep_rows(depth, -1 - step, layers, GAIN_ROWS), :] = joined_gains(
            part[high:, :].astype(float32)
        )
    held[...] = value
    sums = held_gains[:GAIN_ROWS, :]
    for layer in range(1, layers):
        sums = sums + held_gains[layer * GAIN_ROWS : (layer + 1) * GAIN_ROWS, :]
    tail = split_gains(sums)
    place = where_ref[0]
    rows = high // PLANE
    for mask, out in enumerate(outs):
        at = pl.multiple_of((place ^ mask) * rows, rows)
        part = held[pl.ds(at, rows), :]
        if mask:
            tall = out.shape[0] - tail.shape[0]
            out[:tall, :] = padded(part, tall).astype(bfloat16)
            out[tall:, :] = tail.astype(bfloat16)
        else:
            out[:rows, :] = part
            out[rows:, :] = tail


def plane_split_attn(where, own, grad_pieces, gains):
    received = [send_deep(piece, step + 1) for step, piece in enumerate(grad_pieces)]
    rows, columns = own.shape[0] // PLANE, own.shape[1]
    tail = 2 * GAIN_ROWS
    shapes = [((rows + tail, columns), float32)]
    shapes += [((max(rows, 16) + tail, columns), bfloat16)] * (PLANE - 1)
    scratch = [
        pltpu.VMEM(own.shape, float32),
        pltpu.VMEM(((len(received) + 1) * GAIN_ROWS, columns), float32),
    ]
    return call(
        plane_sum_attn_kernel, shapes, where, own, gains, *received, scalars=1, scratch=scratch
    )


def pick_place(refs, place, target, columns, rows):
    value = jnp.zeros((rows, columns.stop - columns.start), float32)
    for mask, ref in enumerate(refs):
        value = jnp.where(place ^ mask == target, ref[:, columns].astype(float32)[:rows], value)
    return value


def place_ffn_kernel(where_ref, own, one, two, three, out_g, out_u, out_d):
    place = where_ref[0]
    refs = (own, one, two, three)
    big = out_g.shape[1] // LANES // PLANE * LANES
    last = PLANE * big
    for mask, ref in enumerate(refs):
        at = pl.ds(pl.multiple_of((place ^ mask) * big, LANES), big)
        for number, out in enumerate((out_g, out_u, out_d)):
            out[:, at] = ref[:, number * big : (number + 1) * big].astype(float32)
    for pair in range(PLANE // 2):
        low = pick_place(refs, place, 2 * pair, slice(3 * big, 3 * big + 2 * LANES), out_g.shape[0])
        high = pick_place(refs, place, 2 * pair + 1, slice(3 * big, 3 * big + 2 * LANES), out_g.shape[0])
        lane = lane_ids((low.shape[0], LANES))
        span = slice(last + pair * LANES, last + (pair + 1) * LANES)
        gu_low, gu_high = low[:, :LANES], high[:, :LANES]
        out_g[:, span] = jnp.where(lane < HALF, gu_low, pltpu.roll(gu_high, HALF, 1))
        out_u[:, span] = jnp.where(lane < HALF, pltpu.roll(gu_low, HALF, 1), gu_high)
        out_d[:, span] = jnp.where(lane < HALF, low[:, LANES:], pltpu.roll(high[:, LANES:], HALF, 1))


def place_attn_kernel(where_ref, own, one, two, three, out_q, out_k, out_v, out_o, out_gains):
    place = where_ref[0]
    refs = (own, one, two, three)
    rows = out_q.shape[0]
    for mask, ref in enumerate(refs):
        at = pl.ds(pl.multiple_of((place ^ mask) * LANES, LANES), LANES)
        out_q[:, at] = ref[:, :LANES].astype(float32)[:rows]
        out_o[:, at] = ref[:, 2 * LANES :].astype(float32)[:rows]
    for pair in range(PLANE // 2):
        low = pick_place(refs, place, 2 * pair, slice(LANES, 2 * LANES), rows)
        high = pick_place(refs, place, 2 * pair + 1, slice(LANES, 2 * LANES), rows)
        lane = lane_ids(low.shape)
        span = slice(pair * LANES, (pair + 1) * LANES)
        out_k[:, span] = jnp.where(lane < HALF, low, pltpu.roll(high, HALF, 1))
        out_v[:, span] = jnp.where(lane < HALF, pltpu.roll(low, HALF, 1), high)
    tails = [joined_gains(ref[ref.shape[0] - 2 * GAIN_ROWS :, :].astype(float32)) for ref in refs]
    out_gains[...] = (tails[0] + tails[1]) + (tails[2] + tails[3])


def gather_rows(local):
    mine = jnp.concatenate([local] + [send_plane(local, mask) for mask in range(1, PLANE)])
    return mine, swap_cores(mine)


def body(
    tokens,
    lengths,
    attn_gain,
    query_gain,
    key_gain,
    ffn_gain,
    w_query,
    w_key,
    w_value,
    w_out,
    w_gate,
    w_up,
    w_down,
    cotangent,
):
    dp = lax.axis_index("dp")
    core = lax.axis_index("tensor")
    layers = lax.axis_size("dp") // PLANE
    where = jnp.stack([dp % PLANE, dp // PLANE, core]).astype(jnp.int32)
    local_rows, model = tokens.shape
    total_rows = local_rows * lax.axis_size("tensor")
    rows = w_query.shape[0]
    q_cols = w_query.shape[1] // PLANE
    kv_cols = w_key.shape[1] // PLANE
    local_kv = kv_cols // HEAD_DIM
    share = q_cols // kv_cols
    attn_cols = 2 * q_cols + 2 * kv_cols
    ff_cols = 3 * (w_gate.shape[1] // LANES // PLANE * LANES) + 2 * LANES

    parts, high = attn_rows(rows)
    tall = max(rows, 16)
    messages = call(
        pack_kernel,
        [((high + 2 * tall, model), bfloat16)] * PLANE,
        where,
        lengths,
        w_query,
        w_key,
        w_value,
        w_out,
        w_gate,
        w_up,
        w_down,
        scalars=2,
    )
    messages = [messages[0]] + [send_plane(messages[m], m) for m in range(1, PLANE)]
    messages, local = ordered(messages, jnp.concatenate([tokens, cotangent]))
    rows_messages = [local] + [send_plane(local, m) for m in range(1, PLANE)]
    attn_piece, ff_piece, lens = call(
        unpack_kernel,
        [
            ((PLANE * rows, attn_cols), bfloat16),
            ((PLANE * rows, ff_cols), bfloat16),
            ((PLANE * 8, LANES), float32),
        ],
        where,
        *messages,
        scalars=1,
        scratch=[
            pltpu.VMEM((PLANE * rows, attn_cols), float32),
            pltpu.VMEM((PLANE * rows, ff_cols), float32),
        ],
    )
    attn_pieces = [attn_piece] + [send_deep(attn_piece, step) for step in range(1, layers)]
    attn_pieces, (ff_piece, rows_messages) = ordered(attn_pieces, (ff_piece, rows_messages))
    columns = [list(range(k, layers * PLANE, PLANE)) for k in range(PLANE)]
    ff_weight = lax.all_gather(
        ff_piece, "dp", axis=0, tiled=True, axis_index_groups=columns
    )
    tok_mine, cot_mine = call(
        split_rows_kernel, [((PLANE * local_rows, model), bfloat16)] * 2, *rows_messages
    )
    tok_other = swap_cores(tok_mine)
    cot_other = swap_cores(cot_mine)

    slots = lengths.shape[1]
    all_lengths = lens.reshape(PLANE, 8, LANES)[:, 0, :slots].astype(jnp.int32)
    ends = jnp.cumsum(all_lengths, axis=1, dtype=jnp.int32)
    row_ids = jnp.arange(total_rows, dtype=jnp.int32)
    begin = jnp.max(
        jnp.where(row_ids[None, :, None] >= ends[:, None, :], ends[:, None, :], 0), axis=2
    )
    position = (row_ids[None, :] - begin).reshape(-1).astype(jnp.float32)
    spread = jnp.arange(LANES, dtype=jnp.int32) % (HEAD_DIM // 2)
    freqs = rope_base ** (-spread.astype(jnp.float32) * 2.0 / HEAD_DIM)
    angles = position[:, None] * freqs[None, :]
    sign = jnp.where(jnp.arange(LANES) % HEAD_DIM < HEAD_DIM // 2, -1.0, 1.0).astype(jnp.float32)
    tables = (jnp.cos(angles), jnp.sin(angles) * sign)
    gains = (
        attn_gain[None, :],
        jnp.concatenate([query_gain, query_gain])[None, :],
        jnp.concatenate([key_gain, key_gain])[None, :],
    )

    inputs = tokens.astype(jnp.float32)
    factor_a = inverse_rms(inputs)
    unit_a = inputs * factor_a
    send, keep, *saved, attn_weight = attn(
        where, ends, tok_mine, tok_other, gains, tables, attn_pieces
    )
    hidden = inputs + plane_total(chip_sum(keep, swap_cores(send)))
    factor_b = inverse_rms(hidden)
    unit_b = hidden * factor_b
    x_mine, x_other = gather_rows((unit_b * ffn_gain).astype(jnp.bfloat16))

    out_send, out_keep, dn_send, dn_keep, ff_grad = ffn(
        where, ends, x_mine, x_other, cot_mine, cot_other, ff_weight
    )
    dn_parts = chip_sum(dn_keep, swap_cores(dn_send))
    dn_parts, out_keep = ordered(dn_parts, out_keep)
    d_normed2 = plane_total(dn_parts)
    grad_out = jnp.where(
        (jnp.arange(local_rows) + core * local_rows < ends[0, slots - 1])[:, None],
        cotangent,
        jnp.zeros_like(cotangent),
    )
    gain_ffn = jnp.sum(d_normed2 * unit_b, axis=0)
    d_hidden = grad_out.astype(jnp.float32) + norm_back(d_normed2 * ffn_gain, unit_b, factor_b)
    h_mine, h_other = gather_rows(d_hidden.astype(jnp.bfloat16))
    own_ff = lax.psum_scatter(
        ff_grad, "dp", scatter_dimension=0, tiled=True, axis_index_groups=columns
    )
    out_parts = chip_sum(out_keep, swap_cores(out_send))
    (h_mine, h_other), out_parts = ordered((h_mine, h_other), out_parts)
    ffn_branch = plane_total(out_parts)
    block_out = (hidden + ffn_branch).astype(jnp.bfloat16)

    send, keep, own_attn, part_gains, *attn_grads = attn_back(
        where, ends, layers, tok_mine, tok_other, gains, tables, (h_mine, h_other), saved,
        attn_weight, gain_ffn[None, :],
    )
    ff_parts = plane_split(where, own_ff)
    ff_parts, keep = ordered(ff_parts, keep)
    dn_parts = chip_sum(keep, swap_cores(send))
    (dn_parts, block_out), own_attn = ordered((dn_parts, block_out), own_attn)
    attn_parts = plane_split_attn(where, own_attn, attn_grads, part_gains)
    d_normed = plane_total(dn_parts)
    ff_parts = [ff_parts[0]] + [send_plane(part, mask + 1) for mask, part in enumerate(ff_parts[1:])]
    attn_parts = [attn_parts[0]] + [
        send_plane(part, mask + 1) for mask, part in enumerate(attn_parts[1:])
    ]
    grad_tokens = d_hidden + norm_back(d_normed * attn_gain, unit_a, factor_a)
    (ff_parts, d_normed), attn_parts = ordered((ff_parts, d_normed), attn_parts)
    grad_gate, grad_up, grad_down = call(
        place_ffn_kernel, [(w_gate.shape, float32)] * 3, where, *ff_parts, scalars=1
    )
    grad_query, grad_key, grad_value, grad_out_w, sums = call(
        place_attn_kernel,
        [(w.shape, float32) for w in (w_query, w_key, w_value, w_out)]
        + [((GAIN_ROWS, attn_cols), float32)],
        where,
        *attn_parts,
        scalars=1,
    )
    sums = sums + swap_cores(sums)
    return (
        block_out,
        grad_tokens,
        sums[:, :LANES].reshape(-1),
        sums[0, 2 * LANES : 2 * LANES + HEAD_DIM],
        sums[0, 2 * LANES + HEAD_DIM :],
        sums[:, LANES : 2 * LANES].reshape(-1),
        grad_query,
        grad_key,
        grad_value,
        grad_out_w,
        grad_gate,
        grad_up,
        grad_down,
    )


def solution(mesh):
    placed = (
        P(("dp", "tensor"), None),
        P("dp", None),
        P(),
        P(),
        P(),
        P(),
        P("dp", "tensor"),
        P("dp", "tensor"),
        P("dp", "tensor"),
        P("dp", "tensor"),
        P("dp", "tensor"),
        P("dp", "tensor"),
        P("dp", "tensor"),
        P(("dp", "tensor"), None),
    )
    return jax.shard_map(
        body,
        mesh=mesh,
        in_specs=placed,
        out_specs=(
            P(("dp", "tensor"), None),
            P(("dp", "tensor"), None),
            P(),
            P(),
            P(),
            P(),
            P("dp", "tensor"),
            P("dp", "tensor"),
            P("dp", "tensor"),
            P("dp", "tensor"),
            P("dp", "tensor"),
            P("dp", "tensor"),
            P("dp", "tensor"),
        ),
        check_vma=False,
    )
```

```python
import jax
import jax.numpy as jnp
from jax import lax
from jax.experimental import pallas as pl
from jax.experimental.pallas import tpu as pltpu
from jax.sharding import PartitionSpec as P

HEAD_DIM = 64


epsilon = 1e-05
rope_base = 1000000.0
masked_score = -1e30


def inverse_rms(values):
    return lax.rsqrt(jnp.mean(values * values, axis=-1, keepdims=True) + epsilon)


def norm_back(grad_unit, unit, factor):
    return factor * (grad_unit - unit * jnp.mean(grad_unit * unit, axis=-1, keepdims=True))


def matmul(first_op, second_op):
    return jnp.dot(first_op, second_op, preferred_element_type=jnp.float32)


def matmul_nt(first_op, second_op):
    return lax.dot_general(
        first_op, second_op, (((1,), (1,)), ((), ())), preferred_element_type=jnp.float32
    )


def matmul_tn(first_op, second_op):
    return lax.dot_general(
        first_op, second_op, (((0,), (0,)), ((), ())), preferred_element_type=jnp.float32
    )


def seq_layout(seq_lengths, total_rows):
    ends = jnp.cumsum(seq_lengths, dtype=jnp.int32)
    starts = ends - seq_lengths
    row_ids = jnp.arange(total_rows, dtype=jnp.int32)
    segment = jnp.sum(
        (row_ids[:, None] >= ends[None, :]).astype(jnp.int32), axis=1, dtype=jnp.int32
    )
    slot_ids = jnp.arange(seq_lengths.shape[0], dtype=jnp.int32)
    picked = (segment[:, None] == slot_ids[None, :]).astype(jnp.int32)
    begin = (
        jnp.sum(picked * starts[None, :], axis=1, dtype=jnp.int32)
        + (segment == seq_lengths.shape[0]).astype(jnp.int32) * ends[-1]
    )
    allowed = (segment[:, None] == segment[None, :]) & (row_ids[:, None] >= row_ids[None, :])
    return (row_ids - begin, row_ids < ends[-1], allowed)


def rope_tables(position, head_size):
    half_dim = head_size // 2
    freqs = rope_base ** (-jnp.arange(half_dim, dtype=jnp.float32) * 2.0 / head_size)
    angles = position.astype(jnp.float32)[:, None] * freqs[None, :]
    return (jnp.cos(angles)[:, None, :], jnp.sin(angles)[:, None, :])


def rotate(values, cosine, sine):
    half_dim = values.shape[-1] // 2
    first_half = values[..., :half_dim]
    second_half = values[..., half_dim:]
    return jnp.concatenate(
        [first_half * cosine - second_half * sine, second_half * cosine + first_half * sine],
        axis=-1,
    )


def rotate_back(grads, cosine, sine):
    half_dim = grads.shape[-1] // 2
    first_half = grads[..., :half_dim]
    second_half = grads[..., half_dim:]
    return jnp.concatenate(
        [first_half * cosine + second_half * sine, second_half * cosine - first_half * sine],
        axis=-1,
    )

PLANE = 4
LANES = 128
HALF = 64
VMEM_BYTES = 60 * 1024 * 1024
COST = pl.CostEstimate(flops=1024, bytes_accessed=1024, transcendentals=0)


def cost(megabytes):
    return pl.CostEstimate(flops=1024, bytes_accessed=megabytes * 1000000, transcendentals=0)
GAIN_ROWS = 8
float32 = jnp.float32
bfloat16 = jnp.bfloat16


def send_plane(values, mask):
    count = lax.axis_size("dp")
    return lax.ppermute(values, "dp", [(i, i ^ mask) for i in range(count)])


def send_deep(values, step):
    count = lax.axis_size("dp")
    return lax.ppermute(values, "dp", [(i, (i + PLANE * step) % count) for i in range(count)])


def swap_cores(values):
    return lax.ppermute(values, "tensor", [(0, 1), (1, 0)])


def call(kernel, outs, *operands, scalars=0, scratch=()):
    specs = [pl.BlockSpec(memory_space=pltpu.SMEM)] * scalars
    specs += [pl.BlockSpec(memory_space=pltpu.VMEM)] * (len(operands) - scalars)
    return pl.pallas_call(
        kernel,
        out_shape=[jax.ShapeDtypeStruct(shape, kind) for shape, kind in outs],
        in_specs=specs,
        out_specs=[pl.BlockSpec(memory_space=pltpu.VMEM)] * len(outs),
        scratch_shapes=list(scratch),
        compiler_params=pltpu.CompilerParams(vmem_limit_bytes=VMEM_BYTES),
        cost_estimate=COST,
    )(*operands)


def after(first, second):
    return lax.optimization_barrier((first, second))[1]


def lane_ids(shape):
    return lax.broadcasted_iota(jnp.int32, shape, len(shape) - 1)


def half_tile(ref, first_tile, place, upper):
    start = pl.multiple_of((first_tile + place // 2) * LANES, LANES)
    tile = ref[:, pl.ds(start, LANES)].astype(float32)
    turned = pltpu.roll(tile, HALF, 1)
    odd = place % 2 == 1
    if upper:
        return jnp.where(odd, tile, turned)
    return jnp.where(odd, turned, tile)


def padded(values, rows):
    if values.shape[0] == rows:
        return values
    blank = jnp.zeros((rows - values.shape[0], values.shape[1]), values.dtype)
    return jnp.concatenate([values, blank], axis=0)


def attn_rows(rows):
    return (2, rows // 2) if rows % 32 == 0 else (1, max(rows, 16))


def pack_kernel(where_ref, lengths_ref, w_q, w_k, w_v, w_o, w_g, w_u, w_d, *outs):
    rows = w_q.shape[0]
    parts, high = attn_rows(rows)
    tall = max(rows, 16)
    big = w_g.shape[1] // LANES // PLANE * LANES
    last = w_g.shape[1] // LANES // PLANE * PLANE
    place = where_ref[0]
    lane = lane_ids((rows, LANES))
    for mask in range(PLANE):
        other = place ^ mask
        out, second = outs[mask], outs[PLANE + mask]
        at = pl.multiple_of(other * LANES, LANES)
        tile = jnp.where(
            lane < HALF, half_tile(w_k, 0, other, False), half_tile(w_v, 0, other, True)
        )
        piece = jnp.concatenate(
            [w_q[:, pl.ds(at, LANES)].astype(float32), tile, w_o[:, pl.ds(at, LANES)].astype(float32)],
            axis=1,
        )
        pieces = [piece[: rows // 2], piece[rows // 2 :]] if parts == 2 else [padded(piece, high)]
        width = piece.shape[1]
        for part, values in enumerate(pieces):
            out[:, part * width : (part + 1) * width] = values.astype(bfloat16)
        free = out.shape[1] - parts * width
        ids = lane_ids((high, free))
        marks = jnp.zeros((high, free), float32)
        for slot in range(lengths_ref.shape[1]):
            marks = jnp.where(ids == free - LANES + slot, lengths_ref[0, slot].astype(float32), marks)
        out[:, parts * width :] = marks.astype(bfloat16)

        at = pl.multiple_of(other * big, LANES)
        small = jnp.where(
            lane < HALF, half_tile(w_g, last, other, False), half_tile(w_u, last, other, True)
        )
        small_down = jnp.where(lane < HALF, half_tile(w_d, last, other, False), 0.0)
        upper = jnp.concatenate(
            [w_g[:, pl.ds(at, big)].astype(float32), w_u[:, pl.ds(at, big)].astype(float32)], axis=1
        )
        lower = jnp.concatenate(
            [w_d[:, pl.ds(at, big)].astype(float32), small, small_down], axis=1
        )
        second[:tall, :] = padded(upper, tall).astype(bfloat16)
        second[tall:, : lower.shape[1]] = padded(lower, tall).astype(bfloat16)
        second[tall:, lower.shape[1] :] = jnp.zeros(
            (tall, second.shape[1] - lower.shape[1]), bfloat16
        )


def unpack_attn_kernel(where_ref, own, one, two, three, attn_out, lens_out, held):
    rows = attn_out.shape[0] // PLANE
    width = attn_out.shape[1]
    parts, _ = attn_rows(rows)
    place = where_ref[0]
    for mask, message in enumerate((own, one, two, three)):
        at = pl.ds(pl.multiple_of((place ^ mask) * rows, rows), rows)
        values = [
            message[:, part * width : (part + 1) * width].astype(float32) for part in range(parts)
        ]
        held[at, :] = jnp.concatenate(values, axis=0) if parts == 2 else values[0][:rows]
        lens = message[:16, message.shape[1] - LANES :].astype(float32)
        lens_out[mask * 8 : (mask + 1) * 8, :] = lens[:8]
    attn_out[...] = held[...].astype(bfloat16)


def unpack_ffn_kernel(where_ref, own, one, two, three, ffn_out, held):
    rows = ffn_out.shape[0] // PLANE
    tall = max(rows, 16)
    place = where_ref[0]
    for mask, message in enumerate((own, one, two, three)):
        at = pl.ds(pl.multiple_of((place ^ mask) * rows, rows), rows)
        full = message.shape[1]
        held[at, :full] = message[:tall, :].astype(float32)[:rows]
        held[at, full:] = message[tall:, : held.shape[1] - full].astype(float32)[:rows]
    ffn_out[...] = held[...].astype(bfloat16)


def head_mean(values):
    low = lane_ids(values.shape) < HALF
    first = jnp.sum(jnp.where(low, values, 0.0), axis=1, keepdims=True)
    second = jnp.sum(jnp.where(low, 0.0, values), axis=1, keepdims=True)
    return jnp.where(low, first, second) * (1.0 / HALF)


def turn_halves(values):
    first = lane_ids(values.shape) % HALF < HALF // 2
    return jnp.where(
        first, pltpu.roll(values, LANES - HALF // 2, 1), pltpu.roll(values, HALF // 2, 1)
    )


def at_head(values, head):
    low = lane_ids(values.shape) < HALF
    if head == 0:
        return jnp.where(low, values, 0.0).astype(bfloat16)
    return jnp.where(low, 0.0, pltpu.roll(values, HALF, 1)).astype(bfloat16)


def group_probs(query, key, begin, row_ids, col_ids):
    scores = matmul_nt(query, key) * HEAD_DIM ** (-0.5)
    scores = jnp.where((col_ids >= begin) & (col_ids <= row_ids), scores, masked_score)
    expd = jnp.exp(scores - jnp.max(scores, axis=1, keepdims=True))
    return expd / jnp.sum(expd, axis=1, keepdims=True)


def group_mask(ends_ref, group, rows):
    row_ids = lax.broadcasted_iota(jnp.int32, (rows, rows), 0)
    col_ids = lax.broadcasted_iota(jnp.int32, (rows, rows), 1)
    begin = jnp.zeros((rows, rows), jnp.int32)
    for slot in range(ends_ref.shape[1]):
        end = ends_ref[group, slot]
        begin = jnp.maximum(begin, jnp.where(row_ids >= end, end, 0))
    return begin, row_ids, col_ids


def group_rows(core, mine, other):
    first = jnp.where(core == 0, mine, other)
    second = jnp.where(core == 0, other, mine)
    return jnp.concatenate([first, second], axis=0)


def deep_rows(depth, step, layers, rows):
    at = lax.rem(depth + step + layers, layers) * rows
    return pl.ds(pl.multiple_of(at, rows), rows)


def attn_kernel(where_ref, ends_ref, tok_m, tok_o, a_gain, q_gain, k_gain, cos, sin, weight, *refs):
    send, keep, pre_out, low_out, mixed_out, held = refs
    group = pl.program_id(0)
    core = where_ref[2]
    local = tok_m.shape[0]

    x = group_rows(core, tok_m[...].astype(float32), tok_o[...].astype(float32))
    normed = (x * inverse_rms(x) * a_gain[...]).astype(bfloat16)
    pre = matmul(normed, weight[:, : 2 * LANES])
    pre_out[...] = pre
    cosine, sine = cos[...], sin[...]
    tiles = []
    for number, gain in enumerate((q_gain[...], k_gain[...])):
        tile = pre[:, number * LANES : (number + 1) * LANES]
        scaled = tile * lax.rsqrt(head_mean(tile * tile) + epsilon) * gain
        tiles.append(scaled * cosine + turn_halves(scaled) * sine)
    lane = lane_ids(tiles[0].shape)
    query = tiles[0].astype(bfloat16)
    key_value = jnp.where(lane < HALF, tiles[1], pre[:, LANES:])
    low_out[:, :LANES] = query
    low_out[:, LANES:] = key_value.astype(bfloat16)
    begin, row_ids, col_ids = group_mask(ends_ref, group, x.shape[0])
    turned = pltpu.roll(key_value, HALF, 1)
    mixed = jnp.zeros(tiles[0].shape, float32)
    for head in range(2):
        probs = group_probs(query, at_head(key_value, head), begin, row_ids, col_ids)
        mixed += matmul(probs.astype(bfloat16), at_head(turned, head))
    mixed = mixed.astype(bfloat16)
    mixed_out[...] = mixed
    held[...] = matmul_nt(mixed, weight[:, 2 * LANES :])
    mine = pl.multiple_of(core * local, local)
    other = pl.multiple_of((1 - core) * local, local)
    send[...] = held[pl.ds(other, local), :].astype(bfloat16)
    keep[...] = held[pl.ds(mine, local), :]


def attn_back_kernel(
    where_ref, ends_ref, tok_m, tok_o, a_gain, q_gain, k_gain, cos, sin, dh_m, dh_o,
    pre_ref, low_ref, mixed_ref, weight, gain_ffn, *refs,
):
    send, keep, grad_out, gains_out, held, total, sum_a, sum_qk = refs
    group = pl.program_id(0)
    core = where_ref[2]
    local = tok_m.shape[0]

    @pl.when(group == 0)
    def _():
        total[...] = jnp.zeros_like(total)
        sum_a[...] = jnp.zeros_like(sum_a)
        sum_qk[...] = jnp.zeros_like(sum_qk)

    x = group_rows(core, tok_m[...].astype(float32), tok_o[...].astype(float32))
    unit_a = x * inverse_rms(x)
    normed = (unit_a * a_gain[...]).astype(bfloat16)
    d_hidden = group_rows(core, dh_m[...], dh_o[...])
    mixed = mixed_ref[...]
    total[:, 2 * LANES :] += matmul_tn(d_hidden, mixed)
    d_mixed = matmul(d_hidden, weight[:, 2 * LANES :]).astype(bfloat16)
    query = low_ref[:, :LANES]
    key_value = low_ref[:, LANES:].astype(float32)
    turned = pltpu.roll(key_value, HALF, 1)
    begin, row_ids, col_ids = group_mask(ends_ref, group, x.shape[0])
    scale = HEAD_DIM ** (-0.5)
    shape = mixed.shape
    d_query = jnp.zeros(shape, float32)
    d_keys, d_values = [], []
    for head in range(2):
        key = at_head(key_value, head)
        probs = group_probs(query, key, begin, row_ids, col_ids)
        d_values.append(matmul_tn(probs.astype(bfloat16), d_mixed))
        d_probs = matmul_nt(d_mixed, at_head(turned, head))
        centre = jnp.sum(probs * d_probs, axis=1, keepdims=True)
        d_scores = (probs * (d_probs - centre)).astype(bfloat16)
        d_query += matmul(d_scores, key)
        d_keys.append(matmul_tn(d_scores, query))
    d_key = d_keys[0] + pltpu.roll(d_keys[1], HALF, 1)
    d_value = pltpu.roll(d_values[0], HALF, 1) + d_values[1]
    lane = lane_ids(shape)
    cosine, sine = cos[...], sin[...]
    tiles = []
    for number, (grad, gain) in enumerate(((d_query, q_gain[...]), (d_key, k_gain[...]))):
        grad = grad * scale
        back = grad * cosine - turn_halves(grad) * sine
        tile = pre_ref[:, number * LANES : (number + 1) * LANES]
        factor = lax.rsqrt(head_mean(tile * tile) + epsilon)
        unit = tile * factor
        sum_qk[number : number + 1, :] += jnp.sum(back * unit, axis=0, keepdims=True)
        back = back * gain
        tiles.append(factor * (back - unit * head_mean(back * unit)))
    tiles[1] = jnp.where(lane < HALF, tiles[1], d_value)
    d_qkv = jnp.concatenate(tiles, axis=1).astype(bfloat16)
    total[:, : 2 * LANES] += matmul_tn(normed, d_qkv)
    held[...] = matmul_nt(d_qkv, weight[:, : 2 * LANES])
    sum_a[...] += jnp.sum(held[...] * unit_a, axis=0, keepdims=True)
    mine = pl.multiple_of(core * local, local)
    other = pl.multiple_of((1 - core) * local, local)
    send[...] = held[pl.ds(other, local), :].astype(bfloat16)
    keep[...] = held[pl.ds(mine, local), :]

    @pl.when(group == pl.num_programs(0) - 1)
    def _():
        for row in range(GAIN_ROWS):
            gains_out[row : row + 1, :LANES] = sum_a[:, row * LANES : (row + 1) * LANES]
            gains_out[row : row + 1, LANES : 2 * LANES] = gain_ffn[:, row * LANES : (row + 1) * LANES]
        q_sum = sum_qk[0:1, :] + pltpu.roll(sum_qk[0:1, :], HALF, 1)
        k_sum = pltpu.roll(sum_qk[1:2, :], HALF, 1)
        qk_sum = jnp.where(lane_ids(q_sum.shape) < HALF, q_sum, k_sum)
        ids = lax.broadcasted_iota(jnp.int32, (GAIN_ROWS, LANES), 0)
        gains_out[:, 2 * LANES :] = jnp.where(ids == 0, qk_sum, 0.0)
        grad_out[...] = total[...].astype(bfloat16)


def attn_specs(rows, width, group_height):
    scalar = pl.BlockSpec(memory_space=pltpu.SMEM)
    block = pl.BlockSpec((rows, width), lambda i: (i, 0))
    gain = pl.BlockSpec((1, width), lambda i: (0, 0))
    small = pl.BlockSpec((1, LANES), lambda i: (0, 0))
    table = pl.BlockSpec((group_height, LANES), lambda i: (i, 0))
    wide = pl.BlockSpec((group_height, 2 * LANES), lambda i: (i, 0))
    return scalar, block, gain, small, table, wide


def whole_spec(shape):
    return pl.BlockSpec(shape, lambda i: (0, 0), pipeline_mode=pl.Buffered(1))


def attn(where, ends, tok_mine, tok_other, gains, tables, weight):
    rows, width = tok_mine.shape
    local = rows // PLANE
    scalar, block, gain, small, table, wide = attn_specs(local, width, 2 * local)
    return pl.pallas_call(
        attn_kernel,
        grid=(PLANE,),
        in_specs=[scalar, scalar, block, block, gain, small, small, table, table]
        + [whole_spec(weight.shape)],
        out_specs=[block, block, wide, wide, table],
        out_shape=[
            jax.ShapeDtypeStruct((rows, width), bfloat16),
            jax.ShapeDtypeStruct((rows, width), float32),
            jax.ShapeDtypeStruct((2 * rows, 2 * LANES), float32),
            jax.ShapeDtypeStruct((2 * rows, 2 * LANES), bfloat16),
            jax.ShapeDtypeStruct((2 * rows, LANES), bfloat16),
        ],
        scratch_shapes=[pltpu.VMEM((2 * local, width), float32)],
        compiler_params=pltpu.CompilerParams(vmem_limit_bytes=VMEM_BYTES),
        cost_estimate=cost(36),
    )(where, ends, tok_mine, tok_other, *gains, *tables, weight)


def attn_back(where, ends, tok_mine, tok_other, gains, tables, dh, saved, weight, gain_ffn):
    rows, width = tok_mine.shape
    local = rows // PLANE
    scalar, block, gain, small, table, wide = attn_specs(local, width, 2 * local)
    columns = weight.shape[1]
    return pl.pallas_call(
        attn_back_kernel,
        grid=(PLANE,),
        in_specs=[scalar, scalar, block, block, gain, small, small, table, table, block, block]
        + [wide, wide, table, whole_spec(weight.shape), gain],
        out_specs=[block, block, whole_spec(weight.shape), whole_spec((GAIN_ROWS, columns))],
        out_shape=[
            jax.ShapeDtypeStruct((rows, width), bfloat16),
            jax.ShapeDtypeStruct((rows, width), float32),
            jax.ShapeDtypeStruct(weight.shape, bfloat16),
            jax.ShapeDtypeStruct((GAIN_ROWS, columns), float32),
        ],
        scratch_shapes=[
            pltpu.VMEM((2 * local, width), float32),
            pltpu.VMEM(weight.shape, float32),
            pltpu.VMEM((1, width), float32),
            pltpu.VMEM((8, LANES), float32),
        ],
        compiler_params=pltpu.CompilerParams(vmem_limit_bytes=VMEM_BYTES),
        cost_estimate=cost(58),
    )(where, ends, tok_mine, tok_other, *gains, *tables, *dh, *saved, weight, gain_ffn)


def ffn_kernel(where_ref, ends_ref, x_o, x_m, g_o, g_m, weight, *refs):
    out_send, out_keep, dn_send, dn_keep, grad_out, total = refs
    step = pl.program_id(0)
    core = where_ref[2]
    both = x_o.shape[1]
    big = both // 2
    local = x_o.shape[0] // 2

    @pl.when(step == 0)
    def _():
        total[...] = jnp.zeros_like(total)

    def live_rows(values, group, at_core):
        ids = lax.broadcasted_iota(jnp.int32, values.shape, 0) + at_core * local
        return jnp.where(ids < ends_ref[group, ends_ref.shape[1] - 1], values, jnp.zeros_like(values))

    x = jnp.concatenate([x_o[...], x_m[...]], axis=0)
    grads = jnp.concatenate(
        [live_rows(g_o[k * local : (k + 1) * local, :], 2 * step + k, 1 - core) for k in range(2)]
        + [live_rows(g_m[k * local : (k + 1) * local, :], 2 * step + k, core) for k in range(2)],
        axis=0,
    )
    half = 2 * local
    w_both = weight[:, :both]
    w_down = weight[:, both : both + big]
    w_small = weight[:, both + big : both + big + LANES]
    w_small_down = weight[:, both + big + LANES :]
    lane = lane_ids((x.shape[0], LANES))

    def parts_of(gate, up, d_act):
        sigma = 1.0 / (1.0 + jnp.exp(-gate))
        silu = gate * sigma
        act = silu * up
        d_gate = d_act * up * sigma * (1.0 + gate * (1.0 - sigma))
        return act, d_gate, d_act * silu

    pre = matmul(x, w_both)
    act, d_gate, d_up = parts_of(pre[:, :big], pre[:, big:], matmul(grads, w_down))
    pre = matmul(x, w_small)
    act_s, d_gate_s, d_up_s = parts_of(
        pre, pltpu.roll(pre, HALF, 1), matmul(grads, w_small_down)
    )
    act_s = jnp.where(lane < HALF, act_s, 0.0).astype(bfloat16)
    d_small = jnp.where(lane < HALF, d_gate_s, pltpu.roll(d_up_s, HALF, 1)).astype(bfloat16)
    act = act.astype(bfloat16)
    d_both = jnp.concatenate([d_gate, d_up], axis=1).astype(bfloat16)

    partial = matmul_nt(act, w_down) + matmul_nt(act_s, w_small_down)
    out_send[...] = partial[:half].astype(bfloat16)
    out_keep[...] = partial[half:]
    partial = matmul_nt(d_both, w_both) + matmul_nt(d_small, w_small)
    dn_send[...] = partial[:half].astype(bfloat16)
    dn_keep[...] = partial[half:]
    total[:, :both] += matmul_tn(x, d_both)
    total[:, both : both + big] += matmul_tn(grads, act)
    total[:, both + big : both + big + LANES] += matmul_tn(x, d_small)
    total[:, both + big + LANES :] += matmul_tn(grads, act_s)

    @pl.when(step == pl.num_programs(0) - 1)
    def _():
        grad_out[...] = total[...].astype(bfloat16)


def ffn(where, ends, x_mine, x_other, g_mine, g_other, weight):
    rows, width = x_mine.shape
    row_spec = pl.BlockSpec((rows // 2, width), lambda i: (i, 0))
    scalar = pl.BlockSpec(memory_space=pltpu.SMEM)
    return pl.pallas_call(
        ffn_kernel,
        grid=(2,),
        in_specs=[scalar, scalar] + [row_spec] * 4 + [whole_spec(weight.shape)],
        out_specs=[row_spec] * 4 + [whole_spec(weight.shape)],
        out_shape=[
            jax.ShapeDtypeStruct((rows, width), bfloat16),
            jax.ShapeDtypeStruct((rows, width), float32),
            jax.ShapeDtypeStruct((rows, width), bfloat16),
            jax.ShapeDtypeStruct((rows, width), float32),
            jax.ShapeDtypeStruct(weight.shape, bfloat16),
        ],
        scratch_shapes=[pltpu.VMEM(weight.shape, float32)],
        compiler_params=pltpu.CompilerParams(vmem_limit_bytes=VMEM_BYTES),
        cost_estimate=cost(74),
    )(where, ends, x_other, x_mine, g_other, g_mine, weight)


def chip_sum_kernel(keep, received, *outs):
    rows = outs[0].shape[0]
    for mask, out in enumerate(outs):
        span = slice(mask * rows, (mask + 1) * rows)
        out[...] = (keep[span, :] + received[span, :].astype(float32)).astype(out.dtype)


def chip_sum(keep, received):
    shape = (keep.shape[0] // PLANE, keep.shape[1])
    outs = [(shape, float32)] + [(shape, bfloat16)] * (PLANE - 1)
    return call(chip_sum_kernel, outs, keep, received)


def plane_total(parts):
    return add_up([parts[0]] + [send_plane(part, mask + 1) for mask, part in enumerate(parts[1:])])


def add_up(parts):
    return sum(part.astype(float32) for part in parts)


def tail_kernel(where_ref, keep, received, own_ff, own, ff_out, *refs):
    messages, held = refs[:-1], refs[-1]
    held[...] = own_ff[...].astype(float32)
    place = where_ref[0]
    local = own.shape[0]
    rows = ff_out.shape[0]
    tall = (messages[0].shape[0] - local) // 2
    width = own.shape[1]
    for mask in range(PLANE):
        span = slice(mask * local, (mask + 1) * local)
        value = keep[span, :] + received[span, :].astype(float32)
        grads = held[pl.ds(pl.multiple_of((place ^ mask) * rows, rows), rows), :]
        if mask == 0:
            own[...] = value
            ff_out[...] = grads
            continue
        out = messages[mask - 1]
        out[:local, :] = value.astype(bfloat16)
        out[local : local + tall, :] = padded(grads[:, :width], tall).astype(bfloat16)
        rest = grads.shape[1] - width
        out[local + tall :, :rest] = padded(grads[:, width:], tall).astype(bfloat16)
        out[local + tall :, rest:] = jnp.zeros((tall, width - rest), bfloat16)


def tail_messages(where, keep, received, own_ff):
    local, width = keep.shape[0] // PLANE, keep.shape[1]
    rows, columns = own_ff.shape[0] // PLANE, own_ff.shape[1]
    message = (local + 2 * max(rows, 16), width)
    return call(
        tail_kernel,
        [((local, width), float32), ((rows, columns), float32)]
        + [(message, bfloat16)] * (PLANE - 1),
        where,
        keep,
        received,
        own_ff,
        scalars=1,
        scratch=[pltpu.VMEM(own_ff.shape, float32)],
    )


def joined_gains(tail):
    return tail[:GAIN_ROWS] + tail[GAIN_ROWS:]


def split_gains(gains):
    top = gains.astype(bfloat16).astype(float32)
    rest = (gains - top).astype(bfloat16).astype(float32)
    return jnp.concatenate([top, rest], axis=0)


def split_attn_kernel(where_ref, own, gains, *refs):
    received, outs = refs[: -PLANE - 2], refs[-PLANE - 2 : -2]
    held, held_gains = refs[-2:]
    layers = len(received) + 1
    depth = where_ref[1]
    for step, part in enumerate((gains,) + received):
        held_gains[deep_rows(depth, -step, layers, GAIN_ROWS), :] = part[...]
    held[...] = own[...].astype(float32)
    sums = held_gains[:GAIN_ROWS, :]
    for layer in range(1, layers):
        sums = sums + held_gains[layer * GAIN_ROWS : (layer + 1) * GAIN_ROWS, :]
    tail = split_gains(sums)
    place = where_ref[0]
    rows = own.shape[0] // PLANE
    for mask, out in enumerate(outs):
        part = held[pl.ds(pl.multiple_of((place ^ mask) * rows, rows), rows), :]
        if mask:
            tall = out.shape[0] - tail.shape[0]
            out[:tall, :] = padded(part, tall).astype(bfloat16)
            out[tall:, :] = tail.astype(bfloat16)
        else:
            out[:rows, :] = part
            out[rows:, :] = tail


def split_attn(where, own, gains, received):
    rows, columns = own.shape[0] // PLANE, own.shape[1]
    tail = 2 * GAIN_ROWS
    shapes = [((rows + tail, columns), float32)]
    shapes += [((max(rows, 16) + tail, columns), bfloat16)] * (PLANE - 1)
    scratch = [
        pltpu.VMEM(own.shape, float32),
        pltpu.VMEM(((len(received) + 1) * GAIN_ROWS, columns), float32),
    ]
    return call(split_attn_kernel, shapes, where, own, gains, *received, scalars=1, scratch=scratch)


def pick_place(refs, place, target, columns, rows):
    value = jnp.zeros((rows, columns.stop - columns.start), float32)
    for mask, ref in enumerate(refs):
        value = jnp.where(place ^ mask == target, ref[:, columns].astype(float32)[:rows], value)
    return value


def place_ffn_kernel(where_ref, own, one, two, three, out_g, out_u, out_d, held):
    place = where_ref[0]
    rows = out_g.shape[0]
    big = out_g.shape[1] // LANES // PLANE * LANES
    last = PLANE * big
    width = one.shape[1]
    tall = max(rows, 16)
    start = one.shape[0] - 2 * tall
    for mask, ref in enumerate((own, one, two, three)):
        if mask:
            top = ref[start : start + tall, :].astype(float32)[:rows]
            rest = ref[start + tall :, : held.shape[2] - width].astype(float32)[:rows]
            held[mask, :, :width] = top
            held[mask, :, width:] = rest
        else:
            held[mask] = ref[...]
        at = pl.ds(pl.multiple_of((place ^ mask) * big, LANES), big)
        for number, out in enumerate((out_g, out_u, out_d)):
            out[:, at] = held[mask, :, number * big : (number + 1) * big]
    for pair in range(PLANE // 2):
        low = held[place ^ (2 * pair), :, 3 * big :]
        high = held[place ^ (2 * pair + 1), :, 3 * big :]
        lane = lane_ids((rows, LANES))
        span = slice(last + pair * LANES, last + (pair + 1) * LANES)
        gu_low, gu_high = low[:, :LANES], high[:, :LANES]
        out_g[:, span] = jnp.where(lane < HALF, gu_low, pltpu.roll(gu_high, HALF, 1))
        out_u[:, span] = jnp.where(lane < HALF, pltpu.roll(gu_low, HALF, 1), gu_high)
        out_d[:, span] = jnp.where(lane < HALF, low[:, LANES:], pltpu.roll(high[:, LANES:], HALF, 1))


def place_attn_kernel(where_ref, own, one, two, three, out_q, out_k, out_v, out_o, out_gains):
    place = where_ref[0]
    refs = (own, one, two, three)
    rows = out_q.shape[0]
    for mask, ref in enumerate(refs):
        at = pl.ds(pl.multiple_of((place ^ mask) * LANES, LANES), LANES)
        out_q[:, at] = ref[:, :LANES].astype(float32)[:rows]
        out_o[:, at] = ref[:, 2 * LANES :].astype(float32)[:rows]
    for pair in range(PLANE // 2):
        low = pick_place(refs, place, 2 * pair, slice(LANES, 2 * LANES), rows)
        high = pick_place(refs, place, 2 * pair + 1, slice(LANES, 2 * LANES), rows)
        lane = lane_ids(low.shape)
        span = slice(pair * LANES, (pair + 1) * LANES)
        out_k[:, span] = jnp.where(lane < HALF, low, pltpu.roll(high, HALF, 1))
        out_v[:, span] = jnp.where(lane < HALF, pltpu.roll(low, HALF, 1), high)
    tails = [joined_gains(ref[ref.shape[0] - 2 * GAIN_ROWS :, :].astype(float32)) for ref in refs]
    out_gains[...] = (tails[0] + tails[1]) + (tails[2] + tails[3])


def plane_parts(local):
    return [local] + [send_plane(local, mask) for mask in range(1, PLANE)]


def both_cores(parts):
    mine = jnp.concatenate(parts)
    return mine, swap_cores(mine)


def gather_rows(local):
    return both_cores(plane_parts(local))


def body(
    tokens,
    lengths,
    attn_gain,
    query_gain,
    key_gain,
    ffn_gain,
    w_query,
    w_key,
    w_value,
    w_out,
    w_gate,
    w_up,
    w_down,
    cotangent,
):
    dp = lax.axis_index("dp")
    core = lax.axis_index("tensor")
    layers = lax.axis_size("dp") // PLANE
    where = jnp.stack([dp % PLANE, dp // PLANE, core]).astype(jnp.int32)
    local_rows, model = tokens.shape
    total_rows = local_rows * lax.axis_size("tensor")
    rows = w_query.shape[0]
    q_cols = w_query.shape[1] // PLANE
    kv_cols = w_key.shape[1] // PLANE
    local_kv = kv_cols // HEAD_DIM
    share = q_cols // kv_cols
    attn_cols = 2 * q_cols + 2 * kv_cols
    ff_cols = 3 * (w_gate.shape[1] // LANES // PLANE * LANES) + 2 * LANES

    parts, high = attn_rows(rows)
    tall = max(rows, 16)
    first = call(
        pack_kernel,
        [((high, model), bfloat16)] * PLANE + [((2 * tall, model), bfloat16)] * PLANE,
        where,
        lengths,
        w_query,
        w_key,
        w_value,
        w_out,
        w_gate,
        w_up,
        w_down,
        scalars=2,
    )
    first, second = first[:PLANE], first[PLANE:]
    attn_piece, lens = call(
        unpack_attn_kernel,
        [((PLANE * rows, attn_cols), bfloat16), ((PLANE * 8, LANES), float32)],
        where,
        first[0],
        *[send_plane(first[m], m) for m in range(1, PLANE)],
        scalars=1,
        scratch=[pltpu.VMEM((PLANE * rows, attn_cols), float32)],
    )
    columns = [list(range(k, layers * PLANE, PLANE)) for k in range(PLANE)]
    attn_weight = lax.all_gather(
        attn_piece, "dp", axis=0, tiled=True, axis_index_groups=columns
    )
    tok_parts = plane_parts(tokens)
    tok_parts = after(attn_piece, tok_parts)
    second = after(tok_parts, second)
    tok_mine, tok_other = both_cores(tok_parts)
    second = [second[0]] + [send_plane(second[m], m) for m in range(1, PLANE)]
    cotangent_sent = after(second, cotangent)
    (ff_piece,) = call(
        unpack_ffn_kernel,
        [((PLANE * rows, ff_cols), bfloat16)],
        where,
        *second,
        scalars=1,
        scratch=[pltpu.VMEM((PLANE * rows, ff_cols), float32)],
    )
    ff_weight = lax.all_gather(ff_piece, "dp", axis=0, tiled=True, axis_index_groups=columns)
    cot_parts = plane_parts(cotangent_sent)
    cot_mine, cot_other = both_cores(cot_parts)
    attn_weight = after(ff_piece, attn_weight)

    slots = lengths.shape[1]
    all_lengths = lens.reshape(PLANE, 8, LANES)[:, 0, :slots].astype(jnp.int32)
    ends = jnp.cumsum(all_lengths, axis=1, dtype=jnp.int32)
    row_ids = jnp.arange(total_rows, dtype=jnp.int32)
    begin = jnp.max(
        jnp.where(row_ids[None, :, None] >= ends[:, None, :], ends[:, None, :], 0), axis=2
    )
    position = (row_ids[None, :] - begin).reshape(-1).astype(jnp.float32)
    spread = jnp.arange(LANES, dtype=jnp.int32) % (HEAD_DIM // 2)
    freqs = rope_base ** (-spread.astype(jnp.float32) * 2.0 / HEAD_DIM)
    angles = position[:, None] * freqs[None, :]
    sign = jnp.where(jnp.arange(LANES) % HEAD_DIM < HEAD_DIM // 2, -1.0, 1.0).astype(jnp.float32)
    tables = (jnp.cos(angles), jnp.sin(angles) * sign)
    gains = (
        attn_gain[None, :],
        jnp.concatenate([query_gain, query_gain])[None, :],
        jnp.concatenate([key_gain, key_gain])[None, :],
    )

    inputs = tokens.astype(jnp.float32)
    factor_a = inverse_rms(inputs)
    unit_a = inputs * factor_a
    send, keep, *saved = attn(where, ends, tok_mine, tok_other, gains, tables, attn_weight)
    send = after(cot_parts, send)
    hidden = inputs + plane_total(chip_sum(keep, swap_cores(send)))
    factor_b = inverse_rms(hidden)
    unit_b = hidden * factor_b
    x_mine, x_other = gather_rows((unit_b * ffn_gain).astype(jnp.bfloat16))

    out_send, out_keep, dn_send, dn_keep, ff_grad = ffn(
        where, ends, x_mine, x_other, cot_mine, cot_other, ff_weight
    )
    dn_parts = chip_sum(dn_keep, swap_cores(dn_send))
    out_keep = after(dn_parts, out_keep)
    d_normed2 = plane_total(dn_parts)
    grad_out = jnp.where(
        (jnp.arange(local_rows) + core * local_rows < ends[0, slots - 1])[:, None],
        cotangent,
        jnp.zeros_like(cotangent),
    )
    gain_ffn = jnp.sum(d_normed2 * unit_b, axis=0)
    d_hidden = grad_out.astype(jnp.float32) + norm_back(d_normed2 * ffn_gain, unit_b, factor_b)
    h_mine, h_other = gather_rows(d_hidden.astype(jnp.bfloat16))
    own_ff = lax.psum_scatter(
        ff_grad, "dp", scatter_dimension=0, tiled=True, axis_index_groups=columns
    )
    out_parts = chip_sum(out_keep, swap_cores(out_send))
    out_parts = after((h_mine, h_other), out_parts)
    ffn_branch = plane_total(out_parts)
    block_out = (hidden + ffn_branch).astype(jnp.bfloat16)

    send, keep, attn_grad, part_gains = attn_back(
        where, ends, tok_mine, tok_other, gains, tables, (h_mine, h_other), saved, attn_weight,
        gain_ffn[None, :],
    )
    send, keep, attn_grad, part_gains = after(block_out, (send, keep, attn_grad, part_gains))
    own_attn = lax.psum_scatter(
        attn_grad, "dp", scatter_dimension=0, tiled=True, axis_index_groups=columns
    )
    far_gains = [send_deep(part_gains, step) for step in range(1, layers)]
    own_dn, own_ff, *messages = tail_messages(where, keep, swap_cores(send), own_ff)
    messages = [send_plane(part, mask + 1) for mask, part in enumerate(messages)]
    own_attn = after(messages, own_attn)
    attn_parts = split_attn(where, own_attn, part_gains, far_gains)
    attn_parts = [attn_parts[0]] + [
        send_plane(part, mask + 1) for mask, part in enumerate(attn_parts[1:])
    ]
    d_normed = own_dn + add_up([part[:local_rows] for part in messages])
    grad_tokens = d_hidden + norm_back(d_normed * attn_gain, unit_a, factor_a)
    grad_gate, grad_up, grad_down = call(
        place_ffn_kernel,
        [(w_gate.shape, float32)] * 3,
        where,
        own_ff,
        *messages,
        scalars=1,
        scratch=[pltpu.VMEM((PLANE, rows, ff_cols), float32)],
    )
    grad_query, grad_key, grad_value, grad_out_w, sums = call(
        place_attn_kernel,
        [(w.shape, float32) for w in (w_query, w_key, w_value, w_out)]
        + [((GAIN_ROWS, attn_cols), float32)],
        where,
        *attn_parts,
        scalars=1,
    )
    sums = sums + swap_cores(sums)
    return (
        block_out,
        grad_tokens,
        sums[:, :LANES].reshape(-1),
        sums[0, 2 * LANES : 2 * LANES + HEAD_DIM],
        sums[0, 2 * LANES + HEAD_DIM :],
        sums[:, LANES : 2 * LANES].reshape(-1),
        grad_query,
        grad_key,
        grad_value,
        grad_out_w,
        grad_gate,
        grad_up,
        grad_down,
    )


def solution(mesh):
    placed = (
        P(("dp", "tensor"), None),
        P("dp", None),
        P(),
        P(),
        P(),
        P(),
        P("dp", "tensor"),
        P("dp", "tensor"),
        P("dp", "tensor"),
        P("dp", "tensor"),
        P("dp", "tensor"),
        P("dp", "tensor"),
        P("dp", "tensor"),
        P(("dp", "tensor"), None),
    )
    return jax.shard_map(
        body,
        mesh=mesh,
        in_specs=placed,
        out_specs=(
            P(("dp", "tensor"), None),
            P(("dp", "tensor"), None),
            P(),
            P(),
            P(),
            P(),
            P("dp", "tensor"),
            P("dp", "tensor"),
            P("dp", "tensor"),
            P("dp", "tensor"),
            P("dp", "tensor"),
            P("dp", "tensor"),
            P("dp", "tensor"),
        ),
        check_vma=False,
    )
```

```python
import jax
import jax.numpy as jnp
from jax import lax
from jax.experimental import pallas as pl
from jax.experimental.pallas import tpu as pltpu
from jax.sharding import PartitionSpec as P

HEAD_DIM = 64


epsilon = 1e-05
rope_base = 1000000.0
masked_score = -1e30


def inverse_rms(values):
    return lax.rsqrt(jnp.mean(values * values, axis=-1, keepdims=True) + epsilon)


def norm_back(grad_unit, unit, factor):
    return factor * (grad_unit - unit * jnp.mean(grad_unit * unit, axis=-1, keepdims=True))


def matmul(first_op, second_op):
    return jnp.dot(first_op, second_op, preferred_element_type=jnp.float32)


def matmul_nt(first_op, second_op):
    return lax.dot_general(
        first_op, second_op, (((1,), (1,)), ((), ())), preferred_element_type=jnp.float32
    )


def matmul_tn(first_op, second_op):
    return lax.dot_general(
        first_op, second_op, (((0,), (0,)), ((), ())), preferred_element_type=jnp.float32
    )


def seq_layout(seq_lengths, total_rows):
    ends = jnp.cumsum(seq_lengths, dtype=jnp.int32)
    starts = ends - seq_lengths
    row_ids = jnp.arange(total_rows, dtype=jnp.int32)
    segment = jnp.sum(
        (row_ids[:, None] >= ends[None, :]).astype(jnp.int32), axis=1, dtype=jnp.int32
    )
    slot_ids = jnp.arange(seq_lengths.shape[0], dtype=jnp.int32)
    picked = (segment[:, None] == slot_ids[None, :]).astype(jnp.int32)
    begin = (
        jnp.sum(picked * starts[None, :], axis=1, dtype=jnp.int32)
        + (segment == seq_lengths.shape[0]).astype(jnp.int32) * ends[-1]
    )
    allowed = (segment[:, None] == segment[None, :]) & (row_ids[:, None] >= row_ids[None, :])
    return (row_ids - begin, row_ids < ends[-1], allowed)


def rope_tables(position, head_size):
    half_dim = head_size // 2
    freqs = rope_base ** (-jnp.arange(half_dim, dtype=jnp.float32) * 2.0 / head_size)
    angles = position.astype(jnp.float32)[:, None] * freqs[None, :]
    return (jnp.cos(angles)[:, None, :], jnp.sin(angles)[:, None, :])


def rotate(values, cosine, sine):
    half_dim = values.shape[-1] // 2
    first_half = values[..., :half_dim]
    second_half = values[..., half_dim:]
    return jnp.concatenate(
        [first_half * cosine - second_half * sine, second_half * cosine + first_half * sine],
        axis=-1,
    )


def rotate_back(grads, cosine, sine):
    half_dim = grads.shape[-1] // 2
    first_half = grads[..., :half_dim]
    second_half = grads[..., half_dim:]
    return jnp.concatenate(
        [first_half * cosine + second_half * sine, second_half * cosine - first_half * sine],
        axis=-1,
    )

PLANE = 4
LANES = 128
HALF = 64
VMEM_BYTES = 60 * 1024 * 1024
COST = pl.CostEstimate(flops=1024, bytes_accessed=1024, transcendentals=0)


def cost(megabytes):
    return pl.CostEstimate(flops=1024, bytes_accessed=megabytes * 1000000, transcendentals=0)
GAIN_ROWS = 8
float32 = jnp.float32
bfloat16 = jnp.bfloat16


def send_plane(values, mask):
    count = lax.axis_size("dp")
    return lax.ppermute(values, "dp", [(i, i ^ mask) for i in range(count)])


def send_deep(values, step):
    count = lax.axis_size("dp")
    return lax.ppermute(values, "dp", [(i, (i + PLANE * step) % count) for i in range(count)])


def swap_cores(values):
    return lax.ppermute(values, "tensor", [(0, 1), (1, 0)])


def call(kernel, outs, *operands, scalars=0, scratch=()):
    specs = [pl.BlockSpec(memory_space=pltpu.SMEM)] * scalars
    specs += [pl.BlockSpec(memory_space=pltpu.VMEM)] * (len(operands) - scalars)
    return pl.pallas_call(
        kernel,
        out_shape=[jax.ShapeDtypeStruct(shape, kind) for shape, kind in outs],
        in_specs=specs,
        out_specs=[pl.BlockSpec(memory_space=pltpu.VMEM)] * len(outs),
        scratch_shapes=list(scratch),
        compiler_params=pltpu.CompilerParams(vmem_limit_bytes=VMEM_BYTES),
        cost_estimate=COST,
    )(*operands)


def after(first, second):
    return lax.optimization_barrier((first, second))[1]


def lane_ids(shape):
    return lax.broadcasted_iota(jnp.int32, shape, len(shape) - 1)


def half_tile(ref, first_tile, place, upper):
    start = pl.multiple_of((first_tile + place // 2) * LANES, LANES)
    tile = ref[:, pl.ds(start, LANES)].astype(float32)
    turned = pltpu.roll(tile, HALF, 1)
    odd = place % 2 == 1
    if upper:
        return jnp.where(odd, tile, turned)
    return jnp.where(odd, turned, tile)


def padded(values, rows):
    if values.shape[0] == rows:
        return values
    blank = jnp.zeros((rows - values.shape[0], values.shape[1]), values.dtype)
    return jnp.concatenate([values, blank], axis=0)


def attn_rows(rows):
    return (2, rows // 2) if rows % 32 == 0 else (1, max(rows, 16))


def pack_attn_kernel(where_ref, lengths_ref, w_q, w_k, w_v, w_o, *outs):
    rows = w_q.shape[0]
    parts, high = attn_rows(rows)
    place = where_ref[0]
    lane = lane_ids((rows, LANES))
    for mask, out in enumerate(outs):
        other = place ^ mask
        at = pl.multiple_of(other * LANES, LANES)
        tile = jnp.where(
            lane < HALF, half_tile(w_k, 0, other, False), half_tile(w_v, 0, other, True)
        )
        piece = jnp.concatenate(
            [w_q[:, pl.ds(at, LANES)].astype(float32), tile, w_o[:, pl.ds(at, LANES)].astype(float32)],
            axis=1,
        )
        pieces = [piece[: rows // 2], piece[rows // 2 :]] if parts == 2 else [padded(piece, high)]
        width = piece.shape[1]
        for part, values in enumerate(pieces):
            out[:, part * width : (part + 1) * width] = values.astype(bfloat16)
        free = out.shape[1] - parts * width
        ids = lane_ids((high, free))
        marks = jnp.zeros((high, free), float32)
        for slot in range(lengths_ref.shape[1]):
            marks = jnp.where(ids == free - LANES + slot, lengths_ref[0, slot].astype(float32), marks)
        out[:, parts * width :] = marks.astype(bfloat16)


def pack_ffn_kernel(where_ref, w_g, w_u, w_d, *outs):
    rows = w_g.shape[0]
    big = w_g.shape[1] // LANES // PLANE * LANES
    half = big // 2
    last = w_g.shape[1] // LANES // PLANE * PLANE
    place = where_ref[0]
    lane = lane_ids((rows, LANES))
    for mask, out in enumerate(outs):
        other = place ^ mask
        parts = []
        for number in range(2):
            at = pl.ds(pl.multiple_of(other * big + number * half, LANES), half)
            parts += [w[:, at].astype(float32) for w in (w_g, w_u, w_d)]
            if number == 0:
                parts.append(
                    jnp.where(
                        lane < HALF,
                        half_tile(w_g, last, other, False),
                        half_tile(w_u, last, other, True),
                    )
                )
                parts.append(jnp.where(lane < HALF, half_tile(w_d, last, other, False), 0.0))
        out[...] = padded(jnp.concatenate(parts, axis=1), out.shape[0]).astype(bfloat16)


def unpack_attn_kernel(where_ref, own, one, two, three, attn_out, lens_out, held):
    rows = attn_out.shape[0] // PLANE
    width = attn_out.shape[1]
    parts, _ = attn_rows(rows)
    place = where_ref[0]
    for mask, message in enumerate((own, one, two, three)):
        at = pl.ds(pl.multiple_of((place ^ mask) * rows, rows), rows)
        values = [
            message[:, part * width : (part + 1) * width].astype(float32) for part in range(parts)
        ]
        held[at, :] = jnp.concatenate(values, axis=0) if parts == 2 else values[0][:rows]
        lens = message[:16, message.shape[1] - LANES :].astype(float32)
        lens_out[mask * 8 : (mask + 1) * 8, :] = lens[:8]
    attn_out[...] = held[...].astype(bfloat16)


def unpack_ffn_kernel(where_ref, own, one, two, three, first_out, second_out, held):
    rows = first_out.shape[0] // PLANE
    place = where_ref[0]
    for mask, message in enumerate((own, one, two, three)):
        at = pl.ds(pl.multiple_of((place ^ mask) * rows, rows), rows)
        held[at, :] = message[...].astype(float32)[:rows]
    width = first_out.shape[1]
    first_out[...] = held[:, :width].astype(bfloat16)
    second_out[...] = held[:, width:].astype(bfloat16)


def head_mean(values):
    low = lane_ids(values.shape) < HALF
    first = jnp.sum(jnp.where(low, values, 0.0), axis=1, keepdims=True)
    second = jnp.sum(jnp.where(low, 0.0, values), axis=1, keepdims=True)
    return jnp.where(low, first, second) * (1.0 / HALF)


def turn_halves(values):
    first = lane_ids(values.shape) % HALF < HALF // 2
    return jnp.where(
        first, pltpu.roll(values, LANES - HALF // 2, 1), pltpu.roll(values, HALF // 2, 1)
    )


def at_head(values, head):
    low = lane_ids(values.shape) < HALF
    if head == 0:
        return jnp.where(low, values, 0.0).astype(bfloat16)
    return jnp.where(low, 0.0, pltpu.roll(values, HALF, 1)).astype(bfloat16)


def group_probs(query, key, begin, row_ids, col_ids):
    scores = matmul_nt(query, key) * HEAD_DIM ** (-0.5)
    scores = jnp.where((col_ids >= begin) & (col_ids <= row_ids), scores, masked_score)
    expd = jnp.exp(scores - jnp.max(scores, axis=1, keepdims=True))
    return expd / jnp.sum(expd, axis=1, keepdims=True)


def group_mask(ends_ref, group, rows):
    row_ids = lax.broadcasted_iota(jnp.int32, (rows, rows), 0)
    col_ids = lax.broadcasted_iota(jnp.int32, (rows, rows), 1)
    begin = jnp.zeros((rows, rows), jnp.int32)
    for slot in range(ends_ref.shape[1]):
        end = ends_ref[group, slot]
        begin = jnp.maximum(begin, jnp.where(row_ids >= end, end, 0))
    return begin, row_ids, col_ids


def group_rows(core, mine, other):
    first = jnp.where(core == 0, mine, other)
    second = jnp.where(core == 0, other, mine)
    return jnp.concatenate([first, second], axis=0)


def deep_rows(depth, step, layers, rows):
    at = lax.rem(depth + step + layers, layers) * rows
    return pl.ds(pl.multiple_of(at, rows), rows)


def attn_kernel(layers, where_ref, ends_ref, tok_m, tok_o, a_gain, q_gain, k_gain, cos, sin, *refs):
    pieces, refs = refs[:layers], refs[layers:]
    send, keep, pre_out, low_out, mixed_out, weight, held = refs
    group = pl.program_id(0)
    depth, core = where_ref[1], where_ref[2]
    local = tok_m.shape[0]

    @pl.when(group == 0)
    def _():
        for step, piece in enumerate(pieces):
            weight[deep_rows(depth, -step, layers, piece.shape[0]), :] = piece[...]

    x = group_rows(core, tok_m[...].astype(float32), tok_o[...].astype(float32))
    normed = (x * inverse_rms(x) * a_gain[...]).astype(bfloat16)
    pre = matmul(normed, weight[:, : 2 * LANES])
    pre_out[...] = pre
    cosine, sine = cos[...], sin[...]
    tiles = []
    for number, gain in enumerate((q_gain[...], k_gain[...])):
        tile = pre[:, number * LANES : (number + 1) * LANES]
        scaled = tile * lax.rsqrt(head_mean(tile * tile) + epsilon) * gain
        tiles.append(scaled * cosine + turn_halves(scaled) * sine)
    lane = lane_ids(tiles[0].shape)
    query = tiles[0].astype(bfloat16)
    key_value = jnp.where(lane < HALF, tiles[1], pre[:, LANES:])
    low_out[:, :LANES] = query
    low_out[:, LANES:] = key_value.astype(bfloat16)
    begin, row_ids, col_ids = group_mask(ends_ref, group, x.shape[0])
    turned = pltpu.roll(key_value, HALF, 1)
    mixed = jnp.zeros(tiles[0].shape, float32)
    for head in range(2):
        probs = group_probs(query, at_head(key_value, head), begin, row_ids, col_ids)
        mixed += matmul(probs.astype(bfloat16), at_head(turned, head))
    mixed = mixed.astype(bfloat16)
    mixed_out[...] = mixed
    held[...] = matmul_nt(mixed, weight[:, 2 * LANES :])
    mine = pl.multiple_of(core * local, local)
    other = pl.multiple_of((1 - core) * local, local)
    send[...] = held[pl.ds(other, local), :].astype(bfloat16)
    keep[...] = held[pl.ds(mine, local), :]


def attn_back_kernel(
    layers, where_ref, ends_ref, tok_m, tok_o, a_gain, q_gain, k_gain, cos, sin, dh_m, dh_o,
    pre_ref, low_ref, mixed_ref, weight, gain_ffn, *refs,
):
    send, keep, own, gains_out = refs[:4]
    pieces = refs[4 : 3 + layers]
    held, total, sum_a, sum_qk = refs[3 + layers :]
    group = pl.program_id(0)
    depth, core = where_ref[1], where_ref[2]
    local = tok_m.shape[0]

    @pl.when(group == 0)
    def _():
        total[...] = jnp.zeros_like(total)
        sum_a[...] = jnp.zeros_like(sum_a)
        sum_qk[...] = jnp.zeros_like(sum_qk)

    x = group_rows(core, tok_m[...].astype(float32), tok_o[...].astype(float32))
    unit_a = x * inverse_rms(x)
    normed = (unit_a * a_gain[...]).astype(bfloat16)
    d_hidden = group_rows(core, dh_m[...], dh_o[...])
    mixed = mixed_ref[...]
    total[:, 2 * LANES :] += matmul_tn(d_hidden, mixed)
    d_mixed = matmul(d_hidden, weight[:, 2 * LANES :]).astype(bfloat16)
    query = low_ref[:, :LANES]
    key_value = low_ref[:, LANES:].astype(float32)
    turned = pltpu.roll(key_value, HALF, 1)
    begin, row_ids, col_ids = group_mask(ends_ref, group, x.shape[0])
    scale = HEAD_DIM ** (-0.5)
    shape = mixed.shape
    d_query = jnp.zeros(shape, float32)
    d_keys, d_values = [], []
    for head in range(2):
        key = at_head(key_value, head)
        probs = group_probs(query, key, begin, row_ids, col_ids)
        d_values.append(matmul_tn(probs.astype(bfloat16), d_mixed))
        d_probs = matmul_nt(d_mixed, at_head(turned, head))
        centre = jnp.sum(probs * d_probs, axis=1, keepdims=True)
        d_scores = (probs * (d_probs - centre)).astype(bfloat16)
        d_query += matmul(d_scores, key)
        d_keys.append(matmul_tn(d_scores, query))
    d_key = d_keys[0] + pltpu.roll(d_keys[1], HALF, 1)
    d_value = pltpu.roll(d_values[0], HALF, 1) + d_values[1]
    lane = lane_ids(shape)
    cosine, sine = cos[...], sin[...]
    tiles = []
    for number, (grad, gain) in enumerate(((d_query, q_gain[...]), (d_key, k_gain[...]))):
        grad = grad * scale
        back = grad * cosine - turn_halves(grad) * sine
        tile = pre_ref[:, number * LANES : (number + 1) * LANES]
        factor = lax.rsqrt(head_mean(tile * tile) + epsilon)
        unit = tile * factor
        sum_qk[number : number + 1, :] += jnp.sum(back * unit, axis=0, keepdims=True)
        back = back * gain
        tiles.append(factor * (back - unit * head_mean(back * unit)))
    tiles[1] = jnp.where(lane < HALF, tiles[1], d_value)
    d_qkv = jnp.concatenate(tiles, axis=1).astype(bfloat16)
    total[:, : 2 * LANES] += matmul_tn(normed, d_qkv)
    held[...] = matmul_nt(d_qkv, weight[:, : 2 * LANES])
    sum_a[...] += jnp.sum(held[...] * unit_a, axis=0, keepdims=True)
    mine = pl.multiple_of(core * local, local)
    other = pl.multiple_of((1 - core) * local, local)
    send[...] = held[pl.ds(other, local), :].astype(bfloat16)
    keep[...] = held[pl.ds(mine, local), :]

    @pl.when(group == pl.num_programs(0) - 1)
    def _():
        for row in range(GAIN_ROWS):
            gains_out[row : row + 1, :LANES] = sum_a[:, row * LANES : (row + 1) * LANES]
            gains_out[row : row + 1, LANES : 2 * LANES] = gain_ffn[:, row * LANES : (row + 1) * LANES]
        q_sum = sum_qk[0:1, :] + pltpu.roll(sum_qk[0:1, :], HALF, 1)
        k_sum = pltpu.roll(sum_qk[1:2, :], HALF, 1)
        qk_sum = jnp.where(lane_ids(q_sum.shape) < HALF, q_sum, k_sum)
        ids = lax.broadcasted_iota(jnp.int32, (GAIN_ROWS, LANES), 0)
        gains_out[:, 2 * LANES :] = jnp.where(ids == 0, qk_sum, 0.0)
        gains = gains_out[...]
        top = gains.astype(bfloat16)
        rest = (gains - top.astype(float32)).astype(bfloat16)
        tail = jnp.concatenate([top.astype(float32), rest.astype(float32)], axis=0).astype(bfloat16)
        rows = own.shape[0]
        own[...] = total[deep_rows(depth, 0, layers, rows), :]
        for index, piece in enumerate(pieces):
            piece[:rows, :] = total[deep_rows(depth, index + 1, layers, rows), :].astype(bfloat16)
            piece[rows:, :] = tail


def attn_specs(rows, width, group_height):
    scalar = pl.BlockSpec(memory_space=pltpu.SMEM)
    block = pl.BlockSpec((rows, width), lambda i: (i, 0))
    gain = pl.BlockSpec((1, width), lambda i: (0, 0))
    small = pl.BlockSpec((1, LANES), lambda i: (0, 0))
    table = pl.BlockSpec((group_height, LANES), lambda i: (i, 0))
    wide = pl.BlockSpec((group_height, 2 * LANES), lambda i: (i, 0))
    return scalar, block, gain, small, table, wide


def whole_spec(shape):
    return pl.BlockSpec(shape, lambda i: (0, 0), pipeline_mode=pl.Buffered(1))


def attn(where, ends, tok_mine, tok_other, gains, tables, pieces):
    layers = len(pieces)
    rows, width = tok_mine.shape
    local = rows // PLANE
    scalar, block, gain, small, table, wide = attn_specs(local, width, 2 * local)
    high, columns = pieces[0].shape
    weight = (layers * high, columns)
    return pl.pallas_call(
        lambda *refs: attn_kernel(layers, *refs),
        grid=(PLANE,),
        in_specs=[scalar, scalar, block, block, gain, small, small, table, table]
        + [whole_spec((high, columns))] * layers,
        out_specs=[block, block, wide, wide, table, whole_spec(weight)],
        out_shape=[
            jax.ShapeDtypeStruct((rows, width), bfloat16),
            jax.ShapeDtypeStruct((rows, width), float32),
            jax.ShapeDtypeStruct((2 * rows, 2 * LANES), float32),
            jax.ShapeDtypeStruct((2 * rows, 2 * LANES), bfloat16),
            jax.ShapeDtypeStruct((2 * rows, LANES), bfloat16),
            jax.ShapeDtypeStruct(weight, bfloat16),
        ],
        scratch_shapes=[pltpu.VMEM((2 * local, width), float32)],
        compiler_params=pltpu.CompilerParams(vmem_limit_bytes=VMEM_BYTES),
        cost_estimate=cost(36),
    )(where, ends, tok_mine, tok_other, *gains, *tables, *pieces)


def attn_back(where, ends, layers, tok_mine, tok_other, gains, tables, dh, saved, weight, gain_ffn):
    rows, width = tok_mine.shape
    local = rows // PLANE
    scalar, block, gain, small, table, wide = attn_specs(local, width, 2 * local)
    high, columns = weight.shape[0] // layers, weight.shape[1]
    tail = 2 * GAIN_ROWS
    return pl.pallas_call(
        lambda *refs: attn_back_kernel(layers, *refs),
        grid=(PLANE,),
        in_specs=[scalar, scalar, block, block, gain, small, small, table, table, block, block]
        + [wide, wide, table, whole_spec(weight.shape), gain],
        out_specs=[block, block, whole_spec((high, columns)), whole_spec((GAIN_ROWS, columns))]
        + [whole_spec((high + tail, columns))] * (layers - 1),
        out_shape=[
            jax.ShapeDtypeStruct((rows, width), bfloat16),
            jax.ShapeDtypeStruct((rows, width), float32),
            jax.ShapeDtypeStruct((high, columns), float32),
            jax.ShapeDtypeStruct((GAIN_ROWS, columns), float32),
        ]
        + [jax.ShapeDtypeStruct((high + tail, columns), bfloat16)] * (layers - 1),
        scratch_shapes=[
            pltpu.VMEM((2 * local, width), float32),
            pltpu.VMEM(weight.shape, float32),
            pltpu.VMEM((1, width), float32),
            pltpu.VMEM((8, LANES), float32),
        ],
        compiler_params=pltpu.CompilerParams(vmem_limit_bytes=VMEM_BYTES),
        cost_estimate=cost(24),
    )(where, ends, tok_mine, tok_other, *gains, *tables, *dh, *saved, weight, gain_ffn)


def live_rows(ends_ref, values, step, core):
    local = values.shape[0] // 2
    parts = []
    for k in range(2):
        part = values[k * local : (k + 1) * local, :]
        ids = lax.broadcasted_iota(jnp.int32, part.shape, 0) + core * local
        end = ends_ref[2 * step + k, ends_ref.shape[1] - 1]
        parts.append(jnp.where(ids < end, part, jnp.zeros_like(part)))
    return parts


def swiglu(gate, up, d_act):
    sigma = 1.0 / (1.0 + jnp.exp(-gate))
    silu = gate * sigma
    d_gate = d_act * up * sigma * (1.0 + gate * (1.0 - sigma))
    return silu * up, d_gate, d_act * silu


def ffn_rows(where_ref, ends_ref, x_o, x_m, g_o, g_m):
    step, core = pl.program_id(0), where_ref[2]
    x = jnp.concatenate([x_o[...], x_m[...]], axis=0)
    grads = live_rows(ends_ref, g_o[...], step, 1 - core) + live_rows(ends_ref, g_m[...], step, core)
    return x, jnp.concatenate(grads, axis=0)


def half_layer(x, grads, weight, total):
    half = x.shape[1] // 4
    pre = matmul(x, weight[:, : 2 * half])
    act, d_gate, d_up = swiglu(
        pre[:, :half], pre[:, half:], matmul(grads, weight[:, 2 * half : 3 * half])
    )
    act = act.astype(bfloat16)
    d_both = jnp.concatenate([d_gate, d_up], axis=1).astype(bfloat16)
    total[:, : 2 * half] += matmul_tn(x, d_both)
    total[:, 2 * half : 3 * half] += matmul_tn(grads, act)
    return act, d_both


def ffn_first_kernel(
    where_ref, ends_ref, x_o, x_m, g_o, g_m, weight, act_out, d_out, grad_out, total
):
    @pl.when(pl.program_id(0) == 0)
    def _():
        total[...] = jnp.zeros_like(total)

    x, grads = ffn_rows(where_ref, ends_ref, x_o, x_m, g_o, g_m)
    half = x.shape[1] // 4
    act, d_both = half_layer(x, grads, weight, total)
    act_out[:, :half] = act
    d_out[:, : 2 * half] = d_both
    pre = matmul(x, weight[:, 3 * half : 3 * half + LANES])
    d_act = matmul(grads, weight[:, 3 * half + LANES :])
    act, d_gate, d_up = swiglu(pre, pltpu.roll(pre, HALF, 1), d_act)
    lane = lane_ids(pre.shape)
    act = jnp.where(lane < HALF, act, 0.0).astype(bfloat16)
    d_both = jnp.where(lane < HALF, d_gate, pltpu.roll(d_up, HALF, 1)).astype(bfloat16)
    total[:, 3 * half : 3 * half + LANES] += matmul_tn(x, d_both)
    total[:, 3 * half + LANES :] += matmul_tn(grads, act)
    act_out[:, half:] = act
    d_out[:, 2 * half :] = d_both

    @pl.when(pl.program_id(0) == pl.num_programs(0) - 1)
    def _():
        grad_out[...] = total[...].astype(bfloat16)


def ffn_second_kernel(
    where_ref, ends_ref, x_o, x_m, g_o, g_m, weight, first_weight, first_act, first_d,
    out_send, out_keep, dn_send, dn_keep, grad_out, total,
):
    @pl.when(pl.program_id(0) == 0)
    def _():
        total[...] = jnp.zeros_like(total)

    x, grads = ffn_rows(where_ref, ends_ref, x_o, x_m, g_o, g_m)
    half = x.shape[1] // 4
    act, d_both = half_layer(x, grads, weight, total)
    height = x.shape[0] // 2
    partial = (
        matmul_nt(d_both, weight[:, : 2 * half])
        + matmul_nt(first_d[:, : 2 * half], first_weight[:, : 2 * half])
        + matmul_nt(first_d[:, 2 * half :], first_weight[:, 3 * half : 3 * half + LANES])
    )
    dn_send[...] = partial[:height].astype(bfloat16)
    dn_keep[...] = partial[height:]
    partial = (
        matmul_nt(act, weight[:, 2 * half :])
        + matmul_nt(first_act[:, :half], first_weight[:, 2 * half : 3 * half])
        + matmul_nt(first_act[:, half:], first_weight[:, 3 * half + LANES :])
    )
    out_send[...] = partial[:height].astype(bfloat16)
    out_keep[...] = partial[height:]

    @pl.when(pl.program_id(0) == pl.num_programs(0) - 1)
    def _():
        grad_out[...] = total[...].astype(bfloat16)


def ffn_specs(rows, width):
    scalar = pl.BlockSpec(memory_space=pltpu.SMEM)
    block = pl.BlockSpec((rows // 2, width), lambda i: (i, 0))
    act = pl.BlockSpec((rows, width // 4 + LANES), lambda i: (i, 0))
    d_both = pl.BlockSpec((rows, width // 2 + LANES), lambda i: (i, 0))
    return scalar, block, act, d_both


def ffn_first(where, ends, x_mine, x_other, g_mine, g_other, weight):
    rows, width = x_mine.shape
    scalar, block, act, d_both = ffn_specs(rows, width)
    return pl.pallas_call(
        ffn_first_kernel,
        grid=(2,),
        in_specs=[scalar, scalar] + [block] * 4 + [whole_spec(weight.shape)],
        out_specs=[act, d_both, whole_spec(weight.shape)],
        out_shape=[
            jax.ShapeDtypeStruct((2 * rows, width // 4 + LANES), bfloat16),
            jax.ShapeDtypeStruct((2 * rows, width // 2 + LANES), bfloat16),
            jax.ShapeDtypeStruct(weight.shape, bfloat16),
        ],
        scratch_shapes=[pltpu.VMEM(weight.shape, float32)],
        compiler_params=pltpu.CompilerParams(vmem_limit_bytes=VMEM_BYTES),
        cost_estimate=cost(25),
    )(where, ends, x_other, x_mine, g_other, g_mine, weight)


def ffn_second(where, ends, x_mine, x_other, g_mine, g_other, weight, first_weight, saved):
    rows, width = x_mine.shape
    scalar, block, act, d_both = ffn_specs(rows, width)
    return pl.pallas_call(
        ffn_second_kernel,
        grid=(2,),
        in_specs=[scalar, scalar]
        + [block] * 4
        + [whole_spec(weight.shape), whole_spec(first_weight.shape), act, d_both],
        out_specs=[block] * 4 + [whole_spec(weight.shape)],
        out_shape=[
            jax.ShapeDtypeStruct((rows, width), bfloat16),
            jax.ShapeDtypeStruct((rows, width), float32),
            jax.ShapeDtypeStruct((rows, width), bfloat16),
            jax.ShapeDtypeStruct((rows, width), float32),
            jax.ShapeDtypeStruct(weight.shape, bfloat16),
        ],
        scratch_shapes=[pltpu.VMEM(weight.shape, float32)],
        compiler_params=pltpu.CompilerParams(vmem_limit_bytes=VMEM_BYTES),
        cost_estimate=cost(50),
    )(where, ends, x_other, x_mine, g_other, g_mine, weight, first_weight, *saved)


def chip_sum_kernel(keep, received, *outs):
    rows = outs[0].shape[0]
    for mask, out in enumerate(outs):
        span = slice(mask * rows, (mask + 1) * rows)
        out[...] = (keep[span, :] + received[span, :].astype(float32)).astype(out.dtype)


def chip_sum(keep, received):
    shape = (keep.shape[0] // PLANE, keep.shape[1])
    outs = [(shape, float32)] + [(shape, bfloat16)] * (PLANE - 1)
    return call(chip_sum_kernel, outs, keep, received)


def plane_total(parts):
    return add_up([parts[0]] + [send_plane(part, mask + 1) for mask, part in enumerate(parts[1:])])


def add_up(parts):
    return sum(part.astype(float32) for part in parts)


def tail_kernel(where_ref, keep, received, own_ff, own, ff_out, *refs):
    messages, held = refs[:-1], refs[-1]
    held[...] = own_ff[...].astype(float32)
    place = where_ref[0]
    local = own.shape[0]
    rows, columns = ff_out.shape
    for mask in range(PLANE):
        span = slice(mask * local, (mask + 1) * local)
        value = keep[span, :] + received[span, :].astype(float32)
        grads = held[pl.ds(pl.multiple_of((place ^ mask) * rows, rows), rows), :]
        if mask == 0:
            own[...] = value
            ff_out[...] = grads
            continue
        out = messages[mask - 1]
        tall = out.shape[0] - local
        out[:local, :] = value.astype(bfloat16)
        out[local:, :columns] = padded(grads, tall).astype(bfloat16)
        if columns < out.shape[1]:
            out[local:, columns:] = jnp.zeros((tall, out.shape[1] - columns), bfloat16)


def tail_messages(where, keep, received, own_ff):
    local, width = keep.shape[0] // PLANE, keep.shape[1]
    rows, columns = own_ff.shape[0] // PLANE, own_ff.shape[1]
    message = (local + max(rows, 16), width)
    own, ff_out, *messages = call(
        tail_kernel,
        [((local, width), float32), ((rows, columns), float32)]
        + [(message, bfloat16)] * (PLANE - 1),
        where,
        keep,
        received,
        own_ff,
        scalars=1,
        scratch=[pltpu.VMEM(own_ff.shape, float32)],
    )
    return own, ff_out, messages


def joined_gains(tail):
    return tail[:GAIN_ROWS] + tail[GAIN_ROWS:]


def split_gains(gains):
    top = gains.astype(bfloat16).astype(float32)
    rest = (gains - top).astype(bfloat16).astype(float32)
    return jnp.concatenate([top, rest], axis=0)


def plane_sum_attn_kernel(where_ref, own, gains, *refs):
    received, outs = refs[: -PLANE - 2], refs[-PLANE - 2 : -2]
    held, held_gains = refs[-2:]
    layers = len(received) + 1
    value = own[...]
    high = own.shape[0]
    depth = where_ref[1]
    held_gains[deep_rows(depth, 0, layers, GAIN_ROWS), :] = joined_gains(split_gains(gains[...]))
    for step, part in enumerate(received):
        value = value + part[:high, :].astype(float32)
        held_gains[deep_rows(depth, -1 - step, layers, GAIN_ROWS), :] = joined_gains(
            part[high:, :].astype(float32)
        )
    held[...] = value
    sums = held_gains[:GAIN_ROWS, :]
    for layer in range(1, layers):
        sums = sums + held_gains[layer * GAIN_ROWS : (layer + 1) * GAIN_ROWS, :]
    tail = split_gains(sums)
    place = where_ref[0]
    rows = high // PLANE
    for mask, out in enumerate(outs):
        at = pl.multiple_of((place ^ mask) * rows, rows)
        part = held[pl.ds(at, rows), :]
        if mask:
            tall = out.shape[0] - tail.shape[0]
            out[:tall, :] = padded(part, tall).astype(bfloat16)
            out[tall:, :] = tail.astype(bfloat16)
        else:
            out[:rows, :] = part
            out[rows:, :] = tail


def plane_split_attn(where, own, received, gains):
    rows, columns = own.shape[0] // PLANE, own.shape[1]
    tail = 2 * GAIN_ROWS
    shapes = [((rows + tail, columns), float32)]
    shapes += [((max(rows, 16) + tail, columns), bfloat16)] * (PLANE - 1)
    scratch = [
        pltpu.VMEM(own.shape, float32),
        pltpu.VMEM(((len(received) + 1) * GAIN_ROWS, columns), float32),
    ]
    return call(
        plane_sum_attn_kernel, shapes, where, own, gains, *received, scalars=1, scratch=scratch
    )


def pick_place(refs, place, target, columns, rows):
    value = jnp.zeros((rows, columns.stop - columns.start), float32)
    for mask, ref in enumerate(refs):
        value = jnp.where(place ^ mask == target, ref[:, columns].astype(float32)[:rows], value)
    return value


def place_ffn_kernel(where_ref, *refs):
    firsts, seconds, (out_g, out_u, out_d, held) = refs[:PLANE], refs[PLANE : 2 * PLANE], refs[2 * PLANE :]
    place = where_ref[0]
    rows = out_g.shape[0]
    big = out_g.shape[1] // LANES // PLANE * LANES
    half = big // 2
    last = PLANE * big
    tall = max(rows, 16)
    for mask in range(PLANE):
        start = firsts[mask].shape[0] - tall if mask else 0
        parts = [ref[start:, :].astype(float32)[:rows] for ref in (firsts[mask], seconds[mask])]
        for part, values in enumerate(parts):
            at = pl.ds(pl.multiple_of((place ^ mask) * big + part * half, LANES), half)
            for number, out in enumerate((out_g, out_u, out_d)):
                out[:, at] = values[:, number * half : (number + 1) * half]
        held[mask] = parts[0][:, 3 * half :]
    for pair in range(PLANE // 2):
        low = held[place ^ (2 * pair)]
        high = held[place ^ (2 * pair + 1)]
        lane = lane_ids((rows, LANES))
        span = slice(last + pair * LANES, last + (pair + 1) * LANES)
        gu_low, gu_high = low[:, :LANES], high[:, :LANES]
        out_g[:, span] = jnp.where(lane < HALF, gu_low, pltpu.roll(gu_high, HALF, 1))
        out_u[:, span] = jnp.where(lane < HALF, pltpu.roll(gu_low, HALF, 1), gu_high)
        out_d[:, span] = jnp.where(lane < HALF, low[:, LANES:], pltpu.roll(high[:, LANES:], HALF, 1))


def place_attn_kernel(where_ref, own, one, two, three, out_q, out_k, out_v, out_o, out_gains):
    place = where_ref[0]
    refs = (own, one, two, three)
    rows = out_q.shape[0]
    for mask, ref in enumerate(refs):
        at = pl.ds(pl.multiple_of((place ^ mask) * LANES, LANES), LANES)
        out_q[:, at] = ref[:, :LANES].astype(float32)[:rows]
        out_o[:, at] = ref[:, 2 * LANES :].astype(float32)[:rows]
    for pair in range(PLANE // 2):
        low = pick_place(refs, place, 2 * pair, slice(LANES, 2 * LANES), rows)
        high = pick_place(refs, place, 2 * pair + 1, slice(LANES, 2 * LANES), rows)
        lane = lane_ids(low.shape)
        span = slice(pair * LANES, (pair + 1) * LANES)
        out_k[:, span] = jnp.where(lane < HALF, low, pltpu.roll(high, HALF, 1))
        out_v[:, span] = jnp.where(lane < HALF, pltpu.roll(low, HALF, 1), high)
    tails = [joined_gains(ref[ref.shape[0] - 2 * GAIN_ROWS :, :].astype(float32)) for ref in refs]
    out_gains[...] = (tails[0] + tails[1]) + (tails[2] + tails[3])


def plane_parts(local):
    return [local] + [send_plane(local, mask) for mask in range(1, PLANE)]


def both_cores(parts):
    mine = jnp.concatenate(parts)
    return mine, swap_cores(mine)


def gather_rows(local):
    return both_cores(plane_parts(local))


def body(
    tokens,
    lengths,
    attn_gain,
    query_gain,
    key_gain,
    ffn_gain,
    w_query,
    w_key,
    w_value,
    w_out,
    w_gate,
    w_up,
    w_down,
    cotangent,
):
    dp = lax.axis_index("dp")
    core = lax.axis_index("tensor")
    layers = lax.axis_size("dp") // PLANE
    where = jnp.stack([dp % PLANE, dp // PLANE, core]).astype(jnp.int32)
    local_rows, model = tokens.shape
    total_rows = local_rows * lax.axis_size("tensor")
    rows = w_query.shape[0]
    q_cols = w_query.shape[1] // PLANE
    kv_cols = w_key.shape[1] // PLANE
    local_kv = kv_cols // HEAD_DIM
    share = q_cols // kv_cols
    attn_cols = 2 * q_cols + 2 * kv_cols
    ff_cols = 3 * (w_gate.shape[1] // LANES // PLANE * LANES) + 2 * LANES

    parts, high = attn_rows(rows)
    tall = max(rows, 16)
    first = call(
        pack_attn_kernel,
        [((high, model), bfloat16)] * PLANE,
        where,
        lengths,
        w_query,
        w_key,
        w_value,
        w_out,
        scalars=2,
    )
    second = call(
        pack_ffn_kernel,
        [((tall, ff_cols), bfloat16)] * PLANE,
        where,
        w_gate,
        w_up,
        w_down,
        scalars=1,
    )
    first = [first[0]] + [send_plane(first[m], m) for m in range(1, PLANE)]
    attn_piece, lens = call(
        unpack_attn_kernel,
        [((PLANE * rows, attn_cols), bfloat16), ((PLANE * 8, LANES), float32)],
        where,
        *first,
        scalars=1,
        scratch=[pltpu.VMEM((PLANE * rows, attn_cols), float32)],
    )
    attn_pieces = [attn_piece] + [send_deep(attn_piece, step) for step in range(1, layers)]
    second = after(first, second)
    second = [second[0]] + [send_plane(second[m], m) for m in range(1, PLANE)]
    second = after(attn_pieces, second)
    ff_first_cols = ff_cols - 3 * model // 4
    ff_pieces = call(
        unpack_ffn_kernel,
        [
            ((PLANE * rows, ff_first_cols), bfloat16),
            ((PLANE * rows, ff_cols - ff_first_cols), bfloat16),
        ],
        where,
        *second,
        scalars=1,
        scratch=[pltpu.VMEM((PLANE * rows, ff_cols), float32)],
    )
    columns = [list(range(k, layers * PLANE, PLANE)) for k in range(PLANE)]
    ff_weights = [
        lax.all_gather(piece, "dp", axis=0, tiled=True, axis_index_groups=columns)
        for piece in ff_pieces
    ]
    attn_pieces = after(ff_pieces, attn_pieces)
    tok_parts = plane_parts(tokens)
    cot_parts = plane_parts(after(second, cotangent))
    tok_mine, tok_other = both_cores(tok_parts)
    cot_mine, cot_other = both_cores(cot_parts)

    slots = lengths.shape[1]
    all_lengths = lens.reshape(PLANE, 8, LANES)[:, 0, :slots].astype(jnp.int32)
    ends = jnp.cumsum(all_lengths, axis=1, dtype=jnp.int32)
    row_ids = jnp.arange(total_rows, dtype=jnp.int32)
    begin = jnp.max(
        jnp.where(row_ids[None, :, None] >= ends[:, None, :], ends[:, None, :], 0), axis=2
    )
    position = (row_ids[None, :] - begin).reshape(-1).astype(jnp.float32)
    spread = jnp.arange(LANES, dtype=jnp.int32) % (HEAD_DIM // 2)
    freqs = rope_base ** (-spread.astype(jnp.float32) * 2.0 / HEAD_DIM)
    angles = position[:, None] * freqs[None, :]
    sign = jnp.where(jnp.arange(LANES) % HEAD_DIM < HEAD_DIM // 2, -1.0, 1.0).astype(jnp.float32)
    tables = (jnp.cos(angles), jnp.sin(angles) * sign)
    gains = (
        attn_gain[None, :],
        jnp.concatenate([query_gain, query_gain])[None, :],
        jnp.concatenate([key_gain, key_gain])[None, :],
    )

    inputs = tokens.astype(jnp.float32)
    factor_a = inverse_rms(inputs)
    unit_a = inputs * factor_a
    send, keep, *saved, attn_weight = attn(
        where, ends, tok_mine, tok_other, gains, tables, attn_pieces
    )
    send = after(cot_parts, send)
    hidden = inputs + plane_total(chip_sum(keep, swap_cores(send)))
    factor_b = inverse_rms(hidden)
    unit_b = hidden * factor_b
    x_mine, x_other = gather_rows((unit_b * ffn_gain).astype(jnp.bfloat16))

    x_and_grads = (x_mine, x_other, cot_mine, cot_other)
    *ff_saved, ff_grad = ffn_first(where, ends, *x_and_grads, ff_weights[0])
    own_first = lax.psum_scatter(
        ff_grad, "dp", scatter_dimension=0, tiled=True, axis_index_groups=columns
    )
    out_send, out_keep, dn_send, dn_keep, ff_grad = ffn_second(
        where, ends, *x_and_grads, ff_weights[1], ff_weights[0], ff_saved
    )
    own_second = lax.psum_scatter(
        ff_grad, "dp", scatter_dimension=0, tiled=True, axis_index_groups=columns
    )
    dn_parts = chip_sum(dn_keep, swap_cores(dn_send))
    out_keep = after(dn_parts, out_keep)
    d_normed2 = plane_total(dn_parts)
    grad_out = jnp.where(
        (jnp.arange(local_rows) + core * local_rows < ends[0, slots - 1])[:, None],
        cotangent,
        jnp.zeros_like(cotangent),
    )
    gain_ffn = jnp.sum(d_normed2 * unit_b, axis=0)
    d_hidden = grad_out.astype(jnp.float32) + norm_back(d_normed2 * ffn_gain, unit_b, factor_b)
    h_mine, h_other = gather_rows(after(own_first, d_hidden.astype(jnp.bfloat16)))
    own_out, ff_first, messages = tail_messages(where, out_keep, swap_cores(out_send), own_first)
    messages = after((h_mine, h_other), messages)
    first_messages = [send_plane(part, mask + 1) for mask, part in enumerate(messages)]
    block_out = hidden + (own_out + add_up([part[:local_rows] for part in first_messages]))
    block_out = block_out.astype(jnp.bfloat16)

    send, keep, own_attn, part_gains, *attn_grads = after(
        (block_out, own_second),
        attn_back(
            where, ends, layers, tok_mine, tok_other, gains, tables, (h_mine, h_other), saved,
            attn_weight, gain_ffn[None, :],
        ),
    )
    attn_grads = [send_deep(piece, step + 1) for step, piece in enumerate(attn_grads)]
    keep = after((attn_grads[0], attn_grads[-1]), keep)
    own_dn, ff_second, messages = tail_messages(where, keep, swap_cores(send), own_second)
    second_messages = [send_plane(part, mask + 1) for mask, part in enumerate(messages)]
    own_attn = after(second_messages[:2], own_attn)
    attn_parts = plane_split_attn(where, own_attn, attn_grads, part_gains)
    attn_parts = [attn_parts[0]] + [
        send_plane(part, mask + 1) for mask, part in enumerate(attn_parts[1:])
    ]
    d_normed = own_dn + add_up([part[:local_rows] for part in second_messages])
    grad_tokens = d_hidden + norm_back(d_normed * attn_gain, unit_a, factor_a)
    grad_gate, grad_up, grad_down = call(
        place_ffn_kernel,
        [(w_gate.shape, float32)] * 3,
        where,
        ff_first,
        *first_messages,
        ff_second,
        *second_messages,
        scalars=1,
        scratch=[pltpu.VMEM((PLANE, rows, 2 * LANES), float32)],
    )
    grad_query, grad_key, grad_value, grad_out_w, sums = call(
        place_attn_kernel,
        [(w.shape, float32) for w in (w_query, w_key, w_value, w_out)]
        + [((GAIN_ROWS, attn_cols), float32)],
        where,
        *attn_parts,
        scalars=1,
    )
    sums = sums + swap_cores(sums)
    return (
        block_out,
        grad_tokens,
        sums[:, :LANES].reshape(-1),
        sums[0, 2 * LANES : 2 * LANES + HEAD_DIM],
        sums[0, 2 * LANES + HEAD_DIM :],
        sums[:, LANES : 2 * LANES].reshape(-1),
        grad_query,
        grad_key,
        grad_value,
        grad_out_w,
        grad_gate,
        grad_up,
        grad_down,
    )


def solution(mesh):
    placed = (
        P(("dp", "tensor"), None),
        P("dp", None),
        P(),
        P(),
        P(),
        P(),
        P("dp", "tensor"),
        P("dp", "tensor"),
        P("dp", "tensor"),
        P("dp", "tensor"),
        P("dp", "tensor"),
        P("dp", "tensor"),
        P("dp", "tensor"),
        P(("dp", "tensor"), None),
    )
    return jax.shard_map(
        body,
        mesh=mesh,
        in_specs=placed,
        out_specs=(
            P(("dp", "tensor"), None),
            P(("dp", "tensor"), None),
            P(),
            P(),
            P(),
            P(),
            P("dp", "tensor"),
            P("dp", "tensor"),
            P("dp", "tensor"),
            P("dp", "tensor"),
            P("dp", "tensor"),
            P("dp", "tensor"),
            P("dp", "tensor"),
        ),
        check_vma=False,
    )
```

```python
import jax
import jax.numpy as jnp
from jax import lax
from jax.experimental import pallas as pl
from jax.experimental.pallas import tpu as pltpu
from jax.sharding import PartitionSpec as P

HEAD_DIM = 64


epsilon = 1e-05
rope_base = 1000000.0
masked_score = -1e30


def inverse_rms(values):
    return lax.rsqrt(jnp.mean(values * values, axis=-1, keepdims=True) + epsilon)


def norm_back(grad_unit, unit, factor):
    return factor * (grad_unit - unit * jnp.mean(grad_unit * unit, axis=-1, keepdims=True))


def matmul(first_op, second_op):
    return jnp.dot(first_op, second_op, preferred_element_type=jnp.float32)


def matmul_nt(first_op, second_op):
    return lax.dot_general(
        first_op, second_op, (((1,), (1,)), ((), ())), preferred_element_type=jnp.float32
    )


def matmul_tn(first_op, second_op):
    return lax.dot_general(
        first_op, second_op, (((0,), (0,)), ((), ())), preferred_element_type=jnp.float32
    )


def seq_layout(seq_lengths, total_rows):
    ends = jnp.cumsum(seq_lengths, dtype=jnp.int32)
    starts = ends - seq_lengths
    row_ids = jnp.arange(total_rows, dtype=jnp.int32)
    segment = jnp.sum(
        (row_ids[:, None] >= ends[None, :]).astype(jnp.int32), axis=1, dtype=jnp.int32
    )
    slot_ids = jnp.arange(seq_lengths.shape[0], dtype=jnp.int32)
    picked = (segment[:, None] == slot_ids[None, :]).astype(jnp.int32)
    begin = (
        jnp.sum(picked * starts[None, :], axis=1, dtype=jnp.int32)
        + (segment == seq_lengths.shape[0]).astype(jnp.int32) * ends[-1]
    )
    allowed = (segment[:, None] == segment[None, :]) & (row_ids[:, None] >= row_ids[None, :])
    return (row_ids - begin, row_ids < ends[-1], allowed)


def rope_tables(position, head_size):
    half_dim = head_size // 2
    freqs = rope_base ** (-jnp.arange(half_dim, dtype=jnp.float32) * 2.0 / head_size)
    angles = position.astype(jnp.float32)[:, None] * freqs[None, :]
    return (jnp.cos(angles)[:, None, :], jnp.sin(angles)[:, None, :])


def rotate(values, cosine, sine):
    half_dim = values.shape[-1] // 2
    first_half = values[..., :half_dim]
    second_half = values[..., half_dim:]
    return jnp.concatenate(
        [first_half * cosine - second_half * sine, second_half * cosine + first_half * sine],
        axis=-1,
    )


def rotate_back(grads, cosine, sine):
    half_dim = grads.shape[-1] // 2
    first_half = grads[..., :half_dim]
    second_half = grads[..., half_dim:]
    return jnp.concatenate(
        [first_half * cosine + second_half * sine, second_half * cosine - first_half * sine],
        axis=-1,
    )

PLANE = 4
LANES = 128
HALF = 64
VMEM_BYTES = 60 * 1024 * 1024
COST = pl.CostEstimate(flops=1024, bytes_accessed=1024, transcendentals=0)


def cost(megabytes):
    return pl.CostEstimate(flops=1024, bytes_accessed=megabytes * 1000000, transcendentals=0)
GAIN_ROWS = 8
float32 = jnp.float32
bfloat16 = jnp.bfloat16


def send_plane(values, mask):
    count = lax.axis_size("dp")
    return lax.ppermute(values, "dp", [(i, i ^ mask) for i in range(count)])


def send_deep(values, step):
    count = lax.axis_size("dp")
    return lax.ppermute(values, "dp", [(i, (i + PLANE * step) % count) for i in range(count)])


def swap_cores(values):
    return lax.ppermute(values, "tensor", [(0, 1), (1, 0)])


def call(kernel, outs, *operands, scalars=0, scratch=()):
    specs = [pl.BlockSpec(memory_space=pltpu.SMEM)] * scalars
    specs += [pl.BlockSpec(memory_space=pltpu.VMEM)] * (len(operands) - scalars)
    return pl.pallas_call(
        kernel,
        out_shape=[jax.ShapeDtypeStruct(shape, kind) for shape, kind in outs],
        in_specs=specs,
        out_specs=[pl.BlockSpec(memory_space=pltpu.VMEM)] * len(outs),
        scratch_shapes=list(scratch),
        compiler_params=pltpu.CompilerParams(vmem_limit_bytes=VMEM_BYTES),
        cost_estimate=COST,
    )(*operands)


def after(first, second):
    return lax.optimization_barrier((first, second))[1]


def lane_ids(shape):
    return lax.broadcasted_iota(jnp.int32, shape, len(shape) - 1)


def half_tile(ref, first_tile, place, upper):
    start = pl.multiple_of((first_tile + place // 2) * LANES, LANES)
    tile = ref[:, pl.ds(start, LANES)].astype(float32)
    turned = pltpu.roll(tile, HALF, 1)
    odd = place % 2 == 1
    if upper:
        return jnp.where(odd, tile, turned)
    return jnp.where(odd, turned, tile)


def padded(values, rows):
    if values.shape[0] == rows:
        return values
    blank = jnp.zeros((rows - values.shape[0], values.shape[1]), values.dtype)
    return jnp.concatenate([values, blank], axis=0)


def attn_rows(rows):
    return (2, rows // 2) if rows % 32 == 0 else (1, max(rows, 16))


def pack_attn_kernel(where_ref, lengths_ref, w_q, w_k, w_v, w_o, *outs):
    rows = w_q.shape[0]
    parts, high = attn_rows(rows)
    place = where_ref[0]
    lane = lane_ids((rows, LANES))
    for mask, out in enumerate(outs):
        other = place ^ mask
        at = pl.multiple_of(other * LANES, LANES)
        tile = jnp.where(
            lane < HALF, half_tile(w_k, 0, other, False), half_tile(w_v, 0, other, True)
        )
        piece = jnp.concatenate(
            [w_q[:, pl.ds(at, LANES)].astype(float32), tile, w_o[:, pl.ds(at, LANES)].astype(float32)],
            axis=1,
        )
        pieces = [piece[: rows // 2], piece[rows // 2 :]] if parts == 2 else [padded(piece, high)]
        width = piece.shape[1]
        for part, values in enumerate(pieces):
            out[:, part * width : (part + 1) * width] = values.astype(bfloat16)
        free = out.shape[1] - parts * width
        ids = lane_ids((high, free))
        marks = jnp.zeros((high, free), float32)
        for slot in range(lengths_ref.shape[1]):
            marks = jnp.where(ids == free - LANES + slot, lengths_ref[0, slot].astype(float32), marks)
        out[:, parts * width :] = marks.astype(bfloat16)


def pack_ffn_kernel(where_ref, w_g, w_u, w_d, *outs):
    rows = w_g.shape[0]
    big = w_g.shape[1] // LANES // PLANE * LANES
    last = w_g.shape[1] // LANES // PLANE * PLANE
    place = where_ref[0]
    lane = lane_ids((rows, LANES))
    for mask, out in enumerate(outs):
        other = place ^ mask
        at = pl.ds(pl.multiple_of(other * big, LANES), big)
        parts = [w[:, at].astype(float32) for w in (w_g, w_u, w_d)]
        parts.append(
            jnp.where(
                lane < HALF, half_tile(w_g, last, other, False), half_tile(w_u, last, other, True)
            )
        )
        parts.append(jnp.where(lane < HALF, half_tile(w_d, last, other, False), 0.0))
        out[...] = padded(jnp.concatenate(parts, axis=1), out.shape[0]).astype(bfloat16)


def unpack_attn_kernel(where_ref, own, one, two, three, attn_out, lens_out, held):
    rows = attn_out.shape[0] // PLANE
    width = attn_out.shape[1]
    parts, _ = attn_rows(rows)
    place = where_ref[0]
    for mask, message in enumerate((own, one, two, three)):
        at = pl.ds(pl.multiple_of((place ^ mask) * rows, rows), rows)
        values = [
            message[:, part * width : (part + 1) * width].astype(float32) for part in range(parts)
        ]
        held[at, :] = jnp.concatenate(values, axis=0) if parts == 2 else values[0][:rows]
        lens = message[:16, message.shape[1] - LANES :].astype(float32)
        lens_out[mask * 8 : (mask + 1) * 8, :] = lens[:8]
    attn_out[...] = held[...].astype(bfloat16)


def unpack_ffn_kernel(where_ref, own, one, two, three, ffn_out, held):
    rows = ffn_out.shape[0] // PLANE
    place = where_ref[0]
    for mask, message in enumerate((own, one, two, three)):
        at = pl.ds(pl.multiple_of((place ^ mask) * rows, rows), rows)
        held[at, :] = message[...].astype(float32)[:rows]
    ffn_out[...] = held[...].astype(bfloat16)


def head_mean(values):
    low = lane_ids(values.shape) < HALF
    first = jnp.sum(jnp.where(low, values, 0.0), axis=1, keepdims=True)
    second = jnp.sum(jnp.where(low, 0.0, values), axis=1, keepdims=True)
    return jnp.where(low, first, second) * (1.0 / HALF)


def turn_halves(values):
    first = lane_ids(values.shape) % HALF < HALF // 2
    return jnp.where(
        first, pltpu.roll(values, LANES - HALF // 2, 1), pltpu.roll(values, HALF // 2, 1)
    )


def at_head(values, head):
    low = lane_ids(values.shape) < HALF
    if head == 0:
        return jnp.where(low, values, 0.0).astype(bfloat16)
    return jnp.where(low, 0.0, pltpu.roll(values, HALF, 1)).astype(bfloat16)


def group_probs(query, key, begin, row_ids, col_ids):
    scores = matmul_nt(query, key) * HEAD_DIM ** (-0.5)
    scores = jnp.where((col_ids >= begin) & (col_ids <= row_ids), scores, masked_score)
    expd = jnp.exp(scores - jnp.max(scores, axis=1, keepdims=True))
    return expd / jnp.sum(expd, axis=1, keepdims=True)


def group_mask(ends_ref, group, rows):
    row_ids = lax.broadcasted_iota(jnp.int32, (rows, rows), 0)
    col_ids = lax.broadcasted_iota(jnp.int32, (rows, rows), 1)
    begin = jnp.zeros((rows, rows), jnp.int32)
    for slot in range(ends_ref.shape[1]):
        end = ends_ref[group, slot]
        begin = jnp.maximum(begin, jnp.where(row_ids >= end, end, 0))
    return begin, row_ids, col_ids


def group_rows(core, mine, other):
    first = jnp.where(core == 0, mine, other)
    second = jnp.where(core == 0, other, mine)
    return jnp.concatenate([first, second], axis=0)


def deep_rows(depth, step, layers, rows):
    at = lax.rem(depth + step + layers, layers) * rows
    return pl.ds(pl.multiple_of(at, rows), rows)


def attn_kernel(layers, where_ref, ends_ref, tok_m, tok_o, a_gain, q_gain, k_gain, cos, sin, *refs):
    pieces, refs = refs[:layers], refs[layers:]
    send, keep, pre_out, low_out, mixed_out, weight, held = refs
    group = pl.program_id(0)
    depth, core = where_ref[1], where_ref[2]
    local = tok_m.shape[0]

    @pl.when(group == 0)
    def _():
        for step, piece in enumerate(pieces):
            weight[deep_rows(depth, -step, layers, piece.shape[0]), :] = piece[...]

    x = group_rows(core, tok_m[...].astype(float32), tok_o[...].astype(float32))
    normed = (x * inverse_rms(x) * a_gain[...]).astype(bfloat16)
    pre = matmul(normed, weight[:, : 2 * LANES])
    pre_out[...] = pre
    cosine, sine = cos[...], sin[...]
    tiles = []
    for number, gain in enumerate((q_gain[...], k_gain[...])):
        tile = pre[:, number * LANES : (number + 1) * LANES]
        scaled = tile * lax.rsqrt(head_mean(tile * tile) + epsilon) * gain
        tiles.append(scaled * cosine + turn_halves(scaled) * sine)
    lane = lane_ids(tiles[0].shape)
    query = tiles[0].astype(bfloat16)
    key_value = jnp.where(lane < HALF, tiles[1], pre[:, LANES:])
    low_out[:, :LANES] = query
    low_out[:, LANES:] = key_value.astype(bfloat16)
    begin, row_ids, col_ids = group_mask(ends_ref, group, x.shape[0])
    turned = pltpu.roll(key_value, HALF, 1)
    mixed = jnp.zeros(tiles[0].shape, float32)
    for head in range(2):
        probs = group_probs(query, at_head(key_value, head), begin, row_ids, col_ids)
        mixed += matmul(probs.astype(bfloat16), at_head(turned, head))
    mixed = mixed.astype(bfloat16)
    mixed_out[...] = mixed
    held[...] = matmul_nt(mixed, weight[:, 2 * LANES :])
    mine = pl.multiple_of(core * local, local)
    other = pl.multiple_of((1 - core) * local, local)
    send[...] = held[pl.ds(other, local), :].astype(bfloat16)
    keep[...] = held[pl.ds(mine, local), :]


def attn_back_kernel(
    layers, where_ref, ends_ref, tok_m, tok_o, a_gain, q_gain, k_gain, cos, sin, dh_m, dh_o,
    pre_ref, low_ref, mixed_ref, weight, gain_ffn, *refs,
):
    send, keep, own, gains_out = refs[:4]
    pieces = refs[4 : 3 + layers]
    held, total, sum_a, sum_qk = refs[3 + layers :]
    group = pl.program_id(0)
    depth, core = where_ref[1], where_ref[2]
    local = tok_m.shape[0]

    @pl.when(group == 0)
    def _():
        total[...] = jnp.zeros_like(total)
        sum_a[...] = jnp.zeros_like(sum_a)
        sum_qk[...] = jnp.zeros_like(sum_qk)

    x = group_rows(core, tok_m[...].astype(float32), tok_o[...].astype(float32))
    unit_a = x * inverse_rms(x)
    normed = (unit_a * a_gain[...]).astype(bfloat16)
    d_hidden = group_rows(core, dh_m[...], dh_o[...])
    mixed = mixed_ref[...]
    total[:, 2 * LANES :] += matmul_tn(d_hidden, mixed)
    d_mixed = matmul(d_hidden, weight[:, 2 * LANES :]).astype(bfloat16)
    query = low_ref[:, :LANES]
    key_value = low_ref[:, LANES:].astype(float32)
    turned = pltpu.roll(key_value, HALF, 1)
    begin, row_ids, col_ids = group_mask(ends_ref, group, x.shape[0])
    scale = HEAD_DIM ** (-0.5)
    shape = mixed.shape
    d_query = jnp.zeros(shape, float32)
    d_keys, d_values = [], []
    for head in range(2):
        key = at_head(key_value, head)
        probs = group_probs(query, key, begin, row_ids, col_ids)
        d_values.append(matmul_tn(probs.astype(bfloat16), d_mixed))
        d_probs = matmul_nt(d_mixed, at_head(turned, head))
        centre = jnp.sum(probs * d_probs, axis=1, keepdims=True)
        d_scores = (probs * (d_probs - centre)).astype(bfloat16)
        d_query += matmul(d_scores, key)
        d_keys.append(matmul_tn(d_scores, query))
    d_key = d_keys[0] + pltpu.roll(d_keys[1], HALF, 1)
    d_value = pltpu.roll(d_values[0], HALF, 1) + d_values[1]
    lane = lane_ids(shape)
    cosine, sine = cos[...], sin[...]
    tiles = []
    for number, (grad, gain) in enumerate(((d_query, q_gain[...]), (d_key, k_gain[...]))):
        grad = grad * scale
        back = grad * cosine - turn_halves(grad) * sine
        tile = pre_ref[:, number * LANES : (number + 1) * LANES]
        factor = lax.rsqrt(head_mean(tile * tile) + epsilon)
        unit = tile * factor
        sum_qk[number : number + 1, :] += jnp.sum(back * unit, axis=0, keepdims=True)
        back = back * gain
        tiles.append(factor * (back - unit * head_mean(back * unit)))
    tiles[1] = jnp.where(lane < HALF, tiles[1], d_value)
    d_qkv = jnp.concatenate(tiles, axis=1).astype(bfloat16)
    total[:, : 2 * LANES] += matmul_tn(normed, d_qkv)
    held[...] = matmul_nt(d_qkv, weight[:, : 2 * LANES])
    sum_a[...] += jnp.sum(held[...] * unit_a, axis=0, keepdims=True)
    mine = pl.multiple_of(core * local, local)
    other = pl.multiple_of((1 - core) * local, local)
    send[...] = held[pl.ds(other, local), :].astype(bfloat16)
    keep[...] = held[pl.ds(mine, local), :]

    @pl.when(group == pl.num_programs(0) - 1)
    def _():
        for row in range(GAIN_ROWS):
            gains_out[row : row + 1, :LANES] = sum_a[:, row * LANES : (row + 1) * LANES]
            gains_out[row : row + 1, LANES : 2 * LANES] = gain_ffn[:, row * LANES : (row + 1) * LANES]
        q_sum = sum_qk[0:1, :] + pltpu.roll(sum_qk[0:1, :], HALF, 1)
        k_sum = pltpu.roll(sum_qk[1:2, :], HALF, 1)
        qk_sum = jnp.where(lane_ids(q_sum.shape) < HALF, q_sum, k_sum)
        ids = lax.broadcasted_iota(jnp.int32, (GAIN_ROWS, LANES), 0)
        gains_out[:, 2 * LANES :] = jnp.where(ids == 0, qk_sum, 0.0)
        gains = gains_out[...]
        top = gains.astype(bfloat16)
        rest = (gains - top.astype(float32)).astype(bfloat16)
        tail = jnp.concatenate([top.astype(float32), rest.astype(float32)], axis=0).astype(bfloat16)
        rows = own.shape[0]
        own[...] = total[deep_rows(depth, 0, layers, rows), :]
        for index, piece in enumerate(pieces):
            piece[:rows, :] = total[deep_rows(depth, index + 1, layers, rows), :].astype(bfloat16)
            piece[rows:, :] = tail


def attn_specs(rows, width, group_height):
    scalar = pl.BlockSpec(memory_space=pltpu.SMEM)
    block = pl.BlockSpec((rows, width), lambda i: (i, 0))
    gain = pl.BlockSpec((1, width), lambda i: (0, 0))
    small = pl.BlockSpec((1, LANES), lambda i: (0, 0))
    table = pl.BlockSpec((group_height, LANES), lambda i: (i, 0))
    wide = pl.BlockSpec((group_height, 2 * LANES), lambda i: (i, 0))
    return scalar, block, gain, small, table, wide


def whole_spec(shape):
    return pl.BlockSpec(shape, lambda i: (0, 0), pipeline_mode=pl.Buffered(1))


def attn(where, ends, tok_mine, tok_other, gains, tables, pieces):
    layers = len(pieces)
    rows, width = tok_mine.shape
    local = rows // PLANE
    scalar, block, gain, small, table, wide = attn_specs(local, width, 2 * local)
    high, columns = pieces[0].shape
    weight = (layers * high, columns)
    return pl.pallas_call(
        lambda *refs: attn_kernel(layers, *refs),
        grid=(PLANE,),
        in_specs=[scalar, scalar, block, block, gain, small, small, table, table]
        + [whole_spec((high, columns))] * layers,
        out_specs=[block, block, wide, wide, table, whole_spec(weight)],
        out_shape=[
            jax.ShapeDtypeStruct((rows, width), bfloat16),
            jax.ShapeDtypeStruct((rows, width), float32),
            jax.ShapeDtypeStruct((2 * rows, 2 * LANES), float32),
            jax.ShapeDtypeStruct((2 * rows, 2 * LANES), bfloat16),
            jax.ShapeDtypeStruct((2 * rows, LANES), bfloat16),
            jax.ShapeDtypeStruct(weight, bfloat16),
        ],
        scratch_shapes=[pltpu.VMEM((2 * local, width), float32)],
        compiler_params=pltpu.CompilerParams(vmem_limit_bytes=VMEM_BYTES),
        cost_estimate=cost(36),
    )(where, ends, tok_mine, tok_other, *gains, *tables, *pieces)


def attn_back(where, ends, layers, tok_mine, tok_other, gains, tables, dh, saved, weight, gain_ffn):
    rows, width = tok_mine.shape
    local = rows // PLANE
    scalar, block, gain, small, table, wide = attn_specs(local, width, 2 * local)
    high, columns = weight.shape[0] // layers, weight.shape[1]
    tail = 2 * GAIN_ROWS
    return pl.pallas_call(
        lambda *refs: attn_back_kernel(layers, *refs),
        grid=(PLANE,),
        in_specs=[scalar, scalar, block, block, gain, small, small, table, table, block, block]
        + [wide, wide, table, whole_spec(weight.shape), gain],
        out_specs=[block, block, whole_spec((high, columns)), whole_spec((GAIN_ROWS, columns))]
        + [whole_spec((high + tail, columns))] * (layers - 1),
        out_shape=[
            jax.ShapeDtypeStruct((rows, width), bfloat16),
            jax.ShapeDtypeStruct((rows, width), float32),
            jax.ShapeDtypeStruct((high, columns), float32),
            jax.ShapeDtypeStruct((GAIN_ROWS, columns), float32),
        ]
        + [jax.ShapeDtypeStruct((high + tail, columns), bfloat16)] * (layers - 1),
        scratch_shapes=[
            pltpu.VMEM((2 * local, width), float32),
            pltpu.VMEM(weight.shape, float32),
            pltpu.VMEM((1, width), float32),
            pltpu.VMEM((8, LANES), float32),
        ],
        compiler_params=pltpu.CompilerParams(vmem_limit_bytes=VMEM_BYTES),
        cost_estimate=cost(24),
    )(where, ends, tok_mine, tok_other, *gains, *tables, *dh, *saved, weight, gain_ffn)


def ffn_kernel(where_ref, ends_ref, x_o, x_m, g_o, g_m, weight, *refs):
    out_send, out_keep, dn_send, dn_keep, grad_out, total = refs
    step = pl.program_id(0)
    core = where_ref[2]
    both = x_o.shape[1]
    big = both // 2
    local = x_o.shape[0] // 2

    @pl.when(step == 0)
    def _():
        total[...] = jnp.zeros_like(total)

    def live_rows(values, group, at_core):
        ids = lax.broadcasted_iota(jnp.int32, values.shape, 0) + at_core * local
        return jnp.where(ids < ends_ref[group, ends_ref.shape[1] - 1], values, jnp.zeros_like(values))

    x = jnp.concatenate([x_o[...], x_m[...]], axis=0)
    grads = jnp.concatenate(
        [live_rows(g_o[k * local : (k + 1) * local, :], 2 * step + k, 1 - core) for k in range(2)]
        + [live_rows(g_m[k * local : (k + 1) * local, :], 2 * step + k, core) for k in range(2)],
        axis=0,
    )
    half = 2 * local
    w_both = weight[:, :both]
    w_down = weight[:, both : both + big]
    w_small = weight[:, both + big : both + big + LANES]
    w_small_down = weight[:, both + big + LANES :]
    lane = lane_ids((x.shape[0], LANES))

    def parts_of(gate, up, d_act):
        sigma = 1.0 / (1.0 + jnp.exp(-gate))
        silu = gate * sigma
        act = silu * up
        d_gate = d_act * up * sigma * (1.0 + gate * (1.0 - sigma))
        return act, d_gate, d_act * silu

    pre = matmul(x, w_both)
    act, d_gate, d_up = parts_of(pre[:, :big], pre[:, big:], matmul(grads, w_down))
    pre = matmul(x, w_small)
    act_s, d_gate_s, d_up_s = parts_of(
        pre, pltpu.roll(pre, HALF, 1), matmul(grads, w_small_down)
    )
    act_s = jnp.where(lane < HALF, act_s, 0.0).astype(bfloat16)
    d_small = jnp.where(lane < HALF, d_gate_s, pltpu.roll(d_up_s, HALF, 1)).astype(bfloat16)
    act = act.astype(bfloat16)
    d_both = jnp.concatenate([d_gate, d_up], axis=1).astype(bfloat16)

    partial = matmul_nt(act, w_down) + matmul_nt(act_s, w_small_down)
    out_send[...] = partial[:half].astype(bfloat16)
    out_keep[...] = partial[half:]
    partial = matmul_nt(d_both, w_both) + matmul_nt(d_small, w_small)
    dn_send[...] = partial[:half].astype(bfloat16)
    dn_keep[...] = partial[half:]
    total[:, :both] += matmul_tn(x, d_both)
    total[:, both : both + big] += matmul_tn(grads, act)
    total[:, both + big : both + big + LANES] += matmul_tn(x, d_small)
    total[:, both + big + LANES :] += matmul_tn(grads, act_s)

    @pl.when(step == pl.num_programs(0) - 1)
    def _():
        grad_out[...] = total[...].astype(bfloat16)


def ffn(where, ends, x_mine, x_other, g_mine, g_other, weight):
    rows, width = x_mine.shape
    row_spec = pl.BlockSpec((rows // 2, width), lambda i: (i, 0))
    scalar = pl.BlockSpec(memory_space=pltpu.SMEM)
    return pl.pallas_call(
        ffn_kernel,
        grid=(2,),
        in_specs=[scalar, scalar] + [row_spec] * 4 + [whole_spec(weight.shape)],
        out_specs=[row_spec] * 4 + [whole_spec(weight.shape)],
        out_shape=[
            jax.ShapeDtypeStruct((rows, width), bfloat16),
            jax.ShapeDtypeStruct((rows, width), float32),
            jax.ShapeDtypeStruct((rows, width), bfloat16),
            jax.ShapeDtypeStruct((rows, width), float32),
            jax.ShapeDtypeStruct(weight.shape, bfloat16),
        ],
        scratch_shapes=[pltpu.VMEM(weight.shape, float32)],
        compiler_params=pltpu.CompilerParams(vmem_limit_bytes=VMEM_BYTES),
        cost_estimate=cost(74),
    )(where, ends, x_other, x_mine, g_other, g_mine, weight)


def chip_sum_kernel(keep, received, *outs):
    rows = outs[0].shape[0]
    for mask, out in enumerate(outs):
        span = slice(mask * rows, (mask + 1) * rows)
        out[...] = (keep[span, :] + received[span, :].astype(float32)).astype(out.dtype)


def chip_sum(keep, received):
    shape = (keep.shape[0] // PLANE, keep.shape[1])
    outs = [(shape, float32)] + [(shape, bfloat16)] * (PLANE - 1)
    return call(chip_sum_kernel, outs, keep, received)


def plane_sent(parts):
    return [parts[0]] + [send_plane(part, mask + 1) for mask, part in enumerate(parts[1:])]


def plane_total(parts):
    return add_up(plane_sent(parts))


def add_up(parts):
    return sum(part.astype(float32) for part in parts)


def tail_kernel(where_ref, keep, received, own_ff, own, ff_out, *refs):
    messages, held = refs[:-1], refs[-1]
    held[...] = own_ff[...].astype(float32)
    place = where_ref[0]
    local = own.shape[0]
    rows = ff_out.shape[0]
    tall = (messages[0].shape[0] - local) // 2
    width = own.shape[1]
    for mask in range(PLANE):
        span = slice(mask * local, (mask + 1) * local)
        value = keep[span, :] + received[span, :].astype(float32)
        grads = held[pl.ds(pl.multiple_of((place ^ mask) * rows, rows), rows), :]
        if mask == 0:
            own[...] = value
            ff_out[...] = grads
            continue
        out = messages[mask - 1]
        out[:local, :] = value.astype(bfloat16)
        out[local : local + tall, :] = padded(grads[:, :width], tall).astype(bfloat16)
        rest = grads.shape[1] - width
        out[local + tall :, :rest] = padded(grads[:, width:], tall).astype(bfloat16)
        out[local + tall :, rest:] = jnp.zeros((tall, width - rest), bfloat16)


def tail_messages(where, keep, received, own_ff):
    local, width = keep.shape[0] // PLANE, keep.shape[1]
    rows, columns = own_ff.shape[0] // PLANE, own_ff.shape[1]
    message = (local + 2 * max(rows, 16), width)
    return call(
        tail_kernel,
        [((local, width), float32), ((rows, columns), float32)]
        + [(message, bfloat16)] * (PLANE - 1),
        where,
        keep,
        received,
        own_ff,
        scalars=1,
        scratch=[pltpu.VMEM(own_ff.shape, float32)],
    )


def joined_gains(tail):
    return tail[:GAIN_ROWS] + tail[GAIN_ROWS:]


def split_gains(gains):
    top = gains.astype(bfloat16).astype(float32)
    rest = (gains - top).astype(bfloat16).astype(float32)
    return jnp.concatenate([top, rest], axis=0)


def plane_sum_attn_kernel(where_ref, own, gains, *refs):
    received, outs = refs[: -PLANE - 2], refs[-PLANE - 2 : -2]
    held, held_gains = refs[-2:]
    layers = len(received) + 1
    value = own[...]
    high = own.shape[0]
    depth = where_ref[1]
    held_gains[deep_rows(depth, 0, layers, GAIN_ROWS), :] = joined_gains(split_gains(gains[...]))
    for step, part in enumerate(received):
        value = value + part[:high, :].astype(float32)
        held_gains[deep_rows(depth, -1 - step, layers, GAIN_ROWS), :] = joined_gains(
            part[high:, :].astype(float32)
        )
    held[...] = value
    sums = held_gains[:GAIN_ROWS, :]
    for layer in range(1, layers):
        sums = sums + held_gains[layer * GAIN_ROWS : (layer + 1) * GAIN_ROWS, :]
    tail = split_gains(sums)
    place = where_ref[0]
    rows = high // PLANE
    for mask, out in enumerate(outs):
        at = pl.multiple_of((place ^ mask) * rows, rows)
        part = held[pl.ds(at, rows), :]
        if mask:
            tall = out.shape[0] - tail.shape[0]
            out[:tall, :] = padded(part, tall).astype(bfloat16)
            out[tall:, :] = tail.astype(bfloat16)
        else:
            out[:rows, :] = part
            out[rows:, :] = tail


def plane_split_attn(where, own, received, gains):
    rows, columns = own.shape[0] // PLANE, own.shape[1]
    tail = 2 * GAIN_ROWS
    shapes = [((rows + tail, columns), float32)]
    shapes += [((max(rows, 16) + tail, columns), bfloat16)] * (PLANE - 1)
    scratch = [
        pltpu.VMEM(own.shape, float32),
        pltpu.VMEM(((len(received) + 1) * GAIN_ROWS, columns), float32),
    ]
    return call(
        plane_sum_attn_kernel, shapes, where, own, gains, *received, scalars=1, scratch=scratch
    )


def pick_place(refs, place, target, columns, rows):
    value = jnp.zeros((rows, columns.stop - columns.start), float32)
    for mask, ref in enumerate(refs):
        value = jnp.where(place ^ mask == target, ref[:, columns].astype(float32)[:rows], value)
    return value


def place_ffn_kernel(where_ref, own, one, two, three, out_g, out_u, out_d, held):
    place = where_ref[0]
    rows = out_g.shape[0]
    big = out_g.shape[1] // LANES // PLANE * LANES
    last = PLANE * big
    width = one.shape[1]
    tall = max(rows, 16)
    start = one.shape[0] - 2 * tall
    for mask, ref in enumerate((own, one, two, three)):
        if mask:
            top = ref[start : start + tall, :].astype(float32)[:rows]
            rest = ref[start + tall :, : held.shape[2] - width].astype(float32)[:rows]
            held[mask, :, :width] = top
            held[mask, :, width:] = rest
        else:
            held[mask] = ref[...]
        at = pl.ds(pl.multiple_of((place ^ mask) * big, LANES), big)
        for number, out in enumerate((out_g, out_u, out_d)):
            out[:, at] = held[mask, :, number * big : (number + 1) * big]
    for pair in range(PLANE // 2):
        low = held[place ^ (2 * pair), :, 3 * big :]
        high = held[place ^ (2 * pair + 1), :, 3 * big :]
        lane = lane_ids((rows, LANES))
        span = slice(last + pair * LANES, last + (pair + 1) * LANES)
        gu_low, gu_high = low[:, :LANES], high[:, :LANES]
        out_g[:, span] = jnp.where(lane < HALF, gu_low, pltpu.roll(gu_high, HALF, 1))
        out_u[:, span] = jnp.where(lane < HALF, pltpu.roll(gu_low, HALF, 1), gu_high)
        out_d[:, span] = jnp.where(lane < HALF, low[:, LANES:], pltpu.roll(high[:, LANES:], HALF, 1))


def place_attn_kernel(where_ref, own, one, two, three, out_q, out_k, out_v, out_o, out_gains):
    place = where_ref[0]
    refs = (own, one, two, three)
    rows = out_q.shape[0]
    for mask, ref in enumerate(refs):
        at = pl.ds(pl.multiple_of((place ^ mask) * LANES, LANES), LANES)
        out_q[:, at] = ref[:, :LANES].astype(float32)[:rows]
        out_o[:, at] = ref[:, 2 * LANES :].astype(float32)[:rows]
    for pair in range(PLANE // 2):
        low = pick_place(refs, place, 2 * pair, slice(LANES, 2 * LANES), rows)
        high = pick_place(refs, place, 2 * pair + 1, slice(LANES, 2 * LANES), rows)
        lane = lane_ids(low.shape)
        span = slice(pair * LANES, (pair + 1) * LANES)
        out_k[:, span] = jnp.where(lane < HALF, low, pltpu.roll(high, HALF, 1))
        out_v[:, span] = jnp.where(lane < HALF, pltpu.roll(low, HALF, 1), high)
    tails = [joined_gains(ref[ref.shape[0] - 2 * GAIN_ROWS :, :].astype(float32)) for ref in refs]
    out_gains[...] = (tails[0] + tails[1]) + (tails[2] + tails[3])


def plane_parts(local):
    return [local] + [send_plane(local, mask) for mask in range(1, PLANE)]


def both_cores(parts):
    mine = jnp.concatenate(parts)
    return mine, swap_cores(mine)


def gather_rows(local):
    return both_cores(plane_parts(local))


def row_tables(lens, slots, total_rows):
    all_lengths = lens.reshape(PLANE, 8, LANES)[:, 0, :slots].astype(jnp.int32)
    ends = jnp.cumsum(all_lengths, axis=1, dtype=jnp.int32)
    row_ids = jnp.arange(total_rows, dtype=jnp.int32)
    begin = jnp.max(
        jnp.where(row_ids[None, :, None] >= ends[:, None, :], ends[:, None, :], 0), axis=2
    )
    position = (row_ids[None, :] - begin).reshape(-1).astype(jnp.float32)
    spread = jnp.arange(LANES, dtype=jnp.int32) % (HEAD_DIM // 2)
    freqs = rope_base ** (-spread.astype(jnp.float32) * 2.0 / HEAD_DIM)
    angles = position[:, None] * freqs[None, :]
    sign = jnp.where(jnp.arange(LANES) % HEAD_DIM < HEAD_DIM // 2, -1.0, 1.0).astype(jnp.float32)
    return ends, (jnp.cos(angles), jnp.sin(angles) * sign)


def body(
    tokens,
    lengths,
    attn_gain,
    query_gain,
    key_gain,
    ffn_gain,
    w_query,
    w_key,
    w_value,
    w_out,
    w_gate,
    w_up,
    w_down,
    cotangent,
):
    dp = lax.axis_index("dp")
    core = lax.axis_index("tensor")
    layers = lax.axis_size("dp") // PLANE
    where = jnp.stack([dp % PLANE, dp // PLANE, core]).astype(jnp.int32)
    local_rows, model = tokens.shape
    total_rows = local_rows * lax.axis_size("tensor")
    rows = w_query.shape[0]
    q_cols = w_query.shape[1] // PLANE
    kv_cols = w_key.shape[1] // PLANE
    local_kv = kv_cols // HEAD_DIM
    share = q_cols // kv_cols
    attn_cols = 2 * q_cols + 2 * kv_cols
    ff_cols = 3 * (w_gate.shape[1] // LANES // PLANE * LANES) + 2 * LANES

    parts, high = attn_rows(rows)
    tall = max(rows, 16)
    first = call(
        pack_attn_kernel,
        [((high, model), bfloat16)] * PLANE,
        where,
        lengths,
        w_query,
        w_key,
        w_value,
        w_out,
        scalars=2,
    )
    second = call(
        pack_ffn_kernel,
        [((tall, ff_cols), bfloat16)] * PLANE,
        where,
        w_gate,
        w_up,
        w_down,
        scalars=1,
    )
    first = [first[0]] + [send_plane(first[m], m) for m in range(1, PLANE)]
    attn_piece, lens = call(
        unpack_attn_kernel,
        [((PLANE * rows, attn_cols), bfloat16), ((PLANE * 8, LANES), float32)],
        where,
        *first,
        scalars=1,
        scratch=[pltpu.VMEM((PLANE * rows, attn_cols), float32)],
    )
    attn_pieces = [attn_piece] + [send_deep(attn_piece, step) for step in range(1, layers)]
    tok_parts = plane_parts(tokens)
    second = after((first, tok_parts), second)
    second = [second[0]] + [send_plane(second[m], m) for m in range(1, PLANE)]
    ends, tables = row_tables(lens, lengths.shape[1], total_rows)
    second = after((attn_pieces, tables), second)
    (ff_piece,) = call(
        unpack_ffn_kernel,
        [((PLANE * rows, ff_cols), bfloat16)],
        where,
        *second,
        scalars=1,
        scratch=[pltpu.VMEM((PLANE * rows, ff_cols), float32)],
    )
    columns = [list(range(k, layers * PLANE, PLANE)) for k in range(PLANE)]
    ff_weight = lax.all_gather(ff_piece, "dp", axis=0, tiled=True, axis_index_groups=columns)
    attn_pieces = after(ff_piece, attn_pieces)
    cot_parts = plane_parts(after(second, cotangent))
    tok_mine, tok_other = both_cores(tok_parts)
    cot_mine, cot_other = both_cores(cot_parts)

    gains = (
        attn_gain[None, :],
        jnp.concatenate([query_gain, query_gain])[None, :],
        jnp.concatenate([key_gain, key_gain])[None, :],
    )

    inputs = tokens.astype(jnp.float32)
    factor_a = inverse_rms(inputs)
    unit_a = inputs * factor_a
    send, keep, *saved, attn_weight = attn(
        where, ends, tok_mine, tok_other, gains, tables, attn_pieces
    )
    send = after(cot_parts, send)
    hidden = inputs + plane_total(chip_sum(keep, swap_cores(send)))
    factor_b = inverse_rms(hidden)
    unit_b = hidden * factor_b
    x_mine, x_other = gather_rows((unit_b * ffn_gain).astype(jnp.bfloat16))

    out_send, out_keep, dn_send, dn_keep, ff_grad = ffn(
        where, ends, x_mine, x_other, cot_mine, cot_other, ff_weight
    )
    own_ff = lax.psum_scatter(
        ff_grad, "dp", scatter_dimension=0, tiled=True, axis_index_groups=columns
    )
    dn_parts = chip_sum(dn_keep, swap_cores(dn_send))
    out_keep = after(dn_parts, out_keep)
    d_normed2 = plane_total(dn_parts)
    grad_out = jnp.where(
        (jnp.arange(local_rows) + core * local_rows < ends[0, lengths.shape[1] - 1])[:, None],
        cotangent,
        jnp.zeros_like(cotangent),
    )
    gain_ffn = jnp.sum(d_normed2 * unit_b, axis=0)
    d_hidden = grad_out.astype(jnp.float32) + norm_back(d_normed2 * ffn_gain, unit_b, factor_b)
    h_mine, h_other = gather_rows(d_hidden.astype(jnp.bfloat16))
    out_parts = chip_sum(out_keep, swap_cores(out_send))
    out_parts = after((h_mine, h_other), out_parts)
    out_parts = plane_sent(out_parts)
    block_out = (hidden + add_up(out_parts)).astype(jnp.bfloat16)

    send, keep, own_attn, part_gains, *attn_grads = after(
        out_parts,
        attn_back(
            where, ends, layers, tok_mine, tok_other, gains, tables, (h_mine, h_other), saved,
            attn_weight, gain_ffn[None, :],
        ),
    )
    attn_grads = [send_deep(piece, step + 1) for step, piece in enumerate(attn_grads)]
    own_dn, own_ff, *messages = tail_messages(where, keep, swap_cores(send), own_ff)
    own_attn = after(messages, own_attn)
    messages = [send_plane(part, mask + 1) for mask, part in enumerate(messages)]
    attn_parts = plane_split_attn(where, own_attn, attn_grads, part_gains)
    attn_parts = after(messages[:2], plane_sent(attn_parts))
    d_normed = own_dn + add_up([part[:local_rows] for part in messages])
    grad_tokens = d_hidden + norm_back(d_normed * attn_gain, unit_a, factor_a)
    grad_gate, grad_up, grad_down = call(
        place_ffn_kernel,
        [(w_gate.shape, float32)] * 3,
        where,
        own_ff,
        *messages,
        scalars=1,
        scratch=[pltpu.VMEM((PLANE, rows, ff_cols), float32)],
    )
    grad_query, grad_key, grad_value, grad_out_w, sums = call(
        place_attn_kernel,
        [(w.shape, float32) for w in (w_query, w_key, w_value, w_out)]
        + [((GAIN_ROWS, attn_cols), float32)],
        where,
        *attn_parts,
        scalars=1,
    )
    sums = sums + swap_cores(sums)
    return (
        block_out,
        grad_tokens,
        sums[:, :LANES].reshape(-1),
        sums[0, 2 * LANES : 2 * LANES + HEAD_DIM],
        sums[0, 2 * LANES + HEAD_DIM :],
        sums[:, LANES : 2 * LANES].reshape(-1),
        grad_query,
        grad_key,
        grad_value,
        grad_out_w,
        grad_gate,
        grad_up,
        grad_down,
    )


def solution(mesh):
    placed = (
        P(("dp", "tensor"), None),
        P("dp", None),
        P(),
        P(),
        P(),
        P(),
        P("dp", "tensor"),
        P("dp", "tensor"),
        P("dp", "tensor"),
        P("dp", "tensor"),
        P("dp", "tensor"),
        P("dp", "tensor"),
        P("dp", "tensor"),
        P(("dp", "tensor"), None),
    )
    return jax.shard_map(
        body,
        mesh=mesh,
        in_specs=placed,
        out_specs=(
            P(("dp", "tensor"), None),
            P(("dp", "tensor"), None),
            P(),
            P(),
            P(),
            P(),
            P("dp", "tensor"),
            P("dp", "tensor"),
            P("dp", "tensor"),
            P("dp", "tensor"),
            P("dp", "tensor"),
            P("dp", "tensor"),
            P("dp", "tensor"),
        ),
        check_vma=False,
    )
```

```python
import jax
import jax.numpy as jnp
from jax import lax
from jax.experimental import pallas as pl
from jax.experimental.pallas import tpu as pltpu
from jax.sharding import PartitionSpec as P

HEAD_DIM = 64


epsilon = 1e-05
rope_base = 1000000.0
masked_score = -1e30


def inverse_rms(values):
    return lax.rsqrt(jnp.mean(values * values, axis=-1, keepdims=True) + epsilon)


def norm_back(grad_unit, unit, factor):
    return factor * (grad_unit - unit * jnp.mean(grad_unit * unit, axis=-1, keepdims=True))


def matmul(first_op, second_op):
    return jnp.dot(first_op, second_op, preferred_element_type=jnp.float32)


def matmul_nt(first_op, second_op):
    return lax.dot_general(
        first_op, second_op, (((1,), (1,)), ((), ())), preferred_element_type=jnp.float32
    )


def matmul_tn(first_op, second_op):
    return lax.dot_general(
        first_op, second_op, (((0,), (0,)), ((), ())), preferred_element_type=jnp.float32
    )


def seq_layout(seq_lengths, total_rows):
    ends = jnp.cumsum(seq_lengths, dtype=jnp.int32)
    starts = ends - seq_lengths
    row_ids = jnp.arange(total_rows, dtype=jnp.int32)
    segment = jnp.sum(
        (row_ids[:, None] >= ends[None, :]).astype(jnp.int32), axis=1, dtype=jnp.int32
    )
    slot_ids = jnp.arange(seq_lengths.shape[0], dtype=jnp.int32)
    picked = (segment[:, None] == slot_ids[None, :]).astype(jnp.int32)
    begin = (
        jnp.sum(picked * starts[None, :], axis=1, dtype=jnp.int32)
        + (segment == seq_lengths.shape[0]).astype(jnp.int32) * ends[-1]
    )
    allowed = (segment[:, None] == segment[None, :]) & (row_ids[:, None] >= row_ids[None, :])
    return (row_ids - begin, row_ids < ends[-1], allowed)


def rope_tables(position, head_size):
    half_dim = head_size // 2
    freqs = rope_base ** (-jnp.arange(half_dim, dtype=jnp.float32) * 2.0 / head_size)
    angles = position.astype(jnp.float32)[:, None] * freqs[None, :]
    return (jnp.cos(angles)[:, None, :], jnp.sin(angles)[:, None, :])


def rotate(values, cosine, sine):
    half_dim = values.shape[-1] // 2
    first_half = values[..., :half_dim]
    second_half = values[..., half_dim:]
    return jnp.concatenate(
        [first_half * cosine - second_half * sine, second_half * cosine + first_half * sine],
        axis=-1,
    )


def rotate_back(grads, cosine, sine):
    half_dim = grads.shape[-1] // 2
    first_half = grads[..., :half_dim]
    second_half = grads[..., half_dim:]
    return jnp.concatenate(
        [first_half * cosine + second_half * sine, second_half * cosine - first_half * sine],
        axis=-1,
    )

PLANE = 4
LANES = 128
HALF = 64
VMEM_BYTES = 60 * 1024 * 1024
COST = pl.CostEstimate(flops=1024, bytes_accessed=1024, transcendentals=0)


def cost(megabytes):
    return pl.CostEstimate(flops=1024, bytes_accessed=megabytes * 1000000, transcendentals=0)
GAIN_ROWS = 8
float32 = jnp.float32
bfloat16 = jnp.bfloat16


def send_plane(values, mask):
    count = lax.axis_size("dp")
    return lax.ppermute(values, "dp", [(i, i ^ mask) for i in range(count)])


def send_deep(values, step):
    count = lax.axis_size("dp")
    return lax.ppermute(values, "dp", [(i, (i + PLANE * step) % count) for i in range(count)])


def swap_cores(values):
    return lax.ppermute(values, "tensor", [(0, 1), (1, 0)])


def call(kernel, outs, *operands, scalars=0, scratch=()):
    specs = [pl.BlockSpec(memory_space=pltpu.SMEM)] * scalars
    specs += [pl.BlockSpec(memory_space=pltpu.VMEM)] * (len(operands) - scalars)
    return pl.pallas_call(
        kernel,
        out_shape=[jax.ShapeDtypeStruct(shape, kind) for shape, kind in outs],
        in_specs=specs,
        out_specs=[pl.BlockSpec(memory_space=pltpu.VMEM)] * len(outs),
        scratch_shapes=list(scratch),
        compiler_params=pltpu.CompilerParams(vmem_limit_bytes=VMEM_BYTES),
        cost_estimate=COST,
    )(*operands)


def after(first, second):
    return lax.optimization_barrier((first, second))[1]


def lane_ids(shape):
    return lax.broadcasted_iota(jnp.int32, shape, len(shape) - 1)


def half_tile(ref, first_tile, place, upper):
    start = pl.multiple_of((first_tile + place // 2) * LANES, LANES)
    tile = ref[:, pl.ds(start, LANES)].astype(float32)
    turned = pltpu.roll(tile, HALF, 1)
    odd = place % 2 == 1
    if upper:
        return jnp.where(odd, tile, turned)
    return jnp.where(odd, turned, tile)


def padded(values, rows):
    if values.shape[0] == rows:
        return values
    blank = jnp.zeros((rows - values.shape[0], values.shape[1]), values.dtype)
    return jnp.concatenate([values, blank], axis=0)


def attn_rows(rows):
    return (2, rows // 2) if rows % 32 == 0 else (1, max(rows, 16))


def pack_attn_kernel(where_ref, lengths_ref, w_q, w_k, w_v, w_o, *outs):
    rows = w_q.shape[0]
    parts, high = attn_rows(rows)
    place = where_ref[0]
    lane = lane_ids((rows, LANES))
    for mask, out in enumerate(outs):
        other = place ^ mask
        at = pl.multiple_of(other * LANES, LANES)
        tile = jnp.where(
            lane < HALF, half_tile(w_k, 0, other, False), half_tile(w_v, 0, other, True)
        )
        piece = jnp.concatenate(
            [w_q[:, pl.ds(at, LANES)].astype(float32), tile, w_o[:, pl.ds(at, LANES)].astype(float32)],
            axis=1,
        )
        pieces = [piece[: rows // 2], piece[rows // 2 :]] if parts == 2 else [padded(piece, high)]
        width = piece.shape[1]
        for part, values in enumerate(pieces):
            out[:, part * width : (part + 1) * width] = values.astype(bfloat16)
        free = out.shape[1] - parts * width
        ids = lane_ids((high, free))
        marks = jnp.zeros((high, free), float32)
        for slot in range(lengths_ref.shape[1]):
            marks = jnp.where(ids == free - LANES + slot, lengths_ref[0, slot].astype(float32), marks)
        out[:, parts * width :] = marks.astype(bfloat16)


def pack_ffn_kernel(where_ref, w_g, w_u, w_d, *outs):
    rows = w_g.shape[0]
    big = w_g.shape[1] // LANES // PLANE * LANES
    last = w_g.shape[1] // LANES // PLANE * PLANE
    place = where_ref[0]
    lane = lane_ids((rows, LANES))
    for mask, out in enumerate(outs):
        other = place ^ mask
        at = pl.ds(pl.multiple_of(other * big, LANES), big)
        parts = [w[:, at].astype(float32) for w in (w_g, w_u, w_d)]
        parts.append(
            jnp.where(
                lane < HALF, half_tile(w_g, last, other, False), half_tile(w_u, last, other, True)
            )
        )
        parts.append(jnp.where(lane < HALF, half_tile(w_d, last, other, False), 0.0))
        out[...] = padded(jnp.concatenate(parts, axis=1), out.shape[0]).astype(bfloat16)


def unpack_attn_kernel(where_ref, own, one, two, three, attn_out, lens_out, held):
    rows = attn_out.shape[0] // PLANE
    width = attn_out.shape[1]
    parts, _ = attn_rows(rows)
    place = where_ref[0]
    for mask, message in enumerate((own, one, two, three)):
        at = pl.ds(pl.multiple_of((place ^ mask) * rows, rows), rows)
        values = [
            message[:, part * width : (part + 1) * width].astype(float32) for part in range(parts)
        ]
        held[at, :] = jnp.concatenate(values, axis=0) if parts == 2 else values[0][:rows]
        lens = message[:16, message.shape[1] - LANES :].astype(float32)
        lens_out[mask * 8 : (mask + 1) * 8, :] = lens[:8]
    attn_out[...] = held[...].astype(bfloat16)


def unpack_ffn_kernel(where_ref, own, one, two, three, ffn_out, held):
    rows = ffn_out.shape[0] // PLANE
    place = where_ref[0]
    for mask, message in enumerate((own, one, two, three)):
        at = pl.ds(pl.multiple_of((place ^ mask) * rows, rows), rows)
        held[at, :] = message[...].astype(float32)[:rows]
    ffn_out[...] = held[...].astype(bfloat16)


def head_mean(values):
    low = lane_ids(values.shape) < HALF
    first = jnp.sum(jnp.where(low, values, 0.0), axis=1, keepdims=True)
    second = jnp.sum(jnp.where(low, 0.0, values), axis=1, keepdims=True)
    return jnp.where(low, first, second) * (1.0 / HALF)


def turn_halves(values):
    first = lane_ids(values.shape) % HALF < HALF // 2
    return jnp.where(
        first, pltpu.roll(values, LANES - HALF // 2, 1), pltpu.roll(values, HALF // 2, 1)
    )


def at_head(values, head):
    low = lane_ids(values.shape) < HALF
    if head == 0:
        return jnp.where(low, values, 0.0).astype(bfloat16)
    return jnp.where(low, 0.0, pltpu.roll(values, HALF, 1)).astype(bfloat16)


def group_probs(query, key, begin, row_ids, col_ids):
    scores = matmul_nt(query, key) * HEAD_DIM ** (-0.5)
    scores = jnp.where((col_ids >= begin) & (col_ids <= row_ids), scores, masked_score)
    expd = jnp.exp(scores - jnp.max(scores, axis=1, keepdims=True))
    return expd / jnp.sum(expd, axis=1, keepdims=True)


def group_mask(ends_ref, group, rows):
    row_ids = lax.broadcasted_iota(jnp.int32, (rows, rows), 0)
    col_ids = lax.broadcasted_iota(jnp.int32, (rows, rows), 1)
    begin = jnp.zeros((rows, rows), jnp.int32)
    for slot in range(ends_ref.shape[1]):
        end = ends_ref[group, slot]
        begin = jnp.maximum(begin, jnp.where(row_ids >= end, end, 0))
    return begin, row_ids, col_ids


def group_rows(core, mine, other):
    first = jnp.where(core == 0, mine, other)
    second = jnp.where(core == 0, other, mine)
    return jnp.concatenate([first, second], axis=0)


def deep_rows(depth, step, layers, rows):
    at = lax.rem(depth + step + layers, layers) * rows
    return pl.ds(pl.multiple_of(at, rows), rows)


def attn_kernel(layers, where_ref, ends_ref, tok_m, tok_o, a_gain, q_gain, k_gain, cos, sin, *refs):
    pieces, refs = refs[:layers], refs[layers:]
    send, keep, pre_out, low_out, mixed_out, weight, held = refs
    group = pl.program_id(0)
    depth, core = where_ref[1], where_ref[2]
    local = tok_m.shape[0]

    @pl.when(group == 0)
    def _():
        for step, piece in enumerate(pieces):
            weight[deep_rows(depth, -step, layers, piece.shape[0]), :] = piece[...]

    x = group_rows(core, tok_m[...].astype(float32), tok_o[...].astype(float32))
    normed = (x * inverse_rms(x) * a_gain[...]).astype(bfloat16)
    pre = matmul(normed, weight[:, : 2 * LANES])
    pre_out[...] = pre
    cosine, sine = cos[...], sin[...]
    tiles = []
    for number, gain in enumerate((q_gain[...], k_gain[...])):
        tile = pre[:, number * LANES : (number + 1) * LANES]
        scaled = tile * lax.rsqrt(head_mean(tile * tile) + epsilon) * gain
        tiles.append(scaled * cosine + turn_halves(scaled) * sine)
    lane = lane_ids(tiles[0].shape)
    query = tiles[0].astype(bfloat16)
    key_value = jnp.where(lane < HALF, tiles[1], pre[:, LANES:])
    low_out[:, :LANES] = query
    low_out[:, LANES:] = key_value.astype(bfloat16)
    begin, row_ids, col_ids = group_mask(ends_ref, group, x.shape[0])
    turned = pltpu.roll(key_value, HALF, 1)
    mixed = jnp.zeros(tiles[0].shape, float32)
    for head in range(2):
        probs = group_probs(query, at_head(key_value, head), begin, row_ids, col_ids)
        mixed += matmul(probs.astype(bfloat16), at_head(turned, head))
    mixed = mixed.astype(bfloat16)
    mixed_out[...] = mixed
    held[...] = matmul_nt(mixed, weight[:, 2 * LANES :])
    mine = pl.multiple_of(core * local, local)
    other = pl.multiple_of((1 - core) * local, local)
    send[...] = held[pl.ds(other, local), :].astype(bfloat16)
    keep[...] = held[pl.ds(mine, local), :]


def attn_back_kernel(
    layers, where_ref, ends_ref, tok_m, tok_o, a_gain, q_gain, k_gain, cos, sin, dh_m, dh_o,
    pre_ref, low_ref, mixed_ref, weight, gain_ffn, *refs,
):
    send, keep, own, gains_out = refs[:4]
    pieces = refs[4 : 3 + layers]
    held, total, sum_a, sum_qk = refs[3 + layers :]
    group = pl.program_id(0)
    depth, core = where_ref[1], where_ref[2]
    local = tok_m.shape[0]

    @pl.when(group == 0)
    def _():
        total[...] = jnp.zeros_like(total)
        sum_a[...] = jnp.zeros_like(sum_a)
        sum_qk[...] = jnp.zeros_like(sum_qk)

    x = group_rows(core, tok_m[...].astype(float32), tok_o[...].astype(float32))
    unit_a = x * inverse_rms(x)
    normed = (unit_a * a_gain[...]).astype(bfloat16)
    d_hidden = group_rows(core, dh_m[...], dh_o[...])
    mixed = mixed_ref[...]
    total[:, 2 * LANES :] += matmul_tn(d_hidden, mixed)
    d_mixed = matmul(d_hidden, weight[:, 2 * LANES :]).astype(bfloat16)
    query = low_ref[:, :LANES]
    key_value = low_ref[:, LANES:].astype(float32)
    turned = pltpu.roll(key_value, HALF, 1)
    begin, row_ids, col_ids = group_mask(ends_ref, group, x.shape[0])
    scale = HEAD_DIM ** (-0.5)
    shape = mixed.shape
    d_query = jnp.zeros(shape, float32)
    d_keys, d_values = [], []
    for head in range(2):
        key = at_head(key_value, head)
        probs = group_probs(query, key, begin, row_ids, col_ids)
        d_values.append(matmul_tn(probs.astype(bfloat16), d_mixed))
        d_probs = matmul_nt(d_mixed, at_head(turned, head))
        centre = jnp.sum(probs * d_probs, axis=1, keepdims=True)
        d_scores = (probs * (d_probs - centre)).astype(bfloat16)
        d_query += matmul(d_scores, key)
        d_keys.append(matmul_tn(d_scores, query))
    d_key = d_keys[0] + pltpu.roll(d_keys[1], HALF, 1)
    d_value = pltpu.roll(d_values[0], HALF, 1) + d_values[1]
    lane = lane_ids(shape)
    cosine, sine = cos[...], sin[...]
    tiles = []
    for number, (grad, gain) in enumerate(((d_query, q_gain[...]), (d_key, k_gain[...]))):
        grad = grad * scale
        back = grad * cosine - turn_halves(grad) * sine
        tile = pre_ref[:, number * LANES : (number + 1) * LANES]
        factor = lax.rsqrt(head_mean(tile * tile) + epsilon)
        unit = tile * factor
        sum_qk[number : number + 1, :] += jnp.sum(back * unit, axis=0, keepdims=True)
        back = back * gain
        tiles.append(factor * (back - unit * head_mean(back * unit)))
    tiles[1] = jnp.where(lane < HALF, tiles[1], d_value)
    d_qkv = jnp.concatenate(tiles, axis=1).astype(bfloat16)
    total[:, : 2 * LANES] += matmul_tn(normed, d_qkv)
    held[...] = matmul_nt(d_qkv, weight[:, : 2 * LANES])
    sum_a[...] += jnp.sum(held[...] * unit_a, axis=0, keepdims=True)
    mine = pl.multiple_of(core * local, local)
    other = pl.multiple_of((1 - core) * local, local)
    send[...] = held[pl.ds(other, local), :].astype(bfloat16)
    keep[...] = held[pl.ds(mine, local), :]

    @pl.when(group == pl.num_programs(0) - 1)
    def _():
        for row in range(GAIN_ROWS):
            gains_out[row : row + 1, :LANES] = sum_a[:, row * LANES : (row + 1) * LANES]
            gains_out[row : row + 1, LANES : 2 * LANES] = gain_ffn[:, row * LANES : (row + 1) * LANES]
        q_sum = sum_qk[0:1, :] + pltpu.roll(sum_qk[0:1, :], HALF, 1)
        k_sum = pltpu.roll(sum_qk[1:2, :], HALF, 1)
        qk_sum = jnp.where(lane_ids(q_sum.shape) < HALF, q_sum, k_sum)
        ids = lax.broadcasted_iota(jnp.int32, (GAIN_ROWS, LANES), 0)
        gains_out[:, 2 * LANES :] = jnp.where(ids == 0, qk_sum, 0.0)
        gains = gains_out[...]
        top = gains.astype(bfloat16)
        rest = (gains - top.astype(float32)).astype(bfloat16)
        tail = jnp.concatenate([top.astype(float32), rest.astype(float32)], axis=0).astype(bfloat16)
        rows = own.shape[0]
        own[...] = total[deep_rows(depth, 0, layers, rows), :]
        for index, piece in enumerate(pieces):
            piece[:rows, :] = total[deep_rows(depth, index + 1, layers, rows), :].astype(bfloat16)
            piece[rows:, :] = tail


def attn_specs(rows, width, group_height):
    scalar = pl.BlockSpec(memory_space=pltpu.SMEM)
    block = pl.BlockSpec((rows, width), lambda i: (i, 0))
    gain = pl.BlockSpec((1, width), lambda i: (0, 0))
    small = pl.BlockSpec((1, LANES), lambda i: (0, 0))
    table = pl.BlockSpec((group_height, LANES), lambda i: (i, 0))
    wide = pl.BlockSpec((group_height, 2 * LANES), lambda i: (i, 0))
    return scalar, block, gain, small, table, wide


def whole_spec(shape):
    return pl.BlockSpec(shape, lambda i: (0, 0), pipeline_mode=pl.Buffered(1))


def attn(where, ends, tok_mine, tok_other, gains, tables, pieces):
    layers = len(pieces)
    rows, width = tok_mine.shape
    local = rows // PLANE
    scalar, block, gain, small, table, wide = attn_specs(local, width, 2 * local)
    high, columns = pieces[0].shape
    weight = (layers * high, columns)
    return pl.pallas_call(
        lambda *refs: attn_kernel(layers, *refs),
        grid=(PLANE,),
        in_specs=[scalar, scalar, block, block, gain, small, small, table, table]
        + [whole_spec((high, columns))] * layers,
        out_specs=[block, block, wide, wide, table, whole_spec(weight)],
        out_shape=[
            jax.ShapeDtypeStruct((rows, width), bfloat16),
            jax.ShapeDtypeStruct((rows, width), float32),
            jax.ShapeDtypeStruct((2 * rows, 2 * LANES), float32),
            jax.ShapeDtypeStruct((2 * rows, 2 * LANES), bfloat16),
            jax.ShapeDtypeStruct((2 * rows, LANES), bfloat16),
            jax.ShapeDtypeStruct(weight, bfloat16),
        ],
        scratch_shapes=[pltpu.VMEM((2 * local, width), float32)],
        compiler_params=pltpu.CompilerParams(vmem_limit_bytes=VMEM_BYTES),
        cost_estimate=cost(36),
    )(where, ends, tok_mine, tok_other, *gains, *tables, *pieces)


def attn_back(where, ends, layers, tok_mine, tok_other, gains, tables, dh, saved, weight, gain_ffn):
    rows, width = tok_mine.shape
    local = rows // PLANE
    scalar, block, gain, small, table, wide = attn_specs(local, width, 2 * local)
    high, columns = weight.shape[0] // layers, weight.shape[1]
    tail = 2 * GAIN_ROWS
    return pl.pallas_call(
        lambda *refs: attn_back_kernel(layers, *refs),
        grid=(PLANE,),
        in_specs=[scalar, scalar, block, block, gain, small, small, table, table, block, block]
        + [wide, wide, table, whole_spec(weight.shape), gain],
        out_specs=[block, block, whole_spec((high, columns)), whole_spec((GAIN_ROWS, columns))]
        + [whole_spec((high + tail, columns))] * (layers - 1),
        out_shape=[
            jax.ShapeDtypeStruct((rows, width), bfloat16),
            jax.ShapeDtypeStruct((rows, width), float32),
            jax.ShapeDtypeStruct((high, columns), float32),
            jax.ShapeDtypeStruct((GAIN_ROWS, columns), float32),
        ]
        + [jax.ShapeDtypeStruct((high + tail, columns), bfloat16)] * (layers - 1),
        scratch_shapes=[
            pltpu.VMEM((2 * local, width), float32),
            pltpu.VMEM(weight.shape, float32),
            pltpu.VMEM((1, width), float32),
            pltpu.VMEM((8, LANES), float32),
        ],
        compiler_params=pltpu.CompilerParams(vmem_limit_bytes=VMEM_BYTES),
        cost_estimate=cost(24),
    )(where, ends, tok_mine, tok_other, *gains, *tables, *dh, *saved, weight, gain_ffn)


def ffn_kernel(where_ref, ends_ref, x_o, x_m, g_o, g_m, weight, *refs):
    out_send, out_keep, dn_send, dn_keep, grad_out, total = refs
    step = pl.program_id(0)
    core = where_ref[2]
    both = x_o.shape[1]
    big = both // 2
    local = x_o.shape[0] // 2

    def live_rows(values, group, at_core):
        ids = lax.broadcasted_iota(jnp.int32, values.shape, 0) + at_core * local
        return jnp.where(ids < ends_ref[group, ends_ref.shape[1] - 1], values, jnp.zeros_like(values))

    x = jnp.concatenate([x_o[...], x_m[...]], axis=0)
    grads = jnp.concatenate(
        [live_rows(g_o[k * local : (k + 1) * local, :], 2 * step + k, 1 - core) for k in range(2)]
        + [live_rows(g_m[k * local : (k + 1) * local, :], 2 * step + k, core) for k in range(2)],
        axis=0,
    )
    half = 2 * local
    w_both = weight[:, :both]
    w_down = weight[:, both : both + big]
    w_small = weight[:, both + big : both + big + LANES]
    w_small_down = weight[:, both + big + LANES :]
    lane = lane_ids((x.shape[0], LANES))

    def parts_of(gate, up, d_act):
        sigma = 1.0 / (1.0 + jnp.exp(-gate))
        silu = gate * sigma
        act = silu * up
        d_gate = d_act * up * sigma * (1.0 + gate * (1.0 - sigma))
        return act, d_gate, d_act * silu

    pre = matmul(x, w_both)
    act, d_gate, d_up = parts_of(pre[:, :big], pre[:, big:], matmul(grads, w_down))
    pre = matmul(x, w_small)
    act_s, d_gate_s, d_up_s = parts_of(
        pre, pltpu.roll(pre, HALF, 1), matmul(grads, w_small_down)
    )
    act_s = jnp.where(lane < HALF, act_s, 0.0).astype(bfloat16)
    d_small = jnp.where(lane < HALF, d_gate_s, pltpu.roll(d_up_s, HALF, 1)).astype(bfloat16)
    act = act.astype(bfloat16)
    d_both = jnp.concatenate([d_gate, d_up], axis=1).astype(bfloat16)

    partial = matmul_nt(act, w_down) + matmul_nt(act_s, w_small_down)
    out_send[...] = partial[:half].astype(bfloat16)
    out_keep[...] = partial[half:]
    partial = matmul_nt(d_both, w_both) + matmul_nt(d_small, w_small)
    dn_send[...] = partial[:half].astype(bfloat16)
    dn_keep[...] = partial[half:]
    spans = (
        (slice(0, both), x, d_both),
        (slice(both, both + big), grads, act),
        (slice(both + big, both + big + LANES), x, d_small),
        (slice(both + big + LANES, total.shape[1]), grads, act_s),
    )

    @pl.when(step == 0)
    def _():
        for span, left, right in spans:
            total[:, span] = matmul_tn(left, right)

    @pl.when(step == 1)
    def _():
        for span, left, right in spans:
            grad_out[:, span] = (total[:, span] + matmul_tn(left, right)).astype(bfloat16)


def ffn(where, ends, x_mine, x_other, g_mine, g_other, weight):
    rows, width = x_mine.shape
    row_spec = pl.BlockSpec((rows // 2, width), lambda i: (i, 0))
    scalar = pl.BlockSpec(memory_space=pltpu.SMEM)
    return pl.pallas_call(
        ffn_kernel,
        grid=(2,),
        in_specs=[scalar, scalar] + [row_spec] * 4 + [whole_spec(weight.shape)],
        out_specs=[row_spec] * 4 + [whole_spec(weight.shape)],
        out_shape=[
            jax.ShapeDtypeStruct((rows, width), bfloat16),
            jax.ShapeDtypeStruct((rows, width), float32),
            jax.ShapeDtypeStruct((rows, width), bfloat16),
            jax.ShapeDtypeStruct((rows, width), float32),
            jax.ShapeDtypeStruct(weight.shape, bfloat16),
        ],
        scratch_shapes=[pltpu.VMEM(weight.shape, float32)],
        compiler_params=pltpu.CompilerParams(vmem_limit_bytes=VMEM_BYTES),
        cost_estimate=cost(74),
    )(where, ends, x_other, x_mine, g_other, g_mine, weight)


def chip_sum_kernel(keep, received, *outs):
    rows = outs[0].shape[0]
    for mask, out in enumerate(outs):
        span = slice(mask * rows, (mask + 1) * rows)
        out[...] = (keep[span, :] + received[span, :].astype(float32)).astype(out.dtype)


def chip_sum(keep, received):
    shape = (keep.shape[0] // PLANE, keep.shape[1])
    outs = [(shape, float32)] + [(shape, bfloat16)] * (PLANE - 1)
    return call(chip_sum_kernel, outs, keep, received)


def plane_sent(parts):
    return [parts[0]] + [send_plane(part, mask + 1) for mask, part in enumerate(parts[1:])]


def plane_total(parts):
    return add_up(plane_sent(parts))


def add_up(parts):
    return sum(part.astype(float32) for part in parts)


def tail_kernel(where_ref, keep, received, own_ff, own, ff_out, *refs):
    messages, held = refs[:-1], refs[-1]
    held[...] = own_ff[...].astype(float32)
    place = where_ref[0]
    local = own.shape[0]
    rows = ff_out.shape[0]
    tall = (messages[0].shape[0] - local) // 2
    width = own.shape[1]
    for mask in range(PLANE):
        span = slice(mask * local, (mask + 1) * local)
        value = keep[span, :] + received[span, :].astype(float32)
        grads = held[pl.ds(pl.multiple_of((place ^ mask) * rows, rows), rows), :]
        if mask == 0:
            own[...] = value
            ff_out[...] = grads
            continue
        out = messages[mask - 1]
        out[:local, :] = value.astype(bfloat16)
        out[local : local + tall, :] = padded(grads[:, :width], tall).astype(bfloat16)
        rest = grads.shape[1] - width
        out[local + tall :, :rest] = padded(grads[:, width:], tall).astype(bfloat16)
        out[local + tall :, rest:] = jnp.zeros((tall, width - rest), bfloat16)


def tail_messages(where, keep, received, own_ff):
    local, width = keep.shape[0] // PLANE, keep.shape[1]
    rows, columns = own_ff.shape[0] // PLANE, own_ff.shape[1]
    message = (local + 2 * max(rows, 16), width)
    return call(
        tail_kernel,
        [((local, width), float32), ((rows, columns), float32)]
        + [(message, bfloat16)] * (PLANE - 1),
        where,
        keep,
        received,
        own_ff,
        scalars=1,
        scratch=[pltpu.VMEM(own_ff.shape, float32)],
    )


def joined_gains(tail):
    return tail[:GAIN_ROWS] + tail[GAIN_ROWS:]


def split_gains(gains):
    top = gains.astype(bfloat16).astype(float32)
    rest = (gains - top).astype(bfloat16).astype(float32)
    return jnp.concatenate([top, rest], axis=0)


def plane_sum_attn_kernel(where_ref, own, gains, *refs):
    received, outs = refs[: -PLANE - 2], refs[-PLANE - 2 : -2]
    held, held_gains = refs[-2:]
    layers = len(received) + 1
    value = own[...]
    high = own.shape[0]
    depth = where_ref[1]
    held_gains[deep_rows(depth, 0, layers, GAIN_ROWS), :] = joined_gains(split_gains(gains[...]))
    for step, part in enumerate(received):
        value = value + part[:high, :].astype(float32)
        held_gains[deep_rows(depth, -1 - step, layers, GAIN_ROWS), :] = joined_gains(
            part[high:, :].astype(float32)
        )
    held[...] = value
    sums = held_gains[:GAIN_ROWS, :]
    for layer in range(1, layers):
        sums = sums + held_gains[layer * GAIN_ROWS : (layer + 1) * GAIN_ROWS, :]
    tail = split_gains(sums)
    place = where_ref[0]
    rows = high // PLANE
    for mask, out in enumerate(outs):
        at = pl.multiple_of((place ^ mask) * rows, rows)
        part = held[pl.ds(at, rows), :]
        if mask:
            tall = out.shape[0] - tail.shape[0]
            out[:tall, :] = padded(part, tall).astype(bfloat16)
            out[tall:, :] = tail.astype(bfloat16)
        else:
            out[:rows, :] = part
            out[rows:, :] = tail


def plane_split_attn(where, own, received, gains):
    rows, columns = own.shape[0] // PLANE, own.shape[1]
    tail = 2 * GAIN_ROWS
    shapes = [((rows + tail, columns), float32)]
    shapes += [((max(rows, 16) + tail, columns), bfloat16)] * (PLANE - 1)
    scratch = [
        pltpu.VMEM(own.shape, float32),
        pltpu.VMEM(((len(received) + 1) * GAIN_ROWS, columns), float32),
    ]
    return call(
        plane_sum_attn_kernel, shapes, where, own, gains, *received, scalars=1, scratch=scratch
    )


def pick_place(refs, place, target, columns, rows):
    value = jnp.zeros((rows, columns.stop - columns.start), float32)
    for mask, ref in enumerate(refs):
        value = jnp.where(place ^ mask == target, ref[:, columns].astype(float32)[:rows], value)
    return value


def place_ffn_kernel(where_ref, own, one, two, three, out_g, out_u, out_d, held):
    place = where_ref[0]
    rows = out_g.shape[0]
    big = out_g.shape[1] // LANES // PLANE * LANES
    last = PLANE * big
    width = one.shape[1]
    tall = max(rows, 16)
    start = one.shape[0] - 2 * tall
    for mask, ref in enumerate((own, one, two, three)):
        if mask:
            top = ref[start : start + tall, :].astype(float32)[:rows]
            rest = ref[start + tall :, : held.shape[2] - width].astype(float32)[:rows]
            held[mask, :, :width] = top
            held[mask, :, width:] = rest
        else:
            held[mask] = ref[...]
        at = pl.ds(pl.multiple_of((place ^ mask) * big, LANES), big)
        for number, out in enumerate((out_g, out_u, out_d)):
            out[:, at] = held[mask, :, number * big : (number + 1) * big]
    for pair in range(PLANE // 2):
        low = held[place ^ (2 * pair), :, 3 * big :]
        high = held[place ^ (2 * pair + 1), :, 3 * big :]
        lane = lane_ids((rows, LANES))
        span = slice(last + pair * LANES, last + (pair + 1) * LANES)
        gu_low, gu_high = low[:, :LANES], high[:, :LANES]
        out_g[:, span] = jnp.where(lane < HALF, gu_low, pltpu.roll(gu_high, HALF, 1))
        out_u[:, span] = jnp.where(lane < HALF, pltpu.roll(gu_low, HALF, 1), gu_high)
        out_d[:, span] = jnp.where(lane < HALF, low[:, LANES:], pltpu.roll(high[:, LANES:], HALF, 1))


def place_attn_kernel(where_ref, own, one, two, three, out_q, out_k, out_v, out_o, out_gains):
    place = where_ref[0]
    refs = (own, one, two, three)
    rows = out_q.shape[0]
    for mask, ref in enumerate(refs):
        at = pl.ds(pl.multiple_of((place ^ mask) * LANES, LANES), LANES)
        out_q[:, at] = ref[:, :LANES].astype(float32)[:rows]
        out_o[:, at] = ref[:, 2 * LANES :].astype(float32)[:rows]
    for pair in range(PLANE // 2):
        low = pick_place(refs, place, 2 * pair, slice(LANES, 2 * LANES), rows)
        high = pick_place(refs, place, 2 * pair + 1, slice(LANES, 2 * LANES), rows)
        lane = lane_ids(low.shape)
        span = slice(pair * LANES, (pair + 1) * LANES)
        out_k[:, span] = jnp.where(lane < HALF, low, pltpu.roll(high, HALF, 1))
        out_v[:, span] = jnp.where(lane < HALF, pltpu.roll(low, HALF, 1), high)
    tails = [joined_gains(ref[ref.shape[0] - 2 * GAIN_ROWS :, :].astype(float32)) for ref in refs]
    out_gains[...] = (tails[0] + tails[1]) + (tails[2] + tails[3])


def plane_parts(local):
    return [local] + [send_plane(local, mask) for mask in range(1, PLANE)]


def both_cores(parts):
    mine = jnp.concatenate(parts)
    return mine, swap_cores(mine)


def gather_rows(local):
    return both_cores(plane_parts(local))


def row_tables(lens, slots, total_rows):
    all_lengths = lens.reshape(PLANE, 8, LANES)[:, 0, :slots].astype(jnp.int32)
    ends = jnp.cumsum(all_lengths, axis=1, dtype=jnp.int32)
    row_ids = jnp.arange(total_rows, dtype=jnp.int32)
    begin = jnp.max(
        jnp.where(row_ids[None, :, None] >= ends[:, None, :], ends[:, None, :], 0), axis=2
    )
    position = (row_ids[None, :] - begin).reshape(-1).astype(jnp.float32)
    spread = jnp.arange(LANES, dtype=jnp.int32) % (HEAD_DIM // 2)
    freqs = rope_base ** (-spread.astype(jnp.float32) * 2.0 / HEAD_DIM)
    angles = position[:, None] * freqs[None, :]
    sign = jnp.where(jnp.arange(LANES) % HEAD_DIM < HEAD_DIM // 2, -1.0, 1.0).astype(jnp.float32)
    return ends, (jnp.cos(angles), jnp.sin(angles) * sign)


def body(
    tokens,
    lengths,
    attn_gain,
    query_gain,
    key_gain,
    ffn_gain,
    w_query,
    w_key,
    w_value,
    w_out,
    w_gate,
    w_up,
    w_down,
    cotangent,
):
    dp = lax.axis_index("dp")
    core = lax.axis_index("tensor")
    layers = lax.axis_size("dp") // PLANE
    where = jnp.stack([dp % PLANE, dp // PLANE, core]).astype(jnp.int32)
    local_rows, model = tokens.shape
    total_rows = local_rows * lax.axis_size("tensor")
    rows = w_query.shape[0]
    q_cols = w_query.shape[1] // PLANE
    kv_cols = w_key.shape[1] // PLANE
    local_kv = kv_cols // HEAD_DIM
    share = q_cols // kv_cols
    attn_cols = 2 * q_cols + 2 * kv_cols
    ff_cols = 3 * (w_gate.shape[1] // LANES // PLANE * LANES) + 2 * LANES

    parts, high = attn_rows(rows)
    tall = max(rows, 16)
    first = call(
        pack_attn_kernel,
        [((high, model), bfloat16)] * PLANE,
        where,
        lengths,
        w_query,
        w_key,
        w_value,
        w_out,
        scalars=2,
    )
    second = call(
        pack_ffn_kernel,
        [((tall, ff_cols), bfloat16)] * PLANE,
        where,
        w_gate,
        w_up,
        w_down,
        scalars=1,
    )
    first = [first[0]] + [send_plane(first[m], m) for m in range(1, PLANE)]
    attn_piece, lens = call(
        unpack_attn_kernel,
        [((PLANE * rows, attn_cols), bfloat16), ((PLANE * 8, LANES), float32)],
        where,
        *first,
        scalars=1,
        scratch=[pltpu.VMEM((PLANE * rows, attn_cols), float32)],
    )
    attn_pieces = [attn_piece] + [send_deep(attn_piece, step) for step in range(1, layers)]
    tok_parts = plane_parts(after(first[1], tokens))
    second = after((first, tok_parts), second)
    second = [second[0]] + [send_plane(second[m], m) for m in range(1, PLANE)]
    ends, tables = row_tables(lens, lengths.shape[1], total_rows)
    second = after((attn_pieces, tables), second)
    (ff_piece,) = call(
        unpack_ffn_kernel,
        [((PLANE * rows, ff_cols), bfloat16)],
        where,
        *second,
        scalars=1,
        scratch=[pltpu.VMEM((PLANE * rows, ff_cols), float32)],
    )
    columns = [list(range(k, layers * PLANE, PLANE)) for k in range(PLANE)]
    ff_weight = lax.all_gather(ff_piece, "dp", axis=0, tiled=True, axis_index_groups=columns)
    attn_pieces = after(ff_piece, attn_pieces)
    cot_parts = plane_parts(after(second, cotangent))
    tok_mine, tok_other = both_cores(tok_parts)
    cot_mine, cot_other = both_cores(cot_parts)

    gains = (
        attn_gain[None, :],
        jnp.concatenate([query_gain, query_gain])[None, :],
        jnp.concatenate([key_gain, key_gain])[None, :],
    )

    inputs = tokens.astype(jnp.float32)
    factor_a = inverse_rms(inputs)
    unit_a = inputs * factor_a
    send, keep, *saved, attn_weight = attn(
        where, ends, tok_mine, tok_other, gains, tables, attn_pieces
    )
    send = after(cot_parts, send)
    hidden = inputs + plane_total(chip_sum(keep, swap_cores(send)))
    factor_b = inverse_rms(hidden)
    unit_b = hidden * factor_b
    x_mine, x_other = gather_rows((unit_b * ffn_gain).astype(jnp.bfloat16))

    out_send, out_keep, dn_send, dn_keep, ff_grad = ffn(
        where, ends, x_mine, x_other, cot_mine, cot_other, ff_weight
    )
    own_ff = lax.psum_scatter(
        ff_grad, "dp", scatter_dimension=0, tiled=True, axis_index_groups=columns
    )
    dn_parts = chip_sum(dn_keep, swap_cores(dn_send))
    out_keep = after(dn_parts, out_keep)
    d_normed2 = plane_total(dn_parts)
    grad_out = jnp.where(
        (jnp.arange(local_rows) + core * local_rows < ends[0, lengths.shape[1] - 1])[:, None],
        cotangent,
        jnp.zeros_like(cotangent),
    )
    gain_ffn = jnp.sum(d_normed2 * unit_b, axis=0)
    d_hidden = grad_out.astype(jnp.float32) + norm_back(d_normed2 * ffn_gain, unit_b, factor_b)
    h_mine, h_other = gather_rows(d_hidden.astype(jnp.bfloat16))
    out_parts = chip_sum(out_keep, swap_cores(out_send))
    out_parts = after((h_mine, h_other), out_parts)
    out_parts = plane_sent(out_parts)
    block_out = (hidden + add_up(out_parts)).astype(jnp.bfloat16)

    send, keep, own_attn, part_gains, *attn_grads = after(
        out_parts,
        attn_back(
            where, ends, layers, tok_mine, tok_other, gains, tables, (h_mine, h_other), saved,
            attn_weight, gain_ffn[None, :],
        ),
    )
    attn_grads = [send_deep(piece, step + 1) for step, piece in enumerate(attn_grads)]
    own_dn, own_ff, *messages = tail_messages(where, keep, swap_cores(send), own_ff)
    own_attn = after((messages, block_out), own_attn)
    attn_parts = plane_split_attn(where, own_attn, attn_grads, part_gains)
    attn_parts = plane_sent(attn_parts)
    messages = messages[:2] + after(attn_parts[1], messages[2:])
    messages = [send_plane(part, mask + 1) for mask, part in enumerate(messages)]
    attn_parts = after(messages[:2], attn_parts)
    d_normed = own_dn + add_up([part[:local_rows] for part in messages])
    grad_tokens = d_hidden + norm_back(d_normed * attn_gain, unit_a, factor_a)
    grad_gate, grad_up, grad_down = call(
        place_ffn_kernel,
        [(w_gate.shape, float32)] * 3,
        where,
        own_ff,
        *messages,
        scalars=1,
        scratch=[pltpu.VMEM((PLANE, rows, ff_cols), float32)],
    )
    grad_query, grad_key, grad_value, grad_out_w, sums = call(
        place_attn_kernel,
        [(w.shape, float32) for w in (w_query, w_key, w_value, w_out)]
        + [((GAIN_ROWS, attn_cols), float32)],
        where,
        *attn_parts,
        scalars=1,
    )
    sums = sums + swap_cores(sums)
    return (
        block_out,
        grad_tokens,
        sums[:, :LANES].reshape(-1),
        sums[0, 2 * LANES : 2 * LANES + HEAD_DIM],
        sums[0, 2 * LANES + HEAD_DIM :],
        sums[:, LANES : 2 * LANES].reshape(-1),
        grad_query,
        grad_key,
        grad_value,
        grad_out_w,
        grad_gate,
        grad_up,
        grad_down,
    )


def solution(mesh):
    placed = (
        P(("dp", "tensor"), None),
        P("dp", None),
        P(),
        P(),
        P(),
        P(),
        P("dp", "tensor"),
        P("dp", "tensor"),
        P("dp", "tensor"),
        P("dp", "tensor"),
        P("dp", "tensor"),
        P("dp", "tensor"),
        P("dp", "tensor"),
        P(("dp", "tensor"), None),
    )
    return jax.shard_map(
        body,
        mesh=mesh,
        in_specs=placed,
        out_specs=(
            P(("dp", "tensor"), None),
            P(("dp", "tensor"), None),
            P(),
            P(),
            P(),
            P(),
            P("dp", "tensor"),
            P("dp", "tensor"),
            P("dp", "tensor"),
            P("dp", "tensor"),
            P("dp", "tensor"),
            P("dp", "tensor"),
            P("dp", "tensor"),
        ),
        check_vma=False,
    )
```

```python
import jax
import jax.numpy as jnp
from jax import lax
from jax.experimental import pallas as pl
from jax.experimental.pallas import tpu as pltpu
from jax.sharding import PartitionSpec as P

HEAD_DIM = 64


epsilon = 1e-05
rope_base = 1000000.0
masked_score = -1e30


def inverse_rms(values):
    return lax.rsqrt(jnp.mean(values * values, axis=-1, keepdims=True) + epsilon)


def norm_back(grad_unit, unit, factor):
    return factor * (grad_unit - unit * jnp.mean(grad_unit * unit, axis=-1, keepdims=True))


def matmul(first_op, second_op):
    return jnp.dot(first_op, second_op, preferred_element_type=jnp.float32)


def matmul_nt(first_op, second_op):
    return lax.dot_general(
        first_op, second_op, (((1,), (1,)), ((), ())), preferred_element_type=jnp.float32
    )


def matmul_tn(first_op, second_op):
    return lax.dot_general(
        first_op, second_op, (((0,), (0,)), ((), ())), preferred_element_type=jnp.float32
    )


def seq_layout(seq_lengths, total_rows):
    ends = jnp.cumsum(seq_lengths, dtype=jnp.int32)
    starts = ends - seq_lengths
    row_ids = jnp.arange(total_rows, dtype=jnp.int32)
    segment = jnp.sum(
        (row_ids[:, None] >= ends[None, :]).astype(jnp.int32), axis=1, dtype=jnp.int32
    )
    slot_ids = jnp.arange(seq_lengths.shape[0], dtype=jnp.int32)
    picked = (segment[:, None] == slot_ids[None, :]).astype(jnp.int32)
    begin = (
        jnp.sum(picked * starts[None, :], axis=1, dtype=jnp.int32)
        + (segment == seq_lengths.shape[0]).astype(jnp.int32) * ends[-1]
    )
    allowed = (segment[:, None] == segment[None, :]) & (row_ids[:, None] >= row_ids[None, :])
    return (row_ids - begin, row_ids < ends[-1], allowed)


def rope_tables(position, head_size):
    half_dim = head_size // 2
    freqs = rope_base ** (-jnp.arange(half_dim, dtype=jnp.float32) * 2.0 / head_size)
    angles = position.astype(jnp.float32)[:, None] * freqs[None, :]
    return (jnp.cos(angles)[:, None, :], jnp.sin(angles)[:, None, :])


def rotate(values, cosine, sine):
    half_dim = values.shape[-1] // 2
    first_half = values[..., :half_dim]
    second_half = values[..., half_dim:]
    return jnp.concatenate(
        [first_half * cosine - second_half * sine, second_half * cosine + first_half * sine],
        axis=-1,
    )


def rotate_back(grads, cosine, sine):
    half_dim = grads.shape[-1] // 2
    first_half = grads[..., :half_dim]
    second_half = grads[..., half_dim:]
    return jnp.concatenate(
        [first_half * cosine + second_half * sine, second_half * cosine - first_half * sine],
        axis=-1,
    )

PLANE = 4
LANES = 128
HALF = 64
VMEM_BYTES = 60 * 1024 * 1024
COST = pl.CostEstimate(flops=1024, bytes_accessed=1024, transcendentals=0)


def cost(megabytes):
    return pl.CostEstimate(flops=1024, bytes_accessed=megabytes * 1000000, transcendentals=0)
GAIN_ROWS = 8
GROUPS_STEP = 2
float32 = jnp.float32
bfloat16 = jnp.bfloat16


def send_plane(values, mask):
    count = lax.axis_size("dp")
    return lax.ppermute(values, "dp", [(i, i ^ mask) for i in range(count)])


def send_deep(values, step):
    count = lax.axis_size("dp")
    return lax.ppermute(values, "dp", [(i, (i + PLANE * step) % count) for i in range(count)])


def swap_cores(values):
    return lax.ppermute(values, "tensor", [(0, 1), (1, 0)])


def call(kernel, outs, *operands, scalars=0, scratch=()):
    specs = [pl.BlockSpec(memory_space=pltpu.SMEM)] * scalars
    specs += [pl.BlockSpec(memory_space=pltpu.VMEM)] * (len(operands) - scalars)
    return pl.pallas_call(
        kernel,
        out_shape=[jax.ShapeDtypeStruct(shape, kind) for shape, kind in outs],
        in_specs=specs,
        out_specs=[pl.BlockSpec(memory_space=pltpu.VMEM)] * len(outs),
        scratch_shapes=list(scratch),
        compiler_params=pltpu.CompilerParams(vmem_limit_bytes=VMEM_BYTES),
        cost_estimate=COST,
    )(*operands)


def after(first, second):
    return lax.optimization_barrier((first, second))[1]


def lane_ids(shape):
    return lax.broadcasted_iota(jnp.int32, shape, len(shape) - 1)


def half_tile(ref, first_tile, place, upper):
    start = pl.multiple_of((first_tile + place // 2) * LANES, LANES)
    tile = ref[:, pl.ds(start, LANES)].astype(float32)
    turned = pltpu.roll(tile, HALF, 1)
    odd = place % 2 == 1
    if upper:
        return jnp.where(odd, tile, turned)
    return jnp.where(odd, turned, tile)


def padded(values, rows):
    if values.shape[0] == rows:
        return values
    blank = jnp.zeros((rows - values.shape[0], values.shape[1]), values.dtype)
    return jnp.concatenate([values, blank], axis=0)


def attn_rows(rows):
    return (2, rows // 2) if rows % 32 == 0 else (1, max(rows, 16))


def pack_attn_kernel(where_ref, lengths_ref, w_q, w_k, w_v, w_o, *outs):
    rows = w_q.shape[0]
    parts, high = attn_rows(rows)
    place = where_ref[0]
    lane = lane_ids((rows, LANES))
    for mask, out in enumerate(outs):
        other = place ^ mask
        at = pl.multiple_of(other * LANES, LANES)
        tile = jnp.where(
            lane < HALF, half_tile(w_k, 0, other, False), half_tile(w_v, 0, other, True)
        )
        piece = jnp.concatenate(
            [w_q[:, pl.ds(at, LANES)].astype(float32), tile, w_o[:, pl.ds(at, LANES)].astype(float32)],
            axis=1,
        )
        pieces = [piece[: rows // 2], piece[rows // 2 :]] if parts == 2 else [padded(piece, high)]
        width = piece.shape[1]
        for part, values in enumerate(pieces):
            out[:, part * width : (part + 1) * width] = values.astype(bfloat16)
        free = out.shape[1] - parts * width
        ids = lane_ids((high, free))
        marks = jnp.zeros((high, free), float32)
        for slot in range(lengths_ref.shape[1]):
            marks = jnp.where(ids == free - LANES + slot, lengths_ref[0, slot].astype(float32), marks)
        out[:, parts * width :] = marks.astype(bfloat16)


def pack_ffn_kernel(where_ref, w_g, w_u, w_d, *outs):
    rows = w_g.shape[0]
    big = w_g.shape[1] // LANES // PLANE * LANES
    last = w_g.shape[1] // LANES // PLANE * PLANE
    place = where_ref[0]
    lane = lane_ids((rows, LANES))
    for mask, out in enumerate(outs):
        other = place ^ mask
        at = pl.ds(pl.multiple_of(other * big, LANES), big)
        parts = [w[:, at].astype(float32) for w in (w_g, w_u, w_d)]
        parts.append(
            jnp.where(
                lane < HALF, half_tile(w_g, last, other, False), half_tile(w_u, last, other, True)
            )
        )
        parts.append(jnp.where(lane < HALF, half_tile(w_d, last, other, False), 0.0))
        out[...] = padded(jnp.concatenate(parts, axis=1), out.shape[0]).astype(bfloat16)


def unpack_attn_kernel(where_ref, own, one, two, three, attn_out, lens_out, held):
    rows = attn_out.shape[0] // PLANE
    width = attn_out.shape[1]
    parts, _ = attn_rows(rows)
    place = where_ref[0]
    for mask, message in enumerate((own, one, two, three)):
        at = pl.ds(pl.multiple_of((place ^ mask) * rows, rows), rows)
        values = [
            message[:, part * width : (part + 1) * width].astype(float32) for part in range(parts)
        ]
        held[at, :] = jnp.concatenate(values, axis=0) if parts == 2 else values[0][:rows]
        lens = message[:16, message.shape[1] - LANES :].astype(float32)
        lens_out[mask * 8 : (mask + 1) * 8, :] = lens[:8]
    attn_out[...] = held[...].astype(bfloat16)


def unpack_ffn_kernel(where_ref, own, one, two, three, ffn_out, held):
    rows = ffn_out.shape[0] // PLANE
    place = where_ref[0]
    for mask, message in enumerate((own, one, two, three)):
        at = pl.ds(pl.multiple_of((place ^ mask) * rows, rows), rows)
        held[at, :] = message[...].astype(float32)[:rows]
    ffn_out[...] = held[...].astype(bfloat16)


def head_mean(values):
    low = lane_ids(values.shape) < HALF
    first = jnp.sum(jnp.where(low, values, 0.0), axis=1, keepdims=True)
    second = jnp.sum(jnp.where(low, 0.0, values), axis=1, keepdims=True)
    return jnp.where(low, first, second) * (1.0 / HALF)


def turn_halves(values):
    first = lane_ids(values.shape) % HALF < HALF // 2
    return jnp.where(
        first, pltpu.roll(values, LANES - HALF // 2, 1), pltpu.roll(values, HALF // 2, 1)
    )


def at_head(values, head):
    low = lane_ids(values.shape) < HALF
    if head == 0:
        return jnp.where(low, values, 0.0).astype(bfloat16)
    return jnp.where(low, 0.0, pltpu.roll(values, HALF, 1)).astype(bfloat16)


def group_probs(query, key, begin, row_ids, col_ids):
    scores = matmul_nt(query, key) * HEAD_DIM ** (-0.5)
    scores = jnp.where((col_ids >= begin) & (col_ids <= row_ids), scores, masked_score)
    expd = jnp.exp(scores - jnp.max(scores, axis=1, keepdims=True))
    return expd / jnp.sum(expd, axis=1, keepdims=True)


def group_mask(ends_ref, group, rows):
    row_ids = lax.broadcasted_iota(jnp.int32, (rows, rows), 0)
    col_ids = lax.broadcasted_iota(jnp.int32, (rows, rows), 1)
    begin = jnp.zeros((rows, rows), jnp.int32)
    for slot in range(ends_ref.shape[1]):
        end = ends_ref[group, slot]
        begin = jnp.maximum(begin, jnp.where(row_ids >= end, end, 0))
    return begin, row_ids, col_ids


def group_rows(core, mine, other):
    first = jnp.where(core == 0, mine, other)
    second = jnp.where(core == 0, other, mine)
    return jnp.concatenate([first, second], axis=0)


def deep_rows(depth, step, layers, rows):
    at = lax.rem(depth + step + layers, layers) * rows
    return pl.ds(pl.multiple_of(at, rows), rows)


def attn_kernel(layers, where_ref, ends_ref, tok_m, tok_o, a_gain, q_gain, k_gain, cos, sin, *refs):
    pieces, refs = refs[:layers], refs[layers:]
    send, keep, pre_out, low_out, mixed_out, weight, held = refs
    step = pl.program_id(0)
    depth, core = where_ref[1], where_ref[2]
    local = tok_m.shape[0] // GROUPS_STEP

    @pl.when(step == 0)
    def _():
        for index, piece in enumerate(pieces):
            weight[deep_rows(depth, -index, layers, piece.shape[0]), :] = piece[...]

    for k in range(GROUPS_STEP):
        block = slice(k * local, (k + 1) * local)
        span = slice(2 * k * local, 2 * (k + 1) * local)
        x = group_rows(core, tok_m[block, :].astype(float32), tok_o[block, :].astype(float32))
        normed = (x * inverse_rms(x) * a_gain[...]).astype(bfloat16)
        pre = matmul(normed, weight[:, : 2 * LANES])
        pre_out[span, :] = pre
        cosine, sine = cos[span, :], sin[span, :]
        tiles = []
        for number, gain in enumerate((q_gain[...], k_gain[...])):
            tile = pre[:, number * LANES : (number + 1) * LANES]
            scaled = tile * lax.rsqrt(head_mean(tile * tile) + epsilon) * gain
            tiles.append(scaled * cosine + turn_halves(scaled) * sine)
        lane = lane_ids(tiles[0].shape)
        query = tiles[0].astype(bfloat16)
        key_value = jnp.where(lane < HALF, tiles[1], pre[:, LANES:])
        low_out[span, :LANES] = query
        low_out[span, LANES:] = key_value.astype(bfloat16)
        begin, row_ids, col_ids = group_mask(ends_ref, GROUPS_STEP * step + k, x.shape[0])
        turned = pltpu.roll(key_value, HALF, 1)
        mixed = jnp.zeros(tiles[0].shape, float32)
        for head in range(2):
            probs = group_probs(query, at_head(key_value, head), begin, row_ids, col_ids)
            mixed += matmul(probs.astype(bfloat16), at_head(turned, head))
        mixed = mixed.astype(bfloat16)
        mixed_out[span, :] = mixed
        held[span, :] = matmul_nt(mixed, weight[:, 2 * LANES :])
        mine = pl.multiple_of(2 * k * local + core * local, local)
        other = pl.multiple_of(2 * k * local + (1 - core) * local, local)
        send[block, :] = held[pl.ds(other, local), :].astype(bfloat16)
        keep[block, :] = held[pl.ds(mine, local), :]


def attn_back_kernel(
    layers, where_ref, ends_ref, tok_m, tok_o, a_gain, q_gain, k_gain, cos, sin, dh_m, dh_o,
    pre_ref, low_ref, mixed_ref, weight, gain_ffn, *refs,
):
    send, keep, own, gains_out = refs[:4]
    pieces = refs[4 : 3 + layers]
    held, total, sum_a, sum_qk = refs[3 + layers :]
    step = pl.program_id(0)
    depth, core = where_ref[1], where_ref[2]
    local = tok_m.shape[0] // GROUPS_STEP
    scale = HEAD_DIM ** (-0.5)

    @pl.when(step == 0)
    def _():
        total[...] = jnp.zeros_like(total)
        sum_a[...] = jnp.zeros_like(sum_a)
        sum_qk[...] = jnp.zeros_like(sum_qk)

    normed_rows, d_qkv_rows, d_hidden_rows = [], [], []
    for k in range(GROUPS_STEP):
        block = slice(k * local, (k + 1) * local)
        span = slice(2 * k * local, 2 * (k + 1) * local)
        x = group_rows(core, tok_m[block, :].astype(float32), tok_o[block, :].astype(float32))
        unit_a = x * inverse_rms(x)
        normed_rows.append((unit_a * a_gain[...]).astype(bfloat16))
        d_hidden = group_rows(core, dh_m[block, :], dh_o[block, :])
        d_hidden_rows.append(d_hidden)
        d_mixed = matmul(d_hidden, weight[:, 2 * LANES :]).astype(bfloat16)
        query = low_ref[span, :LANES]
        key_value = low_ref[span, LANES:].astype(float32)
        turned = pltpu.roll(key_value, HALF, 1)
        begin, row_ids, col_ids = group_mask(ends_ref, GROUPS_STEP * step + k, x.shape[0])
        shape = query.shape
        d_query = jnp.zeros(shape, float32)
        d_keys, d_values = [], []
        for head in range(2):
            key = at_head(key_value, head)
            probs = group_probs(query, key, begin, row_ids, col_ids)
            d_values.append(matmul_tn(probs.astype(bfloat16), d_mixed))
            d_probs = matmul_nt(d_mixed, at_head(turned, head))
            centre = jnp.sum(probs * d_probs, axis=1, keepdims=True)
            d_scores = (probs * (d_probs - centre)).astype(bfloat16)
            d_query += matmul(d_scores, key)
            d_keys.append(matmul_tn(d_scores, query))
        d_key = d_keys[0] + pltpu.roll(d_keys[1], HALF, 1)
        d_value = pltpu.roll(d_values[0], HALF, 1) + d_values[1]
        lane = lane_ids(shape)
        cosine, sine = cos[span, :], sin[span, :]
        tiles = []
        for number, (grad, gain) in enumerate(((d_query, q_gain[...]), (d_key, k_gain[...]))):
            grad = grad * scale
            back = grad * cosine - turn_halves(grad) * sine
            tile = pre_ref[span, number * LANES : (number + 1) * LANES]
            factor = lax.rsqrt(head_mean(tile * tile) + epsilon)
            unit = tile * factor
            sum_qk[number : number + 1, :] += jnp.sum(back * unit, axis=0, keepdims=True)
            back = back * gain
            tiles.append(factor * (back - unit * head_mean(back * unit)))
        tiles[1] = jnp.where(lane < HALF, tiles[1], d_value)
        d_qkv = jnp.concatenate(tiles, axis=1).astype(bfloat16)
        d_qkv_rows.append(d_qkv)
        held[span, :] = matmul_nt(d_qkv, weight[:, : 2 * LANES])
        sum_a[...] += jnp.sum(held[span, :] * unit_a, axis=0, keepdims=True)
        mine = pl.multiple_of(2 * k * local + core * local, local)
        other = pl.multiple_of(2 * k * local + (1 - core) * local, local)
        send[block, :] = held[pl.ds(other, local), :].astype(bfloat16)
        keep[block, :] = held[pl.ds(mine, local), :]
    total[:, : 2 * LANES] += matmul_tn(
        jnp.concatenate(normed_rows, axis=0), jnp.concatenate(d_qkv_rows, axis=0)
    )
    total[:, 2 * LANES :] += matmul_tn(jnp.concatenate(d_hidden_rows, axis=0), mixed_ref[...])

    @pl.when(step == pl.num_programs(0) - 1)
    def _():
        for row in range(GAIN_ROWS):
            gains_out[row : row + 1, :LANES] = sum_a[:, row * LANES : (row + 1) * LANES]
            gains_out[row : row + 1, LANES : 2 * LANES] = gain_ffn[:, row * LANES : (row + 1) * LANES]
        q_sum = sum_qk[0:1, :] + pltpu.roll(sum_qk[0:1, :], HALF, 1)
        k_sum = pltpu.roll(sum_qk[1:2, :], HALF, 1)
        qk_sum = jnp.where(lane_ids(q_sum.shape) < HALF, q_sum, k_sum)
        ids = lax.broadcasted_iota(jnp.int32, (GAIN_ROWS, LANES), 0)
        gains_out[:, 2 * LANES :] = jnp.where(ids == 0, qk_sum, 0.0)
        gains = gains_out[...]
        top = gains.astype(bfloat16)
        rest = (gains - top.astype(float32)).astype(bfloat16)
        tail = jnp.concatenate([top.astype(float32), rest.astype(float32)], axis=0).astype(bfloat16)
        rows = own.shape[0]
        own[...] = total[deep_rows(depth, 0, layers, rows), :]
        for index, piece in enumerate(pieces):
            piece[:rows, :] = total[deep_rows(depth, index + 1, layers, rows), :].astype(bfloat16)
            piece[rows:, :] = tail


def attn_specs(rows, width, group_height):
    scalar = pl.BlockSpec(memory_space=pltpu.SMEM)
    block = pl.BlockSpec((rows, width), lambda i: (i, 0))
    gain = pl.BlockSpec((1, width), lambda i: (0, 0))
    small = pl.BlockSpec((1, LANES), lambda i: (0, 0))
    table = pl.BlockSpec((group_height, LANES), lambda i: (i, 0))
    wide = pl.BlockSpec((group_height, 2 * LANES), lambda i: (i, 0))
    return scalar, block, gain, small, table, wide


def whole_spec(shape):
    return pl.BlockSpec(shape, lambda i: (0, 0), pipeline_mode=pl.Buffered(1))


def attn(where, ends, tok_mine, tok_other, gains, tables, pieces):
    layers = len(pieces)
    rows, width = tok_mine.shape
    local = rows // PLANE
    step = GROUPS_STEP * local
    scalar, block, gain, small, table, wide = attn_specs(step, width, 2 * step)
    high, columns = pieces[0].shape
    weight = (layers * high, columns)
    return pl.pallas_call(
        lambda *refs: attn_kernel(layers, *refs),
        grid=(PLANE // GROUPS_STEP,),
        in_specs=[scalar, scalar, block, block, gain, small, small, table, table]
        + [whole_spec((high, columns))] * layers,
        out_specs=[block, block, wide, wide, table, whole_spec(weight)],
        out_shape=[
            jax.ShapeDtypeStruct((rows, width), bfloat16),
            jax.ShapeDtypeStruct((rows, width), float32),
            jax.ShapeDtypeStruct((2 * rows, 2 * LANES), float32),
            jax.ShapeDtypeStruct((2 * rows, 2 * LANES), bfloat16),
            jax.ShapeDtypeStruct((2 * rows, LANES), bfloat16),
            jax.ShapeDtypeStruct(weight, bfloat16),
        ],
        scratch_shapes=[pltpu.VMEM((2 * step, width), float32)],
        compiler_params=pltpu.CompilerParams(vmem_limit_bytes=VMEM_BYTES),
        cost_estimate=cost(36),
    )(where, ends, tok_mine, tok_other, *gains, *tables, *pieces)


def attn_back(where, ends, layers, tok_mine, tok_other, gains, tables, dh, saved, weight, gain_ffn):
    rows, width = tok_mine.shape
    local = rows // PLANE
    step = GROUPS_STEP * local
    scalar, block, gain, small, table, wide = attn_specs(step, width, 2 * step)
    high, columns = weight.shape[0] // layers, weight.shape[1]
    tail = 2 * GAIN_ROWS
    return pl.pallas_call(
        lambda *refs: attn_back_kernel(layers, *refs),
        grid=(PLANE // GROUPS_STEP,),
        in_specs=[scalar, scalar, block, block, gain, small, small, table, table, block, block]
        + [wide, wide, table, whole_spec(weight.shape), gain],
        out_specs=[block, block, whole_spec((high, columns)), whole_spec((GAIN_ROWS, columns))]
        + [whole_spec((high + tail, columns))] * (layers - 1),
        out_shape=[
            jax.ShapeDtypeStruct((rows, width), bfloat16),
            jax.ShapeDtypeStruct((rows, width), float32),
            jax.ShapeDtypeStruct((high, columns), float32),
            jax.ShapeDtypeStruct((GAIN_ROWS, columns), float32),
        ]
        + [jax.ShapeDtypeStruct((high + tail, columns), bfloat16)] * (layers - 1),
        scratch_shapes=[
            pltpu.VMEM((2 * step, width), float32),
            pltpu.VMEM(weight.shape, float32),
            pltpu.VMEM((1, width), float32),
            pltpu.VMEM((8, LANES), float32),
        ],
        compiler_params=pltpu.CompilerParams(vmem_limit_bytes=VMEM_BYTES),
        cost_estimate=cost(24),
    )(where, ends, tok_mine, tok_other, *gains, *tables, *dh, *saved, weight, gain_ffn)


def ffn_kernel(where_ref, ends_ref, x_o, x_m, g_o, g_m, weight, *refs):
    out_send, out_keep, dn_send, dn_keep, grad_out, total = refs
    step = pl.program_id(0)
    core = where_ref[2]
    both = x_o.shape[1]
    big = both // 2
    local = x_o.shape[0] // 2

    def live_rows(values, group, at_core):
        ids = lax.broadcasted_iota(jnp.int32, values.shape, 0) + at_core * local
        return jnp.where(ids < ends_ref[group, ends_ref.shape[1] - 1], values, jnp.zeros_like(values))

    x = jnp.concatenate([x_o[...], x_m[...]], axis=0)
    grads = jnp.concatenate(
        [live_rows(g_o[k * local : (k + 1) * local, :], 2 * step + k, 1 - core) for k in range(2)]
        + [live_rows(g_m[k * local : (k + 1) * local, :], 2 * step + k, core) for k in range(2)],
        axis=0,
    )
    half = 2 * local
    w_both = weight[:, :both]
    w_down = weight[:, both : both + big]
    w_small = weight[:, both + big : both + big + LANES]
    w_small_down = weight[:, both + big + LANES :]
    lane = lane_ids((x.shape[0], LANES))

    def parts_of(gate, up, d_act):
        sigma = 1.0 / (1.0 + jnp.exp(-gate))
        silu = gate * sigma
        act = silu * up
        d_gate = d_act * up * sigma * (1.0 + gate * (1.0 - sigma))
        return act, d_gate, d_act * silu

    pre = matmul(x, w_both)
    act, d_gate, d_up = parts_of(pre[:, :big], pre[:, big:], matmul(grads, w_down))
    pre = matmul(x, w_small)
    act_s, d_gate_s, d_up_s = parts_of(
        pre, pltpu.roll(pre, HALF, 1), matmul(grads, w_small_down)
    )
    act_s = jnp.where(lane < HALF, act_s, 0.0).astype(bfloat16)
    d_small = jnp.where(lane < HALF, d_gate_s, pltpu.roll(d_up_s, HALF, 1)).astype(bfloat16)
    act = act.astype(bfloat16)
    d_both = jnp.concatenate([d_gate, d_up], axis=1).astype(bfloat16)

    partial = matmul_nt(act, w_down) + matmul_nt(act_s, w_small_down)
    out_send[...] = partial[:half].astype(bfloat16)
    out_keep[...] = partial[half:]
    partial = matmul_nt(d_both, w_both) + matmul_nt(d_small, w_small)
    dn_send[...] = partial[:half].astype(bfloat16)
    dn_keep[...] = partial[half:]
    spans = (
        (slice(0, both), x, d_both),
        (slice(both, both + big), grads, act),
        (slice(both + big, both + big + LANES), x, d_small),
        (slice(both + big + LANES, total.shape[1]), grads, act_s),
    )

    @pl.when(step == 0)
    def _():
        for span, left, right in spans:
            total[:, span] = matmul_tn(left, right)

    @pl.when(step == 1)
    def _():
        for span, left, right in spans:
            grad_out[:, span] = (total[:, span] + matmul_tn(left, right)).astype(bfloat16)


def ffn(where, ends, x_mine, x_other, g_mine, g_other, weight):
    rows, width = x_mine.shape
    row_spec = pl.BlockSpec((rows // 2, width), lambda i: (i, 0))
    scalar = pl.BlockSpec(memory_space=pltpu.SMEM)
    return pl.pallas_call(
        ffn_kernel,
        grid=(2,),
        in_specs=[scalar, scalar] + [row_spec] * 4 + [whole_spec(weight.shape)],
        out_specs=[row_spec] * 4 + [whole_spec(weight.shape)],
        out_shape=[
            jax.ShapeDtypeStruct((rows, width), bfloat16),
            jax.ShapeDtypeStruct((rows, width), float32),
            jax.ShapeDtypeStruct((rows, width), bfloat16),
            jax.ShapeDtypeStruct((rows, width), float32),
            jax.ShapeDtypeStruct(weight.shape, bfloat16),
        ],
        scratch_shapes=[pltpu.VMEM(weight.shape, float32)],
        compiler_params=pltpu.CompilerParams(vmem_limit_bytes=VMEM_BYTES),
        cost_estimate=cost(74),
    )(where, ends, x_other, x_mine, g_other, g_mine, weight)


def chip_sum_kernel(keep, received, *outs):
    rows = outs[0].shape[0]
    for mask, out in enumerate(outs):
        span = slice(mask * rows, (mask + 1) * rows)
        out[...] = (keep[span, :] + received[span, :].astype(float32)).astype(out.dtype)


def chip_sum(keep, received):
    shape = (keep.shape[0] // PLANE, keep.shape[1])
    outs = [(shape, float32)] + [(shape, bfloat16)] * (PLANE - 1)
    return call(chip_sum_kernel, outs, keep, received)


def plane_sent(parts):
    return [parts[0]] + [send_plane(part, mask + 1) for mask, part in enumerate(parts[1:])]


def plane_total(parts):
    return add_up(plane_sent(parts))


def add_up(parts):
    return sum(part.astype(float32) for part in parts)


def tail_kernel(where_ref, keep, received, own_ff, own, ff_out, *refs):
    messages, held = refs[:-1], refs[-1]
    held[...] = own_ff[...].astype(float32)
    place = where_ref[0]
    local = own.shape[0]
    rows = ff_out.shape[0]
    tall = (messages[0].shape[0] - local) // 2
    width = own.shape[1]
    for mask in range(PLANE):
        span = slice(mask * local, (mask + 1) * local)
        value = keep[span, :] + received[span, :].astype(float32)
        grads = held[pl.ds(pl.multiple_of((place ^ mask) * rows, rows), rows), :]
        if mask == 0:
            own[...] = value
            ff_out[...] = grads
            continue
        out = messages[mask - 1]
        out[:local, :] = value.astype(bfloat16)
        out[local : local + tall, :] = padded(grads[:, :width], tall).astype(bfloat16)
        rest = grads.shape[1] - width
        out[local + tall :, :rest] = padded(grads[:, width:], tall).astype(bfloat16)
        out[local + tall :, rest:] = jnp.zeros((tall, width - rest), bfloat16)


def tail_messages(where, keep, received, own_ff):
    local, width = keep.shape[0] // PLANE, keep.shape[1]
    rows, columns = own_ff.shape[0] // PLANE, own_ff.shape[1]
    message = (local + 2 * max(rows, 16), width)
    return call(
        tail_kernel,
        [((local, width), float32), ((rows, columns), float32)]
        + [(message, bfloat16)] * (PLANE - 1),
        where,
        keep,
        received,
        own_ff,
        scalars=1,
        scratch=[pltpu.VMEM(own_ff.shape, float32)],
    )


def joined_gains(tail):
    return tail[:GAIN_ROWS] + tail[GAIN_ROWS:]


def split_gains(gains):
    top = gains.astype(bfloat16).astype(float32)
    rest = (gains - top).astype(bfloat16).astype(float32)
    return jnp.concatenate([top, rest], axis=0)


def plane_sum_attn_kernel(where_ref, own, gains, *refs):
    received, outs = refs[: -PLANE - 2], refs[-PLANE - 2 : -2]
    held, held_gains = refs[-2:]
    layers = len(received) + 1
    value = own[...]
    high = own.shape[0]
    depth = where_ref[1]
    held_gains[deep_rows(depth, 0, layers, GAIN_ROWS), :] = joined_gains(split_gains(gains[...]))
    for step, part in enumerate(received):
        value = value + part[:high, :].astype(float32)
        held_gains[deep_rows(depth, -1 - step, layers, GAIN_ROWS), :] = joined_gains(
            part[high:, :].astype(float32)
        )
    held[...] = value
    sums = held_gains[:GAIN_ROWS, :]
    for layer in range(1, layers):
        sums = sums + held_gains[layer * GAIN_ROWS : (layer + 1) * GAIN_ROWS, :]
    tail = split_gains(sums)
    place = where_ref[0]
    rows = high // PLANE
    for mask, out in enumerate(outs):
        at = pl.multiple_of((place ^ mask) * rows, rows)
        part = held[pl.ds(at, rows), :]
        if mask:
            tall = out.shape[0] - tail.shape[0]
            out[:tall, :] = padded(part, tall).astype(bfloat16)
            out[tall:, :] = tail.astype(bfloat16)
        else:
            out[:rows, :] = part
            out[rows:, :] = tail


def plane_split_attn(where, own, received, gains):
    rows, columns = own.shape[0] // PLANE, own.shape[1]
    tail = 2 * GAIN_ROWS
    shapes = [((rows + tail, columns), float32)]
    shapes += [((max(rows, 16) + tail, columns), bfloat16)] * (PLANE - 1)
    scratch = [
        pltpu.VMEM(own.shape, float32),
        pltpu.VMEM(((len(received) + 1) * GAIN_ROWS, columns), float32),
    ]
    return call(
        plane_sum_attn_kernel, shapes, where, own, gains, *received, scalars=1, scratch=scratch
    )


def pick_place(refs, place, target, columns, rows):
    value = jnp.zeros((rows, columns.stop - columns.start), float32)
    for mask, ref in enumerate(refs):
        value = jnp.where(place ^ mask == target, ref[:, columns].astype(float32)[:rows], value)
    return value


def place_ffn_kernel(where_ref, own, one, two, three, out_g, out_u, out_d, held):
    place = where_ref[0]
    rows = out_g.shape[0]
    big = out_g.shape[1] // LANES // PLANE * LANES
    last = PLANE * big
    width = one.shape[1]
    tall = max(rows, 16)
    start = one.shape[0] - 2 * tall
    for mask, ref in enumerate((own, one, two, three)):
        if mask:
            top = ref[start : start + tall, :].astype(float32)[:rows]
            rest = ref[start + tall :, : held.shape[2] - width].astype(float32)[:rows]
            held[mask, :, :width] = top
            held[mask, :, width:] = rest
        else:
            held[mask] = ref[...]
        at = pl.ds(pl.multiple_of((place ^ mask) * big, LANES), big)
        for number, out in enumerate((out_g, out_u, out_d)):
            out[:, at] = held[mask, :, number * big : (number + 1) * big]
    for pair in range(PLANE // 2):
        low = held[place ^ (2 * pair), :, 3 * big :]
        high = held[place ^ (2 * pair + 1), :, 3 * big :]
        lane = lane_ids((rows, LANES))
        span = slice(last + pair * LANES, last + (pair + 1) * LANES)
        gu_low, gu_high = low[:, :LANES], high[:, :LANES]
        out_g[:, span] = jnp.where(lane < HALF, gu_low, pltpu.roll(gu_high, HALF, 1))
        out_u[:, span] = jnp.where(lane < HALF, pltpu.roll(gu_low, HALF, 1), gu_high)
        out_d[:, span] = jnp.where(lane < HALF, low[:, LANES:], pltpu.roll(high[:, LANES:], HALF, 1))


def place_attn_kernel(where_ref, own, one, two, three, out_q, out_k, out_v, out_o, out_gains):
    place = where_ref[0]
    refs = (own, one, two, three)
    rows = out_q.shape[0]
    for mask, ref in enumerate(refs):
        at = pl.ds(pl.multiple_of((place ^ mask) * LANES, LANES), LANES)
        out_q[:, at] = ref[:, :LANES].astype(float32)[:rows]
        out_o[:, at] = ref[:, 2 * LANES :].astype(float32)[:rows]
    for pair in range(PLANE // 2):
        low = pick_place(refs, place, 2 * pair, slice(LANES, 2 * LANES), rows)
        high = pick_place(refs, place, 2 * pair + 1, slice(LANES, 2 * LANES), rows)
        lane = lane_ids(low.shape)
        span = slice(pair * LANES, (pair + 1) * LANES)
        out_k[:, span] = jnp.where(lane < HALF, low, pltpu.roll(high, HALF, 1))
        out_v[:, span] = jnp.where(lane < HALF, pltpu.roll(low, HALF, 1), high)
    tails = [joined_gains(ref[ref.shape[0] - 2 * GAIN_ROWS :, :].astype(float32)) for ref in refs]
    out_gains[...] = (tails[0] + tails[1]) + (tails[2] + tails[3])


def plane_parts(local):
    return [local] + [send_plane(local, mask) for mask in range(1, PLANE)]


def both_cores(parts):
    mine = jnp.concatenate(parts)
    return mine, swap_cores(mine)


def gather_rows(local):
    return both_cores(plane_parts(local))


def row_tables(lens, slots, total_rows):
    all_lengths = lens.reshape(PLANE, 8, LANES)[:, 0, :slots].astype(jnp.int32)
    ends = jnp.cumsum(all_lengths, axis=1, dtype=jnp.int32)
    row_ids = jnp.arange(total_rows, dtype=jnp.int32)
    begin = jnp.max(
        jnp.where(row_ids[None, :, None] >= ends[:, None, :], ends[:, None, :], 0), axis=2
    )
    position = (row_ids[None, :] - begin).reshape(-1).astype(jnp.float32)
    spread = jnp.arange(LANES, dtype=jnp.int32) % (HEAD_DIM // 2)
    freqs = rope_base ** (-spread.astype(jnp.float32) * 2.0 / HEAD_DIM)
    angles = position[:, None] * freqs[None, :]
    sign = jnp.where(jnp.arange(LANES) % HEAD_DIM < HEAD_DIM // 2, -1.0, 1.0).astype(jnp.float32)
    return ends, (jnp.cos(angles), jnp.sin(angles) * sign)


def body(
    tokens,
    lengths,
    attn_gain,
    query_gain,
    key_gain,
    ffn_gain,
    w_query,
    w_key,
    w_value,
    w_out,
    w_gate,
    w_up,
    w_down,
    cotangent,
):
    dp = lax.axis_index("dp")
    core = lax.axis_index("tensor")
    layers = lax.axis_size("dp") // PLANE
    where = jnp.stack([dp % PLANE, dp // PLANE, core]).astype(jnp.int32)
    local_rows, model = tokens.shape
    total_rows = local_rows * lax.axis_size("tensor")
    rows = w_query.shape[0]
    q_cols = w_query.shape[1] // PLANE
    kv_cols = w_key.shape[1] // PLANE
    local_kv = kv_cols // HEAD_DIM
    share = q_cols // kv_cols
    attn_cols = 2 * q_cols + 2 * kv_cols
    ff_cols = 3 * (w_gate.shape[1] // LANES // PLANE * LANES) + 2 * LANES

    parts, high = attn_rows(rows)
    tall = max(rows, 16)
    first = call(
        pack_attn_kernel,
        [((high, model), bfloat16)] * PLANE,
        where,
        lengths,
        w_query,
        w_key,
        w_value,
        w_out,
        scalars=2,
    )
    second = call(
        pack_ffn_kernel,
        [((tall, ff_cols), bfloat16)] * PLANE,
        where,
        w_gate,
        w_up,
        w_down,
        scalars=1,
    )
    first = after(second, [first[0]] + [send_plane(first[m], m) for m in range(1, PLANE)])
    attn_piece, lens = call(
        unpack_attn_kernel,
        [((PLANE * rows, attn_cols), bfloat16), ((PLANE * 8, LANES), float32)],
        where,
        *first,
        scalars=1,
        scratch=[pltpu.VMEM((PLANE * rows, attn_cols), float32)],
    )
    attn_pieces = [attn_piece] + [send_deep(attn_piece, step) for step in range(1, layers)]
    second = after(first, second)
    second = [second[0]] + [send_plane(second[m], m) for m in range(1, PLANE)]
    ends, tables = row_tables(lens, lengths.shape[1], total_rows)
    second = after((attn_pieces, tables), second)
    (ff_piece,) = call(
        unpack_ffn_kernel,
        [((PLANE * rows, ff_cols), bfloat16)],
        where,
        *second,
        scalars=1,
        scratch=[pltpu.VMEM((PLANE * rows, ff_cols), float32)],
    )
    columns = [list(range(k, layers * PLANE, PLANE)) for k in range(PLANE)]
    ff_weight = lax.all_gather(ff_piece, "dp", axis=0, tiled=True, axis_index_groups=columns)
    attn_pieces = after(ff_piece, attn_pieces)
    tok_parts = plane_parts(after(ff_piece, tokens))
    cot_parts = plane_parts(after(tok_parts, cotangent))
    tok_mine, tok_other = both_cores(tok_parts)
    cot_mine, cot_other = both_cores(cot_parts)

    gains = (
        attn_gain[None, :],
        jnp.concatenate([query_gain, query_gain])[None, :],
        jnp.concatenate([key_gain, key_gain])[None, :],
    )

    inputs = tokens.astype(jnp.float32)
    factor_a = inverse_rms(inputs)
    unit_a = inputs * factor_a
    send, keep, *saved, attn_weight = attn(
        where, ends, tok_mine, tok_other, gains, tables, attn_pieces
    )
    send = after(cot_parts, send)
    hidden = inputs + plane_total(chip_sum(keep, swap_cores(send)))
    factor_b = inverse_rms(hidden)
    unit_b = hidden * factor_b
    x_mine, x_other = gather_rows((unit_b * ffn_gain).astype(jnp.bfloat16))

    out_send, out_keep, dn_send, dn_keep, ff_grad = ffn(
        where, ends, x_mine, x_other, cot_mine, cot_other, ff_weight
    )
    own_ff = lax.psum_scatter(
        ff_grad, "dp", scatter_dimension=0, tiled=True, axis_index_groups=columns
    )
    dn_parts = chip_sum(dn_keep, swap_cores(dn_send))
    out_keep = after(dn_parts, out_keep)
    d_normed2 = plane_total(dn_parts)
    grad_out = jnp.where(
        (jnp.arange(local_rows) + core * local_rows < ends[0, lengths.shape[1] - 1])[:, None],
        cotangent,
        jnp.zeros_like(cotangent),
    )
    gain_ffn = jnp.sum(d_normed2 * unit_b, axis=0)
    d_hidden = grad_out.astype(jnp.float32) + norm_back(d_normed2 * ffn_gain, unit_b, factor_b)
    h_mine, h_other = gather_rows(d_hidden.astype(jnp.bfloat16))
    out_parts = chip_sum(out_keep, swap_cores(out_send))
    out_parts = after((h_mine, h_other), out_parts)
    out_parts = plane_sent(out_parts)
    block_out = (hidden + add_up(out_parts)).astype(jnp.bfloat16)

    send, keep, own_attn, part_gains, *attn_grads = after(
        out_parts,
        attn_back(
            where, ends, layers, tok_mine, tok_other, gains, tables, (h_mine, h_other), saved,
            attn_weight, gain_ffn[None, :],
        ),
    )
    attn_grads = [send_deep(piece, step + 1) for step, piece in enumerate(attn_grads)]
    own_dn, own_ff, *messages = tail_messages(where, keep, swap_cores(send), own_ff)
    own_attn = after(messages, own_attn)
    messages = [send_plane(part, mask + 1) for mask, part in enumerate(messages)]
    attn_parts = plane_split_attn(where, own_attn, attn_grads, part_gains)
    attn_parts = after(messages[:2], plane_sent(attn_parts))
    d_normed = own_dn + add_up([part[:local_rows] for part in messages])
    grad_tokens = d_hidden + norm_back(d_normed * attn_gain, unit_a, factor_a)
    grad_gate, grad_up, grad_down = call(
        place_ffn_kernel,
        [(w_gate.shape, float32)] * 3,
        where,
        own_ff,
        *messages,
        scalars=1,
        scratch=[pltpu.VMEM((PLANE, rows, ff_cols), float32)],
    )
    grad_query, grad_key, grad_value, grad_out_w, sums = call(
        place_attn_kernel,
        [(w.shape, float32) for w in (w_query, w_key, w_value, w_out)]
        + [((GAIN_ROWS, attn_cols), float32)],
        where,
        *attn_parts,
        scalars=1,
    )
    sums = sums + swap_cores(sums)
    return (
        block_out,
        grad_tokens,
        sums[:, :LANES].reshape(-1),
        sums[0, 2 * LANES : 2 * LANES + HEAD_DIM],
        sums[0, 2 * LANES + HEAD_DIM :],
        sums[:, LANES : 2 * LANES].reshape(-1),
        grad_query,
        grad_key,
        grad_value,
        grad_out_w,
        grad_gate,
        grad_up,
        grad_down,
    )


def solution(mesh):
    placed = (
        P(("dp", "tensor"), None),
        P("dp", None),
        P(),
        P(),
        P(),
        P(),
        P("dp", "tensor"),
        P("dp", "tensor"),
        P("dp", "tensor"),
        P("dp", "tensor"),
        P("dp", "tensor"),
        P("dp", "tensor"),
        P("dp", "tensor"),
        P(("dp", "tensor"), None),
    )
    return jax.shard_map(
        body,
        mesh=mesh,
        in_specs=placed,
        out_specs=(
            P(("dp", "tensor"), None),
            P(("dp", "tensor"), None),
            P(),
            P(),
            P(),
            P(),
            P("dp", "tensor"),
            P("dp", "tensor"),
            P("dp", "tensor"),
            P("dp", "tensor"),
            P("dp", "tensor"),
            P("dp", "tensor"),
            P("dp", "tensor"),
        ),
        check_vma=False,
    )
```

```python
import jax
import jax.numpy as jnp
from jax import lax
from jax.experimental import pallas as pl
from jax.experimental.pallas import tpu as pltpu
from jax.sharding import PartitionSpec as P

HEAD_DIM = 64


epsilon = 1e-05
rope_base = 1000000.0
masked_score = -1e30


def inverse_rms(values):
    return lax.rsqrt(jnp.mean(values * values, axis=-1, keepdims=True) + epsilon)


def norm_back(grad_unit, unit, factor):
    return factor * (grad_unit - unit * jnp.mean(grad_unit * unit, axis=-1, keepdims=True))


def matmul(first_op, second_op):
    return jnp.dot(first_op, second_op, preferred_element_type=jnp.float32)


def matmul_nt(first_op, second_op):
    return lax.dot_general(
        first_op, second_op, (((1,), (1,)), ((), ())), preferred_element_type=jnp.float32
    )


def matmul_tn(first_op, second_op):
    return lax.dot_general(
        first_op, second_op, (((0,), (0,)), ((), ())), preferred_element_type=jnp.float32
    )


def seq_layout(seq_lengths, total_rows):
    ends = jnp.cumsum(seq_lengths, dtype=jnp.int32)
    starts = ends - seq_lengths
    row_ids = jnp.arange(total_rows, dtype=jnp.int32)
    segment = jnp.sum(
        (row_ids[:, None] >= ends[None, :]).astype(jnp.int32), axis=1, dtype=jnp.int32
    )
    slot_ids = jnp.arange(seq_lengths.shape[0], dtype=jnp.int32)
    picked = (segment[:, None] == slot_ids[None, :]).astype(jnp.int32)
    begin = (
        jnp.sum(picked * starts[None, :], axis=1, dtype=jnp.int32)
        + (segment == seq_lengths.shape[0]).astype(jnp.int32) * ends[-1]
    )
    allowed = (segment[:, None] == segment[None, :]) & (row_ids[:, None] >= row_ids[None, :])
    return (row_ids - begin, row_ids < ends[-1], allowed)


def rope_tables(position, head_size):
    half_dim = head_size // 2
    freqs = rope_base ** (-jnp.arange(half_dim, dtype=jnp.float32) * 2.0 / head_size)
    angles = position.astype(jnp.float32)[:, None] * freqs[None, :]
    return (jnp.cos(angles)[:, None, :], jnp.sin(angles)[:, None, :])


def rotate(values, cosine, sine):
    half_dim = values.shape[-1] // 2
    first_half = values[..., :half_dim]
    second_half = values[..., half_dim:]
    return jnp.concatenate(
        [first_half * cosine - second_half * sine, second_half * cosine + first_half * sine],
        axis=-1,
    )


def rotate_back(grads, cosine, sine):
    half_dim = grads.shape[-1] // 2
    first_half = grads[..., :half_dim]
    second_half = grads[..., half_dim:]
    return jnp.concatenate(
        [first_half * cosine + second_half * sine, second_half * cosine - first_half * sine],
        axis=-1,
    )

PLANE = 4
LANES = 128
HALF = 64
VMEM_BYTES = 60 * 1024 * 1024
COST = pl.CostEstimate(flops=1024, bytes_accessed=1024, transcendentals=0)


def cost(megabytes):
    return pl.CostEstimate(flops=1024, bytes_accessed=megabytes * 1000000, transcendentals=0)
GAIN_ROWS = 8
GROUPS_STEP = 2
float32 = jnp.float32
bfloat16 = jnp.bfloat16


def send_plane(values, mask):
    count = lax.axis_size("dp")
    return lax.ppermute(values, "dp", [(i, i ^ mask) for i in range(count)])


def send_deep(values, step):
    count = lax.axis_size("dp")
    return lax.ppermute(values, "dp", [(i, (i + PLANE * step) % count) for i in range(count)])


def swap_cores(values):
    return lax.ppermute(values, "tensor", [(0, 1), (1, 0)])


def call(kernel, outs, *operands, scalars=0, scratch=()):
    specs = [pl.BlockSpec(memory_space=pltpu.SMEM)] * scalars
    specs += [pl.BlockSpec(memory_space=pltpu.VMEM)] * (len(operands) - scalars)
    return pl.pallas_call(
        kernel,
        out_shape=[jax.ShapeDtypeStruct(shape, kind) for shape, kind in outs],
        in_specs=specs,
        out_specs=[pl.BlockSpec(memory_space=pltpu.VMEM)] * len(outs),
        scratch_shapes=list(scratch),
        compiler_params=pltpu.CompilerParams(vmem_limit_bytes=VMEM_BYTES),
        cost_estimate=COST,
    )(*operands)


def after(first, second):
    return lax.optimization_barrier((first, second))[1]


def lane_ids(shape):
    return lax.broadcasted_iota(jnp.int32, shape, len(shape) - 1)


def half_tile(ref, first_tile, place, upper):
    start = pl.multiple_of((first_tile + place // 2) * LANES, LANES)
    tile = ref[:, pl.ds(start, LANES)].astype(float32)
    turned = pltpu.roll(tile, HALF, 1)
    odd = place % 2 == 1
    if upper:
        return jnp.where(odd, tile, turned)
    return jnp.where(odd, turned, tile)


def padded(values, rows):
    if values.shape[0] == rows:
        return values
    blank = jnp.zeros((rows - values.shape[0], values.shape[1]), values.dtype)
    return jnp.concatenate([values, blank], axis=0)


def attn_rows(rows):
    return (2, rows // 2) if rows % 32 == 0 else (1, max(rows, 16))


def pack_attn_kernel(where_ref, lengths_ref, w_q, w_k, w_v, w_o, *outs):
    rows = w_q.shape[0]
    parts, high = attn_rows(rows)
    place = where_ref[0]
    lane = lane_ids((rows, LANES))
    for mask, out in enumerate(outs):
        other = place ^ mask
        at = pl.multiple_of(other * LANES, LANES)
        tile = jnp.where(
            lane < HALF, half_tile(w_k, 0, other, False), half_tile(w_v, 0, other, True)
        )
        piece = jnp.concatenate(
            [w_q[:, pl.ds(at, LANES)].astype(float32), tile, w_o[:, pl.ds(at, LANES)].astype(float32)],
            axis=1,
        )
        pieces = [piece[: rows // 2], piece[rows // 2 :]] if parts == 2 else [padded(piece, high)]
        width = piece.shape[1]
        for part, values in enumerate(pieces):
            out[:, part * width : (part + 1) * width] = values.astype(bfloat16)
        free = out.shape[1] - parts * width
        ids = lane_ids((high, free))
        marks = jnp.zeros((high, free), float32)
        for slot in range(lengths_ref.shape[1]):
            marks = jnp.where(ids == free - LANES + slot, lengths_ref[0, slot].astype(float32), marks)
        out[:, parts * width :] = marks.astype(bfloat16)


def pack_ffn_kernel(where_ref, w_g, w_u, w_d, *outs):
    rows = w_g.shape[0]
    big = w_g.shape[1] // LANES // PLANE * LANES
    last = w_g.shape[1] // LANES // PLANE * PLANE
    place = where_ref[0]
    lane = lane_ids((rows, LANES))
    for mask, out in enumerate(outs):
        other = place ^ mask
        at = pl.ds(pl.multiple_of(other * big, LANES), big)
        parts = [w[:, at].astype(float32) for w in (w_g, w_u, w_d)]
        parts.append(
            jnp.where(
                lane < HALF, half_tile(w_g, last, other, False), half_tile(w_u, last, other, True)
            )
        )
        parts.append(jnp.where(lane < HALF, half_tile(w_d, last, other, False), 0.0))
        out[...] = padded(jnp.concatenate(parts, axis=1), out.shape[0]).astype(bfloat16)


def unpack_attn_kernel(where_ref, own, one, two, three, attn_out, lens_out, held):
    rows = attn_out.shape[0] // PLANE
    width = attn_out.shape[1]
    parts, _ = attn_rows(rows)
    place = where_ref[0]
    for mask, message in enumerate((own, one, two, three)):
        at = pl.ds(pl.multiple_of((place ^ mask) * rows, rows), rows)
        values = [
            message[:, part * width : (part + 1) * width].astype(float32) for part in range(parts)
        ]
        held[at, :] = jnp.concatenate(values, axis=0) if parts == 2 else values[0][:rows]
        lens = message[:16, message.shape[1] - LANES :].astype(float32)
        lens_out[mask * 8 : (mask + 1) * 8, :] = lens[:8]
    attn_out[...] = held[...].astype(bfloat16)


def unpack_ffn_kernel(where_ref, own, one, two, three, ffn_out, held):
    rows = ffn_out.shape[0] // PLANE
    place = where_ref[0]
    for mask, message in enumerate((own, one, two, three)):
        at = pl.ds(pl.multiple_of((place ^ mask) * rows, rows), rows)
        held[at, :] = message[...].astype(float32)[:rows]
    ffn_out[...] = held[...].astype(bfloat16)


def head_mean(values):
    low = lane_ids(values.shape) < HALF
    first = jnp.sum(jnp.where(low, values, 0.0), axis=1, keepdims=True)
    second = jnp.sum(jnp.where(low, 0.0, values), axis=1, keepdims=True)
    return jnp.where(low, first, second) * (1.0 / HALF)


def turn_halves(values):
    first = lane_ids(values.shape) % HALF < HALF // 2
    return jnp.where(
        first, pltpu.roll(values, LANES - HALF // 2, 1), pltpu.roll(values, HALF // 2, 1)
    )


def at_head(values, head):
    low = lane_ids(values.shape) < HALF
    if head == 0:
        return jnp.where(low, values, 0.0).astype(bfloat16)
    return jnp.where(low, 0.0, pltpu.roll(values, HALF, 1)).astype(bfloat16)


def group_probs(query, key, begin, row_ids, col_ids):
    scores = matmul_nt(query, key) * HEAD_DIM ** (-0.5)
    scores = jnp.where((col_ids >= begin) & (col_ids <= row_ids), scores, masked_score)
    expd = jnp.exp(scores - jnp.max(scores, axis=1, keepdims=True))
    return expd / jnp.sum(expd, axis=1, keepdims=True)


def group_mask(ends_ref, group, rows):
    row_ids = lax.broadcasted_iota(jnp.int32, (rows, rows), 0)
    col_ids = lax.broadcasted_iota(jnp.int32, (rows, rows), 1)
    begin = jnp.zeros((rows, rows), jnp.int32)
    for slot in range(ends_ref.shape[1]):
        end = ends_ref[group, slot]
        begin = jnp.maximum(begin, jnp.where(row_ids >= end, end, 0))
    return begin, row_ids, col_ids


def group_rows(core, mine, other):
    first = jnp.where(core == 0, mine, other)
    second = jnp.where(core == 0, other, mine)
    return jnp.concatenate([first, second], axis=0)


def deep_rows(depth, step, layers, rows):
    at = lax.rem(depth + step + layers, layers) * rows
    return pl.ds(pl.multiple_of(at, rows), rows)


def attn_kernel(layers, where_ref, ends_ref, tok_m, tok_o, a_gain, q_gain, k_gain, cos, sin, *refs):
    pieces, refs = refs[:layers], refs[layers:]
    send, keep, pre_out, low_out, mixed_out, weight, held = refs
    step = pl.program_id(0)
    depth, core = where_ref[1], where_ref[2]
    local = tok_m.shape[0] // GROUPS_STEP

    @pl.when(step == 0)
    def _():
        for index, piece in enumerate(pieces):
            weight[deep_rows(depth, -index, layers, piece.shape[0]), :] = piece[...]

    for k in range(GROUPS_STEP):
        block = slice(k * local, (k + 1) * local)
        span = slice(2 * k * local, 2 * (k + 1) * local)
        x = group_rows(core, tok_m[block, :].astype(float32), tok_o[block, :].astype(float32))
        normed = (x * inverse_rms(x) * a_gain[...]).astype(bfloat16)
        pre = matmul(normed, weight[:, : 2 * LANES])
        pre_out[span, :] = pre
        cosine, sine = cos[span, :], sin[span, :]
        tiles = []
        for number, gain in enumerate((q_gain[...], k_gain[...])):
            tile = pre[:, number * LANES : (number + 1) * LANES]
            scaled = tile * lax.rsqrt(head_mean(tile * tile) + epsilon) * gain
            tiles.append(scaled * cosine + turn_halves(scaled) * sine)
        lane = lane_ids(tiles[0].shape)
        query = tiles[0].astype(bfloat16)
        key_value = jnp.where(lane < HALF, tiles[1], pre[:, LANES:])
        low_out[span, :LANES] = query
        low_out[span, LANES:] = key_value.astype(bfloat16)
        begin, row_ids, col_ids = group_mask(ends_ref, GROUPS_STEP * step + k, x.shape[0])
        turned = pltpu.roll(key_value, HALF, 1)
        mixed = jnp.zeros(tiles[0].shape, float32)
        for head in range(2):
            probs = group_probs(query, at_head(key_value, head), begin, row_ids, col_ids)
            mixed += matmul(probs.astype(bfloat16), at_head(turned, head))
        mixed = mixed.astype(bfloat16)
        mixed_out[span, :] = mixed
        held[span, :] = matmul_nt(mixed, weight[:, 2 * LANES :])
        mine = pl.multiple_of(2 * k * local + core * local, local)
        other = pl.multiple_of(2 * k * local + (1 - core) * local, local)
        send[block, :] = held[pl.ds(other, local), :].astype(bfloat16)
        keep[block, :] = held[pl.ds(mine, local), :]


def attn_back_kernel(
    layers, where_ref, ends_ref, tok_m, tok_o, a_gain, q_gain, k_gain, cos, sin, dh_m, dh_o,
    pre_ref, low_ref, mixed_ref, weight, gain_ffn, *refs,
):
    send, keep, own, gains_out = refs[:4]
    pieces = refs[4 : 3 + layers]
    held, total, sum_a, sum_qk = refs[3 + layers :]
    step = pl.program_id(0)
    depth, core = where_ref[1], where_ref[2]
    local = tok_m.shape[0] // GROUPS_STEP
    scale = HEAD_DIM ** (-0.5)

    @pl.when(step == 0)
    def _():
        total[...] = jnp.zeros_like(total)
        sum_a[...] = jnp.zeros_like(sum_a)
        sum_qk[...] = jnp.zeros_like(sum_qk)

    normed_rows, d_qkv_rows, d_hidden_rows = [], [], []
    for k in range(GROUPS_STEP):
        block = slice(k * local, (k + 1) * local)
        span = slice(2 * k * local, 2 * (k + 1) * local)
        x = group_rows(core, tok_m[block, :].astype(float32), tok_o[block, :].astype(float32))
        unit_a = x * inverse_rms(x)
        normed_rows.append((unit_a * a_gain[...]).astype(bfloat16))
        d_hidden = group_rows(core, dh_m[block, :], dh_o[block, :])
        d_hidden_rows.append(d_hidden)
        d_mixed = matmul(d_hidden, weight[:, 2 * LANES :]).astype(bfloat16)
        query = low_ref[span, :LANES]
        key_value = low_ref[span, LANES:].astype(float32)
        turned = pltpu.roll(key_value, HALF, 1)
        begin, row_ids, col_ids = group_mask(ends_ref, GROUPS_STEP * step + k, x.shape[0])
        shape = query.shape
        d_query = jnp.zeros(shape, float32)
        d_keys, d_values = [], []
        for head in range(2):
            key = at_head(key_value, head)
            probs = group_probs(query, key, begin, row_ids, col_ids)
            d_values.append(matmul_tn(probs.astype(bfloat16), d_mixed))
            d_probs = matmul_nt(d_mixed, at_head(turned, head))
            centre = jnp.sum(probs * d_probs, axis=1, keepdims=True)
            d_scores = (probs * (d_probs - centre)).astype(bfloat16)
            d_query += matmul(d_scores, key)
            d_keys.append(matmul_tn(d_scores, query))
        d_key = d_keys[0] + pltpu.roll(d_keys[1], HALF, 1)
        d_value = pltpu.roll(d_values[0], HALF, 1) + d_values[1]
        lane = lane_ids(shape)
        cosine, sine = cos[span, :], sin[span, :]
        tiles = []
        for number, (grad, gain) in enumerate(((d_query, q_gain[...]), (d_key, k_gain[...]))):
            grad = grad * scale
            back = grad * cosine - turn_halves(grad) * sine
            tile = pre_ref[span, number * LANES : (number + 1) * LANES]
            factor = lax.rsqrt(head_mean(tile * tile) + epsilon)
            unit = tile * factor
            sum_qk[number : number + 1, :] += jnp.sum(back * unit, axis=0, keepdims=True)
            back = back * gain
            tiles.append(factor * (back - unit * head_mean(back * unit)))
        tiles[1] = jnp.where(lane < HALF, tiles[1], d_value)
        d_qkv = jnp.concatenate(tiles, axis=1).astype(bfloat16)
        d_qkv_rows.append(d_qkv)
        held[span, :] = matmul_nt(d_qkv, weight[:, : 2 * LANES])
        sum_a[...] += jnp.sum(held[span, :] * unit_a, axis=0, keepdims=True)
        mine = pl.multiple_of(2 * k * local + core * local, local)
        other = pl.multiple_of(2 * k * local + (1 - core) * local, local)
        send[block, :] = held[pl.ds(other, local), :].astype(bfloat16)
        keep[block, :] = held[pl.ds(mine, local), :]
    total[:, : 2 * LANES] += matmul_tn(
        jnp.concatenate(normed_rows, axis=0), jnp.concatenate(d_qkv_rows, axis=0)
    )
    total[:, 2 * LANES :] += matmul_tn(jnp.concatenate(d_hidden_rows, axis=0), mixed_ref[...])

    @pl.when(step == pl.num_programs(0) - 1)
    def _():
        for row in range(GAIN_ROWS):
            gains_out[row : row + 1, :LANES] = sum_a[:, row * LANES : (row + 1) * LANES]
            gains_out[row : row + 1, LANES : 2 * LANES] = gain_ffn[:, row * LANES : (row + 1) * LANES]
        q_sum = sum_qk[0:1, :] + pltpu.roll(sum_qk[0:1, :], HALF, 1)
        k_sum = pltpu.roll(sum_qk[1:2, :], HALF, 1)
        qk_sum = jnp.where(lane_ids(q_sum.shape) < HALF, q_sum, k_sum)
        ids = lax.broadcasted_iota(jnp.int32, (GAIN_ROWS, LANES), 0)
        gains_out[:, 2 * LANES :] = jnp.where(ids == 0, qk_sum, 0.0)
        gains = gains_out[...]
        top = gains.astype(bfloat16)
        rest = (gains - top.astype(float32)).astype(bfloat16)
        tail = jnp.concatenate([top.astype(float32), rest.astype(float32)], axis=0).astype(bfloat16)
        rows = own.shape[0]
        own[...] = total[deep_rows(depth, 0, layers, rows), :]
        for index, piece in enumerate(pieces):
            piece[:rows, :] = total[deep_rows(depth, index + 1, layers, rows), :].astype(bfloat16)
            piece[rows:, :] = tail


def attn_specs(rows, width, group_height):
    scalar = pl.BlockSpec(memory_space=pltpu.SMEM)
    block = pl.BlockSpec((rows, width), lambda i: (i, 0))
    gain = pl.BlockSpec((1, width), lambda i: (0, 0))
    small = pl.BlockSpec((1, LANES), lambda i: (0, 0))
    table = pl.BlockSpec((group_height, LANES), lambda i: (i, 0))
    wide = pl.BlockSpec((group_height, 2 * LANES), lambda i: (i, 0))
    return scalar, block, gain, small, table, wide


def whole_spec(shape):
    return pl.BlockSpec(shape, lambda i: (0, 0), pipeline_mode=pl.Buffered(1))


def attn(where, ends, tok_mine, tok_other, gains, tables, pieces):
    layers = len(pieces)
    rows, width = tok_mine.shape
    local = rows // PLANE
    step = GROUPS_STEP * local
    scalar, block, gain, small, table, wide = attn_specs(step, width, 2 * step)
    high, columns = pieces[0].shape
    weight = (layers * high, columns)
    return pl.pallas_call(
        lambda *refs: attn_kernel(layers, *refs),
        grid=(PLANE // GROUPS_STEP,),
        in_specs=[scalar, scalar, block, block, gain, small, small, table, table]
        + [whole_spec((high, columns))] * layers,
        out_specs=[block, block, wide, wide, table, whole_spec(weight)],
        out_shape=[
            jax.ShapeDtypeStruct((rows, width), bfloat16),
            jax.ShapeDtypeStruct((rows, width), float32),
            jax.ShapeDtypeStruct((2 * rows, 2 * LANES), float32),
            jax.ShapeDtypeStruct((2 * rows, 2 * LANES), bfloat16),
            jax.ShapeDtypeStruct((2 * rows, LANES), bfloat16),
            jax.ShapeDtypeStruct(weight, bfloat16),
        ],
        scratch_shapes=[pltpu.VMEM((2 * step, width), float32)],
        compiler_params=pltpu.CompilerParams(vmem_limit_bytes=VMEM_BYTES),
        cost_estimate=cost(36),
    )(where, ends, tok_mine, tok_other, *gains, *tables, *pieces)


def attn_back(where, ends, layers, tok_mine, tok_other, gains, tables, dh, saved, weight, gain_ffn):
    rows, width = tok_mine.shape
    local = rows // PLANE
    step = GROUPS_STEP * local
    scalar, block, gain, small, table, wide = attn_specs(step, width, 2 * step)
    high, columns = weight.shape[0] // layers, weight.shape[1]
    tail = 2 * GAIN_ROWS
    return pl.pallas_call(
        lambda *refs: attn_back_kernel(layers, *refs),
        grid=(PLANE // GROUPS_STEP,),
        in_specs=[scalar, scalar, block, block, gain, small, small, table, table, block, block]
        + [wide, wide, table, whole_spec(weight.shape), gain],
        out_specs=[block, block, whole_spec((high, columns)), whole_spec((GAIN_ROWS, columns))]
        + [whole_spec((high + tail, columns))] * (layers - 1),
        out_shape=[
            jax.ShapeDtypeStruct((rows, width), bfloat16),
            jax.ShapeDtypeStruct((rows, width), float32),
            jax.ShapeDtypeStruct((high, columns), float32),
            jax.ShapeDtypeStruct((GAIN_ROWS, columns), float32),
        ]
        + [jax.ShapeDtypeStruct((high + tail, columns), bfloat16)] * (layers - 1),
        scratch_shapes=[
            pltpu.VMEM((2 * step, width), float32),
            pltpu.VMEM(weight.shape, float32),
            pltpu.VMEM((1, width), float32),
            pltpu.VMEM((8, LANES), float32),
        ],
        compiler_params=pltpu.CompilerParams(vmem_limit_bytes=VMEM_BYTES),
        cost_estimate=cost(24),
    )(where, ends, tok_mine, tok_other, *gains, *tables, *dh, *saved, weight, gain_ffn)


def ffn_kernel(where_ref, ends_ref, x_o, x_m, g_o, g_m, weight, *refs):
    act_out, d_out, grad_out, total = refs
    step = pl.program_id(0)
    core = where_ref[2]
    both = x_o.shape[1]
    big = both // 2
    local = x_o.shape[0] // 2

    def live_rows(values, group, at_core):
        ids = lax.broadcasted_iota(jnp.int32, values.shape, 0) + at_core * local
        return jnp.where(ids < ends_ref[group, ends_ref.shape[1] - 1], values, jnp.zeros_like(values))

    x = jnp.concatenate([x_o[...], x_m[...]], axis=0)
    grads = jnp.concatenate(
        [live_rows(g_o[k * local : (k + 1) * local, :], 2 * step + k, 1 - core) for k in range(2)]
        + [live_rows(g_m[k * local : (k + 1) * local, :], 2 * step + k, core) for k in range(2)],
        axis=0,
    )
    w_both = weight[:, :both]
    w_down = weight[:, both : both + big]
    w_small = weight[:, both + big : both + big + LANES]
    w_small_down = weight[:, both + big + LANES :]
    lane = lane_ids((x.shape[0], LANES))

    def parts_of(gate, up, d_act):
        sigma = 1.0 / (1.0 + jnp.exp(-gate))
        silu = gate * sigma
        act = silu * up
        d_gate = d_act * up * sigma * (1.0 + gate * (1.0 - sigma))
        return act, d_gate, d_act * silu

    pre = matmul(x, w_both)
    act, d_gate, d_up = parts_of(pre[:, :big], pre[:, big:], matmul(grads, w_down))
    pre = matmul(x, w_small)
    act_s, d_gate_s, d_up_s = parts_of(
        pre, pltpu.roll(pre, HALF, 1), matmul(grads, w_small_down)
    )
    act_s = jnp.where(lane < HALF, act_s, 0.0).astype(bfloat16)
    d_small = jnp.where(lane < HALF, d_gate_s, pltpu.roll(d_up_s, HALF, 1)).astype(bfloat16)
    act = act.astype(bfloat16)
    d_both = jnp.concatenate([d_gate, d_up], axis=1).astype(bfloat16)

    act_out[:, :big] = act
    act_out[:, big:] = act_s
    d_out[:, :both] = d_both
    d_out[:, both:] = d_small
    spans = (
        (slice(0, both), x, d_both),
        (slice(both, both + big), grads, act),
        (slice(both + big, both + big + LANES), x, d_small),
        (slice(both + big + LANES, total.shape[1]), grads, act_s),
    )

    @pl.when(step == 0)
    def _():
        for span, left, right in spans:
            total[:, span] = matmul_tn(left, right)

    @pl.when(step == 1)
    def _():
        for span, left, right in spans:
            grad_out[:, span] = (total[:, span] + matmul_tn(left, right)).astype(bfloat16)


def ffn_layer(where, ends, x_mine, x_other, g_mine, g_other, weight):
    rows, width = x_mine.shape
    row_spec = pl.BlockSpec((rows // 2, width), lambda i: (i, 0))
    scalar = pl.BlockSpec(memory_space=pltpu.SMEM)
    widths = (width // 2 + LANES, width + LANES)
    return pl.pallas_call(
        ffn_kernel,
        grid=(2,),
        in_specs=[scalar, scalar] + [row_spec] * 4 + [whole_spec(weight.shape)],
        out_specs=[pl.BlockSpec((rows, w), lambda i: (i, 0)) for w in widths]
        + [whole_spec(weight.shape)],
        out_shape=[jax.ShapeDtypeStruct((2 * rows, w), bfloat16) for w in widths]
        + [jax.ShapeDtypeStruct(weight.shape, bfloat16)],
        scratch_shapes=[pltpu.VMEM(weight.shape, float32)],
        compiler_params=pltpu.CompilerParams(vmem_limit_bytes=VMEM_BYTES),
        cost_estimate=cost(48),
    )(where, ends, x_other, x_mine, g_other, g_mine, weight)


def ffn_apply_kernel(first, values, weight, send, keep):
    width = values.shape[1] - LANES
    big = send.shape[1] // 2
    small = 3 * big if first == 0 else 3 * big + LANES
    partial = matmul_nt(values[:, :width], weight[:, first : first + width])
    partial = partial + matmul_nt(values[:, width:], weight[:, small : small + LANES])
    half = send.shape[0]
    send[...] = partial[:half].astype(bfloat16)
    keep[...] = partial[half:]


def ffn_apply(first, values, weight):
    rows, width = values.shape[0] // 2, weight.shape[0]
    row_spec = pl.BlockSpec((rows // 2, width), lambda i: (i, 0))
    return pl.pallas_call(
        lambda *refs: ffn_apply_kernel(first, *refs),
        grid=(2,),
        in_specs=[
            pl.BlockSpec((rows, values.shape[1]), lambda i: (i, 0)),
            whole_spec(weight.shape),
        ],
        out_specs=[row_spec] * 2,
        out_shape=[
            jax.ShapeDtypeStruct((rows, width), bfloat16),
            jax.ShapeDtypeStruct((rows, width), float32),
        ],
        compiler_params=pltpu.CompilerParams(vmem_limit_bytes=VMEM_BYTES),
        cost_estimate=cost(14),
    )(values, weight)


def chip_sum_kernel(keep, received, *outs):
    for mask, out in enumerate(outs):

        @pl.when(pl.program_id(0) == mask)
        def _(out=out):
            out[...] = (keep[...] + received[...].astype(float32)).astype(out.dtype)


def partner_specs(rows, width):
    return pl.BlockSpec((rows, width), lambda i: (i, 0)), whole_spec((rows, width))


def chip_sum(keep, received):
    rows, width = keep.shape[0] // PLANE, keep.shape[1]
    step, whole = partner_specs(rows, width)
    return pl.pallas_call(
        chip_sum_kernel,
        grid=(PLANE,),
        in_specs=[step, step],
        out_specs=[whole] * PLANE,
        out_shape=[jax.ShapeDtypeStruct((rows, width), float32)]
        + [jax.ShapeDtypeStruct((rows, width), bfloat16)] * (PLANE - 1),
        compiler_params=pltpu.CompilerParams(vmem_limit_bytes=VMEM_BYTES),
        cost_estimate=COST,
    )(keep, received)


def plane_sent(parts):
    return [parts[0]] + [send_plane(part, mask + 1) for mask, part in enumerate(parts[1:])]


def plane_total(parts):
    return add_up(plane_sent(parts))


def add_up(parts):
    return sum(part.astype(float32) for part in parts)


def tail_kernel(where_ref, keep, received, own_ff, own, ff_out, *refs):
    messages, held = refs[:-1], refs[-1]
    place = where_ref[0]
    local = own.shape[0]
    rows = ff_out.shape[0]
    tall = (messages[0].shape[0] - local) // 2
    width = own.shape[1]

    @pl.when(pl.program_id(0) == 0)
    def _():
        held[...] = own_ff[...].astype(float32)

    value = keep[...] + received[...].astype(float32)
    for mask in range(PLANE):

        @pl.when(pl.program_id(0) == mask)
        def _(mask=mask):
            grads = held[pl.ds(pl.multiple_of((place ^ mask) * rows, rows), rows), :]
            if mask == 0:
                own[...] = value
                ff_out[...] = grads
            else:
                out = messages[mask - 1]
                out[:local, :] = value.astype(bfloat16)
                out[local : local + tall, :] = padded(grads[:, :width], tall).astype(bfloat16)
                rest = grads.shape[1] - width
                out[local + tall :, :rest] = padded(grads[:, width:], tall).astype(bfloat16)
                out[local + tall :, rest:] = jnp.zeros((tall, width - rest), bfloat16)


def tail_messages(where, keep, received, own_ff):
    local, width = keep.shape[0] // PLANE, keep.shape[1]
    rows, columns = own_ff.shape[0] // PLANE, own_ff.shape[1]
    message = (local + 2 * max(rows, 16), width)
    step, whole = partner_specs(local, width)
    return pl.pallas_call(
        tail_kernel,
        grid=(PLANE,),
        in_specs=[pl.BlockSpec(memory_space=pltpu.SMEM), step, step, whole_spec(own_ff.shape)],
        out_specs=[whole, whole_spec((rows, columns))] + [whole_spec(message)] * (PLANE - 1),
        out_shape=[
            jax.ShapeDtypeStruct((local, width), float32),
            jax.ShapeDtypeStruct((rows, columns), float32),
        ]
        + [jax.ShapeDtypeStruct(message, bfloat16)] * (PLANE - 1),
        scratch_shapes=[pltpu.VMEM(own_ff.shape, float32)],
        compiler_params=pltpu.CompilerParams(vmem_limit_bytes=VMEM_BYTES),
        cost_estimate=COST,
    )(where, keep, received, own_ff)


def joined_gains(tail):
    return tail[:GAIN_ROWS] + tail[GAIN_ROWS:]


def split_gains(gains):
    top = gains.astype(bfloat16).astype(float32)
    rest = (gains - top).astype(bfloat16).astype(float32)
    return jnp.concatenate([top, rest], axis=0)


def plane_sum_attn_kernel(where_ref, own, gains, *refs):
    received, outs = refs[: -PLANE - 2], refs[-PLANE - 2 : -2]
    held, held_gains = refs[-2:]
    layers = len(received) + 1
    value = own[...]
    high = own.shape[0]
    depth = where_ref[1]
    held_gains[deep_rows(depth, 0, layers, GAIN_ROWS), :] = joined_gains(split_gains(gains[...]))
    for step, part in enumerate(received):
        value = value + part[:high, :].astype(float32)
        held_gains[deep_rows(depth, -1 - step, layers, GAIN_ROWS), :] = joined_gains(
            part[high:, :].astype(float32)
        )
    held[...] = value
    sums = held_gains[:GAIN_ROWS, :]
    for layer in range(1, layers):
        sums = sums + held_gains[layer * GAIN_ROWS : (layer + 1) * GAIN_ROWS, :]
    tail = split_gains(sums)
    place = where_ref[0]
    rows = high // PLANE
    for mask, out in enumerate(outs):
        at = pl.multiple_of((place ^ mask) * rows, rows)
        part = held[pl.ds(at, rows), :]
        if mask:
            tall = out.shape[0] - tail.shape[0]
            out[:tall, :] = padded(part, tall).astype(bfloat16)
            out[tall:, :] = tail.astype(bfloat16)
        else:
            out[:rows, :] = part
            out[rows:, :] = tail


def plane_split_attn(where, own, received, gains):
    rows, columns = own.shape[0] // PLANE, own.shape[1]
    tail = 2 * GAIN_ROWS
    shapes = [((rows + tail, columns), float32)]
    shapes += [((max(rows, 16) + tail, columns), bfloat16)] * (PLANE - 1)
    scratch = [
        pltpu.VMEM(own.shape, float32),
        pltpu.VMEM(((len(received) + 1) * GAIN_ROWS, columns), float32),
    ]
    return call(
        plane_sum_attn_kernel, shapes, where, own, gains, *received, scalars=1, scratch=scratch
    )


def pick_place(refs, place, target, columns, rows):
    value = jnp.zeros((rows, columns.stop - columns.start), float32)
    for mask, ref in enumerate(refs):
        value = jnp.where(place ^ mask == target, ref[:, columns].astype(float32)[:rows], value)
    return value


def place_ffn_kernel(where_ref, own, one, two, three, out_g, out_u, out_d, held):
    place = where_ref[0]
    rows = out_g.shape[0]
    big = out_g.shape[1] // LANES // PLANE * LANES
    last = PLANE * big
    width = one.shape[1]
    tall = max(rows, 16)
    start = one.shape[0] - 2 * tall
    for mask, ref in enumerate((own, one, two, three)):
        if mask:
            top = ref[start : start + tall, :].astype(float32)[:rows]
            rest = ref[start + tall :, : held.shape[2] - width].astype(float32)[:rows]
            held[mask, :, :width] = top
            held[mask, :, width:] = rest
        else:
            held[mask] = ref[...]
        at = pl.ds(pl.multiple_of((place ^ mask) * big, LANES), big)
        for number, out in enumerate((out_g, out_u, out_d)):
            out[:, at] = held[mask, :, number * big : (number + 1) * big]
    for pair in range(PLANE // 2):
        low = held[place ^ (2 * pair), :, 3 * big :]
        high = held[place ^ (2 * pair + 1), :, 3 * big :]
        lane = lane_ids((rows, LANES))
        span = slice(last + pair * LANES, last + (pair + 1) * LANES)
        gu_low, gu_high = low[:, :LANES], high[:, :LANES]
        out_g[:, span] = jnp.where(lane < HALF, gu_low, pltpu.roll(gu_high, HALF, 1))
        out_u[:, span] = jnp.where(lane < HALF, pltpu.roll(gu_low, HALF, 1), gu_high)
        out_d[:, span] = jnp.where(lane < HALF, low[:, LANES:], pltpu.roll(high[:, LANES:], HALF, 1))


def place_attn_kernel(where_ref, own, one, two, three, out_q, out_k, out_v, out_o, out_gains):
    place = where_ref[0]
    refs = (own, one, two, three)
    rows = out_q.shape[0]
    for mask, ref in enumerate(refs):
        at = pl.ds(pl.multiple_of((place ^ mask) * LANES, LANES), LANES)
        out_q[:, at] = ref[:, :LANES].astype(float32)[:rows]
        out_o[:, at] = ref[:, 2 * LANES :].astype(float32)[:rows]
    for pair in range(PLANE // 2):
        low = pick_place(refs, place, 2 * pair, slice(LANES, 2 * LANES), rows)
        high = pick_place(refs, place, 2 * pair + 1, slice(LANES, 2 * LANES), rows)
        lane = lane_ids(low.shape)
        span = slice(pair * LANES, (pair + 1) * LANES)
        out_k[:, span] = jnp.where(lane < HALF, low, pltpu.roll(high, HALF, 1))
        out_v[:, span] = jnp.where(lane < HALF, pltpu.roll(low, HALF, 1), high)
    tails = [joined_gains(ref[ref.shape[0] - 2 * GAIN_ROWS :, :].astype(float32)) for ref in refs]
    out_gains[...] = (tails[0] + tails[1]) + (tails[2] + tails[3])


def plane_parts(local):
    return [local] + [send_plane(local, mask) for mask in range(1, PLANE)]


def both_cores(parts):
    mine = jnp.concatenate(parts)
    return mine, swap_cores(mine)


def gather_rows(local):
    return both_cores(plane_parts(local))


def row_tables(lens, slots, total_rows):
    all_lengths = lens.reshape(PLANE, 8, LANES)[:, 0, :slots].astype(jnp.int32)
    ends = jnp.cumsum(all_lengths, axis=1, dtype=jnp.int32)
    row_ids = jnp.arange(total_rows, dtype=jnp.int32)
    begin = jnp.max(
        jnp.where(row_ids[None, :, None] >= ends[:, None, :], ends[:, None, :], 0), axis=2
    )
    position = (row_ids[None, :] - begin).reshape(-1).astype(jnp.float32)
    spread = jnp.arange(LANES, dtype=jnp.int32) % (HEAD_DIM // 2)
    freqs = rope_base ** (-spread.astype(jnp.float32) * 2.0 / HEAD_DIM)
    angles = position[:, None] * freqs[None, :]
    sign = jnp.where(jnp.arange(LANES) % HEAD_DIM < HEAD_DIM // 2, -1.0, 1.0).astype(jnp.float32)
    return ends, (jnp.cos(angles), jnp.sin(angles) * sign)


def body(
    tokens,
    lengths,
    attn_gain,
    query_gain,
    key_gain,
    ffn_gain,
    w_query,
    w_key,
    w_value,
    w_out,
    w_gate,
    w_up,
    w_down,
    cotangent,
):
    dp = lax.axis_index("dp")
    core = lax.axis_index("tensor")
    layers = lax.axis_size("dp") // PLANE
    where = jnp.stack([dp % PLANE, dp // PLANE, core]).astype(jnp.int32)
    local_rows, model = tokens.shape
    total_rows = local_rows * lax.axis_size("tensor")
    rows = w_query.shape[0]
    q_cols = w_query.shape[1] // PLANE
    kv_cols = w_key.shape[1] // PLANE
    local_kv = kv_cols // HEAD_DIM
    share = q_cols // kv_cols
    attn_cols = 2 * q_cols + 2 * kv_cols
    ff_cols = 3 * (w_gate.shape[1] // LANES // PLANE * LANES) + 2 * LANES

    parts, high = attn_rows(rows)
    tall = max(rows, 16)
    first = call(
        pack_attn_kernel,
        [((high, model), bfloat16)] * PLANE,
        where,
        lengths,
        w_query,
        w_key,
        w_value,
        w_out,
        scalars=2,
    )
    second = call(
        pack_ffn_kernel,
        [((tall, ff_cols), bfloat16)] * PLANE,
        where,
        w_gate,
        w_up,
        w_down,
        scalars=1,
    )
    first = after(second, [first[0]] + [send_plane(first[m], m) for m in range(1, PLANE)])
    attn_piece, lens = call(
        unpack_attn_kernel,
        [((PLANE * rows, attn_cols), bfloat16), ((PLANE * 8, LANES), float32)],
        where,
        *first,
        scalars=1,
        scratch=[pltpu.VMEM((PLANE * rows, attn_cols), float32)],
    )
    attn_pieces = [attn_piece] + [send_deep(attn_piece, step) for step in range(1, layers)]
    second = after(first, second)
    second = [second[0]] + [send_plane(second[m], m) for m in range(1, PLANE)]
    ends, tables = row_tables(lens, lengths.shape[1], total_rows)
    second = after((attn_pieces, tables), second)
    (ff_piece,) = call(
        unpack_ffn_kernel,
        [((PLANE * rows, ff_cols), bfloat16)],
        where,
        *second,
        scalars=1,
        scratch=[pltpu.VMEM((PLANE * rows, ff_cols), float32)],
    )
    columns = [list(range(k, layers * PLANE, PLANE)) for k in range(PLANE)]
    ff_weight = lax.all_gather(ff_piece, "dp", axis=0, tiled=True, axis_index_groups=columns)
    attn_pieces = after(ff_piece, attn_pieces)
    tok_parts = plane_parts(after(ff_piece, tokens))
    cot_parts = plane_parts(after(tok_parts, cotangent))
    tok_mine, tok_other = both_cores(tok_parts)
    cot_mine, cot_other = both_cores(cot_parts)

    gains = (
        attn_gain[None, :],
        jnp.concatenate([query_gain, query_gain])[None, :],
        jnp.concatenate([key_gain, key_gain])[None, :],
    )

    inputs = tokens.astype(jnp.float32)
    factor_a = inverse_rms(inputs)
    unit_a = inputs * factor_a
    send, keep, *saved, attn_weight = attn(
        where, ends, tok_mine, tok_other, gains, tables, attn_pieces
    )
    send = after(cot_parts, send)
    hidden = inputs + plane_total(chip_sum(keep, swap_cores(send)))
    factor_b = inverse_rms(hidden)
    unit_b = hidden * factor_b
    x_mine, x_other = gather_rows((unit_b * ffn_gain).astype(jnp.bfloat16))

    act, d_both, ff_grad = ffn_layer(
        where, ends, x_mine, x_other, cot_mine, cot_other, ff_weight
    )
    own_ff = lax.psum_scatter(
        ff_grad, "dp", scatter_dimension=0, tiled=True, axis_index_groups=columns
    )
    dn_send, dn_keep = ffn_apply(0, d_both, ff_weight)
    dn_parts = plane_sent(chip_sum(dn_keep, swap_cores(dn_send)))
    out_send, out_keep = ffn_apply(model, after(dn_send, act), ff_weight)
    d_normed2 = add_up(after(out_send, dn_parts))
    grad_out = jnp.where(
        (jnp.arange(local_rows) + core * local_rows < ends[0, lengths.shape[1] - 1])[:, None],
        cotangent,
        jnp.zeros_like(cotangent),
    )
    gain_ffn = jnp.sum(d_normed2 * unit_b, axis=0)
    d_hidden = grad_out.astype(jnp.float32) + norm_back(d_normed2 * ffn_gain, unit_b, factor_b)
    h_mine, h_other = gather_rows(d_hidden.astype(jnp.bfloat16))
    out_parts = chip_sum(out_keep, swap_cores(out_send))
    out_parts = after((h_mine, h_other), out_parts)
    out_parts = plane_sent(out_parts)
    block_out = (hidden + add_up(out_parts)).astype(jnp.bfloat16)

    send, keep, own_attn, part_gains, *attn_grads = after(
        out_parts,
        attn_back(
            where, ends, layers, tok_mine, tok_other, gains, tables, (h_mine, h_other), saved,
            attn_weight, gain_ffn[None, :],
        ),
    )
    attn_grads = [send_deep(piece, step + 1) for step, piece in enumerate(attn_grads)]
    own_dn, own_ff, *messages = tail_messages(where, keep, swap_cores(send), own_ff)
    own_attn = after(messages, own_attn)
    messages = [send_plane(part, mask + 1) for mask, part in enumerate(messages)]
    attn_parts = plane_split_attn(where, own_attn, attn_grads, part_gains)
    attn_parts = after(messages[:2], plane_sent(attn_parts))
    d_normed = own_dn + add_up([part[:local_rows] for part in messages])
    grad_tokens = d_hidden + norm_back(d_normed * attn_gain, unit_a, factor_a)
    grad_gate, grad_up, grad_down = call(
        place_ffn_kernel,
        [(w_gate.shape, float32)] * 3,
        where,
        own_ff,
        *messages,
        scalars=1,
        scratch=[pltpu.VMEM((PLANE, rows, ff_cols), float32)],
    )
    grad_query, grad_key, grad_value, grad_out_w, sums = call(
        place_attn_kernel,
        [(w.shape, float32) for w in (w_query, w_key, w_value, w_out)]
        + [((GAIN_ROWS, attn_cols), float32)],
        where,
        *attn_parts,
        scalars=1,
    )
    sums = sums + swap_cores(sums)
    return (
        block_out,
        grad_tokens,
        sums[:, :LANES].reshape(-1),
        sums[0, 2 * LANES : 2 * LANES + HEAD_DIM],
        sums[0, 2 * LANES + HEAD_DIM :],
        sums[:, LANES : 2 * LANES].reshape(-1),
        grad_query,
        grad_key,
        grad_value,
        grad_out_w,
        grad_gate,
        grad_up,
        grad_down,
    )


def solution(mesh):
    placed = (
        P(("dp", "tensor"), None),
        P("dp", None),
        P(),
        P(),
        P(),
        P(),
        P("dp", "tensor"),
        P("dp", "tensor"),
        P("dp", "tensor"),
        P("dp", "tensor"),
        P("dp", "tensor"),
        P("dp", "tensor"),
        P("dp", "tensor"),
        P(("dp", "tensor"), None),
    )
    return jax.shard_map(
        body,
        mesh=mesh,
        in_specs=placed,
        out_specs=(
            P(("dp", "tensor"), None),
            P(("dp", "tensor"), None),
            P(),
            P(),
            P(),
            P(),
            P("dp", "tensor"),
            P("dp", "tensor"),
            P("dp", "tensor"),
            P("dp", "tensor"),
            P("dp", "tensor"),
            P("dp", "tensor"),
            P("dp", "tensor"),
        ),
        check_vma=False,
    )
```

```python
import jax
import jax.numpy as jnp
from jax import lax
from jax.experimental import pallas as pl
from jax.experimental.pallas import tpu as pltpu
from jax.sharding import PartitionSpec as P

HEAD_DIM = 64


epsilon = 1e-05
rope_base = 1000000.0
masked_score = -1e30


def inverse_rms(values):
    return lax.rsqrt(jnp.mean(values * values, axis=-1, keepdims=True) + epsilon)


def norm_back(grad_unit, unit, factor):
    return factor * (grad_unit - unit * jnp.mean(grad_unit * unit, axis=-1, keepdims=True))


def matmul(first_op, second_op):
    return jnp.dot(first_op, second_op, preferred_element_type=jnp.float32)


def matmul_nt(first_op, second_op):
    return lax.dot_general(
        first_op, second_op, (((1,), (1,)), ((), ())), preferred_element_type=jnp.float32
    )


def matmul_tn(first_op, second_op):
    return lax.dot_general(
        first_op, second_op, (((0,), (0,)), ((), ())), preferred_element_type=jnp.float32
    )


def seq_layout(seq_lengths, total_rows):
    ends = jnp.cumsum(seq_lengths, dtype=jnp.int32)
    starts = ends - seq_lengths
    row_ids = jnp.arange(total_rows, dtype=jnp.int32)
    segment = jnp.sum(
        (row_ids[:, None] >= ends[None, :]).astype(jnp.int32), axis=1, dtype=jnp.int32
    )
    slot_ids = jnp.arange(seq_lengths.shape[0], dtype=jnp.int32)
    picked = (segment[:, None] == slot_ids[None, :]).astype(jnp.int32)
    begin = (
        jnp.sum(picked * starts[None, :], axis=1, dtype=jnp.int32)
        + (segment == seq_lengths.shape[0]).astype(jnp.int32) * ends[-1]
    )
    allowed = (segment[:, None] == segment[None, :]) & (row_ids[:, None] >= row_ids[None, :])
    return (row_ids - begin, row_ids < ends[-1], allowed)


def rope_tables(position, head_size):
    half_dim = head_size // 2
    freqs = rope_base ** (-jnp.arange(half_dim, dtype=jnp.float32) * 2.0 / head_size)
    angles = position.astype(jnp.float32)[:, None] * freqs[None, :]
    return (jnp.cos(angles)[:, None, :], jnp.sin(angles)[:, None, :])


def rotate(values, cosine, sine):
    half_dim = values.shape[-1] // 2
    first_half = values[..., :half_dim]
    second_half = values[..., half_dim:]
    return jnp.concatenate(
        [first_half * cosine - second_half * sine, second_half * cosine + first_half * sine],
        axis=-1,
    )


def rotate_back(grads, cosine, sine):
    half_dim = grads.shape[-1] // 2
    first_half = grads[..., :half_dim]
    second_half = grads[..., half_dim:]
    return jnp.concatenate(
        [first_half * cosine + second_half * sine, second_half * cosine - first_half * sine],
        axis=-1,
    )

PLANE = 4
LANES = 128
HALF = 64
VMEM_BYTES = 60 * 1024 * 1024
COST = pl.CostEstimate(flops=1024, bytes_accessed=1024, transcendentals=0)


def cost(megabytes):
    return pl.CostEstimate(flops=1024, bytes_accessed=megabytes * 1000000, transcendentals=0)
GAIN_ROWS = 8
GROUPS_STEP = 2
float32 = jnp.float32
bfloat16 = jnp.bfloat16


def send_plane(values, mask):
    count = lax.axis_size("dp")
    return lax.ppermute(values, "dp", [(i, i ^ mask) for i in range(count)])


def send_deep(values, step):
    count = lax.axis_size("dp")
    return lax.ppermute(values, "dp", [(i, (i + PLANE * step) % count) for i in range(count)])


def swap_cores(values):
    return lax.ppermute(values, "tensor", [(0, 1), (1, 0)])


def call(kernel, outs, *operands, scalars=0, scratch=()):
    specs = [pl.BlockSpec(memory_space=pltpu.SMEM)] * scalars
    specs += [pl.BlockSpec(memory_space=pltpu.VMEM)] * (len(operands) - scalars)
    return pl.pallas_call(
        kernel,
        out_shape=[jax.ShapeDtypeStruct(shape, kind) for shape, kind in outs],
        in_specs=specs,
        out_specs=[pl.BlockSpec(memory_space=pltpu.VMEM)] * len(outs),
        scratch_shapes=list(scratch),
        compiler_params=pltpu.CompilerParams(vmem_limit_bytes=VMEM_BYTES),
        cost_estimate=COST,
    )(*operands)


def after(first, second):
    return lax.optimization_barrier((first, second))[1]


def lane_ids(shape):
    return lax.broadcasted_iota(jnp.int32, shape, len(shape) - 1)


def half_tile(ref, first_tile, place, upper):
    start = pl.multiple_of((first_tile + place // 2) * LANES, LANES)
    tile = ref[:, pl.ds(start, LANES)].astype(float32)
    turned = pltpu.roll(tile, HALF, 1)
    odd = place % 2 == 1
    if upper:
        return jnp.where(odd, tile, turned)
    return jnp.where(odd, turned, tile)


def padded(values, rows):
    if values.shape[0] == rows:
        return values
    blank = jnp.zeros((rows - values.shape[0], values.shape[1]), values.dtype)
    return jnp.concatenate([values, blank], axis=0)


def attn_rows(rows):
    return (2, rows // 2) if rows % 32 == 0 else (1, max(rows, 16))


def pack_attn_kernel(where_ref, lengths_ref, w_q, w_k, w_v, w_o, *outs):
    rows = w_q.shape[0]
    parts, high = attn_rows(rows)
    place = where_ref[0]
    lane = lane_ids((rows, LANES))
    for mask, out in enumerate(outs):
        other = place ^ mask
        at = pl.multiple_of(other * LANES, LANES)
        tile = jnp.where(
            lane < HALF, half_tile(w_k, 0, other, False), half_tile(w_v, 0, other, True)
        )
        piece = jnp.concatenate(
            [w_q[:, pl.ds(at, LANES)].astype(float32), tile, w_o[:, pl.ds(at, LANES)].astype(float32)],
            axis=1,
        )
        pieces = [piece[: rows // 2], piece[rows // 2 :]] if parts == 2 else [padded(piece, high)]
        width = piece.shape[1]
        for part, values in enumerate(pieces):
            out[:, part * width : (part + 1) * width] = values.astype(bfloat16)
        free = out.shape[1] - parts * width
        ids = lane_ids((high, free))
        marks = jnp.zeros((high, free), float32)
        for slot in range(lengths_ref.shape[1]):
            marks = jnp.where(ids == free - LANES + slot, lengths_ref[0, slot].astype(float32), marks)
        out[:, parts * width :] = marks.astype(bfloat16)


def pack_ffn_kernel(where_ref, w_g, w_u, w_d, *outs):
    rows = w_g.shape[0]
    big = w_g.shape[1] // LANES // PLANE * LANES
    last = w_g.shape[1] // LANES // PLANE * PLANE
    place = where_ref[0]
    lane = lane_ids((rows, LANES))
    for mask, out in enumerate(outs):
        other = place ^ mask
        at = pl.ds(pl.multiple_of(other * big, LANES), big)
        parts = [w[:, at].astype(float32) for w in (w_g, w_u, w_d)]
        parts.append(
            jnp.where(
                lane < HALF, half_tile(w_g, last, other, False), half_tile(w_u, last, other, True)
            )
        )
        parts.append(jnp.where(lane < HALF, half_tile(w_d, last, other, False), 0.0))
        out[...] = padded(jnp.concatenate(parts, axis=1), out.shape[0]).astype(bfloat16)


def unpack_attn_kernel(where_ref, own, one, two, three, attn_out, lens_out, held):
    rows = attn_out.shape[0] // PLANE
    width = attn_out.shape[1]
    parts, _ = attn_rows(rows)
    place = where_ref[0]
    for mask, message in enumerate((own, one, two, three)):
        at = pl.ds(pl.multiple_of((place ^ mask) * rows, rows), rows)
        values = [
            message[:, part * width : (part + 1) * width].astype(float32) for part in range(parts)
        ]
        held[at, :] = jnp.concatenate(values, axis=0) if parts == 2 else values[0][:rows]
        lens = message[:16, message.shape[1] - LANES :].astype(float32)
        lens_out[mask * 8 : (mask + 1) * 8, :] = lens[:8]
    attn_out[...] = held[...].astype(bfloat16)


def unpack_ffn_kernel(where_ref, own, one, two, three, ffn_out, held):
    rows = ffn_out.shape[0] // PLANE
    place = where_ref[0]
    for mask, message in enumerate((own, one, two, three)):
        at = pl.ds(pl.multiple_of((place ^ mask) * rows, rows), rows)
        held[at, :] = message[...].astype(float32)[:rows]
    ffn_out[...] = held[...].astype(bfloat16)


def head_mean(values):
    low = lane_ids(values.shape) < HALF
    first = jnp.sum(jnp.where(low, values, 0.0), axis=1, keepdims=True)
    second = jnp.sum(jnp.where(low, 0.0, values), axis=1, keepdims=True)
    return jnp.where(low, first, second) * (1.0 / HALF)


def turn_halves(values):
    first = lane_ids(values.shape) % HALF < HALF // 2
    return jnp.where(
        first, pltpu.roll(values, LANES - HALF // 2, 1), pltpu.roll(values, HALF // 2, 1)
    )


def at_head(values, head):
    low = lane_ids(values.shape) < HALF
    if head == 0:
        return jnp.where(low, values, 0.0).astype(bfloat16)
    return jnp.where(low, 0.0, pltpu.roll(values, HALF, 1)).astype(bfloat16)


def group_probs(query, key, begin, row_ids, col_ids):
    scores = matmul_nt(query, key) * HEAD_DIM ** (-0.5)
    scores = jnp.where((col_ids >= begin) & (col_ids <= row_ids), scores, masked_score)
    expd = jnp.exp(scores - jnp.max(scores, axis=1, keepdims=True))
    return expd / jnp.sum(expd, axis=1, keepdims=True)


def group_mask(ends_ref, group, rows):
    row_ids = lax.broadcasted_iota(jnp.int32, (rows, rows), 0)
    col_ids = lax.broadcasted_iota(jnp.int32, (rows, rows), 1)
    begin = jnp.zeros((rows, rows), jnp.int32)
    for slot in range(ends_ref.shape[1]):
        end = ends_ref[group, slot]
        begin = jnp.maximum(begin, jnp.where(row_ids >= end, end, 0))
    return begin, row_ids, col_ids


def group_rows(core, mine, other):
    first = jnp.where(core == 0, mine, other)
    second = jnp.where(core == 0, other, mine)
    return jnp.concatenate([first, second], axis=0)


def deep_rows(depth, step, layers, rows):
    at = lax.rem(depth + step + layers, layers) * rows
    return pl.ds(pl.multiple_of(at, rows), rows)


def attn_kernel(layers, where_ref, ends_ref, tok_m, tok_o, a_gain, q_gain, k_gain, cos, sin, *refs):
    pieces, refs = refs[:layers], refs[layers:]
    send, keep, pre_out, low_out, mixed_out, weight, held = refs
    step = pl.program_id(0)
    depth, core = where_ref[1], where_ref[2]
    local = tok_m.shape[0] // GROUPS_STEP

    @pl.when(step == 0)
    def _():
        for index, piece in enumerate(pieces):
            weight[deep_rows(depth, -index, layers, piece.shape[0]), :] = piece[...]

    for k in range(GROUPS_STEP):
        block = slice(k * local, (k + 1) * local)
        span = slice(2 * k * local, 2 * (k + 1) * local)
        x = group_rows(core, tok_m[block, :].astype(float32), tok_o[block, :].astype(float32))
        normed = (x * inverse_rms(x) * a_gain[...]).astype(bfloat16)
        pre = matmul(normed, weight[:, : 2 * LANES])
        pre_out[span, :] = pre
        cosine, sine = cos[span, :], sin[span, :]
        tiles = []
        for number, gain in enumerate((q_gain[...], k_gain[...])):
            tile = pre[:, number * LANES : (number + 1) * LANES]
            scaled = tile * lax.rsqrt(head_mean(tile * tile) + epsilon) * gain
            tiles.append(scaled * cosine + turn_halves(scaled) * sine)
        lane = lane_ids(tiles[0].shape)
        query = tiles[0].astype(bfloat16)
        key_value = jnp.where(lane < HALF, tiles[1], pre[:, LANES:])
        low_out[span, :LANES] = query
        low_out[span, LANES:] = key_value.astype(bfloat16)
        begin, row_ids, col_ids = group_mask(ends_ref, GROUPS_STEP * step + k, x.shape[0])
        turned = pltpu.roll(key_value, HALF, 1)
        mixed = jnp.zeros(tiles[0].shape, float32)
        for head in range(2):
            probs = group_probs(query, at_head(key_value, head), begin, row_ids, col_ids)
            mixed += matmul(probs.astype(bfloat16), at_head(turned, head))
        mixed = mixed.astype(bfloat16)
        mixed_out[span, :] = mixed
        held[span, :] = matmul_nt(mixed, weight[:, 2 * LANES :])
        mine = pl.multiple_of(2 * k * local + core * local, local)
        other = pl.multiple_of(2 * k * local + (1 - core) * local, local)
        send[block, :] = held[pl.ds(other, local), :].astype(bfloat16)
        keep[block, :] = held[pl.ds(mine, local), :]


def attn_back_kernel(
    where_ref, ends_ref, tok_m, tok_o, a_gain, q_gain, k_gain, cos, sin, dh_m, dh_o,
    pre_ref, low_ref, mixed_ref, weight, gain_ffn, *refs,
):
    send, keep, grad_out, gains_out, held, total, sum_a, sum_qk = refs
    step = pl.program_id(0)
    core = where_ref[2]
    local = tok_m.shape[0] // GROUPS_STEP
    scale = HEAD_DIM ** (-0.5)

    @pl.when(step == 0)
    def _():
        total[...] = jnp.zeros_like(total)
        sum_a[...] = jnp.zeros_like(sum_a)
        sum_qk[...] = jnp.zeros_like(sum_qk)

    normed_rows, d_qkv_rows, d_hidden_rows = [], [], []
    for k in range(GROUPS_STEP):
        block = slice(k * local, (k + 1) * local)
        span = slice(2 * k * local, 2 * (k + 1) * local)
        x = group_rows(core, tok_m[block, :].astype(float32), tok_o[block, :].astype(float32))
        unit_a = x * inverse_rms(x)
        normed_rows.append((unit_a * a_gain[...]).astype(bfloat16))
        d_hidden = group_rows(core, dh_m[block, :], dh_o[block, :])
        d_hidden_rows.append(d_hidden)
        d_mixed = matmul(d_hidden, weight[:, 2 * LANES :]).astype(bfloat16)
        query = low_ref[span, :LANES]
        key_value = low_ref[span, LANES:].astype(float32)
        turned = pltpu.roll(key_value, HALF, 1)
        begin, row_ids, col_ids = group_mask(ends_ref, GROUPS_STEP * step + k, x.shape[0])
        shape = query.shape
        d_query = jnp.zeros(shape, float32)
        d_keys, d_values = [], []
        for head in range(2):
            key = at_head(key_value, head)
            probs = group_probs(query, key, begin, row_ids, col_ids)
            d_values.append(matmul_tn(probs.astype(bfloat16), d_mixed))
            d_probs = matmul_nt(d_mixed, at_head(turned, head))
            centre = jnp.sum(probs * d_probs, axis=1, keepdims=True)
            d_scores = (probs * (d_probs - centre)).astype(bfloat16)
            d_query += matmul(d_scores, key)
            d_keys.append(matmul_tn(d_scores, query))
        d_key = d_keys[0] + pltpu.roll(d_keys[1], HALF, 1)
        d_value = pltpu.roll(d_values[0], HALF, 1) + d_values[1]
        lane = lane_ids(shape)
        cosine, sine = cos[span, :], sin[span, :]
        tiles = []
        for number, (grad, gain) in enumerate(((d_query, q_gain[...]), (d_key, k_gain[...]))):
            grad = grad * scale
            back = grad * cosine - turn_halves(grad) * sine
            tile = pre_ref[span, number * LANES : (number + 1) * LANES]
            factor = lax.rsqrt(head_mean(tile * tile) + epsilon)
            unit = tile * factor
            sum_qk[number : number + 1, :] += jnp.sum(back * unit, axis=0, keepdims=True)
            back = back * gain
            tiles.append(factor * (back - unit * head_mean(back * unit)))
        tiles[1] = jnp.where(lane < HALF, tiles[1], d_value)
        d_qkv = jnp.concatenate(tiles, axis=1).astype(bfloat16)
        d_qkv_rows.append(d_qkv)
        held[span, :] = matmul_nt(d_qkv, weight[:, : 2 * LANES])
        sum_a[...] += jnp.sum(held[span, :] * unit_a, axis=0, keepdims=True)
        mine = pl.multiple_of(2 * k * local + core * local, local)
        other = pl.multiple_of(2 * k * local + (1 - core) * local, local)
        send[block, :] = held[pl.ds(other, local), :].astype(bfloat16)
        keep[block, :] = held[pl.ds(mine, local), :]
    total[:, : 2 * LANES] += matmul_tn(
        jnp.concatenate(normed_rows, axis=0), jnp.concatenate(d_qkv_rows, axis=0)
    )
    total[:, 2 * LANES :] += matmul_tn(jnp.concatenate(d_hidden_rows, axis=0), mixed_ref[...])

    @pl.when(step == pl.num_programs(0) - 1)
    def _():
        for row in range(GAIN_ROWS):
            gains_out[row : row + 1, :LANES] = sum_a[:, row * LANES : (row + 1) * LANES]
            gains_out[row : row + 1, LANES : 2 * LANES] = gain_ffn[:, row * LANES : (row + 1) * LANES]
        q_sum = sum_qk[0:1, :] + pltpu.roll(sum_qk[0:1, :], HALF, 1)
        k_sum = pltpu.roll(sum_qk[1:2, :], HALF, 1)
        qk_sum = jnp.where(lane_ids(q_sum.shape) < HALF, q_sum, k_sum)
        ids = lax.broadcasted_iota(jnp.int32, (GAIN_ROWS, LANES), 0)
        gains_out[:, 2 * LANES :] = jnp.where(ids == 0, qk_sum, 0.0)
        grad_out[...] = total[...].astype(bfloat16)


def attn_specs(rows, width, group_height):
    scalar = pl.BlockSpec(memory_space=pltpu.SMEM)
    block = pl.BlockSpec((rows, width), lambda i: (i, 0))
    gain = pl.BlockSpec((1, width), lambda i: (0, 0))
    small = pl.BlockSpec((1, LANES), lambda i: (0, 0))
    table = pl.BlockSpec((group_height, LANES), lambda i: (i, 0))
    wide = pl.BlockSpec((group_height, 2 * LANES), lambda i: (i, 0))
    return scalar, block, gain, small, table, wide


def whole_spec(shape):
    return pl.BlockSpec(shape, lambda i: (0, 0), pipeline_mode=pl.Buffered(1))


def attn(where, ends, tok_mine, tok_other, gains, tables, pieces):
    layers = len(pieces)
    rows, width = tok_mine.shape
    local = rows // PLANE
    step = GROUPS_STEP * local
    scalar, block, gain, small, table, wide = attn_specs(step, width, 2 * step)
    high, columns = pieces[0].shape
    weight = (layers * high, columns)
    return pl.pallas_call(
        lambda *refs: attn_kernel(layers, *refs),
        grid=(PLANE // GROUPS_STEP,),
        in_specs=[scalar, scalar, block, block, gain, small, small, table, table]
        + [whole_spec((high, columns))] * layers,
        out_specs=[block, block, wide, wide, table, whole_spec(weight)],
        out_shape=[
            jax.ShapeDtypeStruct((rows, width), bfloat16),
            jax.ShapeDtypeStruct((rows, width), float32),
            jax.ShapeDtypeStruct((2 * rows, 2 * LANES), float32),
            jax.ShapeDtypeStruct((2 * rows, 2 * LANES), bfloat16),
            jax.ShapeDtypeStruct((2 * rows, LANES), bfloat16),
            jax.ShapeDtypeStruct(weight, bfloat16),
        ],
        scratch_shapes=[pltpu.VMEM((2 * step, width), float32)],
        compiler_params=pltpu.CompilerParams(vmem_limit_bytes=VMEM_BYTES),
        cost_estimate=cost(36),
    )(where, ends, tok_mine, tok_other, *gains, *tables, *pieces)


def attn_back(where, ends, tok_mine, tok_other, gains, tables, dh, saved, weight, gain_ffn):
    rows, width = tok_mine.shape
    local = rows // PLANE
    step = GROUPS_STEP * local
    scalar, block, gain, small, table, wide = attn_specs(step, width, 2 * step)
    columns = weight.shape[1]
    return pl.pallas_call(
        attn_back_kernel,
        grid=(PLANE // GROUPS_STEP,),
        in_specs=[scalar, scalar, block, block, gain, small, small, table, table, block, block]
        + [wide, wide, table, whole_spec(weight.shape), gain],
        out_specs=[block, block, whole_spec(weight.shape), whole_spec((GAIN_ROWS, columns))],
        out_shape=[
            jax.ShapeDtypeStruct((rows, width), bfloat16),
            jax.ShapeDtypeStruct((rows, width), float32),
            jax.ShapeDtypeStruct(weight.shape, bfloat16),
            jax.ShapeDtypeStruct((GAIN_ROWS, columns), float32),
        ],
        scratch_shapes=[
            pltpu.VMEM((2 * step, width), float32),
            pltpu.VMEM(weight.shape, float32),
            pltpu.VMEM((1, width), float32),
            pltpu.VMEM((8, LANES), float32),
        ],
        compiler_params=pltpu.CompilerParams(vmem_limit_bytes=VMEM_BYTES),
        cost_estimate=cost(24),
    )(where, ends, tok_mine, tok_other, *gains, *tables, *dh, *saved, weight, gain_ffn)


def ffn_kernel(where_ref, ends_ref, x_o, x_m, g_o, g_m, weight, *refs):
    act_out, d_out, grad_out, total = refs
    step = pl.program_id(0)
    core = where_ref[2]
    both = x_o.shape[1]
    big = both // 2
    local = x_o.shape[0] // 2

    def live_rows(values, group, at_core):
        ids = lax.broadcasted_iota(jnp.int32, values.shape, 0) + at_core * local
        return jnp.where(ids < ends_ref[group, ends_ref.shape[1] - 1], values, jnp.zeros_like(values))

    x = jnp.concatenate([x_o[...], x_m[...]], axis=0)
    grads = jnp.concatenate(
        [live_rows(g_o[k * local : (k + 1) * local, :], 2 * step + k, 1 - core) for k in range(2)]
        + [live_rows(g_m[k * local : (k + 1) * local, :], 2 * step + k, core) for k in range(2)],
        axis=0,
    )
    w_both = weight[:, :both]
    w_down = weight[:, both : both + big]
    w_small = weight[:, both + big : both + big + LANES]
    w_small_down = weight[:, both + big + LANES :]
    lane = lane_ids((x.shape[0], LANES))

    def parts_of(gate, up, d_act):
        sigma = 1.0 / (1.0 + jnp.exp(-gate))
        silu = gate * sigma
        act = silu * up
        d_gate = d_act * up * sigma * (1.0 + gate * (1.0 - sigma))
        return act, d_gate, d_act * silu

    pre = matmul(x, w_both)
    act, d_gate, d_up = parts_of(pre[:, :big], pre[:, big:], matmul(grads, w_down))
    pre = matmul(x, w_small)
    act_s, d_gate_s, d_up_s = parts_of(
        pre, pltpu.roll(pre, HALF, 1), matmul(grads, w_small_down)
    )
    act_s = jnp.where(lane < HALF, act_s, 0.0).astype(bfloat16)
    d_small = jnp.where(lane < HALF, d_gate_s, pltpu.roll(d_up_s, HALF, 1)).astype(bfloat16)
    act = act.astype(bfloat16)
    d_both = jnp.concatenate([d_gate, d_up], axis=1).astype(bfloat16)

    act_out[:, :big] = act
    act_out[:, big:] = act_s
    d_out[:, :both] = d_both
    d_out[:, both:] = d_small
    spans = (
        (slice(0, both), x, d_both),
        (slice(both, both + big), grads, act),
        (slice(both + big, both + big + LANES), x, d_small),
        (slice(both + big + LANES, total.shape[1]), grads, act_s),
    )

    @pl.when(step == 0)
    def _():
        for span, left, right in spans:
            total[:, span] = matmul_tn(left, right)

    @pl.when(step == 1)
    def _():
        for span, left, right in spans:
            grad_out[:, span] = (total[:, span] + matmul_tn(left, right)).astype(bfloat16)


def ffn_layer(where, ends, x_mine, x_other, g_mine, g_other, weight):
    rows, width = x_mine.shape
    row_spec = pl.BlockSpec((rows // 2, width), lambda i: (i, 0))
    scalar = pl.BlockSpec(memory_space=pltpu.SMEM)
    widths = (width // 2 + LANES, width + LANES)
    return pl.pallas_call(
        ffn_kernel,
        grid=(2,),
        in_specs=[scalar, scalar] + [row_spec] * 4 + [whole_spec(weight.shape)],
        out_specs=[pl.BlockSpec((rows, w), lambda i: (i, 0)) for w in widths]
        + [whole_spec(weight.shape)],
        out_shape=[jax.ShapeDtypeStruct((2 * rows, w), bfloat16) for w in widths]
        + [jax.ShapeDtypeStruct(weight.shape, bfloat16)],
        scratch_shapes=[pltpu.VMEM(weight.shape, float32)],
        compiler_params=pltpu.CompilerParams(vmem_limit_bytes=VMEM_BYTES),
        cost_estimate=cost(48),
    )(where, ends, x_other, x_mine, g_other, g_mine, weight)


def ffn_apply_kernel(first, values, weight, send, keep):
    width = values.shape[1] - LANES
    big = send.shape[1] // 2
    small = 3 * big if first == 0 else 3 * big + LANES
    partial = matmul_nt(values[:, :width], weight[:, first : first + width])
    partial = partial + matmul_nt(values[:, width:], weight[:, small : small + LANES])
    half = send.shape[0]
    send[...] = partial[:half].astype(bfloat16)
    keep[...] = partial[half:]


def ffn_apply(first, values, weight):
    rows, width = values.shape[0] // 2, weight.shape[0]
    row_spec = pl.BlockSpec((rows // 2, width), lambda i: (i, 0))
    return pl.pallas_call(
        lambda *refs: ffn_apply_kernel(first, *refs),
        grid=(2,),
        in_specs=[
            pl.BlockSpec((rows, values.shape[1]), lambda i: (i, 0)),
            whole_spec(weight.shape),
        ],
        out_specs=[row_spec] * 2,
        out_shape=[
            jax.ShapeDtypeStruct((rows, width), bfloat16),
            jax.ShapeDtypeStruct((rows, width), float32),
        ],
        compiler_params=pltpu.CompilerParams(vmem_limit_bytes=VMEM_BYTES),
        cost_estimate=cost(14),
    )(values, weight)


def chip_sum_kernel(keep, received, *outs):
    rows = outs[0].shape[0]
    for mask, out in enumerate(outs):
        span = slice(mask * rows, (mask + 1) * rows)
        out[...] = (keep[span, :] + received[span, :].astype(float32)).astype(out.dtype)


def chip_sum(keep, received):
    shape = (keep.shape[0] // PLANE, keep.shape[1])
    outs = [(shape, float32)] + [(shape, bfloat16)] * (PLANE - 1)
    return call(chip_sum_kernel, outs, keep, received)


def plane_sent(parts):
    return [parts[0]] + [send_plane(part, mask + 1) for mask, part in enumerate(parts[1:])]


def plane_total(parts):
    return add_up(plane_sent(parts))


def add_up(parts):
    return sum(part.astype(float32) for part in parts)


def plane_split_kernel(where_ref, own, *refs):
    outs, held = refs[:-1], refs[-1]
    held[...] = own[...].astype(float32)
    place = where_ref[0]
    rows = own.shape[0] // PLANE
    for mask, out in enumerate(outs):
        at = pl.multiple_of((place ^ mask) * rows, rows)
        out[...] = held[pl.ds(at, rows), :].astype(out.dtype)


def plane_split(where, own):
    shape = (own.shape[0] // PLANE, own.shape[1])
    return call(
        plane_split_kernel,
        [(shape, bfloat16)] * PLANE,
        where,
        own,
        scalars=1,
        scratch=[pltpu.VMEM(own.shape, float32)],
    )


def joined_gains(tail):
    return tail[:GAIN_ROWS] + tail[GAIN_ROWS:]


def split_gains(gains):
    top = gains.astype(bfloat16).astype(float32)
    rest = (gains - top).astype(bfloat16).astype(float32)
    return jnp.concatenate([top, rest], axis=0)


def split_attn_kernel(where_ref, own, gains, *refs):
    received, outs = refs[: -PLANE - 2], refs[-PLANE - 2 : -2]
    held, held_gains = refs[-2:]
    layers = len(received) + 1
    depth = where_ref[1]
    for step, part in enumerate((gains,) + received):
        held_gains[deep_rows(depth, -step, layers, GAIN_ROWS), :] = part[...]
    held[...] = own[...].astype(float32)
    sums = held_gains[:GAIN_ROWS, :]
    for layer in range(1, layers):
        sums = sums + held_gains[layer * GAIN_ROWS : (layer + 1) * GAIN_ROWS, :]
    tail = split_gains(sums)
    place = where_ref[0]
    rows = own.shape[0] // PLANE
    for mask, out in enumerate(outs):
        part = held[pl.ds(pl.multiple_of((place ^ mask) * rows, rows), rows), :]
        if mask:
            tall = out.shape[0] - tail.shape[0]
            out[:tall, :] = padded(part, tall).astype(bfloat16)
            out[tall:, :] = tail.astype(bfloat16)
        else:
            out[:rows, :] = part
            out[rows:, :] = tail


def split_attn(where, own, gains, received):
    rows, columns = own.shape[0] // PLANE, own.shape[1]
    tail = 2 * GAIN_ROWS
    shapes = [((rows + tail, columns), float32)]
    shapes += [((max(rows, 16) + tail, columns), bfloat16)] * (PLANE - 1)
    scratch = [
        pltpu.VMEM(own.shape, float32),
        pltpu.VMEM(((len(received) + 1) * GAIN_ROWS, columns), float32),
    ]
    return call(split_attn_kernel, shapes, where, own, gains, *received, scalars=1, scratch=scratch)


def pick_place(refs, place, target, columns, rows):
    value = jnp.zeros((rows, columns.stop - columns.start), float32)
    for mask, ref in enumerate(refs):
        value = jnp.where(place ^ mask == target, ref[:, columns].astype(float32)[:rows], value)
    return value


def place_ffn_kernel(where_ref, own, one, two, three, out_g, out_u, out_d, held):
    place = where_ref[0]
    rows = out_g.shape[0]
    big = out_g.shape[1] // LANES // PLANE * LANES
    last = PLANE * big
    for mask, ref in enumerate((own, one, two, three)):
        held[mask] = ref[...].astype(float32)
        at = pl.ds(pl.multiple_of((place ^ mask) * big, LANES), big)
        for number, out in enumerate((out_g, out_u, out_d)):
            out[:, at] = held[mask, :, number * big : (number + 1) * big]
    for pair in range(PLANE // 2):
        low = held[place ^ (2 * pair), :, 3 * big :]
        high = held[place ^ (2 * pair + 1), :, 3 * big :]
        lane = lane_ids((rows, LANES))
        span = slice(last + pair * LANES, last + (pair + 1) * LANES)
        gu_low, gu_high = low[:, :LANES], high[:, :LANES]
        out_g[:, span] = jnp.where(lane < HALF, gu_low, pltpu.roll(gu_high, HALF, 1))
        out_u[:, span] = jnp.where(lane < HALF, pltpu.roll(gu_low, HALF, 1), gu_high)
        out_d[:, span] = jnp.where(lane < HALF, low[:, LANES:], pltpu.roll(high[:, LANES:], HALF, 1))


def place_attn_kernel(where_ref, own, one, two, three, out_q, out_k, out_v, out_o, out_gains):
    place = where_ref[0]
    refs = (own, one, two, three)
    rows = out_q.shape[0]
    for mask, ref in enumerate(refs):
        at = pl.ds(pl.multiple_of((place ^ mask) * LANES, LANES), LANES)
        out_q[:, at] = ref[:, :LANES].astype(float32)[:rows]
        out_o[:, at] = ref[:, 2 * LANES :].astype(float32)[:rows]
    for pair in range(PLANE // 2):
        low = pick_place(refs, place, 2 * pair, slice(LANES, 2 * LANES), rows)
        high = pick_place(refs, place, 2 * pair + 1, slice(LANES, 2 * LANES), rows)
        lane = lane_ids(low.shape)
        span = slice(pair * LANES, (pair + 1) * LANES)
        out_k[:, span] = jnp.where(lane < HALF, low, pltpu.roll(high, HALF, 1))
        out_v[:, span] = jnp.where(lane < HALF, pltpu.roll(low, HALF, 1), high)
    tails = [joined_gains(ref[ref.shape[0] - 2 * GAIN_ROWS :, :].astype(float32)) for ref in refs]
    out_gains[...] = (tails[0] + tails[1]) + (tails[2] + tails[3])


def plane_parts(local):
    return [local] + [send_plane(local, mask) for mask in range(1, PLANE)]


def both_cores(parts):
    mine = jnp.concatenate(parts)
    return mine, swap_cores(mine)


def gather_rows(local):
    return both_cores(plane_parts(local))


def row_tables(lens, slots, total_rows):
    all_lengths = lens.reshape(PLANE, 8, LANES)[:, 0, :slots].astype(jnp.int32)
    ends = jnp.cumsum(all_lengths, axis=1, dtype=jnp.int32)
    row_ids = jnp.arange(total_rows, dtype=jnp.int32)
    begin = jnp.max(
        jnp.where(row_ids[None, :, None] >= ends[:, None, :], ends[:, None, :], 0), axis=2
    )
    position = (row_ids[None, :] - begin).reshape(-1).astype(jnp.float32)
    spread = jnp.arange(LANES, dtype=jnp.int32) % (HEAD_DIM // 2)
    freqs = rope_base ** (-spread.astype(jnp.float32) * 2.0 / HEAD_DIM)
    angles = position[:, None] * freqs[None, :]
    sign = jnp.where(jnp.arange(LANES) % HEAD_DIM < HEAD_DIM // 2, -1.0, 1.0).astype(jnp.float32)
    return ends, (jnp.cos(angles), jnp.sin(angles) * sign)


def body(
    tokens,
    lengths,
    attn_gain,
    query_gain,
    key_gain,
    ffn_gain,
    w_query,
    w_key,
    w_value,
    w_out,
    w_gate,
    w_up,
    w_down,
    cotangent,
):
    dp = lax.axis_index("dp")
    core = lax.axis_index("tensor")
    layers = lax.axis_size("dp") // PLANE
    where = jnp.stack([dp % PLANE, dp // PLANE, core]).astype(jnp.int32)
    local_rows, model = tokens.shape
    total_rows = local_rows * lax.axis_size("tensor")
    rows = w_query.shape[0]
    q_cols = w_query.shape[1] // PLANE
    kv_cols = w_key.shape[1] // PLANE
    local_kv = kv_cols // HEAD_DIM
    share = q_cols // kv_cols
    attn_cols = 2 * q_cols + 2 * kv_cols
    ff_cols = 3 * (w_gate.shape[1] // LANES // PLANE * LANES) + 2 * LANES

    parts, high = attn_rows(rows)
    tall = max(rows, 16)
    first = call(
        pack_attn_kernel,
        [((high, model), bfloat16)] * PLANE,
        where,
        lengths,
        w_query,
        w_key,
        w_value,
        w_out,
        scalars=2,
    )
    second = call(
        pack_ffn_kernel,
        [((tall, ff_cols), bfloat16)] * PLANE,
        where,
        w_gate,
        w_up,
        w_down,
        scalars=1,
    )
    first = after(second, [first[0]] + [send_plane(first[m], m) for m in range(1, PLANE)])
    attn_piece, lens = call(
        unpack_attn_kernel,
        [((PLANE * rows, attn_cols), bfloat16), ((PLANE * 8, LANES), float32)],
        where,
        *first,
        scalars=1,
        scratch=[pltpu.VMEM((PLANE * rows, attn_cols), float32)],
    )
    attn_pieces = [attn_piece] + [send_deep(attn_piece, step) for step in range(1, layers)]
    second = after(first, second)
    second = [second[0]] + [send_plane(second[m], m) for m in range(1, PLANE)]
    ends, tables = row_tables(lens, lengths.shape[1], total_rows)
    second = after((attn_pieces, tables), second)
    (ff_piece,) = call(
        unpack_ffn_kernel,
        [((PLANE * rows, ff_cols), bfloat16)],
        where,
        *second,
        scalars=1,
        scratch=[pltpu.VMEM((PLANE * rows, ff_cols), float32)],
    )
    columns = [list(range(k, layers * PLANE, PLANE)) for k in range(PLANE)]
    ff_weight = lax.all_gather(ff_piece, "dp", axis=0, tiled=True, axis_index_groups=columns)
    attn_pieces = after(ff_piece, attn_pieces)
    tok_parts = plane_parts(after(ff_piece, tokens))
    cot_parts = plane_parts(after(tok_parts, cotangent))
    tok_mine, tok_other = both_cores(tok_parts)
    cot_mine, cot_other = both_cores(cot_parts)

    gains = (
        attn_gain[None, :],
        jnp.concatenate([query_gain, query_gain])[None, :],
        jnp.concatenate([key_gain, key_gain])[None, :],
    )

    inputs = tokens.astype(jnp.float32)
    factor_a = inverse_rms(inputs)
    unit_a = inputs * factor_a
    send, keep, *saved, attn_weight = attn(
        where, ends, tok_mine, tok_other, gains, tables, attn_pieces
    )
    send = after(cot_parts, send)
    hidden = inputs + plane_total(chip_sum(keep, swap_cores(send)))
    factor_b = inverse_rms(hidden)
    unit_b = hidden * factor_b
    x_mine, x_other = gather_rows((unit_b * ffn_gain).astype(jnp.bfloat16))

    act, d_both, ff_grad = ffn_layer(
        where, ends, x_mine, x_other, cot_mine, cot_other, ff_weight
    )
    own_ff = lax.psum_scatter(
        ff_grad, "dp", scatter_dimension=0, tiled=True, axis_index_groups=columns
    )
    dn_send, dn_keep = ffn_apply(0, d_both, ff_weight)
    dn_parts = plane_sent(chip_sum(dn_keep, swap_cores(dn_send)))
    out_send, out_keep = ffn_apply(model, after(dn_send, act), ff_weight)
    d_normed2 = add_up(after(out_send, dn_parts))
    grad_out = jnp.where(
        (jnp.arange(local_rows) + core * local_rows < ends[0, lengths.shape[1] - 1])[:, None],
        cotangent,
        jnp.zeros_like(cotangent),
    )
    gain_ffn = jnp.sum(d_normed2 * unit_b, axis=0)
    d_hidden = grad_out.astype(jnp.float32) + norm_back(d_normed2 * ffn_gain, unit_b, factor_b)
    h_mine, h_other = gather_rows(d_hidden.astype(jnp.bfloat16))
    out_parts = chip_sum(out_keep, swap_cores(out_send))
    out_parts = after((h_mine, h_other), out_parts)
    out_parts = plane_sent(out_parts)
    block_out = (hidden + add_up(out_parts)).astype(jnp.bfloat16)

    send, keep, attn_grad, part_gains = after(
        out_parts,
        attn_back(
            where, ends, tok_mine, tok_other, gains, tables, (h_mine, h_other), saved,
            attn_weight, gain_ffn[None, :],
        ),
    )
    own_attn = lax.psum_scatter(
        attn_grad, "dp", scatter_dimension=0, tiled=True, axis_index_groups=columns
    )
    ff_parts = plane_split(where, own_ff)
    keep = after(ff_parts, keep)
    ff_parts = plane_sent(ff_parts)
    dn_parts = chip_sum(keep, swap_cores(send))
    part_gains = after(dn_parts, part_gains)
    dn_parts = plane_sent(after(ff_parts[1], dn_parts))
    far_gains = [send_deep(part_gains, step) for step in range(1, layers)]
    own_attn = after((dn_parts[1], block_out, far_gains), own_attn)
    attn_parts = plane_sent(split_attn(where, own_attn, part_gains, far_gains))
    d_normed = add_up(dn_parts)
    grad_tokens = d_hidden + norm_back(d_normed * attn_gain, unit_a, factor_a)
    grad_gate, grad_up, grad_down = call(
        place_ffn_kernel,
        [(w_gate.shape, float32)] * 3,
        where,
        *ff_parts,
        scalars=1,
        scratch=[pltpu.VMEM((PLANE, rows, ff_cols), float32)],
    )
    grad_query, grad_key, grad_value, grad_out_w, sums = call(
        place_attn_kernel,
        [(w.shape, float32) for w in (w_query, w_key, w_value, w_out)]
        + [((GAIN_ROWS, attn_cols), float32)],
        where,
        *attn_parts,
        scalars=1,
    )
    sums = sums + swap_cores(sums)
    return (
        block_out,
        grad_tokens,
        sums[:, :LANES].reshape(-1),
        sums[0, 2 * LANES : 2 * LANES + HEAD_DIM],
        sums[0, 2 * LANES + HEAD_DIM :],
        sums[:, LANES : 2 * LANES].reshape(-1),
        grad_query,
        grad_key,
        grad_value,
        grad_out_w,
        grad_gate,
        grad_up,
        grad_down,
    )


def solution(mesh):
    placed = (
        P(("dp", "tensor"), None),
        P("dp", None),
        P(),
        P(),
        P(),
        P(),
        P("dp", "tensor"),
        P("dp", "tensor"),
        P("dp", "tensor"),
        P("dp", "tensor"),
        P("dp", "tensor"),
        P("dp", "tensor"),
        P("dp", "tensor"),
        P(("dp", "tensor"), None),
    )
    return jax.shard_map(
        body,
        mesh=mesh,
        in_specs=placed,
        out_specs=(
            P(("dp", "tensor"), None),
            P(("dp", "tensor"), None),
            P(),
            P(),
            P(),
            P(),
            P("dp", "tensor"),
            P("dp", "tensor"),
            P("dp", "tensor"),
            P("dp", "tensor"),
            P("dp", "tensor"),
            P("dp", "tensor"),
            P("dp", "tensor"),
        ),
        check_vma=False,
    )
```

```python
import jax
import jax.numpy as jnp
from jax import lax
from jax.experimental import pallas as pl
from jax.experimental.pallas import tpu as pltpu
from jax.sharding import PartitionSpec as P

HEAD_DIM = 64


epsilon = 1e-05
rope_base = 1000000.0
masked_score = -1e30


def inverse_rms(values):
    return lax.rsqrt(jnp.mean(values * values, axis=-1, keepdims=True) + epsilon)


def norm_back(grad_unit, unit, factor):
    return factor * (grad_unit - unit * jnp.mean(grad_unit * unit, axis=-1, keepdims=True))


def matmul(first_op, second_op):
    return jnp.dot(first_op, second_op, preferred_element_type=jnp.float32)


def matmul_nt(first_op, second_op):
    return lax.dot_general(
        first_op, second_op, (((1,), (1,)), ((), ())), preferred_element_type=jnp.float32
    )


def matmul_tn(first_op, second_op):
    return lax.dot_general(
        first_op, second_op, (((0,), (0,)), ((), ())), preferred_element_type=jnp.float32
    )


def seq_layout(seq_lengths, total_rows):
    ends = jnp.cumsum(seq_lengths, dtype=jnp.int32)
    starts = ends - seq_lengths
    row_ids = jnp.arange(total_rows, dtype=jnp.int32)
    segment = jnp.sum(
        (row_ids[:, None] >= ends[None, :]).astype(jnp.int32), axis=1, dtype=jnp.int32
    )
    slot_ids = jnp.arange(seq_lengths.shape[0], dtype=jnp.int32)
    picked = (segment[:, None] == slot_ids[None, :]).astype(jnp.int32)
    begin = (
        jnp.sum(picked * starts[None, :], axis=1, dtype=jnp.int32)
        + (segment == seq_lengths.shape[0]).astype(jnp.int32) * ends[-1]
    )
    allowed = (segment[:, None] == segment[None, :]) & (row_ids[:, None] >= row_ids[None, :])
    return (row_ids - begin, row_ids < ends[-1], allowed)


def rope_tables(position, head_size):
    half_dim = head_size // 2
    freqs = rope_base ** (-jnp.arange(half_dim, dtype=jnp.float32) * 2.0 / head_size)
    angles = position.astype(jnp.float32)[:, None] * freqs[None, :]
    return (jnp.cos(angles)[:, None, :], jnp.sin(angles)[:, None, :])


def rotate(values, cosine, sine):
    half_dim = values.shape[-1] // 2
    first_half = values[..., :half_dim]
    second_half = values[..., half_dim:]
    return jnp.concatenate(
        [first_half * cosine - second_half * sine, second_half * cosine + first_half * sine],
        axis=-1,
    )


def rotate_back(grads, cosine, sine):
    half_dim = grads.shape[-1] // 2
    first_half = grads[..., :half_dim]
    second_half = grads[..., half_dim:]
    return jnp.concatenate(
        [first_half * cosine + second_half * sine, second_half * cosine - first_half * sine],
        axis=-1,
    )

PLANE = 4
LANES = 128
HALF = 64
VMEM_BYTES = 60 * 1024 * 1024
COST = pl.CostEstimate(flops=1024, bytes_accessed=1024, transcendentals=0)


def cost(megabytes):
    return pl.CostEstimate(flops=1024, bytes_accessed=megabytes * 1000000, transcendentals=0)
GAIN_ROWS = 8
GROUPS_STEP = 2
float32 = jnp.float32
bfloat16 = jnp.bfloat16


def send_plane(values, mask):
    count = lax.axis_size("dp")
    return lax.ppermute(values, "dp", [(i, i ^ mask) for i in range(count)])


def send_deep(values, step):
    count = lax.axis_size("dp")
    return lax.ppermute(values, "dp", [(i, (i + PLANE * step) % count) for i in range(count)])


def swap_cores(values):
    return lax.ppermute(values, "tensor", [(0, 1), (1, 0)])


def call(kernel, outs, *operands, scalars=0, scratch=()):
    specs = [pl.BlockSpec(memory_space=pltpu.SMEM)] * scalars
    specs += [pl.BlockSpec(memory_space=pltpu.VMEM)] * (len(operands) - scalars)
    return pl.pallas_call(
        kernel,
        out_shape=[jax.ShapeDtypeStruct(shape, kind) for shape, kind in outs],
        in_specs=specs,
        out_specs=[pl.BlockSpec(memory_space=pltpu.VMEM)] * len(outs),
        scratch_shapes=list(scratch),
        compiler_params=pltpu.CompilerParams(vmem_limit_bytes=VMEM_BYTES),
        cost_estimate=COST,
    )(*operands)


def after(first, second):
    return lax.optimization_barrier((first, second))[1]


def lane_ids(shape):
    return lax.broadcasted_iota(jnp.int32, shape, len(shape) - 1)


def half_tile(ref, first_tile, place, upper):
    start = pl.multiple_of((first_tile + place // 2) * LANES, LANES)
    tile = ref[:, pl.ds(start, LANES)].astype(float32)
    turned = pltpu.roll(tile, HALF, 1)
    odd = place % 2 == 1
    if upper:
        return jnp.where(odd, tile, turned)
    return jnp.where(odd, turned, tile)


def padded(values, rows):
    if values.shape[0] == rows:
        return values
    blank = jnp.zeros((rows - values.shape[0], values.shape[1]), values.dtype)
    return jnp.concatenate([values, blank], axis=0)


def attn_rows(rows):
    return (2, rows // 2) if rows % 32 == 0 else (1, max(rows, 16))


def pack_attn_kernel(where_ref, lengths_ref, w_q, w_k, w_v, w_o, *outs):
    rows = w_q.shape[0]
    parts, high = attn_rows(rows)
    place = where_ref[0]
    lane = lane_ids((rows, LANES))
    for mask, out in enumerate(outs):
        other = place ^ mask
        at = pl.multiple_of(other * LANES, LANES)
        tile = jnp.where(
            lane < HALF, half_tile(w_k, 0, other, False), half_tile(w_v, 0, other, True)
        )
        piece = jnp.concatenate(
            [w_q[:, pl.ds(at, LANES)].astype(float32), tile, w_o[:, pl.ds(at, LANES)].astype(float32)],
            axis=1,
        )
        pieces = [piece[: rows // 2], piece[rows // 2 :]] if parts == 2 else [padded(piece, high)]
        width = piece.shape[1]
        for part, values in enumerate(pieces):
            out[:, part * width : (part + 1) * width] = values.astype(bfloat16)
        free = out.shape[1] - parts * width
        ids = lane_ids((high, free))
        marks = jnp.zeros((high, free), float32)
        for slot in range(lengths_ref.shape[1]):
            marks = jnp.where(ids == free - LANES + slot, lengths_ref[0, slot].astype(float32), marks)
        out[:, parts * width :] = marks.astype(bfloat16)


def pack_ffn_kernel(where_ref, w_g, w_u, w_d, *outs):
    rows = w_g.shape[0]
    big = w_g.shape[1] // LANES // PLANE * LANES
    last = w_g.shape[1] // LANES // PLANE * PLANE
    place = where_ref[0]
    lane = lane_ids((rows, LANES))
    for mask, out in enumerate(outs):
        other = place ^ mask
        at = pl.ds(pl.multiple_of(other * big, LANES), big)
        parts = [w[:, at].astype(float32) for w in (w_g, w_u, w_d)]
        parts.append(
            jnp.where(
                lane < HALF, half_tile(w_g, last, other, False), half_tile(w_u, last, other, True)
            )
        )
        parts.append(jnp.where(lane < HALF, half_tile(w_d, last, other, False), 0.0))
        out[...] = padded(jnp.concatenate(parts, axis=1), out.shape[0]).astype(bfloat16)


def unpack_attn_kernel(where_ref, own, one, two, three, attn_out, lens_out, held):
    rows = attn_out.shape[0] // PLANE
    width = attn_out.shape[1]
    parts, _ = attn_rows(rows)
    place = where_ref[0]
    for mask, message in enumerate((own, one, two, three)):
        at = pl.ds(pl.multiple_of((place ^ mask) * rows, rows), rows)
        values = [
            message[:, part * width : (part + 1) * width].astype(float32) for part in range(parts)
        ]
        held[at, :] = jnp.concatenate(values, axis=0) if parts == 2 else values[0][:rows]
        lens = message[:16, message.shape[1] - LANES :].astype(float32)
        lens_out[mask * 8 : (mask + 1) * 8, :] = lens[:8]
    attn_out[...] = held[...].astype(bfloat16)


def unpack_ffn_kernel(where_ref, own, one, two, three, ffn_out, held):
    rows = ffn_out.shape[0] // PLANE
    place = where_ref[0]
    for mask, message in enumerate((own, one, two, three)):
        at = pl.ds(pl.multiple_of((place ^ mask) * rows, rows), rows)
        held[at, :] = message[...].astype(float32)[:rows]
    ffn_out[...] = held[...].astype(bfloat16)


def head_mean(values):
    low = lane_ids(values.shape) < HALF
    first = jnp.sum(jnp.where(low, values, 0.0), axis=1, keepdims=True)
    second = jnp.sum(jnp.where(low, 0.0, values), axis=1, keepdims=True)
    return jnp.where(low, first, second) * (1.0 / HALF)


def turn_halves(values):
    first = lane_ids(values.shape) % HALF < HALF // 2
    return jnp.where(
        first, pltpu.roll(values, LANES - HALF // 2, 1), pltpu.roll(values, HALF // 2, 1)
    )


def at_head(values, head):
    low = lane_ids(values.shape) < HALF
    if head == 0:
        return jnp.where(low, values, 0.0).astype(bfloat16)
    return jnp.where(low, 0.0, pltpu.roll(values, HALF, 1)).astype(bfloat16)


def group_probs(query, key, begin, row_ids, col_ids):
    scores = matmul_nt(query, key) * HEAD_DIM ** (-0.5)
    scores = jnp.where((col_ids >= begin) & (col_ids <= row_ids), scores, masked_score)
    expd = jnp.exp(scores - jnp.max(scores, axis=1, keepdims=True))
    return expd / jnp.sum(expd, axis=1, keepdims=True)


def group_mask(ends_ref, group, rows):
    row_ids = lax.broadcasted_iota(jnp.int32, (rows, rows), 0)
    col_ids = lax.broadcasted_iota(jnp.int32, (rows, rows), 1)
    begin = jnp.zeros((rows, rows), jnp.int32)
    for slot in range(ends_ref.shape[1]):
        end = ends_ref[group, slot]
        begin = jnp.maximum(begin, jnp.where(row_ids >= end, end, 0))
    return begin, row_ids, col_ids


def group_rows(core, mine, other):
    first = jnp.where(core == 0, mine, other)
    second = jnp.where(core == 0, other, mine)
    return jnp.concatenate([first, second], axis=0)


def deep_rows(depth, step, layers, rows):
    at = lax.rem(depth + step + layers, layers) * rows
    return pl.ds(pl.multiple_of(at, rows), rows)


def attn_kernel(layers, where_ref, ends_ref, tok_m, tok_o, a_gain, q_gain, k_gain, cos, sin, *refs):
    pieces, refs = refs[:layers], refs[layers:]
    send, keep, pre_out, low_out, mixed_out, weight, held = refs
    step = pl.program_id(0)
    depth, core = where_ref[1], where_ref[2]
    local = tok_m.shape[0] // GROUPS_STEP

    @pl.when(step == 0)
    def _():
        for index, piece in enumerate(pieces):
            weight[deep_rows(depth, -index, layers, piece.shape[0]), :] = piece[...]

    for k in range(GROUPS_STEP):
        block = slice(k * local, (k + 1) * local)
        span = slice(2 * k * local, 2 * (k + 1) * local)
        x = group_rows(core, tok_m[block, :].astype(float32), tok_o[block, :].astype(float32))
        normed = (x * inverse_rms(x) * a_gain[...]).astype(bfloat16)
        pre = matmul(normed, weight[:, : 2 * LANES])
        pre_out[span, :] = pre
        cosine, sine = cos[span, :], sin[span, :]
        tiles = []
        for number, gain in enumerate((q_gain[...], k_gain[...])):
            tile = pre[:, number * LANES : (number + 1) * LANES]
            scaled = tile * lax.rsqrt(head_mean(tile * tile) + epsilon) * gain
            tiles.append(scaled * cosine + turn_halves(scaled) * sine)
        lane = lane_ids(tiles[0].shape)
        query = tiles[0].astype(bfloat16)
        key_value = jnp.where(lane < HALF, tiles[1], pre[:, LANES:])
        low_out[span, :LANES] = query
        low_out[span, LANES:] = key_value.astype(bfloat16)
        begin, row_ids, col_ids = group_mask(ends_ref, GROUPS_STEP * step + k, x.shape[0])
        turned = pltpu.roll(key_value, HALF, 1)
        mixed = jnp.zeros(tiles[0].shape, float32)
        for head in range(2):
            probs = group_probs(query, at_head(key_value, head), begin, row_ids, col_ids)
            mixed += matmul(probs.astype(bfloat16), at_head(turned, head))
        mixed = mixed.astype(bfloat16)
        mixed_out[span, :] = mixed
        held[span, :] = matmul_nt(mixed, weight[:, 2 * LANES :])
        mine = pl.multiple_of(2 * k * local + core * local, local)
        other = pl.multiple_of(2 * k * local + (1 - core) * local, local)
        send[block, :] = held[pl.ds(other, local), :].astype(bfloat16)
        keep[block, :] = held[pl.ds(mine, local), :].astype(bfloat16)


def attn_back_kernel(
    where_ref, ends_ref, tok_m, tok_o, a_gain, q_gain, k_gain, cos, sin, dh_m, dh_o,
    pre_ref, low_ref, mixed_ref, weight, gain_ffn, *refs,
):
    send, keep, grad_out, gains_out, held, total, sum_a, sum_qk = refs
    step = pl.program_id(0)
    core = where_ref[2]
    local = tok_m.shape[0] // GROUPS_STEP
    scale = HEAD_DIM ** (-0.5)

    @pl.when(step == 0)
    def _():
        total[...] = jnp.zeros_like(total)
        sum_a[...] = jnp.zeros_like(sum_a)
        sum_qk[...] = jnp.zeros_like(sum_qk)

    normed_rows, d_qkv_rows, d_hidden_rows = [], [], []
    for k in range(GROUPS_STEP):
        block = slice(k * local, (k + 1) * local)
        span = slice(2 * k * local, 2 * (k + 1) * local)
        x = group_rows(core, tok_m[block, :].astype(float32), tok_o[block, :].astype(float32))
        unit_a = x * inverse_rms(x)
        normed_rows.append((unit_a * a_gain[...]).astype(bfloat16))
        d_hidden = group_rows(core, dh_m[block, :], dh_o[block, :])
        d_hidden_rows.append(d_hidden)
        d_mixed = matmul(d_hidden, weight[:, 2 * LANES :]).astype(bfloat16)
        query = low_ref[span, :LANES]
        key_value = low_ref[span, LANES:].astype(float32)
        turned = pltpu.roll(key_value, HALF, 1)
        begin, row_ids, col_ids = group_mask(ends_ref, GROUPS_STEP * step + k, x.shape[0])
        shape = query.shape
        d_query = jnp.zeros(shape, float32)
        d_keys, d_values = [], []
        for head in range(2):
            key = at_head(key_value, head)
            probs = group_probs(query, key, begin, row_ids, col_ids)
            d_values.append(matmul_tn(probs.astype(bfloat16), d_mixed))
            d_probs = matmul_nt(d_mixed, at_head(turned, head))
            centre = jnp.sum(probs * d_probs, axis=1, keepdims=True)
            d_scores = (probs * (d_probs - centre)).astype(bfloat16)
            d_query += matmul(d_scores, key)
            d_keys.append(matmul_tn(d_scores, query))
        d_key = d_keys[0] + pltpu.roll(d_keys[1], HALF, 1)
        d_value = pltpu.roll(d_values[0], HALF, 1) + d_values[1]
        lane = lane_ids(shape)
        cosine, sine = cos[span, :], sin[span, :]
        tiles = []
        for number, (grad, gain) in enumerate(((d_query, q_gain[...]), (d_key, k_gain[...]))):
            grad = grad * scale
            back = grad * cosine - turn_halves(grad) * sine
            tile = pre_ref[span, number * LANES : (number + 1) * LANES]
            factor = lax.rsqrt(head_mean(tile * tile) + epsilon)
            unit = tile * factor
            sum_qk[number : number + 1, :] += jnp.sum(back * unit, axis=0, keepdims=True)
            back = back * gain
            tiles.append(factor * (back - unit * head_mean(back * unit)))
        tiles[1] = jnp.where(lane < HALF, tiles[1], d_value)
        d_qkv = jnp.concatenate(tiles, axis=1).astype(bfloat16)
        d_qkv_rows.append(d_qkv)
        held[span, :] = matmul_nt(d_qkv, weight[:, : 2 * LANES])
        sum_a[...] += jnp.sum(held[span, :] * unit_a, axis=0, keepdims=True)
        mine = pl.multiple_of(2 * k * local + core * local, local)
        other = pl.multiple_of(2 * k * local + (1 - core) * local, local)
        send[block, :] = held[pl.ds(other, local), :].astype(bfloat16)
        keep[block, :] = held[pl.ds(mine, local), :].astype(bfloat16)
    total[:, : 2 * LANES] += matmul_tn(
        jnp.concatenate(normed_rows, axis=0), jnp.concatenate(d_qkv_rows, axis=0)
    )
    total[:, 2 * LANES :] += matmul_tn(jnp.concatenate(d_hidden_rows, axis=0), mixed_ref[...])

    @pl.when(step == pl.num_programs(0) - 1)
    def _():
        for row in range(GAIN_ROWS):
            gains_out[row : row + 1, :LANES] = sum_a[:, row * LANES : (row + 1) * LANES]
            gains_out[row : row + 1, LANES : 2 * LANES] = gain_ffn[:, row * LANES : (row + 1) * LANES]
        q_sum = sum_qk[0:1, :] + pltpu.roll(sum_qk[0:1, :], HALF, 1)
        k_sum = pltpu.roll(sum_qk[1:2, :], HALF, 1)
        qk_sum = jnp.where(lane_ids(q_sum.shape) < HALF, q_sum, k_sum)
        ids = lax.broadcasted_iota(jnp.int32, (GAIN_ROWS, LANES), 0)
        gains_out[:, 2 * LANES :] = jnp.where(ids == 0, qk_sum, 0.0)
        grad_out[...] = total[...].astype(bfloat16)


def attn_specs(rows, width, group_height):
    scalar = pl.BlockSpec(memory_space=pltpu.SMEM)
    block = pl.BlockSpec((rows, width), lambda i: (i, 0))
    gain = pl.BlockSpec((1, width), lambda i: (0, 0))
    small = pl.BlockSpec((1, LANES), lambda i: (0, 0))
    table = pl.BlockSpec((group_height, LANES), lambda i: (i, 0))
    wide = pl.BlockSpec((group_height, 2 * LANES), lambda i: (i, 0))
    return scalar, block, gain, small, table, wide


def whole_spec(shape):
    return pl.BlockSpec(shape, lambda i: (0, 0), pipeline_mode=pl.Buffered(1))


def attn(where, ends, tok_mine, tok_other, gains, tables, pieces):
    layers = len(pieces)
    rows, width = tok_mine.shape
    local = rows // PLANE
    step = GROUPS_STEP * local
    scalar, block, gain, small, table, wide = attn_specs(step, width, 2 * step)
    high, columns = pieces[0].shape
    weight = (layers * high, columns)
    return pl.pallas_call(
        lambda *refs: attn_kernel(layers, *refs),
        grid=(PLANE // GROUPS_STEP,),
        in_specs=[scalar, scalar, block, block, gain, small, small, table, table]
        + [whole_spec((high, columns))] * layers,
        out_specs=[block, block, wide, wide, table, whole_spec(weight)],
        out_shape=[
            jax.ShapeDtypeStruct((rows, width), bfloat16),
            jax.ShapeDtypeStruct((rows, width), bfloat16),
            jax.ShapeDtypeStruct((2 * rows, 2 * LANES), float32),
            jax.ShapeDtypeStruct((2 * rows, 2 * LANES), bfloat16),
            jax.ShapeDtypeStruct((2 * rows, LANES), bfloat16),
            jax.ShapeDtypeStruct(weight, bfloat16),
        ],
        scratch_shapes=[pltpu.VMEM((2 * step, width), float32)],
        compiler_params=pltpu.CompilerParams(vmem_limit_bytes=VMEM_BYTES),
        cost_estimate=cost(36),
    )(where, ends, tok_mine, tok_other, *gains, *tables, *pieces)


def attn_back(where, ends, tok_mine, tok_other, gains, tables, dh, saved, weight, gain_ffn):
    rows, width = tok_mine.shape
    local = rows // PLANE
    step = GROUPS_STEP * local
    scalar, block, gain, small, table, wide = attn_specs(step, width, 2 * step)
    columns = weight.shape[1]
    return pl.pallas_call(
        attn_back_kernel,
        grid=(PLANE // GROUPS_STEP,),
        in_specs=[scalar, scalar, block, block, gain, small, small, table, table, block, block]
        + [wide, wide, table, whole_spec(weight.shape), gain],
        out_specs=[block, block, whole_spec(weight.shape), whole_spec((GAIN_ROWS, columns))],
        out_shape=[
            jax.ShapeDtypeStruct((rows, width), bfloat16),
            jax.ShapeDtypeStruct((rows, width), bfloat16),
            jax.ShapeDtypeStruct(weight.shape, bfloat16),
            jax.ShapeDtypeStruct((GAIN_ROWS, columns), float32),
        ],
        scratch_shapes=[
            pltpu.VMEM((2 * step, width), float32),
            pltpu.VMEM(weight.shape, float32),
            pltpu.VMEM((1, width), float32),
            pltpu.VMEM((8, LANES), float32),
        ],
        compiler_params=pltpu.CompilerParams(vmem_limit_bytes=VMEM_BYTES),
        cost_estimate=cost(24),
    )(where, ends, tok_mine, tok_other, *gains, *tables, *dh, *saved, weight, gain_ffn)


def ffn_kernel(where_ref, ends_ref, x_o, x_m, g_o, g_m, weight, *refs):
    act_out, d_out, grad_out, total = refs
    step = pl.program_id(0)
    core = where_ref[2]
    both = x_o.shape[1]
    big = both // 2
    local = x_o.shape[0] // 2

    def live_rows(values, group, at_core):
        ids = lax.broadcasted_iota(jnp.int32, values.shape, 0) + at_core * local
        return jnp.where(ids < ends_ref[group, ends_ref.shape[1] - 1], values, jnp.zeros_like(values))

    x = jnp.concatenate([x_o[...], x_m[...]], axis=0)
    grads = jnp.concatenate(
        [live_rows(g_o[k * local : (k + 1) * local, :], 2 * step + k, 1 - core) for k in range(2)]
        + [live_rows(g_m[k * local : (k + 1) * local, :], 2 * step + k, core) for k in range(2)],
        axis=0,
    )
    w_both = weight[:, :both]
    w_down = weight[:, both : both + big]
    w_small = weight[:, both + big : both + big + LANES]
    w_small_down = weight[:, both + big + LANES :]
    lane = lane_ids((x.shape[0], LANES))

    def parts_of(gate, up, d_act):
        sigma = 1.0 / (1.0 + jnp.exp(-gate))
        silu = gate * sigma
        act = silu * up
        d_gate = d_act * up * sigma * (1.0 + gate * (1.0 - sigma))
        return act, d_gate, d_act * silu

    pre = matmul(x, w_both)
    act, d_gate, d_up = parts_of(pre[:, :big], pre[:, big:], matmul(grads, w_down))
    pre = matmul(x, w_small)
    act_s, d_gate_s, d_up_s = parts_of(
        pre, pltpu.roll(pre, HALF, 1), matmul(grads, w_small_down)
    )
    act_s = jnp.where(lane < HALF, act_s, 0.0).astype(bfloat16)
    d_small = jnp.where(lane < HALF, d_gate_s, pltpu.roll(d_up_s, HALF, 1)).astype(bfloat16)
    act = act.astype(bfloat16)
    d_both = jnp.concatenate([d_gate, d_up], axis=1).astype(bfloat16)

    act_out[:, :big] = act
    act_out[:, big:] = act_s
    d_out[:, :both] = d_both
    d_out[:, both:] = d_small
    spans = (
        (slice(0, both), x, d_both),
        (slice(both, both + big), grads, act),
        (slice(both + big, both + big + LANES), x, d_small),
        (slice(both + big + LANES, total.shape[1]), grads, act_s),
    )

    @pl.when(step == 0)
    def _():
        for span, left, right in spans:
            total[:, span] = matmul_tn(left, right)

    @pl.when(step == 1)
    def _():
        for span, left, right in spans:
            grad_out[:, span] = (total[:, span] + matmul_tn(left, right)).astype(bfloat16)


def ffn_layer(where, ends, x_mine, x_other, g_mine, g_other, weight):
    rows, width = x_mine.shape
    row_spec = pl.BlockSpec((rows // 2, width), lambda i: (i, 0))
    scalar = pl.BlockSpec(memory_space=pltpu.SMEM)
    widths = (width // 2 + LANES, width + LANES)
    return pl.pallas_call(
        ffn_kernel,
        grid=(2,),
        in_specs=[scalar, scalar] + [row_spec] * 4 + [whole_spec(weight.shape)],
        out_specs=[pl.BlockSpec((rows, w), lambda i: (i, 0)) for w in widths]
        + [whole_spec(weight.shape)],
        out_shape=[jax.ShapeDtypeStruct((2 * rows, w), bfloat16) for w in widths]
        + [jax.ShapeDtypeStruct(weight.shape, bfloat16)],
        scratch_shapes=[pltpu.VMEM(weight.shape, float32)],
        compiler_params=pltpu.CompilerParams(vmem_limit_bytes=VMEM_BYTES),
        cost_estimate=cost(48),
    )(where, ends, x_other, x_mine, g_other, g_mine, weight)


def ffn_apply_kernel(values, weight, small, send, keep):
    width = weight.shape[1]
    partial = matmul_nt(values[:, :width], weight[...])
    partial = partial + matmul_nt(values[:, width:], small[...])
    half = send.shape[0]
    send[...] = partial[:half].astype(bfloat16)
    keep[...] = partial[half:].astype(bfloat16)


def ffn_apply(first, last, values, weight):
    rows, width = values.shape[0] // 2, weight.shape[0]
    columns = values.shape[1] - LANES
    row_spec = pl.BlockSpec((rows // 2, width), lambda i: (i, 0))

    def column_spec(start, size):
        return pl.BlockSpec(
            (width, size), lambda i: (0, start // size), pipeline_mode=pl.Buffered(1)
        )

    return pl.pallas_call(
        ffn_apply_kernel,
        grid=(2,),
        in_specs=[
            pl.BlockSpec((rows, values.shape[1]), lambda i: (i, 0)),
            column_spec(first, columns),
            column_spec(last, LANES),
        ],
        out_specs=[row_spec] * 2,
        out_shape=[jax.ShapeDtypeStruct((rows, width), bfloat16)] * 2,
        compiler_params=pltpu.CompilerParams(vmem_limit_bytes=VMEM_BYTES),
        cost_estimate=cost(14),
    )(values, weight, weight)


def chip_sum_kernel(keep, received, *outs):
    rows = outs[0].shape[0]
    for mask, out in enumerate(outs):
        span = slice(mask * rows, (mask + 1) * rows)
        total = keep[span, :].astype(float32) + received[span, :].astype(float32)
        out[...] = total.astype(out.dtype)


def chip_sum(keep, received):
    shape = (keep.shape[0] // PLANE, keep.shape[1])
    outs = [(shape, float32)] + [(shape, bfloat16)] * (PLANE - 1)
    return call(chip_sum_kernel, outs, keep, received)


def plane_sent(parts):
    return [parts[0]] + [send_plane(part, mask + 1) for mask, part in enumerate(parts[1:])]


def plane_total(parts):
    return add_up(plane_sent(parts))


def add_up(parts):
    return sum(part.astype(float32) for part in parts)


def plane_split_kernel(where_ref, own, *refs):
    outs, held = refs[:-1], refs[-1]
    held[...] = own[...].astype(float32)
    place = where_ref[0]
    rows = own.shape[0] // PLANE
    for mask, out in enumerate(outs):
        at = pl.multiple_of((place ^ mask) * rows, rows)
        out[...] = held[pl.ds(at, rows), :].astype(out.dtype)


def plane_split(where, own):
    shape = (own.shape[0] // PLANE, own.shape[1])
    return call(
        plane_split_kernel,
        [(shape, bfloat16)] * PLANE,
        where,
        own,
        scalars=1,
        scratch=[pltpu.VMEM(own.shape, float32)],
    )


def joined_gains(tail):
    return tail[:GAIN_ROWS] + tail[GAIN_ROWS:]


def split_gains(gains):
    top = gains.astype(bfloat16).astype(float32)
    rest = (gains - top).astype(bfloat16).astype(float32)
    return jnp.concatenate([top, rest], axis=0)


def split_attn_kernel(where_ref, own, gains, *refs):
    received, outs = refs[: -PLANE - 2], refs[-PLANE - 2 : -2]
    held, held_gains = refs[-2:]
    layers = len(received) + 1
    depth = where_ref[1]
    for step, part in enumerate((gains,) + received):
        held_gains[deep_rows(depth, -step, layers, GAIN_ROWS), :] = part[...]
    held[...] = own[...].astype(float32)
    sums = held_gains[:GAIN_ROWS, :]
    for layer in range(1, layers):
        sums = sums + held_gains[layer * GAIN_ROWS : (layer + 1) * GAIN_ROWS, :]
    tail = split_gains(sums)
    place = where_ref[0]
    rows = own.shape[0] // PLANE
    for mask, out in enumerate(outs):
        part = held[pl.ds(pl.multiple_of((place ^ mask) * rows, rows), rows), :]
        if mask:
            tall = out.shape[0] - tail.shape[0]
            out[:tall, :] = padded(part, tall).astype(bfloat16)
            out[tall:, :] = tail.astype(bfloat16)
        else:
            out[:rows, :] = part
            out[rows:, :] = tail


def split_attn(where, own, gains, received):
    rows, columns = own.shape[0] // PLANE, own.shape[1]
    tail = 2 * GAIN_ROWS
    shapes = [((rows + tail, columns), float32)]
    shapes += [((max(rows, 16) + tail, columns), bfloat16)] * (PLANE - 1)
    scratch = [
        pltpu.VMEM(own.shape, float32),
        pltpu.VMEM(((len(received) + 1) * GAIN_ROWS, columns), float32),
    ]
    return call(split_attn_kernel, shapes, where, own, gains, *received, scalars=1, scratch=scratch)


def pick_place(refs, place, target, columns, rows):
    value = jnp.zeros((rows, columns.stop - columns.start), float32)
    for mask, ref in enumerate(refs):
        value = jnp.where(place ^ mask == target, ref[:, columns].astype(float32)[:rows], value)
    return value


def place_ffn_kernel(where_ref, own, one, two, three, out_g, out_u, out_d, held):
    place = where_ref[0]
    rows = out_g.shape[0]
    big = out_g.shape[1] // LANES // PLANE * LANES
    last = PLANE * big
    for mask, ref in enumerate((own, one, two, three)):
        held[mask] = ref[...].astype(float32)
        at = pl.ds(pl.multiple_of((place ^ mask) * big, LANES), big)
        for number, out in enumerate((out_g, out_u, out_d)):
            out[:, at] = held[mask, :, number * big : (number + 1) * big]
    for pair in range(PLANE // 2):
        low = held[place ^ (2 * pair), :, 3 * big :]
        high = held[place ^ (2 * pair + 1), :, 3 * big :]
        lane = lane_ids((rows, LANES))
        span = slice(last + pair * LANES, last + (pair + 1) * LANES)
        gu_low, gu_high = low[:, :LANES], high[:, :LANES]
        out_g[:, span] = jnp.where(lane < HALF, gu_low, pltpu.roll(gu_high, HALF, 1))
        out_u[:, span] = jnp.where(lane < HALF, pltpu.roll(gu_low, HALF, 1), gu_high)
        out_d[:, span] = jnp.where(lane < HALF, low[:, LANES:], pltpu.roll(high[:, LANES:], HALF, 1))


def place_attn_kernel(where_ref, own, one, two, three, out_q, out_k, out_v, out_o, out_gains):
    place = where_ref[0]
    refs = (own, one, two, three)
    rows = out_q.shape[0]
    for mask, ref in enumerate(refs):
        at = pl.ds(pl.multiple_of((place ^ mask) * LANES, LANES), LANES)
        out_q[:, at] = ref[:, :LANES].astype(float32)[:rows]
        out_o[:, at] = ref[:, 2 * LANES :].astype(float32)[:rows]
    for pair in range(PLANE // 2):
        low = pick_place(refs, place, 2 * pair, slice(LANES, 2 * LANES), rows)
        high = pick_place(refs, place, 2 * pair + 1, slice(LANES, 2 * LANES), rows)
        lane = lane_ids(low.shape)
        span = slice(pair * LANES, (pair + 1) * LANES)
        out_k[:, span] = jnp.where(lane < HALF, low, pltpu.roll(high, HALF, 1))
        out_v[:, span] = jnp.where(lane < HALF, pltpu.roll(low, HALF, 1), high)
    tails = [joined_gains(ref[ref.shape[0] - 2 * GAIN_ROWS :, :].astype(float32)) for ref in refs]
    out_gains[...] = (tails[0] + tails[1]) + (tails[2] + tails[3])


def plane_parts(local):
    return [local] + [send_plane(local, mask) for mask in range(1, PLANE)]


def both_cores(parts):
    mine = jnp.concatenate(parts)
    return mine, swap_cores(mine)


def gather_rows(local):
    return both_cores(plane_parts(local))


def row_tables(lens, slots, total_rows):
    all_lengths = lens.reshape(PLANE, 8, LANES)[:, 0, :slots].astype(jnp.int32)
    ends = jnp.cumsum(all_lengths, axis=1, dtype=jnp.int32)
    row_ids = jnp.arange(total_rows, dtype=jnp.int32)
    begin = jnp.max(
        jnp.where(row_ids[None, :, None] >= ends[:, None, :], ends[:, None, :], 0), axis=2
    )
    position = (row_ids[None, :] - begin).reshape(-1).astype(jnp.float32)
    spread = jnp.arange(LANES, dtype=jnp.int32) % (HEAD_DIM // 2)
    freqs = rope_base ** (-spread.astype(jnp.float32) * 2.0 / HEAD_DIM)
    angles = position[:, None] * freqs[None, :]
    sign = jnp.where(jnp.arange(LANES) % HEAD_DIM < HEAD_DIM // 2, -1.0, 1.0).astype(jnp.float32)
    return ends, (jnp.cos(angles), jnp.sin(angles) * sign)


def body(
    tokens,
    lengths,
    attn_gain,
    query_gain,
    key_gain,
    ffn_gain,
    w_query,
    w_key,
    w_value,
    w_out,
    w_gate,
    w_up,
    w_down,
    cotangent,
):
    dp = lax.axis_index("dp")
    core = lax.axis_index("tensor")
    layers = lax.axis_size("dp") // PLANE
    where = jnp.stack([dp % PLANE, dp // PLANE, core]).astype(jnp.int32)
    local_rows, model = tokens.shape
    total_rows = local_rows * lax.axis_size("tensor")
    rows = w_query.shape[0]
    q_cols = w_query.shape[1] // PLANE
    kv_cols = w_key.shape[1] // PLANE
    local_kv = kv_cols // HEAD_DIM
    share = q_cols // kv_cols
    attn_cols = 2 * q_cols + 2 * kv_cols
    ff_cols = 3 * (w_gate.shape[1] // LANES // PLANE * LANES) + 2 * LANES

    parts, high = attn_rows(rows)
    tall = max(rows, 16)
    first = call(
        pack_attn_kernel,
        [((high, model), bfloat16)] * PLANE,
        where,
        lengths,
        w_query,
        w_key,
        w_value,
        w_out,
        scalars=2,
    )
    second = call(
        pack_ffn_kernel,
        [((tall, ff_cols), bfloat16)] * PLANE,
        where,
        w_gate,
        w_up,
        w_down,
        scalars=1,
    )
    first = after(second, [first[0]] + [send_plane(first[m], m) for m in range(1, PLANE)])
    attn_piece, lens = call(
        unpack_attn_kernel,
        [((PLANE * rows, attn_cols), bfloat16), ((PLANE * 8, LANES), float32)],
        where,
        *first,
        scalars=1,
        scratch=[pltpu.VMEM((PLANE * rows, attn_cols), float32)],
    )
    attn_pieces = [attn_piece] + [send_deep(attn_piece, step) for step in range(1, layers)]
    second = after(first, second)
    second = [second[0]] + [send_plane(second[m], m) for m in range(1, PLANE)]
    ends, tables = row_tables(lens, lengths.shape[1], total_rows)
    second = after((attn_pieces, tables), second)
    (ff_piece,) = call(
        unpack_ffn_kernel,
        [((PLANE * rows, ff_cols), bfloat16)],
        where,
        *second,
        scalars=1,
        scratch=[pltpu.VMEM((PLANE * rows, ff_cols), float32)],
    )
    columns = [list(range(k, layers * PLANE, PLANE)) for k in range(PLANE)]
    ff_weight = lax.all_gather(ff_piece, "dp", axis=0, tiled=True, axis_index_groups=columns)
    attn_pieces = after(ff_piece, attn_pieces)
    tok_parts = plane_parts(after(ff_piece, tokens))
    cot_parts = plane_parts(after(tok_parts, cotangent))
    tok_mine, tok_other = both_cores(tok_parts)
    cot_mine, cot_other = both_cores(cot_parts)

    gains = (
        attn_gain[None, :],
        jnp.concatenate([query_gain, query_gain])[None, :],
        jnp.concatenate([key_gain, key_gain])[None, :],
    )

    inputs = tokens.astype(jnp.float32)
    factor_a = inverse_rms(inputs)
    unit_a = inputs * factor_a
    send, keep, *saved, attn_weight = attn(
        where, ends, tok_mine, tok_other, gains, tables, attn_pieces
    )
    send = after(cot_parts, send)
    hidden = inputs + plane_total(chip_sum(keep, swap_cores(send)))
    factor_b = inverse_rms(hidden)
    unit_b = hidden * factor_b
    x_mine, x_other = gather_rows((unit_b * ffn_gain).astype(jnp.bfloat16))

    act, d_both, ff_grad = ffn_layer(
        where, ends, x_mine, x_other, cot_mine, cot_other, ff_weight
    )
    own_ff = lax.psum_scatter(
        ff_grad, "dp", scatter_dimension=0, tiled=True, axis_index_groups=columns
    )
    dn_send, dn_keep = ffn_apply(0, ff_cols - 2 * LANES, d_both, ff_weight)
    dn_parts = plane_sent(chip_sum(dn_keep, swap_cores(dn_send)))
    out_send, out_keep = ffn_apply(model, ff_cols - LANES, after(dn_send, act), ff_weight)
    d_normed2 = add_up(after(out_send, dn_parts))
    grad_out = jnp.where(
        (jnp.arange(local_rows) + core * local_rows < ends[0, lengths.shape[1] - 1])[:, None],
        cotangent,
        jnp.zeros_like(cotangent),
    )
    gain_ffn = jnp.sum(d_normed2 * unit_b, axis=0)
    d_hidden = grad_out.astype(jnp.float32) + norm_back(d_normed2 * ffn_gain, unit_b, factor_b)
    h_mine, h_other = gather_rows(d_hidden.astype(jnp.bfloat16))
    out_parts = chip_sum(out_keep, swap_cores(out_send))
    out_parts = after((h_mine, h_other), out_parts)
    out_parts = plane_sent(out_parts)
    block_out = (hidden + add_up(out_parts)).astype(jnp.bfloat16)

    send, keep, attn_grad, part_gains = after(
        out_parts,
        attn_back(
            where, ends, tok_mine, tok_other, gains, tables, (h_mine, h_other), saved,
            attn_weight, gain_ffn[None, :],
        ),
    )
    own_attn = lax.psum_scatter(
        attn_grad, "dp", scatter_dimension=0, tiled=True, axis_index_groups=columns
    )
    ff_parts = plane_split(where, own_ff)
    keep = after(ff_parts, keep)
    ff_parts = plane_sent(ff_parts)
    dn_parts = chip_sum(keep, swap_cores(send))
    part_gains = after(dn_parts, part_gains + swap_cores(part_gains))
    dn_parts = plane_sent(after(ff_parts[1], dn_parts))
    far_gains = [send_deep(part_gains, step) for step in range(1, layers)]
    own_attn = after((dn_parts[1], block_out, far_gains), own_attn)
    attn_parts = plane_sent(split_attn(where, own_attn, part_gains, far_gains))
    d_normed = add_up(dn_parts)
    grad_tokens = d_hidden + norm_back(d_normed * attn_gain, unit_a, factor_a)
    grad_gate, grad_up, grad_down = call(
        place_ffn_kernel,
        [(w_gate.shape, float32)] * 3,
        where,
        *ff_parts,
        scalars=1,
        scratch=[pltpu.VMEM((PLANE, rows, ff_cols), float32)],
    )
    grad_query, grad_key, grad_value, grad_out_w, sums = call(
        place_attn_kernel,
        [(w.shape, float32) for w in (w_query, w_key, w_value, w_out)]
        + [((GAIN_ROWS, attn_cols), float32)],
        where,
        *attn_parts,
        scalars=1,
    )
    return (
        block_out,
        grad_tokens,
        sums[:, :LANES].reshape(-1),
        sums[0, 2 * LANES : 2 * LANES + HEAD_DIM],
        sums[0, 2 * LANES + HEAD_DIM :],
        sums[:, LANES : 2 * LANES].reshape(-1),
        grad_query,
        grad_key,
        grad_value,
        grad_out_w,
        grad_gate,
        grad_up,
        grad_down,
    )


def solution(mesh):
    placed = (
        P(("dp", "tensor"), None),
        P("dp", None),
        P(),
        P(),
        P(),
        P(),
        P("dp", "tensor"),
        P("dp", "tensor"),
        P("dp", "tensor"),
        P("dp", "tensor"),
        P("dp", "tensor"),
        P("dp", "tensor"),
        P("dp", "tensor"),
        P(("dp", "tensor"), None),
    )
    return jax.shard_map(
        body,
        mesh=mesh,
        in_specs=placed,
        out_specs=(
            P(("dp", "tensor"), None),
            P(("dp", "tensor"), None),
            P(),
            P(),
            P(),
            P(),
            P("dp", "tensor"),
            P("dp", "tensor"),
            P("dp", "tensor"),
            P("dp", "tensor"),
            P("dp", "tensor"),
            P("dp", "tensor"),
            P("dp", "tensor"),
        ),
        check_vma=False,
    )
```

```python
import jax
import jax.numpy as jnp
from jax import lax
from jax.experimental import pallas as pl
from jax.experimental.pallas import tpu as pltpu
from jax.sharding import PartitionSpec as P

HEAD_DIM = 64


epsilon = 1e-05
rope_base = 1000000.0
masked_score = -1e30


def inverse_rms(values):
    return lax.rsqrt(jnp.mean(values * values, axis=-1, keepdims=True) + epsilon)


def norm_back(grad_unit, unit, factor):
    return factor * (grad_unit - unit * jnp.mean(grad_unit * unit, axis=-1, keepdims=True))


def matmul(first_op, second_op):
    return jnp.dot(first_op, second_op, preferred_element_type=jnp.float32)


def matmul_nt(first_op, second_op):
    return lax.dot_general(
        first_op, second_op, (((1,), (1,)), ((), ())), preferred_element_type=jnp.float32
    )


def matmul_tn(first_op, second_op):
    return lax.dot_general(
        first_op, second_op, (((0,), (0,)), ((), ())), preferred_element_type=jnp.float32
    )


def seq_layout(seq_lengths, total_rows):
    ends = jnp.cumsum(seq_lengths, dtype=jnp.int32)
    starts = ends - seq_lengths
    row_ids = jnp.arange(total_rows, dtype=jnp.int32)
    segment = jnp.sum(
        (row_ids[:, None] >= ends[None, :]).astype(jnp.int32), axis=1, dtype=jnp.int32
    )
    slot_ids = jnp.arange(seq_lengths.shape[0], dtype=jnp.int32)
    picked = (segment[:, None] == slot_ids[None, :]).astype(jnp.int32)
    begin = (
        jnp.sum(picked * starts[None, :], axis=1, dtype=jnp.int32)
        + (segment == seq_lengths.shape[0]).astype(jnp.int32) * ends[-1]
    )
    allowed = (segment[:, None] == segment[None, :]) & (row_ids[:, None] >= row_ids[None, :])
    return (row_ids - begin, row_ids < ends[-1], allowed)


def rope_tables(position, head_size):
    half_dim = head_size // 2
    freqs = rope_base ** (-jnp.arange(half_dim, dtype=jnp.float32) * 2.0 / head_size)
    angles = position.astype(jnp.float32)[:, None] * freqs[None, :]
    return (jnp.cos(angles)[:, None, :], jnp.sin(angles)[:, None, :])


def rotate(values, cosine, sine):
    half_dim = values.shape[-1] // 2
    first_half = values[..., :half_dim]
    second_half = values[..., half_dim:]
    return jnp.concatenate(
        [first_half * cosine - second_half * sine, second_half * cosine + first_half * sine],
        axis=-1,
    )


def rotate_back(grads, cosine, sine):
    half_dim = grads.shape[-1] // 2
    first_half = grads[..., :half_dim]
    second_half = grads[..., half_dim:]
    return jnp.concatenate(
        [first_half * cosine + second_half * sine, second_half * cosine - first_half * sine],
        axis=-1,
    )

PLANE = 4
LANES = 128
HALF = 64
VMEM_BYTES = 60 * 1024 * 1024
COST = pl.CostEstimate(flops=1024, bytes_accessed=1024, transcendentals=0)


def cost(megabytes):
    return pl.CostEstimate(flops=1024, bytes_accessed=megabytes * 1000000, transcendentals=0)
GAIN_ROWS = 8
GROUPS_STEP = 2
float32 = jnp.float32
bfloat16 = jnp.bfloat16


def send_plane(values, mask):
    count = lax.axis_size("dp")
    return lax.ppermute(values, "dp", [(i, i ^ mask) for i in range(count)])


def send_deep(values, step):
    count = lax.axis_size("dp")
    return lax.ppermute(values, "dp", [(i, (i + PLANE * step) % count) for i in range(count)])


def swap_cores(values):
    return lax.ppermute(values, "tensor", [(0, 1), (1, 0)])


def call(kernel, outs, *operands, scalars=0, scratch=()):
    specs = [pl.BlockSpec(memory_space=pltpu.SMEM)] * scalars
    specs += [pl.BlockSpec(memory_space=pltpu.VMEM)] * (len(operands) - scalars)
    return pl.pallas_call(
        kernel,
        out_shape=[jax.ShapeDtypeStruct(shape, kind) for shape, kind in outs],
        in_specs=specs,
        out_specs=[pl.BlockSpec(memory_space=pltpu.VMEM)] * len(outs),
        scratch_shapes=list(scratch),
        compiler_params=pltpu.CompilerParams(vmem_limit_bytes=VMEM_BYTES),
        cost_estimate=COST,
    )(*operands)


def after(first, second):
    return lax.optimization_barrier((first, second))[1]


def lane_ids(shape):
    return lax.broadcasted_iota(jnp.int32, shape, len(shape) - 1)


def half_tile(ref, first_tile, place, upper):
    start = pl.multiple_of((first_tile + place // 2) * LANES, LANES)
    tile = ref[:, pl.ds(start, LANES)].astype(float32)
    turned = pltpu.roll(tile, HALF, 1)
    odd = place % 2 == 1
    if upper:
        return jnp.where(odd, tile, turned)
    return jnp.where(odd, turned, tile)


def padded(values, rows):
    if values.shape[0] == rows:
        return values
    blank = jnp.zeros((rows - values.shape[0], values.shape[1]), values.dtype)
    return jnp.concatenate([values, blank], axis=0)


def attn_rows(rows):
    return (2, rows // 2) if rows % 32 == 0 else (1, max(rows, 16))


def pack_attn_kernel(where_ref, lengths_ref, w_q, w_k, w_v, w_o, *outs):
    rows = w_q.shape[0]
    parts, high = attn_rows(rows)
    place = where_ref[0]
    lane = lane_ids((rows, LANES))
    for mask, out in enumerate(outs):
        other = place ^ mask
        at = pl.multiple_of(other * LANES, LANES)
        tile = jnp.where(
            lane < HALF, half_tile(w_k, 0, other, False), half_tile(w_v, 0, other, True)
        )
        piece = jnp.concatenate(
            [w_q[:, pl.ds(at, LANES)].astype(float32), tile, w_o[:, pl.ds(at, LANES)].astype(float32)],
            axis=1,
        )
        pieces = [piece[: rows // 2], piece[rows // 2 :]] if parts == 2 else [padded(piece, high)]
        width = piece.shape[1]
        for part, values in enumerate(pieces):
            out[:, part * width : (part + 1) * width] = values.astype(bfloat16)
        free = out.shape[1] - parts * width
        ids = lane_ids((high, free))
        marks = jnp.zeros((high, free), float32)
        for slot in range(lengths_ref.shape[1]):
            marks = jnp.where(ids == free - LANES + slot, lengths_ref[0, slot].astype(float32), marks)
        out[:, parts * width :] = marks.astype(bfloat16)


def pack_ffn_kernel(where_ref, w_g, w_u, w_d, *outs):
    rows = w_g.shape[0]
    big = w_g.shape[1] // LANES // PLANE * LANES
    last = w_g.shape[1] // LANES // PLANE * PLANE
    place = where_ref[0]
    lane = lane_ids((rows, LANES))
    for mask, out in enumerate(outs):
        other = place ^ mask
        at = pl.ds(pl.multiple_of(other * big, LANES), big)
        parts = [w[:, at].astype(float32) for w in (w_g, w_u, w_d)]
        parts.append(
            jnp.where(
                lane < HALF, half_tile(w_g, last, other, False), half_tile(w_u, last, other, True)
            )
        )
        parts.append(jnp.where(lane < HALF, half_tile(w_d, last, other, False), 0.0))
        out[...] = padded(jnp.concatenate(parts, axis=1), out.shape[0]).astype(bfloat16)


def unpack_attn_kernel(where_ref, own, one, two, three, attn_out, lens_out, held):
    rows = attn_out.shape[0] // PLANE
    width = attn_out.shape[1]
    parts, high = attn_rows(rows)
    place = where_ref[0]
    for mask, message in enumerate((own, one, two, three)):
        start = (place ^ mask) * rows
        if parts == 2:
            for part in range(parts):
                at = pl.ds(pl.multiple_of(start + part * high, high), high)
                attn_out[at, :] = message[:, part * width : (part + 1) * width]
        else:
            at = pl.ds(pl.multiple_of(start, rows), rows)
            held[at, :] = message[:, :width].astype(float32)[:rows]
        lens = message[:16, message.shape[1] - LANES :].astype(float32)
        lens_out[mask * 8 : (mask + 1) * 8, :] = lens[:8]
    if parts != 2:
        attn_out[...] = held[...].astype(bfloat16)


def unpack_ffn_kernel(where_ref, own, one, two, three, ffn_out, held):
    rows = ffn_out.shape[0] // PLANE
    place = where_ref[0]
    direct = rows % 16 == 0
    for mask, message in enumerate((own, one, two, three)):
        at = pl.ds(pl.multiple_of((place ^ mask) * rows, rows), rows)
        if direct:
            ffn_out[at, :] = message[...]
        else:
            held[at, :] = message[...].astype(float32)[:rows]
    if not direct:
        ffn_out[...] = held[...].astype(bfloat16)


def head_mean(values):
    low = lane_ids(values.shape) < HALF
    first = jnp.sum(jnp.where(low, values, 0.0), axis=1, keepdims=True)
    second = jnp.sum(jnp.where(low, 0.0, values), axis=1, keepdims=True)
    return jnp.where(low, first, second) * (1.0 / HALF)


def turn_halves(values):
    first = lane_ids(values.shape) % HALF < HALF // 2
    return jnp.where(
        first, pltpu.roll(values, LANES - HALF // 2, 1), pltpu.roll(values, HALF // 2, 1)
    )


def at_head(values, head):
    low = lane_ids(values.shape) < HALF
    if head == 0:
        return jnp.where(low, values, 0.0).astype(bfloat16)
    return jnp.where(low, 0.0, pltpu.roll(values, HALF, 1)).astype(bfloat16)


def group_probs(query, key, begin, row_ids, col_ids):
    scores = matmul_nt(query, key) * HEAD_DIM ** (-0.5)
    scores = jnp.where((col_ids >= begin) & (col_ids <= row_ids), scores, masked_score)
    expd = jnp.exp(scores - jnp.max(scores, axis=1, keepdims=True))
    return expd / jnp.sum(expd, axis=1, keepdims=True)


def group_mask(ends_ref, group, rows):
    row_ids = lax.broadcasted_iota(jnp.int32, (rows, rows), 0)
    col_ids = lax.broadcasted_iota(jnp.int32, (rows, rows), 1)
    begin = jnp.zeros((rows, rows), jnp.int32)
    for slot in range(ends_ref.shape[1]):
        end = ends_ref[group, slot]
        begin = jnp.maximum(begin, jnp.where(row_ids >= end, end, 0))
    return begin, row_ids, col_ids


def group_rows(core, mine, other):
    first = jnp.where(core == 0, mine, other)
    second = jnp.where(core == 0, other, mine)
    return jnp.concatenate([first, second], axis=0)


def deep_rows(depth, step, layers, rows):
    at = lax.rem(depth + step + layers, layers) * rows
    return pl.ds(pl.multiple_of(at, rows), rows)


def attn_kernel(layers, where_ref, ends_ref, tok_m, tok_o, a_gain, q_gain, k_gain, cos, sin, *refs):
    pieces, refs = refs[:layers], refs[layers:]
    send, keep, pre_out, low_out, mixed_out, weight, held = refs
    step = pl.program_id(0)
    depth, core = where_ref[1], where_ref[2]
    local = tok_m.shape[0] // GROUPS_STEP

    @pl.when(step == 0)
    def _():
        for index, piece in enumerate(pieces):
            weight[deep_rows(depth, -index, layers, piece.shape[0]), :] = piece[...]

    for k in range(GROUPS_STEP):
        block = slice(k * local, (k + 1) * local)
        span = slice(2 * k * local, 2 * (k + 1) * local)
        x = group_rows(core, tok_m[block, :].astype(float32), tok_o[block, :].astype(float32))
        normed = (x * inverse_rms(x) * a_gain[...]).astype(bfloat16)
        pre = matmul(normed, weight[:, : 2 * LANES])
        pre_out[span, :] = pre
        cosine, sine = cos[span, :], sin[span, :]
        tiles = []
        for number, gain in enumerate((q_gain[...], k_gain[...])):
            tile = pre[:, number * LANES : (number + 1) * LANES]
            scaled = tile * lax.rsqrt(head_mean(tile * tile) + epsilon) * gain
            tiles.append(scaled * cosine + turn_halves(scaled) * sine)
        lane = lane_ids(tiles[0].shape)
        query = tiles[0].astype(bfloat16)
        key_value = jnp.where(lane < HALF, tiles[1], pre[:, LANES:])
        low_out[span, :LANES] = query
        low_out[span, LANES:] = key_value.astype(bfloat16)
        begin, row_ids, col_ids = group_mask(ends_ref, GROUPS_STEP * step + k, x.shape[0])
        turned = pltpu.roll(key_value, HALF, 1)
        mixed = jnp.zeros(tiles[0].shape, float32)
        for head in range(2):
            probs = group_probs(query, at_head(key_value, head), begin, row_ids, col_ids)
            mixed += matmul(probs.astype(bfloat16), at_head(turned, head))
        mixed = mixed.astype(bfloat16)
        mixed_out[span, :] = mixed
        held[span, :] = matmul_nt(mixed, weight[:, 2 * LANES :])
        mine = pl.multiple_of(2 * k * local + core * local, local)
        other = pl.multiple_of(2 * k * local + (1 - core) * local, local)
        send[block, :] = held[pl.ds(other, local), :].astype(bfloat16)
        keep[block, :] = held[pl.ds(mine, local), :].astype(bfloat16)


def attn_back_kernel(
    where_ref, ends_ref, tok_m, tok_o, a_gain, q_gain, k_gain, cos, sin, dh_m, dh_o,
    pre_ref, low_ref, mixed_ref, weight, gain_ffn, *refs,
):
    send, keep, grad_out, gains_out, held, total, sum_a, sum_qk = refs
    step = pl.program_id(0)
    core = where_ref[2]
    local = tok_m.shape[0] // GROUPS_STEP
    scale = HEAD_DIM ** (-0.5)

    @pl.when(step == 0)
    def _():
        total[...] = jnp.zeros_like(total)
        sum_a[...] = jnp.zeros_like(sum_a)
        sum_qk[...] = jnp.zeros_like(sum_qk)

    normed_rows, d_qkv_rows, d_hidden_rows = [], [], []
    for k in range(GROUPS_STEP):
        block = slice(k * local, (k + 1) * local)
        span = slice(2 * k * local, 2 * (k + 1) * local)
        x = group_rows(core, tok_m[block, :].astype(float32), tok_o[block, :].astype(float32))
        unit_a = x * inverse_rms(x)
        normed_rows.append((unit_a * a_gain[...]).astype(bfloat16))
        d_hidden = group_rows(core, dh_m[block, :], dh_o[block, :])
        d_hidden_rows.append(d_hidden)
        d_mixed = matmul(d_hidden, weight[:, 2 * LANES :]).astype(bfloat16)
        query = low_ref[span, :LANES]
        key_value = low_ref[span, LANES:].astype(float32)
        turned = pltpu.roll(key_value, HALF, 1)
        begin, row_ids, col_ids = group_mask(ends_ref, GROUPS_STEP * step + k, x.shape[0])
        shape = query.shape
        d_query = jnp.zeros(shape, float32)
        d_keys, d_values = [], []
        for head in range(2):
            key = at_head(key_value, head)
            probs = group_probs(query, key, begin, row_ids, col_ids)
            d_values.append(matmul_tn(probs.astype(bfloat16), d_mixed))
            d_probs = matmul_nt(d_mixed, at_head(turned, head))
            centre = jnp.sum(probs * d_probs, axis=1, keepdims=True)
            d_scores = (probs * (d_probs - centre)).astype(bfloat16)
            d_query += matmul(d_scores, key)
            d_keys.append(matmul_tn(d_scores, query))
        d_key = d_keys[0] + pltpu.roll(d_keys[1], HALF, 1)
        d_value = pltpu.roll(d_values[0], HALF, 1) + d_values[1]
        lane = lane_ids(shape)
        cosine, sine = cos[span, :], sin[span, :]
        tiles = []
        for number, (grad, gain) in enumerate(((d_query, q_gain[...]), (d_key, k_gain[...]))):
            grad = grad * scale
            back = grad * cosine - turn_halves(grad) * sine
            tile = pre_ref[span, number * LANES : (number + 1) * LANES]
            factor = lax.rsqrt(head_mean(tile * tile) + epsilon)
            unit = tile * factor
            sum_qk[number : number + 1, :] += jnp.sum(back * unit, axis=0, keepdims=True)
            back = back * gain
            tiles.append(factor * (back - unit * head_mean(back * unit)))
        tiles[1] = jnp.where(lane < HALF, tiles[1], d_value)
        d_qkv = jnp.concatenate(tiles, axis=1).astype(bfloat16)
        d_qkv_rows.append(d_qkv)
        held[span, :] = matmul_nt(d_qkv, weight[:, : 2 * LANES])
        sum_a[...] += jnp.sum(held[span, :] * unit_a, axis=0, keepdims=True)
        mine = pl.multiple_of(2 * k * local + core * local, local)
        other = pl.multiple_of(2 * k * local + (1 - core) * local, local)
        send[block, :] = held[pl.ds(other, local), :].astype(bfloat16)
        keep[block, :] = held[pl.ds(mine, local), :].astype(bfloat16)
    total[:, : 2 * LANES] += matmul_tn(
        jnp.concatenate(normed_rows, axis=0), jnp.concatenate(d_qkv_rows, axis=0)
    )
    total[:, 2 * LANES :] += matmul_tn(jnp.concatenate(d_hidden_rows, axis=0), mixed_ref[...])

    @pl.when(step == pl.num_programs(0) - 1)
    def _():
        for row in range(GAIN_ROWS):
            gains_out[row : row + 1, :LANES] = sum_a[:, row * LANES : (row + 1) * LANES]
            gains_out[row : row + 1, LANES : 2 * LANES] = gain_ffn[:, row * LANES : (row + 1) * LANES]
        q_sum = sum_qk[0:1, :] + pltpu.roll(sum_qk[0:1, :], HALF, 1)
        k_sum = pltpu.roll(sum_qk[1:2, :], HALF, 1)
        qk_sum = jnp.where(lane_ids(q_sum.shape) < HALF, q_sum, k_sum)
        ids = lax.broadcasted_iota(jnp.int32, (GAIN_ROWS, LANES), 0)
        gains_out[:, 2 * LANES :] = jnp.where(ids == 0, qk_sum, 0.0)
        grad_out[...] = total[...].astype(bfloat16)


def attn_specs(rows, width, group_height):
    scalar = pl.BlockSpec(memory_space=pltpu.SMEM)
    block = pl.BlockSpec((rows, width), lambda i: (i, 0))
    gain = pl.BlockSpec((1, width), lambda i: (0, 0))
    small = pl.BlockSpec((1, LANES), lambda i: (0, 0))
    table = pl.BlockSpec((group_height, LANES), lambda i: (i, 0))
    wide = pl.BlockSpec((group_height, 2 * LANES), lambda i: (i, 0))
    return scalar, block, gain, small, table, wide


def whole_spec(shape):
    return pl.BlockSpec(shape, lambda i: (0, 0), pipeline_mode=pl.Buffered(1))


def attn(where, ends, tok_mine, tok_other, gains, tables, pieces):
    layers = len(pieces)
    rows, width = tok_mine.shape
    local = rows // PLANE
    step = GROUPS_STEP * local
    scalar, block, gain, small, table, wide = attn_specs(step, width, 2 * step)
    high, columns = pieces[0].shape
    weight = (layers * high, columns)
    return pl.pallas_call(
        lambda *refs: attn_kernel(layers, *refs),
        grid=(PLANE // GROUPS_STEP,),
        in_specs=[scalar, scalar, block, block, gain, small, small, table, table]
        + [whole_spec((high, columns))] * layers,
        out_specs=[block, block, wide, wide, table, whole_spec(weight)],
        out_shape=[
            jax.ShapeDtypeStruct((rows, width), bfloat16),
            jax.ShapeDtypeStruct((rows, width), bfloat16),
            jax.ShapeDtypeStruct((2 * rows, 2 * LANES), float32),
            jax.ShapeDtypeStruct((2 * rows, 2 * LANES), bfloat16),
            jax.ShapeDtypeStruct((2 * rows, LANES), bfloat16),
            jax.ShapeDtypeStruct(weight, bfloat16),
        ],
        scratch_shapes=[pltpu.VMEM((2 * step, width), float32)],
        compiler_params=pltpu.CompilerParams(vmem_limit_bytes=VMEM_BYTES),
        cost_estimate=cost(36),
    )(where, ends, tok_mine, tok_other, *gains, *tables, *pieces)


def attn_back(where, ends, tok_mine, tok_other, gains, tables, dh, saved, weight, gain_ffn):
    rows, width = tok_mine.shape
    local = rows // PLANE
    step = GROUPS_STEP * local
    scalar, block, gain, small, table, wide = attn_specs(step, width, 2 * step)
    columns = weight.shape[1]
    return pl.pallas_call(
        attn_back_kernel,
        grid=(PLANE // GROUPS_STEP,),
        in_specs=[scalar, scalar, block, block, gain, small, small, table, table, block, block]
        + [wide, wide, table, whole_spec(weight.shape), gain],
        out_specs=[block, block, whole_spec(weight.shape), whole_spec((GAIN_ROWS, columns))],
        out_shape=[
            jax.ShapeDtypeStruct((rows, width), bfloat16),
            jax.ShapeDtypeStruct((rows, width), bfloat16),
            jax.ShapeDtypeStruct(weight.shape, bfloat16),
            jax.ShapeDtypeStruct((GAIN_ROWS, columns), float32),
        ],
        scratch_shapes=[
            pltpu.VMEM((2 * step, width), float32),
            pltpu.VMEM(weight.shape, float32),
            pltpu.VMEM((1, width), float32),
            pltpu.VMEM((8, LANES), float32),
        ],
        compiler_params=pltpu.CompilerParams(vmem_limit_bytes=VMEM_BYTES),
        cost_estimate=cost(24),
    )(where, ends, tok_mine, tok_other, *gains, *tables, *dh, *saved, weight, gain_ffn)


def ffn_kernel(where_ref, ends_ref, x_o, x_m, g_o, g_m, weight, *refs):
    act_out, d_out, grad_out, total = refs
    step = pl.program_id(0)
    core = where_ref[2]
    both = x_o.shape[1]
    big = both // 2
    local = x_o.shape[0] // 2

    def live_rows(values, group, at_core):
        ids = lax.broadcasted_iota(jnp.int32, values.shape, 0) + at_core * local
        return jnp.where(ids < ends_ref[group, ends_ref.shape[1] - 1], values, jnp.zeros_like(values))

    x = jnp.concatenate([x_o[...], x_m[...]], axis=0)
    grads = jnp.concatenate(
        [live_rows(g_o[k * local : (k + 1) * local, :], 2 * step + k, 1 - core) for k in range(2)]
        + [live_rows(g_m[k * local : (k + 1) * local, :], 2 * step + k, core) for k in range(2)],
        axis=0,
    )
    w_both = weight[:, :both]
    w_down = weight[:, both : both + big]
    w_small = weight[:, both + big : both + big + LANES]
    w_small_down = weight[:, both + big + LANES :]
    lane = lane_ids((x.shape[0], LANES))

    def parts_of(gate, up, d_act):
        sigma = 1.0 / (1.0 + jnp.exp(-gate))
        silu = gate * sigma
        act = silu * up
        d_gate = d_act * up * sigma * (1.0 + gate * (1.0 - sigma))
        return act, d_gate, d_act * silu

    pre = matmul(x, w_both)
    act, d_gate, d_up = parts_of(pre[:, :big], pre[:, big:], matmul(grads, w_down))
    pre = matmul(x, w_small)
    act_s, d_gate_s, d_up_s = parts_of(
        pre, pltpu.roll(pre, HALF, 1), matmul(grads, w_small_down)
    )
    act_s = jnp.where(lane < HALF, act_s, 0.0).astype(bfloat16)
    d_small = jnp.where(lane < HALF, d_gate_s, pltpu.roll(d_up_s, HALF, 1)).astype(bfloat16)
    act = act.astype(bfloat16)
    d_both = jnp.concatenate([d_gate, d_up], axis=1).astype(bfloat16)

    act_out[:, :big] = act
    act_out[:, big:] = act_s
    d_out[:, :both] = d_both
    d_out[:, both:] = d_small
    spans = (
        (slice(0, both), x, d_both),
        (slice(both, both + big), grads, act),
        (slice(both + big, both + big + LANES), x, d_small),
        (slice(both + big + LANES, total.shape[1]), grads, act_s),
    )

    @pl.when(step == 0)
    def _():
        for span, left, right in spans:
            total[:, span] = matmul_tn(left, right)

    @pl.when(step == 1)
    def _():
        for span, left, right in spans:
            grad_out[:, span] = (total[:, span] + matmul_tn(left, right)).astype(bfloat16)


def ffn_layer(where, ends, x_mine, x_other, g_mine, g_other, weight):
    rows, width = x_mine.shape
    row_spec = pl.BlockSpec((rows // 2, width), lambda i: (i, 0))
    scalar = pl.BlockSpec(memory_space=pltpu.SMEM)
    widths = (width // 2 + LANES, width + LANES)
    return pl.pallas_call(
        ffn_kernel,
        grid=(2,),
        in_specs=[scalar, scalar] + [row_spec] * 4 + [whole_spec(weight.shape)],
        out_specs=[pl.BlockSpec((rows, w), lambda i: (i, 0)) for w in widths]
        + [whole_spec(weight.shape)],
        out_shape=[jax.ShapeDtypeStruct((2 * rows, w), bfloat16) for w in widths]
        + [jax.ShapeDtypeStruct(weight.shape, bfloat16)],
        scratch_shapes=[pltpu.VMEM(weight.shape, float32)],
        compiler_params=pltpu.CompilerParams(vmem_limit_bytes=VMEM_BYTES),
        cost_estimate=cost(48),
    )(where, ends, x_other, x_mine, g_other, g_mine, weight)


def ffn_apply_kernel(values, weight, small, send, keep):
    width = weight.shape[1]
    partial = matmul_nt(values[:, :width], weight[...])
    partial = partial + matmul_nt(values[:, width:], small[...])
    half = send.shape[0]
    send[...] = partial[:half].astype(bfloat16)
    keep[...] = partial[half:].astype(bfloat16)


def ffn_apply(first, last, values, weight):
    rows, width = values.shape[0] // 2, weight.shape[0]
    columns = values.shape[1] - LANES
    row_spec = pl.BlockSpec((rows // 2, width), lambda i: (i, 0))

    def column_spec(start, size):
        return pl.BlockSpec(
            (width, size), lambda i: (0, start // size), pipeline_mode=pl.Buffered(1)
        )

    return pl.pallas_call(
        ffn_apply_kernel,
        grid=(2,),
        in_specs=[
            pl.BlockSpec((rows, values.shape[1]), lambda i: (i, 0)),
            column_spec(first, columns),
            column_spec(last, LANES),
        ],
        out_specs=[row_spec] * 2,
        out_shape=[jax.ShapeDtypeStruct((rows, width), bfloat16)] * 2,
        compiler_params=pltpu.CompilerParams(vmem_limit_bytes=VMEM_BYTES),
        cost_estimate=cost(14),
    )(values, weight, weight)


def chip_sum_kernel(keep, received, *outs):
    rows = outs[0].shape[0]
    for mask, out in enumerate(outs):
        span = slice(mask * rows, (mask + 1) * rows)
        total = keep[span, :].astype(float32) + received[span, :].astype(float32)
        out[...] = total.astype(out.dtype)


def chip_sum(keep, received):
    shape = (keep.shape[0] // PLANE, keep.shape[1])
    outs = [(shape, float32)] + [(shape, bfloat16)] * (PLANE - 1)
    return call(chip_sum_kernel, outs, keep, received)


def plane_sent(parts):
    return [parts[0]] + [send_plane(part, mask + 1) for mask, part in enumerate(parts[1:])]


def plane_total(parts):
    return add_up(plane_sent(parts))


def add_up(parts):
    return sum(part.astype(float32) for part in parts)


def plane_split_kernel(where_ref, own, *refs):
    outs, held = refs[:-1], refs[-1]
    held[...] = own[...].astype(float32)
    place = where_ref[0]
    rows = own.shape[0] // PLANE
    for mask, out in enumerate(outs):
        at = pl.multiple_of((place ^ mask) * rows, rows)
        out[...] = held[pl.ds(at, rows), :].astype(out.dtype)


def plane_split(where, own):
    shape = (own.shape[0] // PLANE, own.shape[1])
    return call(
        plane_split_kernel,
        [(shape, bfloat16)] * PLANE,
        where,
        own,
        scalars=1,
        scratch=[pltpu.VMEM(own.shape, float32)],
    )


def joined_gains(tail):
    return tail[:GAIN_ROWS] + tail[GAIN_ROWS:]


def split_gains(gains):
    top = gains.astype(bfloat16).astype(float32)
    rest = (gains - top).astype(bfloat16).astype(float32)
    return jnp.concatenate([top, rest], axis=0)


def split_attn_kernel(where_ref, own, gains, *refs):
    received, outs = refs[: -PLANE - 2], refs[-PLANE - 2 : -2]
    held, held_gains = refs[-2:]
    layers = len(received) + 1
    depth = where_ref[1]
    for step, part in enumerate((gains,) + received):
        held_gains[deep_rows(depth, -step, layers, GAIN_ROWS), :] = part[...]
    held[...] = own[...].astype(float32)
    sums = held_gains[:GAIN_ROWS, :]
    for layer in range(1, layers):
        sums = sums + held_gains[layer * GAIN_ROWS : (layer + 1) * GAIN_ROWS, :]
    tail = split_gains(sums)
    place = where_ref[0]
    rows = own.shape[0] // PLANE
    for mask, out in enumerate(outs):
        part = held[pl.ds(pl.multiple_of((place ^ mask) * rows, rows), rows), :]
        if mask:
            tall = out.shape[0] - tail.shape[0]
            out[:tall, :] = padded(part, tall).astype(bfloat16)
            out[tall:, :] = tail.astype(bfloat16)
        else:
            out[:rows, :] = part
            out[rows:, :] = tail


def split_attn(where, own, gains, received):
    rows, columns = own.shape[0] // PLANE, own.shape[1]
    tail = 2 * GAIN_ROWS
    shapes = [((rows + tail, columns), float32)]
    shapes += [((max(rows, 16) + tail, columns), bfloat16)] * (PLANE - 1)
    scratch = [
        pltpu.VMEM(own.shape, float32),
        pltpu.VMEM(((len(received) + 1) * GAIN_ROWS, columns), float32),
    ]
    return call(split_attn_kernel, shapes, where, own, gains, *received, scalars=1, scratch=scratch)


def pick_place(refs, place, target, columns, rows):
    value = jnp.zeros((rows, columns.stop - columns.start), float32)
    for mask, ref in enumerate(refs):
        value = jnp.where(place ^ mask == target, ref[:, columns].astype(float32)[:rows], value)
    return value


def place_ffn_kernel(where_ref, own, one, two, three, out_g, out_u, out_d, held):
    place = where_ref[0]
    rows = out_g.shape[0]
    big = out_g.shape[1] // LANES // PLANE * LANES
    last = PLANE * big
    for mask, ref in enumerate((own, one, two, three)):
        held[mask] = ref[...].astype(float32)
        at = pl.ds(pl.multiple_of((place ^ mask) * big, LANES), big)
        for number, out in enumerate((out_g, out_u, out_d)):
            out[:, at] = held[mask, :, number * big : (number + 1) * big]
    for pair in range(PLANE // 2):
        low = held[place ^ (2 * pair), :, 3 * big :]
        high = held[place ^ (2 * pair + 1), :, 3 * big :]
        lane = lane_ids((rows, LANES))
        span = slice(last + pair * LANES, last + (pair + 1) * LANES)
        gu_low, gu_high = low[:, :LANES], high[:, :LANES]
        out_g[:, span] = jnp.where(lane < HALF, gu_low, pltpu.roll(gu_high, HALF, 1))
        out_u[:, span] = jnp.where(lane < HALF, pltpu.roll(gu_low, HALF, 1), gu_high)
        out_d[:, span] = jnp.where(lane < HALF, low[:, LANES:], pltpu.roll(high[:, LANES:], HALF, 1))


def place_attn_kernel(
    where_ref, own, one, two, three, out_q, out_k, out_v, out_o, gain_a, gain_f, gain_q, gain_k
):
    place = where_ref[0]
    refs = (own, one, two, three)
    rows = out_q.shape[0]
    for mask, ref in enumerate(refs):
        at = pl.ds(pl.multiple_of((place ^ mask) * LANES, LANES), LANES)
        out_q[:, at] = ref[:, :LANES].astype(float32)[:rows]
        out_o[:, at] = ref[:, 2 * LANES :].astype(float32)[:rows]
    for pair in range(PLANE // 2):
        low = pick_place(refs, place, 2 * pair, slice(LANES, 2 * LANES), rows)
        high = pick_place(refs, place, 2 * pair + 1, slice(LANES, 2 * LANES), rows)
        lane = lane_ids(low.shape)
        span = slice(pair * LANES, (pair + 1) * LANES)
        out_k[:, span] = jnp.where(lane < HALF, low, pltpu.roll(high, HALF, 1))
        out_v[:, span] = jnp.where(lane < HALF, pltpu.roll(low, HALF, 1), high)
    tails = [joined_gains(ref[ref.shape[0] - 2 * GAIN_ROWS :, :].astype(float32)) for ref in refs]
    sums = (tails[0] + tails[1]) + (tails[2] + tails[3])
    gain_a[...] = sums[:, :LANES]
    gain_f[...] = sums[:, LANES : 2 * LANES]
    pair = sums[:, 2 * LANES :]
    gain_q[...] = pair[:1, :HALF]
    gain_k[...] = pltpu.roll(pair, HALF, 1)[:1, :HALF]


def plane_parts(local):
    return [local] + [send_plane(local, mask) for mask in range(1, PLANE)]


def both_cores(parts):
    mine = jnp.concatenate(parts)
    return mine, swap_cores(mine)


def gather_rows(local):
    return both_cores(plane_parts(local))


def row_tables(lens, slots, total_rows):
    all_lengths = lens.reshape(PLANE, 8, LANES)[:, 0, :slots].astype(jnp.int32)
    ends = jnp.cumsum(all_lengths, axis=1, dtype=jnp.int32)
    row_ids = jnp.arange(total_rows, dtype=jnp.int32)
    begin = jnp.max(
        jnp.where(row_ids[None, :, None] >= ends[:, None, :], ends[:, None, :], 0), axis=2
    )
    position = (row_ids[None, :] - begin).reshape(-1).astype(jnp.float32)
    spread = jnp.arange(LANES, dtype=jnp.int32) % (HEAD_DIM // 2)
    freqs = rope_base ** (-spread.astype(jnp.float32) * 2.0 / HEAD_DIM)
    angles = position[:, None] * freqs[None, :]
    sign = jnp.where(jnp.arange(LANES) % HEAD_DIM < HEAD_DIM // 2, -1.0, 1.0).astype(jnp.float32)
    return ends, (jnp.cos(angles), jnp.sin(angles) * sign)


def body(
    tokens,
    lengths,
    attn_gain,
    query_gain,
    key_gain,
    ffn_gain,
    w_query,
    w_key,
    w_value,
    w_out,
    w_gate,
    w_up,
    w_down,
    cotangent,
):
    dp = lax.axis_index("dp")
    core = lax.axis_index("tensor")
    layers = lax.axis_size("dp") // PLANE
    where = jnp.stack([dp % PLANE, dp // PLANE, core]).astype(jnp.int32)
    local_rows, model = tokens.shape
    total_rows = local_rows * lax.axis_size("tensor")
    rows = w_query.shape[0]
    q_cols = w_query.shape[1] // PLANE
    kv_cols = w_key.shape[1] // PLANE
    local_kv = kv_cols // HEAD_DIM
    share = q_cols // kv_cols
    attn_cols = 2 * q_cols + 2 * kv_cols
    ff_cols = 3 * (w_gate.shape[1] // LANES // PLANE * LANES) + 2 * LANES

    parts, high = attn_rows(rows)
    tall = max(rows, 16)
    first = call(
        pack_attn_kernel,
        [((high, model), bfloat16)] * PLANE,
        where,
        lengths,
        w_query,
        w_key,
        w_value,
        w_out,
        scalars=2,
    )
    second = call(
        pack_ffn_kernel,
        [((tall, ff_cols), bfloat16)] * PLANE,
        where,
        w_gate,
        w_up,
        w_down,
        scalars=1,
    )
    first = after(second, [first[0]] + [send_plane(first[m], m) for m in range(1, PLANE)])
    attn_piece, lens = call(
        unpack_attn_kernel,
        [((PLANE * rows, attn_cols), bfloat16), ((PLANE * 8, LANES), float32)],
        where,
        *first,
        scalars=1,
        scratch=[pltpu.VMEM((PLANE * rows, attn_cols), float32)],
    )
    attn_pieces = [attn_piece] + [send_deep(attn_piece, step) for step in range(1, layers)]
    second = after(first, second)
    second = [second[0]] + [send_plane(second[m], m) for m in range(1, PLANE)]
    ends, tables = row_tables(lens, lengths.shape[1], total_rows)
    second = after((attn_pieces, tables), second)
    (ff_piece,) = call(
        unpack_ffn_kernel,
        [((PLANE * rows, ff_cols), bfloat16)],
        where,
        *second,
        scalars=1,
        scratch=[pltpu.VMEM((PLANE * rows, ff_cols), float32)],
    )
    columns = [list(range(k, layers * PLANE, PLANE)) for k in range(PLANE)]
    ff_weight = lax.all_gather(ff_piece, "dp", axis=0, tiled=True, axis_index_groups=columns)
    attn_pieces = after(ff_piece, attn_pieces)
    tok_parts = plane_parts(after(ff_piece, tokens))
    cot_parts = plane_parts(after(tok_parts, cotangent))
    tok_mine, tok_other = both_cores(tok_parts)
    cot_mine, cot_other = both_cores(cot_parts)

    gains = (
        attn_gain[None, :],
        jnp.concatenate([query_gain, query_gain])[None, :],
        jnp.concatenate([key_gain, key_gain])[None, :],
    )

    inputs = tokens.astype(jnp.float32)
    factor_a = inverse_rms(inputs)
    unit_a = inputs * factor_a
    send, keep, *saved, attn_weight = attn(
        where, ends, tok_mine, tok_other, gains, tables, attn_pieces
    )
    send = after(cot_parts, send)
    hidden = inputs + plane_total(chip_sum(keep, swap_cores(send)))
    factor_b = inverse_rms(hidden)
    unit_b = hidden * factor_b
    x_mine, x_other = gather_rows((unit_b * ffn_gain).astype(jnp.bfloat16))

    act, d_both, ff_grad = ffn_layer(
        where, ends, x_mine, x_other, cot_mine, cot_other, ff_weight
    )
    own_ff = lax.psum_scatter(
        ff_grad, "dp", scatter_dimension=0, tiled=True, axis_index_groups=columns
    )
    dn_send, dn_keep = ffn_apply(0, ff_cols - 2 * LANES, d_both, ff_weight)
    dn_parts = plane_sent(chip_sum(dn_keep, swap_cores(dn_send)))
    out_send, out_keep = ffn_apply(model, ff_cols - LANES, after(dn_send, act), ff_weight)
    d_normed2 = add_up(after(out_send, dn_parts))
    grad_out = jnp.where(
        (jnp.arange(local_rows) + core * local_rows < ends[0, lengths.shape[1] - 1])[:, None],
        cotangent,
        jnp.zeros_like(cotangent),
    )
    gain_ffn = jnp.sum(d_normed2 * unit_b, axis=0)
    d_hidden = grad_out.astype(jnp.float32) + norm_back(d_normed2 * ffn_gain, unit_b, factor_b)
    h_mine, h_other = gather_rows(d_hidden.astype(jnp.bfloat16))
    out_parts = chip_sum(out_keep, swap_cores(out_send))
    out_parts = after((h_mine, h_other), out_parts)
    out_parts = plane_sent(out_parts)
    block_out = (hidden + add_up(out_parts)).astype(jnp.bfloat16)

    send, keep, attn_grad, part_gains = after(
        out_parts,
        attn_back(
            where, ends, tok_mine, tok_other, gains, tables, (h_mine, h_other), saved,
            attn_weight, gain_ffn[None, :],
        ),
    )
    own_attn = lax.psum_scatter(
        attn_grad, "dp", scatter_dimension=0, tiled=True, axis_index_groups=columns
    )
    ff_parts = plane_split(where, own_ff)
    keep = after(ff_parts, keep)
    ff_parts = plane_sent(ff_parts)
    dn_parts = chip_sum(keep, swap_cores(send))
    part_gains = after(dn_parts, part_gains + swap_cores(part_gains))
    dn_parts = plane_sent(after(ff_parts[1], dn_parts))
    far_gains = [send_deep(part_gains, step) for step in range(1, layers)]
    own_attn = after((dn_parts[1], block_out, far_gains), own_attn)
    attn_parts = plane_sent(split_attn(where, own_attn, part_gains, far_gains))
    d_normed = add_up(dn_parts)
    grad_tokens = d_hidden + norm_back(d_normed * attn_gain, unit_a, factor_a)
    grad_gate, grad_up, grad_down = call(
        place_ffn_kernel,
        [(w_gate.shape, float32)] * 3,
        where,
        *ff_parts,
        scalars=1,
        scratch=[pltpu.VMEM((PLANE, rows, ff_cols), float32)],
    )
    grad_query, grad_key, grad_value, grad_out_w, *sums = call(
        place_attn_kernel,
        [(w.shape, float32) for w in (w_query, w_key, w_value, w_out)]
        + [((GAIN_ROWS, LANES), float32)] * 2
        + [((1, HEAD_DIM), float32)] * 2,
        where,
        *attn_parts,
        scalars=1,
    )
    return (
        block_out,
        grad_tokens,
        sums[0].reshape(-1),
        sums[2].reshape(-1),
        sums[3].reshape(-1),
        sums[1].reshape(-1),
        grad_query,
        grad_key,
        grad_value,
        grad_out_w,
        grad_gate,
        grad_up,
        grad_down,
    )


def solution(mesh):
    placed = (
        P(("dp", "tensor"), None),
        P("dp", None),
        P(),
        P(),
        P(),
        P(),
        P("dp", "tensor"),
        P("dp", "tensor"),
        P("dp", "tensor"),
        P("dp", "tensor"),
        P("dp", "tensor"),
        P("dp", "tensor"),
        P("dp", "tensor"),
        P(("dp", "tensor"), None),
    )
    return jax.shard_map(
        body,
        mesh=mesh,
        in_specs=placed,
        out_specs=(
            P(("dp", "tensor"), None),
            P(("dp", "tensor"), None),
            P(),
            P(),
            P(),
            P(),
            P("dp", "tensor"),
            P("dp", "tensor"),
            P("dp", "tensor"),
            P("dp", "tensor"),
            P("dp", "tensor"),
            P("dp", "tensor"),
            P("dp", "tensor"),
        ),
        check_vma=False,
    )
```

```python
import jax
import jax.numpy as jnp
from jax import lax
from jax.experimental import pallas as pl
from jax.experimental.pallas import tpu as pltpu
from jax.sharding import PartitionSpec as P

HEAD_DIM = 64


epsilon = 1e-05
rope_base = 1000000.0
masked_score = -1e30


def inverse_rms(values):
    return lax.rsqrt(jnp.mean(values * values, axis=-1, keepdims=True) + epsilon)


def norm_back(grad_unit, unit, factor):
    return factor * (grad_unit - unit * jnp.mean(grad_unit * unit, axis=-1, keepdims=True))


def matmul(first_op, second_op):
    return jnp.dot(first_op, second_op, preferred_element_type=jnp.float32)


def matmul_nt(first_op, second_op):
    return lax.dot_general(
        first_op, second_op, (((1,), (1,)), ((), ())), preferred_element_type=jnp.float32
    )


def matmul_tn(first_op, second_op):
    return lax.dot_general(
        first_op, second_op, (((0,), (0,)), ((), ())), preferred_element_type=jnp.float32
    )


def seq_layout(seq_lengths, total_rows):
    ends = jnp.cumsum(seq_lengths, dtype=jnp.int32)
    starts = ends - seq_lengths
    row_ids = jnp.arange(total_rows, dtype=jnp.int32)
    segment = jnp.sum(
        (row_ids[:, None] >= ends[None, :]).astype(jnp.int32), axis=1, dtype=jnp.int32
    )
    slot_ids = jnp.arange(seq_lengths.shape[0], dtype=jnp.int32)
    picked = (segment[:, None] == slot_ids[None, :]).astype(jnp.int32)
    begin = (
        jnp.sum(picked * starts[None, :], axis=1, dtype=jnp.int32)
        + (segment == seq_lengths.shape[0]).astype(jnp.int32) * ends[-1]
    )
    allowed = (segment[:, None] == segment[None, :]) & (row_ids[:, None] >= row_ids[None, :])
    return (row_ids - begin, row_ids < ends[-1], allowed)


def rope_tables(position, head_size):
    half_dim = head_size // 2
    freqs = rope_base ** (-jnp.arange(half_dim, dtype=jnp.float32) * 2.0 / head_size)
    angles = position.astype(jnp.float32)[:, None] * freqs[None, :]
    return (jnp.cos(angles)[:, None, :], jnp.sin(angles)[:, None, :])


def rotate(values, cosine, sine):
    half_dim = values.shape[-1] // 2
    first_half = values[..., :half_dim]
    second_half = values[..., half_dim:]
    return jnp.concatenate(
        [first_half * cosine - second_half * sine, second_half * cosine + first_half * sine],
        axis=-1,
    )


def rotate_back(grads, cosine, sine):
    half_dim = grads.shape[-1] // 2
    first_half = grads[..., :half_dim]
    second_half = grads[..., half_dim:]
    return jnp.concatenate(
        [first_half * cosine + second_half * sine, second_half * cosine - first_half * sine],
        axis=-1,
    )

PLANE = 4
LANES = 128
HALF = 64
VMEM_BYTES = 60 * 1024 * 1024
COST = pl.CostEstimate(flops=1024, bytes_accessed=1024, transcendentals=0)


def cost(megabytes):
    return pl.CostEstimate(flops=1024, bytes_accessed=megabytes * 1000000, transcendentals=0)
GAIN_ROWS = 8
GROUPS_STEP = 2
float32 = jnp.float32
bfloat16 = jnp.bfloat16


def send_plane(values, mask):
    count = lax.axis_size("dp")
    return lax.ppermute(values, "dp", [(i, i ^ mask) for i in range(count)])


def send_deep(values, step):
    count = lax.axis_size("dp")
    return lax.ppermute(values, "dp", [(i, (i + PLANE * step) % count) for i in range(count)])


def swap_cores(values):
    return lax.ppermute(values, "tensor", [(0, 1), (1, 0)])


def call(kernel, outs, *operands, scalars=0, scratch=()):
    specs = [pl.BlockSpec(memory_space=pltpu.SMEM)] * scalars
    specs += [pl.BlockSpec(memory_space=pltpu.VMEM)] * (len(operands) - scalars)
    return pl.pallas_call(
        kernel,
        out_shape=[jax.ShapeDtypeStruct(shape, kind) for shape, kind in outs],
        in_specs=specs,
        out_specs=[pl.BlockSpec(memory_space=pltpu.VMEM)] * len(outs),
        scratch_shapes=list(scratch),
        compiler_params=pltpu.CompilerParams(vmem_limit_bytes=VMEM_BYTES),
        cost_estimate=COST,
    )(*operands)


def after(first, second):
    return lax.optimization_barrier((first, second))[1]


def lane_ids(shape):
    return lax.broadcasted_iota(jnp.int32, shape, len(shape) - 1)


def half_tile(ref, first_tile, place, upper):
    start = pl.multiple_of((first_tile + place // 2) * LANES, LANES)
    tile = ref[:, pl.ds(start, LANES)].astype(float32)
    turned = pltpu.roll(tile, HALF, 1)
    odd = place % 2 == 1
    if upper:
        return jnp.where(odd, tile, turned)
    return jnp.where(odd, turned, tile)


def padded(values, rows):
    if values.shape[0] == rows:
        return values
    blank = jnp.zeros((rows - values.shape[0], values.shape[1]), values.dtype)
    return jnp.concatenate([values, blank], axis=0)


def attn_rows(rows):
    return (2, rows // 2) if rows % 32 == 0 else (1, max(rows, 16))


def pack_attn_kernel(where_ref, lengths_ref, w_q, w_k, w_v, w_o, *outs):
    rows = w_q.shape[0]
    parts, high = attn_rows(rows)
    place = where_ref[0]
    lane = lane_ids((rows, LANES))
    for mask, out in enumerate(outs):
        other = place ^ mask
        at = pl.multiple_of(other * LANES, LANES)
        tile = jnp.where(
            lane < HALF, half_tile(w_k, 0, other, False), half_tile(w_v, 0, other, True)
        )
        piece = jnp.concatenate(
            [w_q[:, pl.ds(at, LANES)].astype(float32), tile, w_o[:, pl.ds(at, LANES)].astype(float32)],
            axis=1,
        )
        pieces = [piece[: rows // 2], piece[rows // 2 :]] if parts == 2 else [padded(piece, high)]
        width = piece.shape[1]
        for part, values in enumerate(pieces):
            out[:, part * width : (part + 1) * width] = values.astype(bfloat16)
        free = out.shape[1] - parts * width
        ids = lane_ids((high, free))
        marks = jnp.zeros((high, free), float32)
        for slot in range(lengths_ref.shape[1]):
            marks = jnp.where(ids == free - LANES + slot, lengths_ref[0, slot].astype(float32), marks)
        out[:, parts * width :] = marks.astype(bfloat16)


def pack_ffn_kernel(where_ref, w_g, w_u, w_d, *outs):
    rows = w_g.shape[0]
    big = w_g.shape[1] // LANES // PLANE * LANES
    last = w_g.shape[1] // LANES // PLANE * PLANE
    place = where_ref[0]
    lane = lane_ids((rows, LANES))
    for mask, out in enumerate(outs):
        other = place ^ mask
        at = pl.ds(pl.multiple_of(other * big, LANES), big)
        parts = [w[:, at].astype(float32) for w in (w_g, w_u, w_d)]
        parts.append(
            jnp.where(
                lane < HALF, half_tile(w_g, last, other, False), half_tile(w_u, last, other, True)
            )
        )
        parts.append(jnp.where(lane < HALF, half_tile(w_d, last, other, False), 0.0))
        out[...] = padded(jnp.concatenate(parts, axis=1), out.shape[0]).astype(bfloat16)


def unpack_attn_kernel(where_ref, own, one, two, three, attn_out, lens_out, held):
    rows = attn_out.shape[0] // PLANE
    width = attn_out.shape[1]
    parts, high = attn_rows(rows)
    place = where_ref[0]
    for mask, message in enumerate((own, one, two, three)):
        start = (place ^ mask) * rows
        if parts == 2:
            for part in range(parts):
                at = pl.ds(pl.multiple_of(start + part * high, high), high)
                attn_out[at, :] = message[:, part * width : (part + 1) * width]
        else:
            at = pl.ds(pl.multiple_of(start, rows), rows)
            held[at, :] = message[:, :width].astype(float32)[:rows]
        lens = message[:16, message.shape[1] - LANES :].astype(float32)
        lens_out[mask * 8 : (mask + 1) * 8, :] = lens[:8]
    if parts != 2:
        attn_out[...] = held[...].astype(bfloat16)


def unpack_ffn_kernel(where_ref, own, one, two, three, ffn_out, held):
    rows = ffn_out.shape[0] // PLANE
    place = where_ref[0]
    direct = rows % 16 == 0
    for mask, message in enumerate((own, one, two, three)):
        at = pl.ds(pl.multiple_of((place ^ mask) * rows, rows), rows)
        if direct:
            ffn_out[at, :] = message[...]
        else:
            held[at, :] = message[...].astype(float32)[:rows]
    if not direct:
        ffn_out[...] = held[...].astype(bfloat16)


def head_mean(values):
    low = lane_ids(values.shape) < HALF
    first = jnp.sum(jnp.where(low, values, 0.0), axis=1, keepdims=True)
    second = jnp.sum(jnp.where(low, 0.0, values), axis=1, keepdims=True)
    return jnp.where(low, first, second) * (1.0 / HALF)


def turn_halves(values):
    first = lane_ids(values.shape) % HALF < HALF // 2
    return jnp.where(
        first, pltpu.roll(values, LANES - HALF // 2, 1), pltpu.roll(values, HALF // 2, 1)
    )


def at_head(values, head):
    low = lane_ids(values.shape) < HALF
    if head == 0:
        return jnp.where(low, values, 0.0).astype(bfloat16)
    return jnp.where(low, 0.0, pltpu.roll(values, HALF, 1)).astype(bfloat16)


def group_probs(query, key, begin, row_ids, col_ids):
    scores = matmul_nt(query, key) * HEAD_DIM ** (-0.5)
    scores = jnp.where((col_ids >= begin) & (col_ids <= row_ids), scores, masked_score)
    expd = jnp.exp(scores - jnp.max(scores, axis=1, keepdims=True))
    return expd / jnp.sum(expd, axis=1, keepdims=True)


def group_mask(ends_ref, group, rows):
    row_ids = lax.broadcasted_iota(jnp.int32, (rows, rows), 0)
    col_ids = lax.broadcasted_iota(jnp.int32, (rows, rows), 1)
    begin = jnp.zeros((rows, rows), jnp.int32)
    for slot in range(ends_ref.shape[1]):
        end = ends_ref[group, slot]
        begin = jnp.maximum(begin, jnp.where(row_ids >= end, end, 0))
    return begin, row_ids, col_ids


def group_rows(core, mine, other):
    first = jnp.where(core == 0, mine, other)
    second = jnp.where(core == 0, other, mine)
    return jnp.concatenate([first, second], axis=0)


def deep_rows(depth, step, layers, rows):
    at = lax.rem(depth + step + layers, layers) * rows
    return pl.ds(pl.multiple_of(at, rows), rows)


def attn_kernel(layers, where_ref, ends_ref, tok_m, tok_o, a_gain, q_gain, k_gain, cos, sin, *refs):
    pieces, refs = refs[:layers], refs[layers:]
    send, keep, pre_out, low_out, mixed_out, weight, held = refs
    step = pl.program_id(0)
    depth, core = where_ref[1], where_ref[2]
    local = tok_m.shape[0] // GROUPS_STEP

    @pl.when(step == 0)
    def _():
        for index, piece in enumerate(pieces):
            weight[deep_rows(depth, -index, layers, piece.shape[0]), :] = piece[...]

    for k in range(GROUPS_STEP):
        block = slice(k * local, (k + 1) * local)
        span = slice(2 * k * local, 2 * (k + 1) * local)
        x = group_rows(core, tok_m[block, :].astype(float32), tok_o[block, :].astype(float32))
        normed = (x * inverse_rms(x) * a_gain[...]).astype(bfloat16)
        pre = matmul(normed, weight[:, : 2 * LANES])
        pre_out[span, :] = pre
        cosine, sine = cos[span, :], sin[span, :]
        tiles = []
        for number, gain in enumerate((q_gain[...], k_gain[...])):
            tile = pre[:, number * LANES : (number + 1) * LANES]
            scaled = tile * lax.rsqrt(head_mean(tile * tile) + epsilon) * gain
            tiles.append(scaled * cosine + turn_halves(scaled) * sine)
        lane = lane_ids(tiles[0].shape)
        query = tiles[0].astype(bfloat16)
        key_value = jnp.where(lane < HALF, tiles[1], pre[:, LANES:])
        low_out[span, :LANES] = query
        low_out[span, LANES:] = key_value.astype(bfloat16)
        begin, row_ids, col_ids = group_mask(ends_ref, GROUPS_STEP * step + k, x.shape[0])
        turned = pltpu.roll(key_value, HALF, 1)
        mixed = jnp.zeros(tiles[0].shape, float32)
        for head in range(2):
            probs = group_probs(query, at_head(key_value, head), begin, row_ids, col_ids)
            mixed += matmul(probs.astype(bfloat16), at_head(turned, head))
        mixed = mixed.astype(bfloat16)
        mixed_out[span, :] = mixed
        held[span, :] = matmul_nt(mixed, weight[:, 2 * LANES :])
        mine = pl.multiple_of(2 * k * local + core * local, local)
        other = pl.multiple_of(2 * k * local + (1 - core) * local, local)
        send[block, :] = held[pl.ds(other, local), :].astype(bfloat16)
        keep[block, :] = held[pl.ds(mine, local), :].astype(bfloat16)


def attn_back_kernel(
    where_ref, ends_ref, tok_m, tok_o, a_gain, q_gain, k_gain, cos, sin, dh_m, dh_o,
    pre_ref, low_ref, mixed_ref, weight, gain_ffn, *refs,
):
    send, keep, grad_out, gains_out, held, total, sum_a, sum_qk = refs
    step = pl.program_id(0)
    core = where_ref[2]
    local = tok_m.shape[0] // GROUPS_STEP
    scale = HEAD_DIM ** (-0.5)

    @pl.when(step == 0)
    def _():
        total[...] = jnp.zeros_like(total)
        sum_a[...] = jnp.zeros_like(sum_a)
        sum_qk[...] = jnp.zeros_like(sum_qk)

    normed_rows, d_qkv_rows, d_hidden_rows = [], [], []
    for k in range(GROUPS_STEP):
        block = slice(k * local, (k + 1) * local)
        span = slice(2 * k * local, 2 * (k + 1) * local)
        x = group_rows(core, tok_m[block, :].astype(float32), tok_o[block, :].astype(float32))
        unit_a = x * inverse_rms(x)
        normed_rows.append((unit_a * a_gain[...]).astype(bfloat16))
        d_hidden = group_rows(core, dh_m[block, :], dh_o[block, :])
        d_hidden_rows.append(d_hidden)
        d_mixed = matmul(d_hidden, weight[:, 2 * LANES :]).astype(bfloat16)
        query = low_ref[span, :LANES]
        key_value = low_ref[span, LANES:].astype(float32)
        turned = pltpu.roll(key_value, HALF, 1)
        begin, row_ids, col_ids = group_mask(ends_ref, GROUPS_STEP * step + k, x.shape[0])
        shape = query.shape
        d_query = jnp.zeros(shape, float32)
        d_keys, d_values = [], []
        for head in range(2):
            key = at_head(key_value, head)
            probs = group_probs(query, key, begin, row_ids, col_ids)
            d_values.append(matmul_tn(probs.astype(bfloat16), d_mixed))
            d_probs = matmul_nt(d_mixed, at_head(turned, head))
            centre = jnp.sum(probs * d_probs, axis=1, keepdims=True)
            d_scores = (probs * (d_probs - centre)).astype(bfloat16)
            d_query += matmul(d_scores, key)
            d_keys.append(matmul_tn(d_scores, query))
        d_key = d_keys[0] + pltpu.roll(d_keys[1], HALF, 1)
        d_value = pltpu.roll(d_values[0], HALF, 1) + d_values[1]
        lane = lane_ids(shape)
        cosine, sine = cos[span, :], sin[span, :]
        tiles = []
        for number, (grad, gain) in enumerate(((d_query, q_gain[...]), (d_key, k_gain[...]))):
            grad = grad * scale
            back = grad * cosine - turn_halves(grad) * sine
            tile = pre_ref[span, number * LANES : (number + 1) * LANES]
            factor = lax.rsqrt(head_mean(tile * tile) + epsilon)
            unit = tile * factor
            sum_qk[number : number + 1, :] += jnp.sum(back * unit, axis=0, keepdims=True)
            back = back * gain
            tiles.append(factor * (back - unit * head_mean(back * unit)))
        tiles[1] = jnp.where(lane < HALF, tiles[1], d_value)
        d_qkv = jnp.concatenate(tiles, axis=1).astype(bfloat16)
        d_qkv_rows.append(d_qkv)
        held[span, :] = matmul_nt(d_qkv, weight[:, : 2 * LANES])
        sum_a[...] += jnp.sum(held[span, :] * unit_a, axis=0, keepdims=True)
        mine = pl.multiple_of(2 * k * local + core * local, local)
        other = pl.multiple_of(2 * k * local + (1 - core) * local, local)
        send[block, :] = held[pl.ds(other, local), :].astype(bfloat16)
        keep[block, :] = held[pl.ds(mine, local), :].astype(bfloat16)
    total[:, : 2 * LANES] += matmul_tn(
        jnp.concatenate(normed_rows, axis=0), jnp.concatenate(d_qkv_rows, axis=0)
    )
    total[:, 2 * LANES :] += matmul_tn(jnp.concatenate(d_hidden_rows, axis=0), mixed_ref[...])

    @pl.when(step == pl.num_programs(0) - 1)
    def _():
        for row in range(GAIN_ROWS):
            gains_out[row : row + 1, :LANES] = sum_a[:, row * LANES : (row + 1) * LANES]
            gains_out[row : row + 1, LANES : 2 * LANES] = gain_ffn[:, row * LANES : (row + 1) * LANES]
        q_sum = sum_qk[0:1, :] + pltpu.roll(sum_qk[0:1, :], HALF, 1)
        k_sum = pltpu.roll(sum_qk[1:2, :], HALF, 1)
        qk_sum = jnp.where(lane_ids(q_sum.shape) < HALF, q_sum, k_sum)
        ids = lax.broadcasted_iota(jnp.int32, (GAIN_ROWS, LANES), 0)
        gains_out[:, 2 * LANES :] = jnp.where(ids == 0, qk_sum, 0.0)
        grad_out[...] = total[...].astype(bfloat16)


def attn_specs(rows, width, group_height):
    scalar = pl.BlockSpec(memory_space=pltpu.SMEM)
    block = pl.BlockSpec((rows, width), lambda i: (i, 0))
    gain = pl.BlockSpec((1, width), lambda i: (0, 0))
    small = pl.BlockSpec((1, LANES), lambda i: (0, 0))
    table = pl.BlockSpec((group_height, LANES), lambda i: (i, 0))
    wide = pl.BlockSpec((group_height, 2 * LANES), lambda i: (i, 0))
    return scalar, block, gain, small, table, wide


def whole_spec(shape):
    return pl.BlockSpec(shape, lambda i: (0, 0), pipeline_mode=pl.Buffered(1))


def attn(where, ends, tok_mine, tok_other, gains, tables, pieces):
    layers = len(pieces)
    rows, width = tok_mine.shape
    local = rows // PLANE
    step = GROUPS_STEP * local
    scalar, block, gain, small, table, wide = attn_specs(step, width, 2 * step)
    high, columns = pieces[0].shape
    weight = (layers * high, columns)
    return pl.pallas_call(
        lambda *refs: attn_kernel(layers, *refs),
        grid=(PLANE // GROUPS_STEP,),
        in_specs=[scalar, scalar, block, block, gain, small, small, table, table]
        + [whole_spec((high, columns))] * layers,
        out_specs=[block, block, wide, wide, table, whole_spec(weight)],
        out_shape=[
            jax.ShapeDtypeStruct((rows, width), bfloat16),
            jax.ShapeDtypeStruct((rows, width), bfloat16),
            jax.ShapeDtypeStruct((2 * rows, 2 * LANES), float32),
            jax.ShapeDtypeStruct((2 * rows, 2 * LANES), bfloat16),
            jax.ShapeDtypeStruct((2 * rows, LANES), bfloat16),
            jax.ShapeDtypeStruct(weight, bfloat16),
        ],
        scratch_shapes=[pltpu.VMEM((2 * step, width), float32)],
        compiler_params=pltpu.CompilerParams(vmem_limit_bytes=VMEM_BYTES),
        cost_estimate=cost(36),
    )(where, ends, tok_mine, tok_other, *gains, *tables, *pieces)


def attn_back(where, ends, tok_mine, tok_other, gains, tables, dh, saved, weight, gain_ffn):
    rows, width = tok_mine.shape
    local = rows // PLANE
    step = GROUPS_STEP * local
    scalar, block, gain, small, table, wide = attn_specs(step, width, 2 * step)
    columns = weight.shape[1]
    return pl.pallas_call(
        attn_back_kernel,
        grid=(PLANE // GROUPS_STEP,),
        in_specs=[scalar, scalar, block, block, gain, small, small, table, table, block, block]
        + [wide, wide, table, whole_spec(weight.shape), gain],
        out_specs=[block, block, whole_spec(weight.shape), whole_spec((GAIN_ROWS, columns))],
        out_shape=[
            jax.ShapeDtypeStruct((rows, width), bfloat16),
            jax.ShapeDtypeStruct((rows, width), bfloat16),
            jax.ShapeDtypeStruct(weight.shape, bfloat16),
            jax.ShapeDtypeStruct((GAIN_ROWS, columns), float32),
        ],
        scratch_shapes=[
            pltpu.VMEM((2 * step, width), float32),
            pltpu.VMEM(weight.shape, float32),
            pltpu.VMEM((1, width), float32),
            pltpu.VMEM((8, LANES), float32),
        ],
        compiler_params=pltpu.CompilerParams(vmem_limit_bytes=VMEM_BYTES),
        cost_estimate=cost(24),
    )(where, ends, tok_mine, tok_other, *gains, *tables, *dh, *saved, weight, gain_ffn)


def ffn_kernel(where_ref, ends_ref, x_o, x_m, g_o, g_m, weight, *refs):
    act_out, d_out, grad_out, total = refs
    step = pl.program_id(0)
    core = where_ref[2]
    both = x_o.shape[1]
    big = both // 2
    local = x_o.shape[0] // 2

    def live_rows(values, group, at_core):
        ids = lax.broadcasted_iota(jnp.int32, values.shape, 0) + at_core * local
        return jnp.where(ids < ends_ref[group, ends_ref.shape[1] - 1], values, jnp.zeros_like(values))

    x = jnp.concatenate([x_o[...], x_m[...]], axis=0)
    grads = jnp.concatenate(
        [live_rows(g_o[k * local : (k + 1) * local, :], 2 * step + k, 1 - core) for k in range(2)]
        + [live_rows(g_m[k * local : (k + 1) * local, :], 2 * step + k, core) for k in range(2)],
        axis=0,
    )
    w_both = weight[:, :both]
    w_down = weight[:, both : both + big]
    w_small = weight[:, both + big : both + big + LANES]
    w_small_down = weight[:, both + big + LANES :]
    lane = lane_ids((x.shape[0], LANES))

    def parts_of(gate, up, d_act):
        sigma = 0.5 * jnp.tanh(0.5 * gate) + 0.5
        silu = gate * sigma
        act = silu * up
        d_gate = d_act * up * sigma * (1.0 + gate * (1.0 - sigma))
        return act, d_gate, d_act * silu

    pre = matmul(x, w_both)
    act, d_gate, d_up = parts_of(pre[:, :big], pre[:, big:], matmul(grads, w_down))
    pre = matmul(x, w_small)
    act_s, d_gate_s, d_up_s = parts_of(
        pre, pltpu.roll(pre, HALF, 1), matmul(grads, w_small_down)
    )
    act_s = jnp.where(lane < HALF, act_s, 0.0).astype(bfloat16)
    d_small = jnp.where(lane < HALF, d_gate_s, pltpu.roll(d_up_s, HALF, 1)).astype(bfloat16)
    act = act.astype(bfloat16)
    d_both = jnp.concatenate([d_gate, d_up], axis=1).astype(bfloat16)

    act_out[:, :big] = act
    act_out[:, big:] = act_s
    d_out[:, :both] = d_both
    d_out[:, both:] = d_small
    spans = (
        (slice(0, both), x, d_both),
        (slice(both, both + big), grads, act),
        (slice(both + big, both + big + LANES), x, d_small),
        (slice(both + big + LANES, total.shape[1]), grads, act_s),
    )

    @pl.when(step == 0)
    def _():
        for span, left, right in spans:
            total[:, span] = matmul_tn(left, right)

    @pl.when(step == 1)
    def _():
        for span, left, right in spans:
            grad_out[:, span] = (total[:, span] + matmul_tn(left, right)).astype(bfloat16)


def ffn_layer(where, ends, x_mine, x_other, g_mine, g_other, weight):
    rows, width = x_mine.shape
    row_spec = pl.BlockSpec((rows // 2, width), lambda i: (i, 0))
    scalar = pl.BlockSpec(memory_space=pltpu.SMEM)
    widths = (width // 2 + LANES, width + LANES)
    return pl.pallas_call(
        ffn_kernel,
        grid=(2,),
        in_specs=[scalar, scalar] + [row_spec] * 4 + [whole_spec(weight.shape)],
        out_specs=[pl.BlockSpec((rows, w), lambda i: (i, 0)) for w in widths]
        + [whole_spec(weight.shape)],
        out_shape=[jax.ShapeDtypeStruct((2 * rows, w), bfloat16) for w in widths]
        + [jax.ShapeDtypeStruct(weight.shape, bfloat16)],
        scratch_shapes=[pltpu.VMEM(weight.shape, float32)],
        compiler_params=pltpu.CompilerParams(vmem_limit_bytes=VMEM_BYTES),
        cost_estimate=cost(48),
    )(where, ends, x_other, x_mine, g_other, g_mine, weight)


def ffn_apply_kernel(values, weight, small, send, keep):
    width = weight.shape[1]
    partial = matmul_nt(values[:, :width], weight[...])
    partial = partial + matmul_nt(values[:, width:], small[...])
    half = send.shape[0]
    send[...] = partial[:half].astype(bfloat16)
    keep[...] = partial[half:].astype(bfloat16)


def ffn_apply(first, last, values, weight):
    rows, width = values.shape[0] // 2, weight.shape[0]
    columns = values.shape[1] - LANES
    row_spec = pl.BlockSpec((rows // 2, width), lambda i: (i, 0))

    def column_spec(start, size):
        return pl.BlockSpec(
            (width, size), lambda i: (0, start // size), pipeline_mode=pl.Buffered(1)
        )

    return pl.pallas_call(
        ffn_apply_kernel,
        grid=(2,),
        in_specs=[
            pl.BlockSpec((rows, values.shape[1]), lambda i: (i, 0)),
            column_spec(first, columns),
            column_spec(last, LANES),
        ],
        out_specs=[row_spec] * 2,
        out_shape=[jax.ShapeDtypeStruct((rows, width), bfloat16)] * 2,
        compiler_params=pltpu.CompilerParams(vmem_limit_bytes=VMEM_BYTES),
        cost_estimate=cost(14),
    )(values, weight, weight)


def chip_sum_kernel(keep, received, *outs):
    rows = outs[0].shape[0]
    for mask, out in enumerate(outs):
        span = slice(mask * rows, (mask + 1) * rows)
        total = keep[span, :].astype(float32) + received[span, :].astype(float32)
        out[...] = total.astype(out.dtype)


def chip_sum(keep, received):
    shape = (keep.shape[0] // PLANE, keep.shape[1])
    outs = [(shape, float32)] + [(shape, bfloat16)] * (PLANE - 1)
    return call(chip_sum_kernel, outs, keep, received)


def plane_sent(parts):
    return [parts[0]] + [send_plane(part, mask + 1) for mask, part in enumerate(parts[1:])]


def plane_total(parts):
    return add_up(plane_sent(parts))


def add_up(parts):
    return sum(part.astype(float32) for part in parts)


def plane_split_kernel(where_ref, own, *refs):
    outs, held = refs[:-1], refs[-1]
    held[...] = own[...].astype(float32)
    place = where_ref[0]
    rows = own.shape[0] // PLANE
    for mask, out in enumerate(outs):
        at = pl.multiple_of((place ^ mask) * rows, rows)
        out[...] = held[pl.ds(at, rows), :].astype(out.dtype)


def plane_split(where, own):
    shape = (own.shape[0] // PLANE, own.shape[1])
    return call(
        plane_split_kernel,
        [(shape, bfloat16)] * PLANE,
        where,
        own,
        scalars=1,
        scratch=[pltpu.VMEM(own.shape, float32)],
    )


def joined_gains(tail):
    return tail[:GAIN_ROWS] + tail[GAIN_ROWS:]


def split_gains(gains):
    top = gains.astype(bfloat16).astype(float32)
    rest = (gains - top).astype(bfloat16).astype(float32)
    return jnp.concatenate([top, rest], axis=0)


def split_attn_kernel(where_ref, own, gains, *refs):
    received, outs = refs[: -PLANE - 2], refs[-PLANE - 2 : -2]
    held, held_gains = refs[-2:]
    layers = len(received) + 1
    depth = where_ref[1]
    for step, part in enumerate((gains,) + received):
        held_gains[deep_rows(depth, -step, layers, GAIN_ROWS), :] = part[...]
    held[...] = own[...].astype(float32)
    sums = held_gains[:GAIN_ROWS, :]
    for layer in range(1, layers):
        sums = sums + held_gains[layer * GAIN_ROWS : (layer + 1) * GAIN_ROWS, :]
    tail = split_gains(sums)
    place = where_ref[0]
    rows = own.shape[0] // PLANE
    for mask, out in enumerate(outs):
        part = held[pl.ds(pl.multiple_of((place ^ mask) * rows, rows), rows), :]
        if mask:
            tall = out.shape[0] - tail.shape[0]
            out[:tall, :] = padded(part, tall).astype(bfloat16)
            out[tall:, :] = tail.astype(bfloat16)
        else:
            out[:rows, :] = part
            out[rows:, :] = tail


def split_attn(where, own, gains, received):
    rows, columns = own.shape[0] // PLANE, own.shape[1]
    tail = 2 * GAIN_ROWS
    shapes = [((rows + tail, columns), float32)]
    shapes += [((max(rows, 16) + tail, columns), bfloat16)] * (PLANE - 1)
    scratch = [
        pltpu.VMEM(own.shape, float32),
        pltpu.VMEM(((len(received) + 1) * GAIN_ROWS, columns), float32),
    ]
    return call(split_attn_kernel, shapes, where, own, gains, *received, scalars=1, scratch=scratch)


def pick_place(refs, place, target, columns, rows):
    value = jnp.zeros((rows, columns.stop - columns.start), float32)
    for mask, ref in enumerate(refs):
        value = jnp.where(place ^ mask == target, ref[:, columns].astype(float32)[:rows], value)
    return value


def place_ffn_kernel(where_ref, own, one, two, three, out_g, out_u, out_d, held):
    place = where_ref[0]
    rows = out_g.shape[0]
    big = out_g.shape[1] // LANES // PLANE * LANES
    last = PLANE * big
    for mask, ref in enumerate((own, one, two, three)):
        held[mask] = ref[...].astype(float32)
        at = pl.ds(pl.multiple_of((place ^ mask) * big, LANES), big)
        for number, out in enumerate((out_g, out_u, out_d)):
            out[:, at] = held[mask, :, number * big : (number + 1) * big]
    for pair in range(PLANE // 2):
        low = held[place ^ (2 * pair), :, 3 * big :]
        high = held[place ^ (2 * pair + 1), :, 3 * big :]
        lane = lane_ids((rows, LANES))
        span = slice(last + pair * LANES, last + (pair + 1) * LANES)
        gu_low, gu_high = low[:, :LANES], high[:, :LANES]
        out_g[:, span] = jnp.where(lane < HALF, gu_low, pltpu.roll(gu_high, HALF, 1))
        out_u[:, span] = jnp.where(lane < HALF, pltpu.roll(gu_low, HALF, 1), gu_high)
        out_d[:, span] = jnp.where(lane < HALF, low[:, LANES:], pltpu.roll(high[:, LANES:], HALF, 1))


def place_attn_kernel(
    where_ref, own, one, two, three, out_q, out_k, out_v, out_o, gain_a, gain_f, gain_q, gain_k
):
    place = where_ref[0]
    refs = (own, one, two, three)
    rows = out_q.shape[0]
    for mask, ref in enumerate(refs):
        at = pl.ds(pl.multiple_of((place ^ mask) * LANES, LANES), LANES)
        out_q[:, at] = ref[:, :LANES].astype(float32)[:rows]
        out_o[:, at] = ref[:, 2 * LANES :].astype(float32)[:rows]
    for pair in range(PLANE // 2):
        low = pick_place(refs, place, 2 * pair, slice(LANES, 2 * LANES), rows)
        high = pick_place(refs, place, 2 * pair + 1, slice(LANES, 2 * LANES), rows)
        lane = lane_ids(low.shape)
        span = slice(pair * LANES, (pair + 1) * LANES)
        out_k[:, span] = jnp.where(lane < HALF, low, pltpu.roll(high, HALF, 1))
        out_v[:, span] = jnp.where(lane < HALF, pltpu.roll(low, HALF, 1), high)
    tails = [joined_gains(ref[ref.shape[0] - 2 * GAIN_ROWS :, :].astype(float32)) for ref in refs]
    sums = (tails[0] + tails[1]) + (tails[2] + tails[3])
    gain_a[...] = sums[:, :LANES]
    gain_f[...] = sums[:, LANES : 2 * LANES]
    pair = sums[:, 2 * LANES :]
    gain_q[...] = pair[:1, :HALF]
    gain_k[...] = pltpu.roll(pair, HALF, 1)[:1, :HALF]


def plane_parts(local):
    return [local] + [send_plane(local, mask) for mask in range(1, PLANE)]


def both_cores(parts):
    mine = jnp.concatenate(parts)
    return mine, swap_cores(mine)


def gather_rows(local):
    return both_cores(plane_parts(local))


def row_tables(lens, slots, total_rows):
    all_lengths = lens.reshape(PLANE, 8, LANES)[:, 0, :slots].astype(jnp.int32)
    ends = jnp.cumsum(all_lengths, axis=1, dtype=jnp.int32)
    row_ids = jnp.arange(total_rows, dtype=jnp.int32)
    begin = jnp.max(
        jnp.where(row_ids[None, :, None] >= ends[:, None, :], ends[:, None, :], 0), axis=2
    )
    position = (row_ids[None, :] - begin).reshape(-1).astype(jnp.float32)
    spread = jnp.arange(LANES, dtype=jnp.int32) % (HEAD_DIM // 2)
    freqs = rope_base ** (-spread.astype(jnp.float32) * 2.0 / HEAD_DIM)
    angles = position[:, None] * freqs[None, :]
    sign = jnp.where(jnp.arange(LANES) % HEAD_DIM < HEAD_DIM // 2, -1.0, 1.0).astype(jnp.float32)
    return ends, (jnp.cos(angles), jnp.sin(angles) * sign)


def body(
    tokens,
    lengths,
    attn_gain,
    query_gain,
    key_gain,
    ffn_gain,
    w_query,
    w_key,
    w_value,
    w_out,
    w_gate,
    w_up,
    w_down,
    cotangent,
):
    dp = lax.axis_index("dp")
    core = lax.axis_index("tensor")
    layers = lax.axis_size("dp") // PLANE
    where = jnp.stack([dp % PLANE, dp // PLANE, core]).astype(jnp.int32)
    local_rows, model = tokens.shape
    total_rows = local_rows * lax.axis_size("tensor")
    rows = w_query.shape[0]
    q_cols = w_query.shape[1] // PLANE
    kv_cols = w_key.shape[1] // PLANE
    local_kv = kv_cols // HEAD_DIM
    share = q_cols // kv_cols
    attn_cols = 2 * q_cols + 2 * kv_cols
    ff_cols = 3 * (w_gate.shape[1] // LANES // PLANE * LANES) + 2 * LANES

    parts, high = attn_rows(rows)
    tall = max(rows, 16)
    first = call(
        pack_attn_kernel,
        [((high, model), bfloat16)] * PLANE,
        where,
        lengths,
        w_query,
        w_key,
        w_value,
        w_out,
        scalars=2,
    )
    second = call(
        pack_ffn_kernel,
        [((tall, ff_cols), bfloat16)] * PLANE,
        where,
        w_gate,
        w_up,
        w_down,
        scalars=1,
    )
    first = after(second, [first[0]] + [send_plane(first[m], m) for m in range(1, PLANE)])
    attn_piece, lens = call(
        unpack_attn_kernel,
        [((PLANE * rows, attn_cols), bfloat16), ((PLANE * 8, LANES), float32)],
        where,
        *first,
        scalars=1,
        scratch=[pltpu.VMEM((PLANE * rows, attn_cols), float32)],
    )
    attn_pieces = [attn_piece] + [send_deep(attn_piece, step) for step in range(1, layers)]
    second = after(first, second)
    second = [second[0]] + [send_plane(second[m], m) for m in range(1, PLANE)]
    ends, tables = row_tables(lens, lengths.shape[1], total_rows)
    second = after((attn_pieces, tables), second)
    (ff_piece,) = call(
        unpack_ffn_kernel,
        [((PLANE * rows, ff_cols), bfloat16)],
        where,
        *second,
        scalars=1,
        scratch=[pltpu.VMEM((PLANE * rows, ff_cols), float32)],
    )
    columns = [list(range(k, layers * PLANE, PLANE)) for k in range(PLANE)]
    ff_weight = lax.all_gather(ff_piece, "dp", axis=0, tiled=True, axis_index_groups=columns)
    attn_pieces = after(ff_piece, attn_pieces)
    tok_parts = plane_parts(after(ff_piece, tokens))
    cot_parts = plane_parts(after(tok_parts, cotangent))
    tok_mine, tok_other = both_cores(tok_parts)
    cot_mine, cot_other = both_cores(cot_parts)

    gains = (
        attn_gain[None, :],
        jnp.concatenate([query_gain, query_gain])[None, :],
        jnp.concatenate([key_gain, key_gain])[None, :],
    )

    inputs = tokens.astype(jnp.float32)
    factor_a = inverse_rms(inputs)
    unit_a = inputs * factor_a
    send, keep, *saved, attn_weight = attn(
        where, ends, tok_mine, tok_other, gains, tables, attn_pieces
    )
    send = after(cot_parts, send)
    hidden = inputs + plane_total(chip_sum(keep, swap_cores(send)))
    factor_b = inverse_rms(hidden)
    unit_b = hidden * factor_b
    x_mine, x_other = gather_rows((unit_b * ffn_gain).astype(jnp.bfloat16))

    act, d_both, ff_grad = ffn_layer(
        where, ends, x_mine, x_other, cot_mine, cot_other, ff_weight
    )
    own_ff = lax.psum_scatter(
        ff_grad, "dp", scatter_dimension=0, tiled=True, axis_index_groups=columns
    )
    dn_send, dn_keep = ffn_apply(0, ff_cols - 2 * LANES, d_both, ff_weight)
    dn_parts = plane_sent(chip_sum(dn_keep, swap_cores(dn_send)))
    out_send, out_keep = ffn_apply(model, ff_cols - LANES, after(dn_send, act), ff_weight)
    d_normed2 = add_up(after(out_send, dn_parts))
    grad_out = jnp.where(
        (jnp.arange(local_rows) + core * local_rows < ends[0, lengths.shape[1] - 1])[:, None],
        cotangent,
        jnp.zeros_like(cotangent),
    )
    gain_ffn = jnp.sum(d_normed2 * unit_b, axis=0)
    d_hidden = grad_out.astype(jnp.float32) + norm_back(d_normed2 * ffn_gain, unit_b, factor_b)
    h_mine, h_other = gather_rows(d_hidden.astype(jnp.bfloat16))
    out_parts = chip_sum(out_keep, swap_cores(out_send))
    out_parts = after((h_mine, h_other), out_parts)
    out_parts = plane_sent(out_parts)
    block_out = (hidden + add_up(out_parts)).astype(jnp.bfloat16)

    send, keep, attn_grad, part_gains = after(
        out_parts,
        attn_back(
            where, ends, tok_mine, tok_other, gains, tables, (h_mine, h_other), saved,
            attn_weight, gain_ffn[None, :],
        ),
    )
    own_attn = lax.psum_scatter(
        attn_grad, "dp", scatter_dimension=0, tiled=True, axis_index_groups=columns
    )
    ff_parts = plane_split(where, own_ff)
    keep = after(ff_parts, keep)
    ff_parts = plane_sent(ff_parts)
    dn_parts = chip_sum(keep, swap_cores(send))
    part_gains = after(dn_parts, part_gains + swap_cores(part_gains))
    dn_parts = plane_sent(after(ff_parts[1], dn_parts))
    far_gains = [send_deep(part_gains, step) for step in range(1, layers)]
    own_attn = after((dn_parts[1], block_out, far_gains), own_attn)
    attn_parts = plane_sent(split_attn(where, own_attn, part_gains, far_gains))
    d_normed = add_up(dn_parts)
    grad_tokens = d_hidden + norm_back(d_normed * attn_gain, unit_a, factor_a)
    grad_gate, grad_up, grad_down = call(
        place_ffn_kernel,
        [(w_gate.shape, float32)] * 3,
        where,
        *ff_parts,
        scalars=1,
        scratch=[pltpu.VMEM((PLANE, rows, ff_cols), float32)],
    )
    grad_query, grad_key, grad_value, grad_out_w, *sums = call(
        place_attn_kernel,
        [(w.shape, float32) for w in (w_query, w_key, w_value, w_out)]
        + [((GAIN_ROWS, LANES), float32)] * 2
        + [((1, HEAD_DIM), float32)] * 2,
        where,
        *attn_parts,
        scalars=1,
    )
    return (
        block_out,
        grad_tokens,
        sums[0].reshape(-1),
        sums[2].reshape(-1),
        sums[3].reshape(-1),
        sums[1].reshape(-1),
        grad_query,
        grad_key,
        grad_value,
        grad_out_w,
        grad_gate,
        grad_up,
        grad_down,
    )


def solution(mesh):
    placed = (
        P(("dp", "tensor"), None),
        P("dp", None),
        P(),
        P(),
        P(),
        P(),
        P("dp", "tensor"),
        P("dp", "tensor"),
        P("dp", "tensor"),
        P("dp", "tensor"),
        P("dp", "tensor"),
        P("dp", "tensor"),
        P("dp", "tensor"),
        P(("dp", "tensor"), None),
    )
    return jax.shard_map(
        body,
        mesh=mesh,
        in_specs=placed,
        out_specs=(
            P(("dp", "tensor"), None),
            P(("dp", "tensor"), None),
            P(),
            P(),
            P(),
            P(),
            P("dp", "tensor"),
            P("dp", "tensor"),
            P("dp", "tensor"),
            P("dp", "tensor"),
            P("dp", "tensor"),
            P("dp", "tensor"),
            P("dp", "tensor"),
        ),
        check_vma=False,
    )
```
